32 devices in a mesh: dp: 8 (over y, x, core), expert: 4 (over z).
Axes of the slice: x: 2, y: 2, z: 4, core: 2. Of those that a mesh axis runs over, the one named last changes fastest.
Arguments:
- image_tokens: bfloat16 [6304, 768], P(('dp', 'expert')), may hold values from -6 to 6
- norm_gains: float32 [2, 2, 768], P(None, None, 'dp'), may hold values from 0.5 to 1.5
- biases: float32 [2, 5, 768], P(None, None, 'dp'), may hold values from -2 to 2
- w_qkv: bfloat16 [2, 768, 2304], P(None, 'dp'), may hold values from -0.21875 to 0.21875
- w_out: bfloat16 [2, 768, 768], P(None, 'dp'), may hold values from -1.25 to 1.25
- w_router: float32 [2, 768, 4], P(None, 'dp'), may hold values from -0.15625 to 0.15625
- router_noise: float32 [2, 6304, 4], P(None, ('dp', 'expert')), may hold values from -3 to 3
- w_in: bfloat16 [2, 4, 768, 3072], P(None, 'expert', 'dp'), may hold values from -0.21875 to 0.21875
- b_in: float32 [2, 4, 3072], P(None, 'expert', 'dp'), may hold values from -2 to 2
- w_outexp: bfloat16 [2, 4, 3072, 768], P(None, 'expert', 'dp'), may hold values from -0.625 to 0.625
- b_expout: float32 [2, 4, 768], P(None, 'expert', 'dp'), may hold values from -3.2 to 3.2
- routes: int32 [2, 6304, 2], P(None, ('dp', 'expert')), may hold values from 0 to 3, all different within a row
- seat_order: int32 [2, 32, 394], P(None, ('dp', 'expert')), may hold values from 0 to 393, each once within a row
- cotangent: bfloat16 [6304, 768], P(('dp', 'expert')), may hold values from -6 to 6
Outputs:
- mixed: float32 [6304, 768], P(('dp', 'expert'))
- grad_tokens: float32 [6304, 768], P(('dp', 'expert'))
- grad_gains: float32 [2, 2, 768], P(None, None, 'dp')
- grad_biases: float32 [2, 5, 768], P(None, None, 'dp')
- grad_qkv: float32 [2, 768, 2304], P(None, 'dp')
- grad_out: float32 [2, 768, 768], P(None, 'dp')
- grad_router: float32 [2, 768, 4], P(None, 'dp')
- grad_in: float32 [2, 4, 768, 3072], P(None, 'expert', 'dp')
- grad_in_bias: float32 [2, 4, 3072], P(None, 'expert', 'dp')
- grad_outexp: float32 [2, 4, 3072, 768], P(None, 'expert', 'dp')
- grad_expout_bias: float32 [2, 4, 768], P(None, 'expert', 'dp')
The draws below stay inside these ranges and needn't reach their ends.
Inputs may be any that keep to these rules, and one draw needn't show every extreme that they name: `routes`: the two experts of a token differ, and every expert is named by some token. `seat_order`: each device's row of 394 numbers holds each number once.
All inputs are finite; a program needn't handle non-finite values.
Results may differ from the reference program's by a relative error of at most 0.035.
Values may be sent and summed in bfloat16 or wider, within the bound.
No kernel may reach another device: no remote copies, remote signals or barrier semaphores. Data moves between devices by JAX's collectives and lax.ppermute only.
A program may use at most 192 MiB of HBM per device.

```python
import jax
import jax.numpy as jnp
from jax import lax

D = 768
HEADS = 12
HEAD_DIM = 64
FF = 3072
SEQ = 197
LAYERS = 2
TOK_DEV = 197
TOKENS = 6304
EXPERTS = 4
PAIRS = 394
CAP = 98
DEVICES = 32


def block_scale(own_key, extent, shards, low, top_value):
    level = 1.0
    for position, shards_of in shards:
        heights = jax.random.uniform(jax.random.fold_in(jax.random.fold_in(own_key, 6), position), (shards_of,), jnp.float32, low / len(shards), top_value / len(shards))
        level = level * jnp.repeat(jnp.exp(heights), extent[position] // shards_of).reshape((-1,) + (1,) * (len(extent) - 1 - position))
    return level


def choose_distinct(key, rows, number_of, top, lift):
    sequence = jax.random.permutation(jax.random.fold_in(key, 1), number_of)
    boost = sequence
    for power in range(3):
        boost = boost * boost // number_of
    boost = boost * lift // number_of
    lots = jax.random.randint(jax.random.fold_in(key, 2), (rows, number_of), 0, 4096) + boost
    holders = jax.random.permutation(jax.random.fold_in(key, 3), rows)[jnp.arange(number_of) % rows]
    lots = jnp.where(jnp.arange(rows)[:, None] == holders[None, :], 1 << 14, lots)
    merit = lots * number_of + jnp.arange(number_of)
    return lax.top_k(merit.astype(jnp.int32), top)[1].astype(jnp.int32)


def scatter_about(stream_key, shape, spread, limit, shards=(), kind=jnp.bfloat16):
    factor_of = block_scale(stream_key, shape, shards, -0.22, 0.18) if shards else 1.0
    entries = jax.random.normal(stream_key, shape, jnp.float32) * spread * factor_of
    return jnp.minimum(jnp.maximum(entries, -limit), limit).astype(kind)


def setup_inputs(seed: int = 0) -> dict:
    key_of = jax.random.split(jax.random.key(seed), 15)
    return {
        "image_tokens": scatter_about(key_of[0], (TOKENS, D), 1.0, 6.0, ((0, 32),)),
        "norm_gains": jnp.clip(1.0 + 0.1 * jax.random.normal(key_of[1], (LAYERS, 2, D), jnp.float32), 0.5, 1.5),
        "biases": scatter_about(key_of[2], (LAYERS, 5, D), 0.3, 2.0, ((2, 8),), jnp.float32),
        "w_qkv": scatter_about(key_of[3], (LAYERS, D, 3 * D), D ** -0.5, 0.21875, ((1, 8),)),
        "w_out": scatter_about(key_of[4], (LAYERS, D, D), (D // 32) ** -0.5, 1.25, ((1, 8),)),
        "w_router": scatter_about(key_of[5], (LAYERS, D, EXPERTS), (2 * D) ** -0.5, 0.15625, ((1, 8),), jnp.float32),
        "router_noise": scatter_about(key_of[6], (LAYERS, TOKENS, EXPERTS), 0.5, 3.0, ((1, 32),), jnp.float32),
        "w_in": scatter_about(key_of[7], (LAYERS, EXPERTS, D, FF), D ** -0.5, 0.21875, ((1, 4), (2, 8))),
        "b_in": scatter_about(key_of[8], (LAYERS, EXPERTS, FF), 0.3, 2.0, ((1, 4), (2, 8)), jnp.float32),
        "w_outexp": scatter_about(key_of[9], (LAYERS, EXPERTS, FF, D), (FF // 32) ** -0.5, 0.625, ((1, 4), (2, 8))),
        "b_expout": scatter_about(key_of[10], (LAYERS, EXPERTS, D), 0.8, 3.2, ((1, 4), (2, 8)), jnp.float32),
        "routes": choose_distinct(key_of[11], LAYERS * TOKENS, EXPERTS, 2, 4096).reshape((LAYERS, TOKENS, 2)),
        "seat_order": jax.vmap(lambda own: jax.random.permutation(own, PAIRS))(jax.random.split(key_of[12], LAYERS * DEVICES)).reshape((LAYERS, DEVICES, PAIRS)).astype(jnp.int32),
        "cotangent": scatter_about(key_of[13], (TOKENS, D), 1.0, 6.0, ((0, 32),)),
    }


EPS = 1e-06
HIGH = lax.Precision.HIGHEST

@jax.custom_vjp
def low(v):
    return lax.optimization_barrier(v.astype(jnp.bfloat16)).astype(jnp.float32)

@jax.custom_vjp
def low_back(v):
    return v

def low_keep(v):
    return (low(v), None)

def low_pass(kept, grad):
    return (grad,)

def back_keep(v):
    return (v, None)

def back_low(kept, grad):
    return (low(grad),)
low.defvjp(low_keep, low_pass)
low_back.defvjp(back_keep, back_low)

def layer_norm(x, gain, shift):
    centered = x - lax.optimization_barrier(jnp.mean(x, -1, keepdims=True))
    rstd = lax.rsqrt(lax.optimization_barrier(jnp.mean(centered * centered, -1, keepdims=True)) + EPS)
    return centered * rstd * gain + shift

def seat_pairs(pair_expert, seat_rows):
    count = pair_expert.shape[0]
    inverse = jnp.zeros((count,), jnp.int32).at[seat_rows].set(jnp.arange(count, dtype=jnp.int32))
    sorted_expert = pair_expert[inverse]
    onehot = (sorted_expert[:, None] == jnp.arange(EXPERTS, dtype=jnp.int32)[None, :]).astype(jnp.int32)
    before = jnp.cumsum(onehot, 0) - onehot
    rank = lax.optimization_barrier(jnp.sum(before * onehot, 1))[seat_rows]
    valid = rank < CAP
    slot = jnp.where(valid, pair_expert * CAP + rank, EXPERTS * CAP).astype(jnp.int32)
    pair_token = (jnp.arange(count, dtype=jnp.int32) // 2).astype(jnp.int32)
    slot_token = jnp.zeros((EXPERTS * CAP,), jnp.int32).at[slot].set(pair_token, mode='drop')
    slot_used = jnp.zeros((EXPERTS * CAP,), jnp.float32).at[slot].set(1.0, mode='drop')
    return (jnp.minimum(slot, EXPERTS * CAP - 1), valid, slot_token, slot_used)

def attention_block(x, gain, shift, w_qkv, w_out, bias_q, bias_v, bias_out):
    images = x.shape[0]
    a = low(layer_norm(x, gain, shift))
    qkv = jnp.einsum('bsd,de->bse', a, w_qkv, precision=HIGH)
    qkv = qkv + jnp.concatenate([bias_q, jnp.zeros_like(bias_q), bias_v])
    qkv = low(low_back(qkv)).reshape(images, SEQ, 3, HEADS, HEAD_DIM)
    query, keys, values = (qkv[:, :, 0], qkv[:, :, 1], qkv[:, :, 2])
    scores = low_back(jnp.einsum('bqhd,bkhd->bhqk', query, keys, precision=HIGH) * HEAD_DIM ** (-0.5))
    probs = low(jax.nn.softmax(scores, -1))
    mixed = jnp.einsum('bhqk,bkhd->bqhd', probs, values, precision=HIGH).reshape(images, SEQ, D)
    mixed = low(low_back(mixed))
    branch = low_back(jnp.einsum('bsd,de->bse', mixed, w_out, precision=HIGH) + bias_out)
    return x + branch

def attention_step(gains, biases, w_qkv, w_out, layer):

    def step(block):
        return attention_block(block, gains[layer, 0], biases[layer, 0], w_qkv[layer], w_out[layer], biases[layer, 2], biases[layer, 3], biases[layer, 4])
    return jax.checkpoint(step)

def expert_rows(operands):
    rows, weight_in, bias_in, weight_out, bias_out = operands
    pre = low_back(jnp.dot(rows, weight_in, precision=HIGH) + bias_in)
    hidden = low(jax.nn.gelu(pre))
    return low(low_back(jnp.dot(hidden, weight_out, precision=HIGH) + bias_out))

def take_rows(rows, index):
    return rows[index]

def moe_block(x1, gain, shift, w_router, w_in, b_in, w_oe, b_oe, noise, route_rows, seat_rows):
    moe_in = layer_norm(x1, gain, shift)
    gates = jax.nn.softmax(jnp.dot(moe_in, w_router, precision=HIGH) + noise, -1)
    pair_gate = jnp.take_along_axis(gates, route_rows, 1)
    slot, valid, slot_token, slot_used = jax.vmap(seat_pairs)(route_rows.reshape(DEVICES, PAIRS), seat_rows)
    rows_low = low(moe_in).reshape(DEVICES, TOK_DEV, D)
    buffers = jax.vmap(take_rows)(rows_low, slot_token) * slot_used[:, :, None]
    buffers = low_back(buffers)
    per_expert = buffers.reshape(DEVICES, EXPERTS, CAP, D).transpose(1, 0, 2, 3).reshape(EXPERTS, DEVICES * CAP, D)
    outs = lax.map(jax.checkpoint(expert_rows), (per_expert, w_in, b_in, w_oe, b_oe))
    back = outs.reshape(EXPERTS, DEVICES, CAP, D).transpose(1, 0, 2, 3).reshape(DEVICES, EXPERTS * CAP, D)
    pieces = jax.vmap(take_rows)(back, slot).reshape(TOKENS, 2, D)
    weight = jnp.where(valid.reshape(TOKENS, 2), pair_gate, 0.0)
    return x1 + lax.optimization_barrier(jnp.sum(weight[:, :, None] * pieces, 1))

def forward(tokens, gains, biases, w_qkv, w_out, w_router, w_in, b_in, w_oe, b_oe, noise, routes, seats):
    state = tokens
    for layer in range(LAYERS):
        groups = state.reshape(-1, 16, SEQ, D)
        state = lax.map(attention_step(gains, biases, w_qkv, w_out, layer), groups).reshape(TOKENS, D)
        state = moe_block(state, gains[layer, 1], biases[layer, 1], w_router[layer], w_in[layer], b_in[layer], w_oe[layer], b_oe[layer], noise[layer], routes[layer], seats[layer])
    return state

def reference(image_tokens, norm_gains, biases, w_qkv, w_out, w_router, router_noise, w_in, b_in, w_outexp, b_expout, routes, seat_order, cotangent):

    def run(tokens, gains, shifts, wide_qkv, wide_out, router, wide_in, bias_in, wide_oe, bias_oe):
        return forward(tokens, gains, shifts, wide_qkv, wide_out, router, wide_in, bias_in, wide_oe, bias_oe, router_noise, routes, seat_order)
    mixed, pull = jax.vjp(run, image_tokens.astype(jnp.float32), norm_gains, biases, w_qkv.astype(jnp.float32), w_out.astype(jnp.float32), w_router, w_in.astype(jnp.float32), b_in, w_outexp.astype(jnp.float32), b_expout)
    grads = pull(cotangent.astype(jnp.float32))
    return (mixed, grads[0], grads[1], grads[2], grads[3], grads[4], grads[5], grads[6], grads[7], grads[8], grads[9])
```

```python
import functools

import jax
import jax.numpy as jnp
from jax import lax
from jax.experimental import pallas as pl
from jax.experimental.pallas import tpu as pltpu
from jax.sharding import PartitionSpec as P

HEADS = 12
HEAD_DIM = 64
SEQ = 197
EPS = 1e-06
BF = jnp.bfloat16
F32 = jnp.float32
LANES = 128
NEG = -1e30
VMEM_LIMIT = 60 * 1024 * 1024


def up(value, step):
    return -(-value // step) * step


def dot(left, right):
    return lax.dot_general(left, right, (((1,), (0,)), ((), ())), preferred_element_type=F32)


def dot_nt(left, right):
    return lax.dot_general(left, right, (((1,), (1,)), ((), ())), preferred_element_type=F32)


def dot_tn(left, right):
    return lax.dot_general(left, right, (((0,), (0,)), ((), ())), preferred_element_type=F32)


def norm_rows(x):
    centered = x - jnp.mean(x, -1, keepdims=True)
    rstd = lax.rsqrt(jnp.mean(centered * centered, -1, keepdims=True) + EPS)
    return centered * rstd, rstd


def norm_back(grad_hat, normed, rstd):
    return rstd * (
        grad_hat
        - jnp.mean(grad_hat, -1, keepdims=True)
        - normed * jnp.mean(grad_hat * normed, -1, keepdims=True)
    )


def split(value):
    high = value.astype(BF)
    return high, (value - high.astype(F32)).astype(BF)


def join(refs):
    return jnp.concatenate([ref[...].astype(F32) for ref in refs], 0).astype(BF)


def part(value, refs):
    rows = refs[0].shape[0]
    for number, ref in enumerate(refs):
        ref[...] = value[number * rows : (number + 1) * rows].astype(ref.dtype)


def seat_mask(cols_ref, pair, seats):
    column = cols_ref[:, pair : pair + 1]
    return lax.broadcasted_iota(jnp.int32, (column.shape[0], seats), 1) == column


def token_mask(rows_ref, pair, seats):
    row = rows_ref[pair : pair + 1, :]
    return lax.broadcasted_iota(jnp.int32, (seats, row.shape[1]), 0) == row


def one(mask):
    return jnp.where(mask, 1.0, 0.0).astype(BF)


def pair_gate(gates, cols_ref, pair):
    route = cols_ref[:, 2 + pair : 3 + pair]
    lanes = lax.broadcasted_iota(jnp.int32, gates.shape, 1)
    return jnp.sum(jnp.where(lanes == route, gates, 0.0), -1, keepdims=True)


def combine(x1, gates, cols_ref, returned):
    total = x1
    for pair in range(2):
        piece = dot(one(seat_mask(cols_ref, pair, returned.shape[0])), returned)
        total = total + pair_gate(gates, cols_ref, pair) * piece
    return total


def seat_grads(grad, gates, cols_ref, rows_ref, seats):
    total = None
    for pair in range(2):
        scaled = (pair_gate(gates, cols_ref, pair) * grad).astype(BF)
        piece = dot(one(token_mask(rows_ref, pair, seats)), scaled)
        total = piece if total is None else total + piece
    return total


def head_masks():
    lanes = lax.broadcasted_iota(jnp.int32, (1, 2 * HEAD_DIM), 1)
    return (lanes < HEAD_DIM, lanes >= HEAD_DIM)


def head_probs(query, keys, mask, tokens):
    query = jnp.where(mask, query, 0).astype(F32) * HEAD_DIM ** (-0.5)
    scores = dot_nt(query.astype(BF), keys)
    lanes = lax.broadcasted_iota(jnp.int32, scores.shape, 1)
    scores = jnp.where(lanes < tokens, scores, NEG)
    raised = jnp.exp(scores - jnp.max(scores, -1, keepdims=True))
    return raised * (1.0 / jnp.sum(raised, -1, keepdims=True))


class Blocks:
    def __init__(self, arrays, offsets):
        self.arrays, self.offsets = arrays, offsets


def fetch_plan(refs, offsets, me, targets, sems, first):
    copies = []
    number = first
    for ref, offs in zip(refs, offsets):
        rows = ref.shape[1]
        for k, off in enumerate(offs):
            place = 0 if off is None else pl.multiple_of((me ^ off) * rows, rows)
            for scratch, start, width, into in targets:
                copies.append(
                    pltpu.make_async_copy(
                        ref.at[k, :, pl.ds(start, width)],
                        scratch.at[pl.ds(place, rows), pl.ds(into, width)],
                        sems.at[number],
                    )
                )
                number += 1
    return copies


def spread_plan(scratch, outs, offsets, me, sems, first, columns):
    copies = []
    number = first
    start, width = columns
    for out, offs in zip(outs, offsets):
        rows = out.shape[1]
        for k, off in enumerate(offs):
            place = 0 if off is None else pl.multiple_of((me ^ off) * rows, rows)
            copies.append(
                pltpu.make_async_copy(
                    scratch.at[pl.ds(place, rows), pl.ds(start, width)],
                    out.at[k],
                    sems.at[number],
                )
            )
            number += 1
    return copies


def count(offsets):
    return sum(len(offs) for offs in offsets)


VM = pl.BlockSpec(memory_space=pltpu.VMEM)
ANY = pl.BlockSpec(memory_space=pl.ANY)
SM = pl.BlockSpec(memory_space=pltpu.SMEM)


def call(kernel, name, args, specs, outs, out_specs, scratch, flops, moved):
    return pl.pallas_call(
        kernel,
        name=name,
        in_specs=specs,
        out_specs=out_specs,
        out_shape=outs,
        scratch_shapes=scratch,
        compiler_params=pltpu.CompilerParams(vmem_limit_bytes=VMEM_LIMIT),
        cost_estimate=pl.CostEstimate(flops=flops, bytes_accessed=moved, transcendentals=0),
    )(*args)


def sds(shape, dtype):
    return jax.ShapeDtypeStruct(shape, dtype)


def attn_fwd(me, first, x_args, a_blocks, b_blocks, vecs, router, noise, cols, rows, tokens, cap_pad):
    padded, width = noise.shape[0], vecs.shape[1]
    owners = len(x_args[3]) if not first else None
    experts = noise_experts = cap_pad[1]
    cap = cap_pad[0]
    seats = experts * cap
    na, nb = len(a_blocks.arrays), len(b_blocks.arrays)
    half = 2 * width
    total = count(a_blocks.offsets) + 2 * count(b_blocks.offsets)

    def kernel(*refs):
        refs = list(refs)
        me_ref = refs.pop(0)
        if first:
            tok_ref = refs.pop(0)
        else:
            below_x1, below_gates, below_cols = refs.pop(0), refs.pop(0), refs.pop(0)
            below_blocks = [refs.pop(0) for _ in range(owners)]
        a_refs = [refs.pop(0) for _ in range(na)]
        b_refs = [refs.pop(0) for _ in range(nb)]
        vec_ref, router_ref, noise_ref, cols_ref, rows_ref = (refs.pop(0) for _ in range(5))
        x_out, x1_out, a_out, qkv_out, o_out, gates_out, m_out = (refs.pop(0) for _ in range(7))
        seat_outs = [refs.pop(0) for _ in range(experts)]
        wqkv, wout, sems = refs
        index = me_ref[0]
        copies_a = fetch_plan(a_refs, a_blocks.offsets, index, [(wqkv, 0, half, 0)], sems, 0)
        copies_b = fetch_plan(
            b_refs,
            b_blocks.offsets,
            index,
            [(wqkv, 0, width, half), (wout, width, width, 0)],
            sems,
            len(copies_a),
        )
        for copy in copies_a + copies_b:
            copy.start()
        vec = lambda k: vec_ref[k : k + 1, :]
        if first:
            x_out[...] = jnp.zeros_like(x_out)
            x_out[0:tokens, :] = tok_ref[...].astype(F32)
            x = x_out[...]
        else:
            x = combine(below_x1[...], below_gates[...], below_cols, join(below_blocks))
            x_out[...] = x
        normed, rstd = norm_rows(x)
        a_low = (normed * vec(0) + vec(2)).astype(BF)
        a_out[...] = a_low
        for copy in copies_a + copies_b:
            copy.wait()
        for k in range(3):
            piece = dot(a_low, wqkv[:, k * width : (k + 1) * width])
            if k == 0:
                piece = piece + vec(4)
            if k == 2:
                piece = piece + vec(5)
            qkv_out[:, k * width : (k + 1) * width] = piece.astype(BF)
        masks = head_masks()
        for two in range(HEADS // 2):
            at = two * 2 * HEAD_DIM
            query = qkv_out[:, at : at + 2 * HEAD_DIM]
            keys = qkv_out[:, width + at : width + at + 2 * HEAD_DIM]
            values = qkv_out[:, 2 * width + at : 2 * width + at + 2 * HEAD_DIM]
            mixed = None
            for mask in masks:
                probs = head_probs(query, keys, mask, tokens).astype(BF)
                piece = dot(probs, jnp.where(mask, values, 0).astype(BF))
                mixed = piece if mixed is None else mixed + piece
            o_out[:, at : at + 2 * HEAD_DIM] = mixed.astype(BF)
        x1 = x + dot(o_out[...], wout[...]) + vec(6)
        x1_out[...] = x1
        normed2, rstd2 = norm_rows(x1)
        moe = normed2 * vec(1) + vec(3)
        high, low = split(moe)
        logits = dot(high, router_ref[...]) + dot(low, router_ref[...]) + noise_ref[...]
        lanes = lax.broadcasted_iota(jnp.int32, logits.shape, 1)
        logits = jnp.where(lanes < experts, logits, NEG)
        raised = jnp.exp(logits - jnp.max(logits, -1, keepdims=True))
        gates_out[...] = raised / jnp.sum(raised, -1, keepdims=True)
        m_out[...] = high
        chosen = jnp.logical_or(token_mask(rows_ref, 0, seats), token_mask(rows_ref, 1, seats))
        part(dot(one(chosen), high), seat_outs)

    args = [me]
    specs = [SM]
    if first:
        args += [x_args[0]]
        specs += [VM]
    else:
        args += [x_args[0], x_args[1], x_args[2], *x_args[3]]
        specs += [VM] * (3 + owners)
    args += [*a_blocks.arrays, *b_blocks.arrays, vecs, router, noise, cols, rows]
    specs += [ANY] * (na + nb) + [VM] * 5
    outs = [
        sds((padded, width), F32),
        sds((padded, width), F32),
        sds((padded, width), BF),
        sds((padded, 3 * width), BF),
        sds((padded, width), BF),
        sds((padded, LANES), F32),
        sds((padded, width), BF),
    ] + [sds((cap, width), BF)] * experts
    result = call(
        kernel,
        "attn_fwd",
        args,
        specs,
        outs,
        [VM] * len(outs),
        [
            pltpu.VMEM((width, 3 * width), BF),
            pltpu.VMEM((width, width), BF),
            pltpu.SemaphoreType.DMA((total,)),
        ],
        flops=4 * 2 * padded * width * width * 4,
        moved=20 << 20,
    )
    return result[:7], result[7:]


def expert_fwd(me, seat_blocks, in_blocks, oe_blocks, bias_in, bias_oe):
    owners = len(seat_blocks)
    cap, width = seat_blocks[0].shape
    seats = owners * cap
    hidden = bias_in.shape[1]
    ni, no = len(in_blocks.arrays), len(oe_blocks.arrays)
    total = count(in_blocks.offsets) + count(oe_blocks.offsets)
    step = width

    def kernel(*refs):
        refs = list(refs)
        me_ref = refs.pop(0)
        seat_refs = [refs.pop(0) for _ in range(owners)]
        in_refs = [refs.pop(0) for _ in range(ni)]
        oe_refs = [refs.pop(0) for _ in range(no)]
        bin_ref, boe_ref = refs.pop(0), refs.pop(0)
        rows_out, h_out, slope_out = refs.pop(0), refs.pop(0), refs.pop(0)
        outs = [refs.pop(0) for _ in range(owners)]
        win, woe, sems = refs
        index = me_ref[0]
        copies_in = fetch_plan(in_refs, in_blocks.offsets, index, [(win, 0, hidden, 0)], sems, 0)
        copies_oe = fetch_plan(
            oe_refs, oe_blocks.offsets, index, [(woe, 0, width, 0)], sems, len(copies_in)
        )
        for copy in copies_in + copies_oe:
            copy.start()
        rows = join(seat_refs)
        rows_out[...] = rows
        for copy in copies_in:
            copy.wait()
        total_out = None
        for at in range(0, hidden, step):
            pre = dot(rows, win[:, at : at + step]) + bin_ref[:, at : at + step]
            square = pre * pre
            bend = jnp.tanh(0.7978845608028654 * (pre + 0.044715 * square * pre))
            h = (0.5 * pre * (1.0 + bend)).astype(BF)
            slope = 0.5 * (1.0 + bend) + 0.5 * pre * (1.0 - bend * bend) * (
                0.7978845608028654 * (1.0 + 0.134145 * square)
            )
            h_out[:, at : at + step] = h
            slope_out[:, at : at + step] = slope.astype(BF)
            if at == 0:
                for copy in copies_oe:
                    copy.wait()
            piece = dot(h, woe[at : at + step, :])
            total_out = piece if total_out is None else total_out + piece
        part(total_out + boe_ref[...], outs)

    shapes = [
        sds((seats, width), BF),
        sds((seats, hidden), BF),
        sds((seats, hidden), BF),
    ] + [sds((cap, width), BF)] * owners
    result = call(
        kernel,
        "expert_fwd",
        [me, *seat_blocks, *in_blocks.arrays, *oe_blocks.arrays, bias_in, bias_oe],
        [SM] + [VM] * owners + [ANY] * (ni + no) + [VM] * 2,
        shapes,
        [VM] * len(shapes),
        [
            pltpu.VMEM((width, hidden), BF),
            pltpu.VMEM((hidden, width), BF),
            pltpu.SemaphoreType.DMA((total,)),
        ],
        flops=8 * seats * width * hidden,
        moved=20 << 20,
    )
    return result[:3], result[3:]


def top_seats(cotangent, gates, cols, rows, seats, tokens, experts):
    padded, width = cols.shape[0], cotangent.shape[1]

    def kernel(cot_ref, gates_ref, cols_ref, rows_ref, grad_out, *outs):
        grad_out[...] = jnp.zeros_like(grad_out)
        grad_out[0:tokens, :] = cot_ref[...].astype(F32)
        part(seat_grads(grad_out[...], gates_ref[...], cols_ref, rows_ref, seats), outs)

    shapes = [sds((padded, width), F32)] + [sds((seats // experts, width), BF)] * experts
    result = call(
        kernel,
        "top_seats",
        [cotangent, gates, cols, rows],
        [VM] * 4,
        shapes,
        [VM] * len(shapes),
        [],
        flops=4 * seats * padded * width,
        moved=4 << 20,
    )
    return result[0], result[1:]


def gate_back(grad, x1, gates, cols, router, returned, tokens, last):
    padded, width = grad.shape
    owners = len(returned)

    def kernel(*refs):
        refs = list(refs)
        grad_ref = refs.pop(0)
        x1_ref = refs.pop(0) if last else None
        gates_ref, cols_ref, router_ref = (refs.pop(0) for _ in range(3))
        blocks = [refs.pop(0) for _ in range(owners)]
        dz_out, moe_out = refs.pop(0), refs.pop(0)
        back = join(blocks)
        grad_here = grad_ref[...]
        gates_here = gates_ref[...]
        lanes = lax.broadcasted_iota(jnp.int32, gates_here.shape, 1)
        d_gates = jnp.zeros_like(gates_here)
        mixed = x1_ref[...] if last else None
        for pair in range(2):
            piece = dot(one(seat_mask(cols_ref, pair, back.shape[0])), back)
            if last:
                mixed = mixed + pair_gate(gates_here, cols_ref, pair) * piece
            d_pair = jnp.sum(grad_here * piece, -1, keepdims=True)
            d_gates = d_gates + jnp.where(lanes == cols_ref[:, 2 + pair : 3 + pair], d_pair, 0.0)
        dz = gates_here * (d_gates - jnp.sum(d_gates * gates_here, -1, keepdims=True))
        dz_out[...] = dz
        high, low = split(dz)
        moe_out[...] = dot_nt(high, router_ref[...]) + dot_nt(low, router_ref[...])
        if last:
            refs.pop(0)[...] = mixed[0:tokens, :]

    shapes = [sds((padded, LANES), F32), sds((padded, width), F32)]
    if last:
        shapes.append(sds((tokens, width), F32))
    return call(
        kernel,
        "gate_back",
        [grad] + ([x1] if last else []) + [gates, cols, router, *returned],
        [VM] * (4 + owners + int(last)),
        shapes,
        [VM] * len(shapes),
        [],
        flops=6 * padded * width * 512,
        moved=5 << 20,
    )


def expert_back(me, grad_blocks, slope, in_blocks, oe_blocks):
    owners = len(grad_blocks)
    cap, width = grad_blocks[0].shape
    seats, hidden = slope.shape
    ni, no = len(in_blocks.arrays), len(oe_blocks.arrays)
    total = count(in_blocks.offsets) + count(oe_blocks.offsets)
    step = width

    def kernel(*refs):
        refs = list(refs)
        me_ref = refs.pop(0)
        seat_refs = [refs.pop(0) for _ in range(owners)]
        slope_ref = refs.pop(0)
        in_refs = [refs.pop(0) for _ in range(ni)]
        oe_refs = [refs.pop(0) for _ in range(no)]
        grad_out, pre_out = refs.pop(0), refs.pop(0)
        outs = [refs.pop(0) for _ in range(owners)]
        win, woe, sems = refs
        index = me_ref[0]
        copies_oe = fetch_plan(oe_refs, oe_blocks.offsets, index, [(woe, 0, width, 0)], sems, 0)
        copies_in = fetch_plan(
            in_refs, in_blocks.offsets, index, [(win, 0, hidden, 0)], sems, len(copies_oe)
        )
        for copy in copies_oe + copies_in:
            copy.start()
        grad = join(seat_refs)
        grad_out[...] = grad
        for copy in copies_oe:
            copy.wait()
        total_out = None
        for at in range(0, hidden, step):
            d_hidden = dot_nt(grad, woe[at : at + step, :])
            d_pre = (d_hidden * slope_ref[:, at : at + step].astype(F32)).astype(BF)
            pre_out[:, at : at + step] = d_pre
            if at == 0:
                for copy in copies_in:
                    copy.wait()
            piece = dot_nt(d_pre, win[:, at : at + step])
            total_out = piece if total_out is None else total_out + piece
        part(total_out, outs)

    shapes = [sds((seats, width), BF), sds((seats, hidden), BF)]
    shapes += [sds((cap, width), BF)] * owners
    result = call(
        kernel,
        "expert_back",
        [me, *grad_blocks, slope, *in_blocks.arrays, *oe_blocks.arrays],
        [SM] + [VM] * (owners + 1) + [ANY] * (ni + no),
        shapes,
        [VM] * len(shapes),
        [
            pltpu.VMEM((width, hidden), BF),
            pltpu.VMEM((hidden, width), BF),
            pltpu.SemaphoreType.DMA((total,)),
        ],
        flops=8 * seats * width * hidden,
        moved=20 << 20,
    )
    return result[0], result[1], result[2:]


def expert_grads(me, rows, h, grad, d_pre, plan_in, plan_oe):
    seats, width = rows.shape
    hidden = h.shape[1]
    total = count([offs for _, offs in plan_in]) + count([offs for _, offs in plan_oe])

    def kernel(me_ref, rows_ref, h_ref, grad_ref, pre_ref, *refs):
        refs = list(refs)
        in_outs = [refs.pop(0) for _ in plan_in]
        oe_outs = [refs.pop(0) for _ in plan_oe]
        bin_out, boe_out = refs.pop(0), refs.pop(0)
        win, woe, sems = refs
        index = me_ref[0]
        step = width
        for at in range(0, hidden, step):
            woe[at : at + step, :] = dot_tn(h_ref[:, at : at + step], grad_ref[...]).astype(BF)
        copies_oe = spread_plan(
            woe, oe_outs, [offs for _, offs in plan_oe], index, sems, 0, (0, width)
        )
        for copy in copies_oe:
            copy.start()
        for at in range(0, hidden, step):
            win[:, at : at + step] = dot_tn(rows_ref[...], pre_ref[:, at : at + step]).astype(BF)
        copies_in = spread_plan(
            win, in_outs, [offs for _, offs in plan_in], index, sems, len(copies_oe), (0, hidden)
        )
        for copy in copies_in:
            copy.start()
        bin_out[...] = jnp.sum(pre_ref[...].astype(F32), 0, keepdims=True)
        boe_out[...] = jnp.sum(grad_ref[...].astype(F32), 0, keepdims=True)
        for copy in copies_oe + copies_in:
            copy.wait()

    shapes = [sds(shape, BF) for shape, _ in plan_in] + [sds(shape, BF) for shape, _ in plan_oe]
    shapes += [sds((1, hidden), F32), sds((1, width), F32)]
    result = call(
        kernel,
        "expert_grads",
        [me, rows, h, grad, d_pre],
        [SM] + [VM] * 4,
        shapes,
        [ANY] * (len(plan_in) + len(plan_oe)) + [VM] * 2,
        [
            pltpu.VMEM((width, hidden), BF),
            pltpu.VMEM((hidden, width), BF),
            pltpu.SemaphoreType.DMA((total,)),
        ],
        flops=8 * seats * width * hidden,
        moved=20 << 20,
    )
    cut = len(plan_in)
    more = cut + len(plan_oe)
    return result[:cut], result[cut:more], result[more], result[more + 1]


def attn_back(me, back_blocks, moe_part, grad, x, x1, qkv, cols, vecs, a_blocks, b_blocks, below, tokens):
    padded, width = grad.shape
    owners = len(back_blocks)
    cap = back_blocks[0].shape[0]
    seats = owners * cap
    na, nb = len(a_blocks.arrays), len(b_blocks.arrays)
    half = 2 * width
    total = count(a_blocks.offsets) + 2 * count(b_blocks.offsets)

    def kernel(*refs):
        refs = list(refs)
        me_ref = refs.pop(0)
        back_refs = [refs.pop(0) for _ in range(owners)]
        part_ref, grad_ref, x_ref, x1_ref, qkv_ref, cols_ref, vec_ref = (
            refs.pop(0) for _ in range(7)
        )
        a_refs = [refs.pop(0) for _ in range(na)]
        b_refs = [refs.pop(0) for _ in range(nb)]
        if below is not None:
            gates_ref, below_cols, below_rows = (refs.pop(0) for _ in range(3))
        dx_out, dy_out, dqkv_out, small_out = (refs.pop(0) for _ in range(4))
        seat_outs = [refs.pop(0) for _ in range(owners)] if below is not None else None
        wqkv, wout, sems = refs
        index = me_ref[0]
        copies_b = fetch_plan(
            b_refs,
            b_blocks.offsets,
            index,
            [(wqkv, 0, width, half), (wout, width, width, 0)],
            sems,
            0,
        )
        copies_a = fetch_plan(
            a_refs, a_blocks.offsets, index, [(wqkv, 0, half, 0)], sems, len(copies_b)
        )
        for copy in copies_b + copies_a:
            copy.start()
        vec = lambda k: vec_ref[k : k + 1, :]
        chosen = jnp.logical_or(seat_mask(cols_ref, 0, seats), seat_mask(cols_ref, 1, seats))
        d_moe = dot(one(chosen), join(back_refs)) + part_ref[...]
        normed2, rstd2 = norm_rows(x1_ref[...])
        small_out[...] = jnp.zeros_like(small_out)
        small_out[1:2, :] = jnp.sum(d_moe * normed2, 0, keepdims=True)
        small_out[3:4, :] = jnp.sum(d_moe, 0, keepdims=True)
        d_x1 = grad_ref[...] + norm_back(d_moe * vec(1), normed2, rstd2)
        dy = d_x1.astype(BF)
        dy_out[...] = dy
        small_out[6:7, :] = jnp.sum(dy.astype(F32), 0, keepdims=True)
        for copy in copies_b + copies_a:
            copy.wait()
        d_mixed = dot_nt(dy, wout[...]).astype(BF)
        masks = head_masks()
        scale = HEAD_DIM ** (-0.5)
        for two in range(HEADS // 2):
            at = two * 2 * HEAD_DIM
            query = qkv_ref[:, at : at + 2 * HEAD_DIM]
            keys = qkv_ref[:, width + at : width + at + 2 * HEAD_DIM]
            values = qkv_ref[:, 2 * width + at : 2 * width + at + 2 * HEAD_DIM]
            d_o = d_mixed[:, at : at + 2 * HEAD_DIM]
            sums = None
            for mask in masks:
                probs = head_probs(query, keys, mask, tokens)
                d_here = jnp.where(mask, d_o, 0).astype(BF)
                d_probs = dot_nt(d_here, values)
                d_values = dot_tn(probs.astype(BF), d_here)
                d_scores = probs * (d_probs - jnp.sum(d_probs * probs, -1, keepdims=True))
                d_scores = d_scores.astype(BF)
                d_query = dot(d_scores, jnp.where(mask, keys, 0).astype(BF))
                d_keys = dot_tn(d_scores, jnp.where(mask, query, 0).astype(BF))
                here = (d_query, d_keys, d_values)
                sums = here if sums is None else tuple(s + h for s, h in zip(sums, here))
            dqkv_out[:, at : at + 2 * HEAD_DIM] = (sums[0] * scale).astype(BF)
            dqkv_out[:, width + at : width + at + 2 * HEAD_DIM] = (sums[1] * scale).astype(BF)
            dqkv_out[:, 2 * width + at : 2 * width + at + 2 * HEAD_DIM] = sums[2].astype(BF)
        d_normed = None
        for k in range(3):
            here = dqkv_out[:, k * width : (k + 1) * width]
            if k != 1:
                row = 4 if k == 0 else 5
                small_out[row : row + 1, :] = jnp.sum(here.astype(F32), 0, keepdims=True)
            piece = dot_nt(here, wqkv[:, k * width : (k + 1) * width])
            d_normed = piece if d_normed is None else d_normed + piece
        normed1, rstd1 = norm_rows(x_ref[...])
        small_out[0:1, :] = jnp.sum(d_normed * normed1, 0, keepdims=True)
        small_out[2:3, :] = jnp.sum(d_normed, 0, keepdims=True)
        d_x = d_x1 + norm_back(d_normed * vec(0), normed1, rstd1)
        dx_out[...] = d_x[0 : dx_out.shape[0], :]
        if below is not None:
            part(seat_grads(d_x, gates_ref[...], below_cols, below_rows, seats), seat_outs)

    shapes = [
        sds((padded if below is not None else tokens, width), F32),
        sds((padded, width), BF),
        sds((padded, 3 * width), BF),
        sds((16, width), F32),
    ]
    args = [me, *back_blocks, moe_part, grad, x, x1, qkv, cols, vecs]
    args += [*a_blocks.arrays, *b_blocks.arrays]
    specs = [SM] + [VM] * (owners + 7) + [ANY] * (na + nb)
    if below is not None:
        shapes += [sds((cap, width), BF)] * owners
        args += list(below)
        specs += [VM] * 3
    result = call(
        kernel,
        "attn_back",
        args,
        specs,
        shapes,
        [VM] * len(shapes),
        [
            pltpu.VMEM((width, 3 * width), BF),
            pltpu.VMEM((width, width), BF),
            pltpu.SemaphoreType.DMA((total,)),
        ],
        flops=4 * 2 * padded * width * width * 8,
        moved=25 << 20,
    )
    return result[:4], result[4:]


def attn_grads(me, a_low, o_low, moe_low, dqkv, dy, dz, small, plan_a, plan_b):
    padded, width = a_low.shape
    half = 2 * width
    total = count([offs for _, offs in plan_a]) + count([offs for _, offs in plan_b])

    def kernel(me_ref, a_ref, o_ref, moe_ref, dqkv_ref, dy_ref, dz_ref, small_ref, *refs):
        refs = list(refs)
        a_outs = [refs.pop(0) for _ in plan_a]
        b_outs = [refs.pop(0) for _ in plan_b]
        wide, sems = refs
        index = me_ref[0]
        for k in range(2):
            wide[:, k * width : (k + 1) * width] = dot_tn(
                a_ref[...], dqkv_ref[:, k * width : (k + 1) * width]
            ).astype(BF)
        copies_a = spread_plan(
            wide, a_outs, [offs for _, offs in plan_a], index, sems, 0, (0, half)
        )
        for copy in copies_a:
            copy.start()
        wide[:, half : half + width] = dot_tn(a_ref[...], dqkv_ref[:, half : half + width]).astype(
            BF
        )
        wide[:, half + width : 2 * half] = dot_tn(o_ref[...], dy_ref[...]).astype(BF)
        high, low = split(dz_ref[...])
        d_router = dot_tn(moe_ref[...], high) + dot_tn(moe_ref[...], low)
        rows = jnp.concatenate(
            [jnp.zeros((16, width), F32), small_ref[...], jnp.zeros((LANES - 32, width), F32)], 0
        )
        wide[:, 2 * half : 2 * half + LANES] = (d_router + rows.T).astype(BF)
        copies_b = spread_plan(
            wide,
            b_outs,
            [offs for _, offs in plan_b],
            index,
            sems,
            len(copies_a),
            (half, half + LANES),
        )
        for copy in copies_b:
            copy.start()
        for copy in copies_a + copies_b:
            copy.wait()

    shapes = [sds(shape, BF) for shape, _ in plan_a + plan_b]
    result = call(
        kernel,
        "attn_grads",
        [me, a_low, o_low, moe_low, dqkv, dy, dz, small],
        [SM] + [VM] * 7,
        shapes,
        [ANY] * len(shapes),
        [pltpu.VMEM((width, 2 * half + LANES), BF), pltpu.SemaphoreType.DMA((total,))],
        flops=2 * padded * width * width * 8,
        moved=12 << 20,
    )
    return result[: len(plan_a)], result[len(plan_a) :]


def swap(value, axis, bit):
    size = lax.axis_size(axis)
    return lax.ppermute(value, axis, [(i, i ^ bit) for i in range(size)])


def chip_bits():
    bits = []
    bit = 2
    while bit < lax.axis_size("dp"):
        bits.append(bit)
        bit *= 2
    return bits


def gather(shard, bits):
    held, offsets = shard[None], [0]
    pieces = []
    for number, bit in enumerate(bits):
        other = swap(held, "dp", bit)
        theirs = [off ^ bit for off in offsets]
        if number + 1 < len(bits):
            held = jnp.concatenate([held, other], 0)
            offsets = offsets + theirs
        else:
            pieces += [(held, offsets), (other, theirs)]
    if not bits:
        pieces.append((held, offsets))
    pieces += [(swap(value, "dp", 1), [off ^ 1 for off in offs]) for value, offs in pieces]
    return pieces


def as_blocks(pieces, me):
    rows, width = pieces[0][0].shape[1:]
    if rows % 16 == 0:
        return Blocks([value for value, _ in pieces], [offs for _, offs in pieces])
    full = jnp.zeros((lax.axis_size("dp") * rows, width), BF)
    for value, offs in pieces:
        for k, off in enumerate(offs):
            full = lax.dynamic_update_slice(full, value[k], ((me ^ off) * rows, 0))
    return Blocks([full[None]], [[None]])


def halving_order(bits):
    order = [0]
    for bit in reversed(bits):
        order = order + [off ^ bit for off in order]
    return order


def send_plan(rows, width, bits):
    order = halving_order(bits)
    if rows % 16 == 0:
        mine = [((len(order), rows, width), order)]
        return mine + [((len(order), rows, width), [off ^ 1 for off in order])]
    size = 2 * len(order)
    return [((1, size * rows, width), [None])]


def reduce_shards(arrays, rows, bits, me):
    order = halving_order(bits)
    if len(arrays) == 1:
        whole = arrays[0].reshape((-1, rows) + arrays[0].shape[2:])
        mine = whole[me ^ jnp.array(order, jnp.int32)]
        theirs = whole[me ^ 1 ^ jnp.array(order, jnp.int32)]
    else:
        mine, theirs = arrays
    held = mine.astype(F32) + swap(theirs, "dp", 1).astype(F32)
    for bit in bits:
        low = held.astype(BF)
        half = low.shape[0] // 2
        held = low[:half].astype(F32) + swap(low[half:], "dp", bit).astype(F32)
    return held[0]


def sum_over_experts(value):
    bit = 1
    while bit < lax.axis_size("expert"):
        low = value.astype(BF)
        value = low.astype(F32) + swap(low, "expert", bit).astype(F32)
        bit *= 2
    return value


def exchange(blocks):
    return [blocks[0]] + [swap(blocks[k], "expert", k) for k in range(1, len(blocks))]


def place_pairs(routes, seat_rows, padded, cap, cap_pad):
    layers, tokens, _ = routes.shape
    expert = routes.reshape(layers, 2 * tokens)
    same = expert[:, :, None] == expert[:, None, :]
    ahead = seat_rows[:, :, None] > seat_rows[:, None, :]
    rank = jnp.sum(jnp.logical_and(same, ahead).astype(jnp.int32), 2)
    near = expert ^ lax.axis_index("expert")
    seat = jnp.where(rank < cap, near * cap_pad + rank, -1).reshape(layers, tokens, 2)
    cols = jnp.concatenate([seat, routes], 2)
    cols = jnp.pad(cols, ((0, 0), (0, padded - tokens), (0, 0)), constant_values=-1)
    rows = jnp.transpose(cols, (0, 2, 1))
    return cols, jnp.pad(rows, ((0, 0), (0, 4), (0, 0)), constant_values=-1)


def per_device(
    image_tokens,
    norm_gains,
    biases,
    w_qkv,
    w_out,
    w_router,
    router_noise,
    w_in,
    b_in,
    w_outexp,
    b_expout,
    routes,
    seat_order,
    cotangent,
):
    layers = w_qkv.shape[0]
    tokens, width = image_tokens.shape
    experts = w_router.shape[2]
    dp = lax.axis_size("dp")
    assert tokens == SEQ and experts == lax.axis_size("expert")
    assert width == HEADS * HEAD_DIM
    padded = up(tokens, 16)
    cap = 2 * tokens // experts
    cap_pad = up(cap, 8)
    seats = experts * cap_pad
    shard = w_qkv.shape[1]
    hidden_shard = w_outexp.shape[2]
    index = lax.axis_index("dp")
    me = index.astype(jnp.int32).reshape(1)
    bits = chip_bits()
    back_bits = bits[::-1]

    per = hidden_shard // shard
    small = jnp.concatenate(
        [
            norm_gains,
            biases,
            jnp.transpose(w_router, (0, 2, 1)),
            b_in.reshape(layers, per, shard),
            b_expout.reshape(layers, 1, shard),
        ],
        1,
    )
    small = lax.all_gather(small, "dp", axis=0)
    wide = jnp.transpose(small, (1, 2, 0, 3))
    vecs = wide[:, :7].reshape(layers, 7, width)
    vecs = jnp.pad(vecs, ((0, 0), (0, 1), (0, 0)))
    router = jnp.transpose(wide[:, 7 : 7 + experts].reshape(layers, experts, width), (0, 2, 1))
    router = jnp.pad(router, ((0, 0), (0, 0), (0, LANES - experts))).astype(BF)
    at = 7 + experts
    bias_in = jnp.transpose(wide[:, at : at + per], (0, 2, 1, 3)).reshape(layers, 1, -1)
    bias_oe = wide[:, at + per].reshape(layers, 1, width)

    noise = jnp.pad(
        router_noise, ((0, 0), (0, padded - tokens), (0, LANES - experts))
    )
    cols, rows = place_pairs(routes, seat_order[:, 0], padded, cap, cap_pad)

    attn_blocks, expert_blocks = [], []
    for layer in range(layers):
        left = w_qkv[layer][:, : 2 * width]
        right = jnp.concatenate([w_qkv[layer][:, 2 * width :], w_out[layer]], 1)
        attn_blocks.append(
            (
                as_blocks(gather(left, bits), index),
                as_blocks(gather(right, back_bits), index),
            )
        )
        expert_blocks.append(
            (
                as_blocks(gather(w_in[layer, 0], bits), index),
                as_blocks(gather(w_outexp[layer, 0], back_bits), index),
            )
        )

    saved = []
    x_args = (image_tokens,)
    for layer in range(layers):
        kept, sent = attn_fwd(
            me,
            layer == 0,
            x_args,
            *attn_blocks[layer],
            vecs[layer],
            router[layer],
            noise[layer],
            cols[layer],
            rows[layer],
            tokens,
            (cap_pad, experts),
        )
        held, made = expert_fwd(
            me, exchange(sent), *expert_blocks[layer], bias_in[layer], bias_oe[layer]
        )
        returned = exchange(made)
        saved.append((kept, held, returned))
        x_args = (kept[1], kept[5], cols[layer], returned)

    last = layers - 1
    grad, grad_seats = top_seats(
        cotangent, saved[last][0][5], cols[last], rows[last], seats, tokens, experts
    )
    mixed = None
    grads = [None] * layers
    for layer in reversed(range(layers)):
        (x, x1, a_low, qkv, o_low, gates, moe_low), (seat_rows, h, slope), returned = saved[layer]
        parts = gate_back(
            grad, x1, gates, cols[layer], router[layer], returned, tokens, layer == last
        )
        dz, moe_part = parts[0], parts[1]
        if layer == last:
            mixed = parts[2]
        d_out, d_pre, d_rows = expert_back(
            me, exchange(grad_seats), slope, *expert_blocks[layer]
        )
        d_back = exchange(d_rows)
        below = None
        if layer > 0:
            below = (saved[layer - 1][0][5], cols[layer - 1], rows[layer - 1])
        (grad, dy, dqkv, small_grads), grad_seats = attn_back(
            me,
            d_back,
            moe_part,
            grad,
            x,
            x1,
            qkv,
            cols[layer],
            vecs[layer],
            *attn_blocks[layer],
            below,
            tokens,
        )
        g_in, g_oe, g_bin, g_boe = expert_grads(
            me,
            seat_rows,
            h,
            d_out,
            d_pre,
            send_plan(shard, w_in.shape[3], bits),
            send_plan(hidden_shard, width, back_bits),
        )
        g_left, g_right = attn_grads(
            me,
            a_low,
            o_low,
            moe_low,
            dqkv,
            dy,
            dz,
            small_grads,
            send_plan(shard, 2 * width, bits),
            send_plan(shard, 2 * width + LANES, back_bits),
        )
        sum_in = reduce_shards(g_in, shard, bits, index)
        sum_oe = reduce_shards(g_oe, hidden_shard, back_bits, index)
        sum_left = sum_over_experts(reduce_shards(g_left, shard, bits, index))
        sum_right = sum_over_experts(reduce_shards(g_right, shard, back_bits, index))
        biases_here = jnp.concatenate([g_bin.reshape(dp, -1), g_boe.reshape(dp, -1)], 1)
        grads[layer] = (sum_left, sum_right, sum_in, sum_oe, biases_here)

    expert_small = lax.psum_scatter(
        jnp.stack([item[4] for item in grads], 1), "dp", scatter_dimension=0, tiled=False
    )
    left = jnp.stack([item[0] for item in grads])
    right = jnp.stack([item[1] for item in grads])
    tail = jnp.transpose(right[:, :, 2 * width :], (0, 2, 1))
    return (
        mixed,
        grad,
        tail[:, 16:18],
        tail[:, 18:23],
        jnp.concatenate([left, right[:, :, :width]], 2),
        right[:, :, width : 2 * width],
        jnp.transpose(tail[:, :experts], (0, 2, 1)),
        jnp.stack([item[2] for item in grads])[:, None],
        expert_small[:, None, :hidden_shard],
        jnp.stack([item[3] for item in grads])[:, None],
        expert_small[:, None, hidden_shard:],
    )


def solution(mesh):
    return jax.shard_map(
        per_device,
        mesh=mesh,
        in_specs=(
            P(("dp", "expert"), None),
            P(None, None, "dp"),
            P(None, None, "dp"),
            P(None, "dp", None),
            P(None, "dp", None),
            P(None, "dp", None),
            P(None, ("dp", "expert"), None),
            P(None, "expert", "dp", None),
            P(None, "expert", "dp"),
            P(None, "expert", "dp", None),
            P(None, "expert", "dp"),
            P(None, ("dp", "expert"), None),
            P(None, ("dp", "expert"), None),
            P(("dp", "expert"), None),
        ),
        out_specs=(
            P(("dp", "expert"), None),
            P(("dp", "expert"), None),
            P(None, None, "dp"),
            P(None, None, "dp"),
            P(None, "dp", None),
            P(None, "dp", None),
            P(None, "dp", None),
            P(None, "expert", "dp", None),
            P(None, "expert", "dp"),
            P(None, "expert", "dp", None),
            P(None, "expert", "dp"),
        ),
        check_vma=False,
    )
```

```python
import functools

import jax
import jax.numpy as jnp
from jax import lax
from jax.experimental import pallas as pl
from jax.experimental.pallas import tpu as pltpu
from jax.sharding import PartitionSpec as P

HEADS = 12
HEAD_DIM = 64
SEQ = 197
EPS = 1e-06
BF = jnp.bfloat16
F32 = jnp.float32
LANES = 128
NEG = -1e30
VMEM_LIMIT = 60 * 1024 * 1024


def up(value, step):
    return -(-value // step) * step


def dot(left, right):
    return lax.dot_general(left, right, (((1,), (0,)), ((), ())), preferred_element_type=F32)


def dot_nt(left, right):
    return lax.dot_general(left, right, (((1,), (1,)), ((), ())), preferred_element_type=F32)


def dot_tn(left, right):
    return lax.dot_general(left, right, (((0,), (0,)), ((), ())), preferred_element_type=F32)


def norm_rows(x):
    centered = x - jnp.mean(x, -1, keepdims=True)
    rstd = lax.rsqrt(jnp.mean(centered * centered, -1, keepdims=True) + EPS)
    return centered * rstd, rstd


def norm_back(grad_hat, normed, rstd):
    return rstd * (
        grad_hat
        - jnp.mean(grad_hat, -1, keepdims=True)
        - normed * jnp.mean(grad_hat * normed, -1, keepdims=True)
    )


def split(value):
    high = value.astype(BF)
    return high, (value - high.astype(F32)).astype(BF)


def join(refs):
    return jnp.concatenate([ref[...].astype(F32) for ref in refs], 0).astype(BF)


def part(value, refs):
    rows = refs[0].shape[0]
    for number, ref in enumerate(refs):
        ref[...] = value[number * rows : (number + 1) * rows].astype(ref.dtype)


def seat_mask(cols_ref, pair, seats):
    column = cols_ref[:, pair : pair + 1]
    return lax.broadcasted_iota(jnp.int32, (column.shape[0], seats), 1) == column


def token_mask(rows_ref, pair, seats):
    row = rows_ref[pair : pair + 1, :]
    return lax.broadcasted_iota(jnp.int32, (seats, row.shape[1]), 0) == row


def one(mask):
    return jnp.where(mask, 1.0, 0.0).astype(BF)


def pair_gate(gates, cols_ref, pair):
    route = cols_ref[:, 2 + pair : 3 + pair]
    lanes = lax.broadcasted_iota(jnp.int32, gates.shape, 1)
    return jnp.sum(jnp.where(lanes == route, gates, 0.0), -1, keepdims=True)


def combine(x1, gates, cols_ref, returned):
    total = x1
    for pair in range(2):
        piece = dot(one(seat_mask(cols_ref, pair, returned.shape[0])), returned)
        total = total + pair_gate(gates, cols_ref, pair) * piece
    return total


def seat_grads(grad, gates, cols_ref, rows_ref, seats):
    total = None
    for pair in range(2):
        scaled = (pair_gate(gates, cols_ref, pair) * grad).astype(BF)
        piece = dot(one(token_mask(rows_ref, pair, seats)), scaled)
        total = piece if total is None else total + piece
    return total


def head_masks():
    lanes = lax.broadcasted_iota(jnp.int32, (1, 2 * HEAD_DIM), 1)
    return (lanes < HEAD_DIM, lanes >= HEAD_DIM)


def head_probs(query, keys, mask, tokens):
    query = jnp.where(mask, query, 0).astype(F32) * HEAD_DIM ** (-0.5)
    scores = dot_nt(query.astype(BF), keys)
    lanes = lax.broadcasted_iota(jnp.int32, scores.shape, 1)
    scores = jnp.where(lanes < tokens, scores, NEG)
    raised = jnp.exp(scores - jnp.max(scores, -1, keepdims=True))
    return raised * (1.0 / jnp.sum(raised, -1, keepdims=True))


VM = pl.BlockSpec(memory_space=pltpu.VMEM)
ANY = pl.BlockSpec(memory_space=pl.ANY)
SM = pl.BlockSpec(memory_space=pltpu.SMEM)


def sds(shape, dtype):
    return jax.ShapeDtypeStruct(tuple(shape), dtype)


class Order:
    token = None


def call(kernel, name, args, specs, outs, out_specs, scratch, aliases=None):
    after = []
    if Order.token is not None and not any(Order.token is arg for arg in args):
        after = [Order.token]
    given = len(args)

    def body(*refs):
        return kernel(*refs[:given], *refs[given + len(after) :])

    result = pl.pallas_call(
        body,
        name=name,
        in_specs=list(specs) + [ANY] * len(after),
        out_specs=out_specs,
        out_shape=outs,
        scratch_shapes=scratch,
        input_output_aliases=aliases or {},
        compiler_params=pltpu.CompilerParams(vmem_limit_bytes=VMEM_LIMIT),
    )(*args, *after)
    Order.token = result[0] if isinstance(result, (tuple, list)) else result
    return result


def hold(values, after):
    def kernel(*refs):
        pass

    return call(
        kernel,
        "hold",
        [*values, *after],
        [ANY] * (len(values) + len(after)),
        [sds(value.shape, value.dtype) for value in values],
        [ANY] * len(values),
        [],
        {i: i for i in range(len(values))},
    )


def move(name, args, copies, outs):
    total = len(copies)

    def kernel(*refs):
        ins, rest = refs[: len(args)], refs[len(args) :]
        results, held = rest[: len(outs)], rest[len(outs) : len(outs) + total]
        in_sems, out_sems = rest[-2:]
        loads = [
            pltpu.make_async_copy(ins[i].at[where], held[n], in_sems.at[n])
            for n, (i, where, _, _, _) in enumerate(copies)
        ]
        stores = [
            pltpu.make_async_copy(held[n], results[o].at[into], out_sems.at[n])
            for n, (_, _, o, into, _) in enumerate(copies)
        ]
        start(loads)
        for load, store in zip(loads, stores):
            load.wait()
            store.start()
        wait(stores)

    return call(
        kernel,
        name,
        args,
        [ANY] * len(args),
        outs,
        [ANY] * len(outs),
        [pltpu.VMEM(shape, BF) for *_, shape in copies]
        + [pltpu.SemaphoreType.DMA((total,)), pltpu.SemaphoreType.DMA((total,))],
    )


def fold(name, args, block, tasks, outs, aliases=None):
    terms = [(t, term) for t, (listed, _, _) in enumerate(tasks) for term in listed]
    writes = [(t, write) for t, (_, _, listed) in enumerate(tasks) for write in listed]
    wide = [t for t, task in enumerate(tasks) if task[1] == F32]
    slim = [t for t, task in enumerate(tasks) if task[1] != F32]

    def kernel(*refs):
        ins, rest = refs[: len(args)], refs[len(args) :]
        results = rest[: len(outs)]
        loaded, wide_ref, slim_ref, in_sems, out_sems = rest[len(outs) :]
        loads = [
            pltpu.make_async_copy(ins[i].at[where], loaded.at[n], in_sems.at[n])
            for n, (_, (i, where)) in enumerate(terms)
        ]
        for copy in loads:
            copy.start()
        stores = []
        for t, (_, kind, _) in enumerate(tasks):
            total = None
            for n, (task, _) in enumerate(terms):
                if task == t:
                    loads[n].wait()
                    piece = loaded[n].astype(F32)
                    total = piece if total is None else total + piece
            holder = wide_ref.at[wide.index(t)] if kind == F32 else slim_ref.at[slim.index(t)]
            holder[...] = total.astype(kind)
            for n, (task, (o, into, within)) in enumerate(writes):
                if task == t:
                    copy = pltpu.make_async_copy(
                        holder.at[within], results[o].at[into], out_sems.at[n]
                    )
                    copy.start()
                    stores.append(copy)
        for copy in stores:
            copy.wait()

    return call(
        kernel,
        name,
        args,
        [ANY] * len(args),
        outs,
        [ANY] * len(outs),
        [
            pltpu.VMEM((len(terms), *block), BF),
            pltpu.VMEM((max(len(wide), 1), *(block if wide else (16, LANES))), F32),
            pltpu.VMEM((max(len(slim), 1), *(block if slim else (16, LANES))), BF),
            pltpu.SemaphoreType.DMA((len(terms),)),
            pltpu.SemaphoreType.DMA((len(writes),)),
        ],
        aliases=aliases,
    )


ALL = slice(None)


class Weights:
    def __init__(self, arrays, places):
        self.arrays, self.places = list(arrays), places


OWNERS = -1


def attn_targets(width, rows, wqkv, wout):
    return {
        0: [(wqkv, 0, 2 * width, 0, rows, 0)],
        1: [(wqkv, 0, width, 2 * width, rows, 0), (wout, width, width, 0, rows, 0)],
    }


def expert_targets(width, hidden, rows, whole, win, woe):
    if whole:
        return {0: [(win, 0, hidden, 0, rows, 0)], 1: [(woe, 0, width, 0, rows, 0)]}
    per = hidden // width
    return {
        0: [(win, 0, hidden, 0, rows, 0)],
        1: [(woe, q * width, width, 0, per * rows, q * rows) for q in range(per)],
    }


def copies_in(weights):
    return 4 * sum(
        len(parts) if array.ndim == 3 else array.shape[0]
        for array, (off, parts) in zip(weights.arrays, weights.places)
    )


def fetch(refs, weights, me, targets, part_number, sems):
    copies = []
    for ref, (off, parts) in zip(refs, weights.places):
        rows = ref.shape[-2]
        if off == OWNERS:
            sources = [(d, (d, part_number)) for d in range(ref.shape[0])]
        elif isinstance(off, tuple):
            sources = [(me ^ o, (k, part_number)) for k, o in enumerate(off)]
        elif part_number in parts:
            at = None if off is None else me ^ off
            sources = [(at, (parts.index(part_number),))]
        else:
            sources = []
        for at, where in sources:
            for scratch, first, size, into, times, plus in targets[part_number]:
                place = 0 if at is None else at * times + plus
                if off not in (None, OWNERS):
                    place = pl.multiple_of(place, 16)
                copies.append(
                    pltpu.make_async_copy(
                        ref.at[(*where, ALL, pl.ds(first, size))],
                        scratch.at[pl.ds(place, rows), pl.ds(into, size)],
                        sems.at[len(copies)],
                    )
                )
    return copies


def start(copies):
    for copy in copies:
        copy.start()


def wait(copies):
    for copy in copies:
        copy.wait()


def small_rows(per, experts):
    return up(7 + experts + per + 1, 8)


def pack_small(norm_gains, biases, w_router, b_in, b_expout):
    layers, shard, experts = w_router.shape
    per = b_in.shape[2] // shard
    height = small_rows(per, experts)

    def kernel(gain_ref, bias_ref, router_ref, in_ref, oe_ref, out, square):
        out[...] = jnp.zeros_like(out)
        for layer in range(layers):
            at = layer * height
            out[at : at + 2, 0:shard] = gain_ref[layer]
            out[at + 2 : at + 7, 0:shard] = bias_ref[layer]
            square[...] = jnp.zeros_like(square)
            square[0:shard, 0:experts] = router_ref[layer]
            turned = square[...].T
            out[at + 7 : at + 7 + experts, :] = turned[0:experts, :]
            at = at + 7 + experts
            for q in range(per):
                out[at + q : at + q + 1, 0:shard] = in_ref[layer, :, q * shard : (q + 1) * shard]
            out[at + per : at + per + 1, 0:shard] = oe_ref[layer]

    return call(
        kernel,
        "pack_small",
        [norm_gains, biases, w_router, b_in, b_expout],
        [VM] * 5,
        sds((layers * height, LANES), F32),
        VM,
        [pltpu.VMEM((LANES, LANES), F32)],
    )


def unpack_small(gathered, layers, shard, per, experts):
    shards = gathered.shape[0]
    width = shards * shard
    height = small_rows(per, experts)

    def kernel(ref, *refs):
        tall = refs[-1]
        for layer in range(layers):
            vec, router, bias_in, bias_oe = refs[4 * layer : 4 * layer + 4]
            at = layer * height
            vec[...] = jnp.zeros_like(vec)
            tall[...] = jnp.zeros_like(tall)
            for d in range(shards):
                here = slice(d * shard, (d + 1) * shard)
                vec[0:7, here] = ref[d, at : at + 7, 0:shard]
                tall[0:experts, here] = ref[d, at + 7 : at + 7 + experts, 0:shard]
                row = at + 7 + experts
                for q in range(per):
                    first = (d * per + q) * shard
                    bias_in[:, first : first + shard] = ref[d, row + q : row + q + 1, 0:shard]
                bias_oe[:, here] = ref[d, row + per : row + per + 1, 0:shard]
            router[...] = tall[...].T.astype(BF)

    shapes = []
    for _ in range(layers):
        shapes += [
            sds((8, width), F32),
            sds((width, LANES), BF),
            sds((1, width * per), F32),
            sds((1, width), F32),
        ]
    outs = call(
        kernel,
        "unpack_small",
        [gathered],
        [VM],
        shapes,
        [VM] * len(shapes),
        [pltpu.VMEM((LANES, width), F32)],
    )
    return [outs[4 * layer : 4 * layer + 4] for layer in range(layers)]


def place_pairs(routes, seat_order, padded, cap, cap_pad, z):
    layers, tokens, _ = routes.shape
    tall = up(padded, LANES)

    def kernel(z_ref, route_ref, order_ref, *refs):
        outs, wide = refs[:-1], refs[-1]
        lanes = lax.broadcasted_iota(jnp.int32, (tokens, LANES), 1)
        lanes_tall = lax.broadcasted_iota(jnp.int32, (tall, LANES), 1)
        for layer in range(layers):
            given = jnp.full((tokens, LANES), -1.0, F32)
            for k in range(2):
                given = jnp.where(lanes == k, route_ref[layer, :, k : k + 1].astype(F32), given)
                given = jnp.where(lanes == 2 + k, order_ref[layer, :, k : k + 1].astype(F32), given)
            wide[...] = jnp.full((tall, LANES), -1.0, F32)
            wide[0:tokens, :] = given
            table = wide[...]
            turned = table.T
            seats = []
            for k in range(2):
                expert, order = table[:, k : k + 1], table[:, 2 + k : 3 + k]
                rank = jnp.zeros((tall, 1), F32)
                for j in range(2):
                    ahead = jnp.logical_and(
                        turned[j : j + 1, :] == expert, turned[2 + j : 3 + j, :] < order
                    )
                    rank = rank + jnp.sum(jnp.where(ahead, 1.0, 0.0), -1, keepdims=True)
                expert, rank = expert.astype(jnp.int32), rank.astype(jnp.int32)
                near = jnp.bitwise_xor(expert, z_ref[0])
                good = jnp.logical_and(expert >= 0, rank < cap)
                seats.append(jnp.where(good, near * cap_pad + rank, -1).astype(F32))
            table = jnp.where(lanes_tall == 2, table[:, 0:1], table)
            table = jnp.where(lanes_tall == 3, wide[:, 1:2], table)
            table = jnp.where(lanes_tall == 0, seats[0], table)
            table = jnp.where(lanes_tall == 1, seats[1], table)
            cols, rows = outs[2 * layer], outs[2 * layer + 1]
            cols[...] = table[0:padded, :].astype(jnp.int32)
            rows[...] = table.T[0:8, 0:padded].astype(jnp.int32)

    shapes = []
    for _ in range(layers):
        shapes += [sds((padded, LANES), jnp.int32), sds((8, padded), jnp.int32)]
    outs = call(
        kernel,
        "place_pairs",
        [z, routes, seat_order],
        [SM, VM, VM],
        shapes,
        [VM] * len(shapes),
        [pltpu.VMEM((tall, LANES), F32)],
    )
    return outs[0::2], outs[1::2]


def attn_fwd(me, layer, x_args, weights, vecs, router, noise, cols, rows, cap):
    first = len(x_args) == 1
    padded, width = cols.shape[0], vecs.shape[1]
    tokens, experts = noise.shape[1:]
    seats = experts * cap
    owners = 0 if first else len(x_args[3])
    count = len(weights.arrays)
    shard = weights.arrays[0].shape[-2]

    def kernel(*refs):
        refs = list(refs)
        me_ref = refs.pop(0)
        if first:
            tok_ref = refs.pop(0)
        else:
            below_x1, below_gates, below_cols = refs.pop(0), refs.pop(0), refs.pop(0)
            below_blocks = [refs.pop(0) for _ in range(owners)]
        w_refs = [refs.pop(0) for _ in range(count)]
        vec_ref, router_ref, noise_ref, cols_ref, rows_ref = (refs.pop(0) for _ in range(5))
        x_out, x1_out, a_out, qkv_out, o_out, gates_out, m_out = (refs.pop(0) for _ in range(7))
        seat_outs = [refs.pop(0) for _ in range(experts)]
        wqkv, wout, sems, more_sems = refs
        targets = attn_targets(width, shard, wqkv, wout)
        left = fetch(w_refs, weights, me_ref[0], targets, 0, sems)
        right = fetch(w_refs, weights, me_ref[0], targets, 1, more_sems)
        start(left + right)
        vec = lambda k: vec_ref[k : k + 1, :]
        if first:
            x_out[...] = jnp.zeros_like(x_out)
            x_out[0:tokens, :] = tok_ref[...].astype(F32)
            x = x_out[...]
        else:
            x = combine(below_x1[...], below_gates[...], below_cols, join(below_blocks))
            x_out[...] = x
        normed, rstd = norm_rows(x)
        a_low = (normed * vec(0) + vec(2)).astype(BF)
        a_out[...] = a_low
        gates_out[...] = jnp.zeros_like(gates_out)
        gates_out[0:tokens, 0:experts] = noise_ref[layer]
        noise_here = gates_out[...]
        wait(left)
        for k in range(3):
            if k == 2:
                wait(right)
            piece = dot(a_low, wqkv[:, k * width : (k + 1) * width])
            if k == 0:
                piece = piece + vec(4)
            if k == 2:
                piece = piece + vec(5)
            qkv_out[:, k * width : (k + 1) * width] = piece.astype(BF)
        masks = head_masks()
        for two in range(HEADS // 2):
            at = two * 2 * HEAD_DIM
            query = qkv_out[:, at : at + 2 * HEAD_DIM]
            keys = qkv_out[:, width + at : width + at + 2 * HEAD_DIM]
            values = qkv_out[:, 2 * width + at : 2 * width + at + 2 * HEAD_DIM]
            mixed = None
            for mask in masks:
                probs = head_probs(query, keys, mask, tokens).astype(BF)
                piece = dot(probs, jnp.where(mask, values, 0).astype(BF))
                mixed = piece if mixed is None else mixed + piece
            o_out[:, at : at + 2 * HEAD_DIM] = mixed.astype(BF)
        x1 = x + dot(o_out[...], wout[...]) + vec(6)
        x1_out[...] = x1
        normed2, rstd2 = norm_rows(x1)
        moe = normed2 * vec(1) + vec(3)
        high, low = split(moe)
        logits = dot(high, router_ref[...]) + dot(low, router_ref[...]) + noise_here
        lanes = lax.broadcasted_iota(jnp.int32, logits.shape, 1)
        logits = jnp.where(lanes < experts, logits, NEG)
        raised = jnp.exp(logits - jnp.max(logits, -1, keepdims=True))
        gates_out[...] = raised / jnp.sum(raised, -1, keepdims=True)
        m_out[...] = high
        chosen = jnp.logical_or(token_mask(rows_ref, 0, seats), token_mask(rows_ref, 1, seats))
        part(dot(one(chosen), high), seat_outs)

    args = [me]
    specs = [SM]
    if first:
        args += [x_args[0]]
        specs += [VM]
    else:
        args += [x_args[0], x_args[1], x_args[2], *x_args[3]]
        specs += [VM] * (3 + owners)
    args += [*weights.arrays, vecs, router, noise, cols, rows]
    specs += [ANY] * count + [VM] * 5
    outs = [
        sds((padded, width), F32),
        sds((padded, width), F32),
        sds((padded, width), BF),
        sds((padded, 3 * width), BF),
        sds((padded, width), BF),
        sds((padded, LANES), F32),
        sds((padded, width), BF),
    ] + [sds((cap, width), BF)] * experts
    result = call(
        kernel,
        "attn_fwd",
        args,
        specs,
        outs,
        [VM] * len(outs),
        [
            pltpu.VMEM((width, 3 * width), BF),
            pltpu.VMEM((width, width), BF),
            pltpu.SemaphoreType.DMA((copies_in(weights),)),
            pltpu.SemaphoreType.DMA((copies_in(weights),)),
        ],
    )
    return result[:7], result[7:]


def expert_fwd(me, seat_blocks, weights, bias_in, bias_oe):
    owners = len(seat_blocks)
    cap, width = seat_blocks[0].shape
    seats = owners * cap
    hidden = bias_in.shape[1]
    count = len(weights.arrays)
    shard = weights.arrays[0].shape[-2]
    whole = weights.places[0][0] is None
    step = width

    def kernel(*refs):
        refs = list(refs)
        me_ref = refs.pop(0)
        seat_refs = [refs.pop(0) for _ in range(owners)]
        w_refs = [refs.pop(0) for _ in range(count)]
        bin_ref, boe_ref = refs.pop(0), refs.pop(0)
        rows_out, h_out, slope_out = refs.pop(0), refs.pop(0), refs.pop(0)
        outs = [refs.pop(0) for _ in range(owners)]
        win, woe, sems, more_sems = refs
        targets = expert_targets(width, hidden, shard, whole, win, woe)
        left = fetch(w_refs, weights, me_ref[0], targets, 0, sems)
        right = fetch(w_refs, weights, me_ref[0], targets, 1, more_sems)
        start(left + right)
        rows = join(seat_refs)
        rows_out[...] = rows
        wait(left)
        total_out = None
        for at in range(0, hidden, step):
            pre = dot(rows, win[:, at : at + step]) + bin_ref[:, at : at + step]
            square = pre * pre
            bend = jnp.tanh(0.7978845608028654 * (pre + 0.044715 * square * pre))
            h = (0.5 * pre * (1.0 + bend)).astype(BF)
            slope = 0.5 * (1.0 + bend) + 0.5 * pre * (1.0 - bend * bend) * (
                0.7978845608028654 * (1.0 + 0.134145 * square)
            )
            h_out[:, at : at + step] = h
            slope_out[:, at : at + step] = slope.astype(BF)
            if at == 0:
                wait(right)
            piece = dot(h, woe[at : at + step, :])
            total_out = piece if total_out is None else total_out + piece
        part(total_out + boe_ref[...], outs)

    shapes = [
        sds((seats, width), BF),
        sds((seats, hidden), BF),
        sds((seats, hidden), BF),
    ] + [sds((cap, width), BF)] * owners
    result = call(
        kernel,
        "expert_fwd",
        [me, *seat_blocks, *weights.arrays, bias_in, bias_oe],
        [SM] + [VM] * owners + [ANY] * count + [VM] * 2,
        shapes,
        [VM] * len(shapes),
        [
            pltpu.VMEM((width, hidden), BF),
            pltpu.VMEM((hidden, width), BF),
            pltpu.SemaphoreType.DMA((copies_in(weights),)),
            pltpu.SemaphoreType.DMA((copies_in(weights),)),
        ],
    )
    return result[:3], result[3:]


def top_seats(cotangent, gates, cols, rows, cap, experts):
    tokens, width = cotangent.shape
    padded = cols.shape[0]

    def kernel(cot_ref, gates_ref, cols_ref, rows_ref, *refs):
        grad_out, *outs = refs
        grad_out[...] = jnp.zeros_like(grad_out)
        grad_out[0:tokens, :] = cot_ref[...].astype(F32)
        part(seat_grads(grad_out[...], gates_ref[...], cols_ref, rows_ref, cap * experts), outs)

    shapes = [sds((padded, width), F32)] + [sds((cap, width), BF)] * experts
    result = call(
        kernel,
        "top_seats",
        [cotangent, gates, cols, rows],
        [VM] * 4,
        shapes,
        [VM] * len(shapes),
        [],
    )
    return result[0], result[1:]


def gate_back(grad, x1, gates, cols, router, returned, tokens, last):
    padded, width = grad.shape
    owners = len(returned)

    def kernel(*refs):
        refs = list(refs)
        grad_ref = refs.pop(0)
        x1_ref = refs.pop(0) if last else None
        gates_ref, cols_ref, router_ref = (refs.pop(0) for _ in range(3))
        blocks = [refs.pop(0) for _ in range(owners)]
        dz_out, moe_out = refs.pop(0), refs.pop(0)
        back = join(blocks)
        grad_here = grad_ref[...]
        gates_here = gates_ref[...]
        lanes = lax.broadcasted_iota(jnp.int32, gates_here.shape, 1)
        d_gates = jnp.zeros_like(gates_here)
        mixed = x1_ref[...] if last else None
        for pair in range(2):
            piece = dot(one(seat_mask(cols_ref, pair, back.shape[0])), back)
            if last:
                mixed = mixed + pair_gate(gates_here, cols_ref, pair) * piece
            d_pair = jnp.sum(grad_here * piece, -1, keepdims=True)
            d_gates = d_gates + jnp.where(lanes == cols_ref[:, 2 + pair : 3 + pair], d_pair, 0.0)
        dz = gates_here * (d_gates - jnp.sum(d_gates * gates_here, -1, keepdims=True))
        dz_out[...] = dz
        high, low = split(dz)
        moe_out[...] = dot_nt(high, router_ref[...]) + dot_nt(low, router_ref[...])
        if last:
            refs.pop(0)[...] = mixed[0:tokens, :]

    shapes = [sds((padded, LANES), F32), sds((padded, width), F32)]
    if last:
        shapes.append(sds((tokens, width), F32))
    return call(
        kernel,
        "gate_back",
        [grad] + ([x1] if last else []) + [gates, cols, router, *returned],
        [VM] * (4 + owners + int(last)),
        shapes,
        [VM] * len(shapes),
        [],
    )


def expert_back(me, grad_blocks, slope, weights):
    owners = len(grad_blocks)
    cap, width = grad_blocks[0].shape
    seats, hidden = slope.shape
    count = len(weights.arrays)
    shard = weights.arrays[0].shape[-2]
    whole = weights.places[0][0] is None
    step = width

    def kernel(*refs):
        refs = list(refs)
        me_ref = refs.pop(0)
        seat_refs = [refs.pop(0) for _ in range(owners)]
        slope_ref = refs.pop(0)
        w_refs = [refs.pop(0) for _ in range(count)]
        grad_out, pre_out = refs.pop(0), refs.pop(0)
        outs = [refs.pop(0) for _ in range(owners)]
        win, woe, sems, more_sems = refs
        targets = expert_targets(width, hidden, shard, whole, win, woe)
        right = fetch(w_refs, weights, me_ref[0], targets, 1, sems)
        left = fetch(w_refs, weights, me_ref[0], targets, 0, more_sems)
        start(right + left)
        grad = join(seat_refs)
        grad_out[...] = grad
        wait(right)
        total_out = None
        for at in range(0, hidden, step):
            d_hidden = dot_nt(grad, woe[at : at + step, :])
            d_pre = (d_hidden * slope_ref[:, at : at + step].astype(F32)).astype(BF)
            pre_out[:, at : at + step] = d_pre
            if at == 0:
                wait(left)
            piece = dot_nt(d_pre, win[:, at : at + step])
            total_out = piece if total_out is None else total_out + piece
        part(total_out, outs)

    shapes = [sds((seats, width), BF), sds((seats, hidden), BF)]
    shapes += [sds((cap, width), BF)] * owners
    result = call(
        kernel,
        "expert_back",
        [me, *grad_blocks, slope, *weights.arrays],
        [SM] + [VM] * (owners + 1) + [ANY] * count,
        shapes,
        [VM] * len(shapes),
        [
            pltpu.VMEM((width, hidden), BF),
            pltpu.VMEM((hidden, width), BF),
            pltpu.SemaphoreType.DMA((copies_in(weights),)),
            pltpu.SemaphoreType.DMA((copies_in(weights),)),
        ],
    )
    return result[0], result[1], result[2:]


def spread(wide, index, outs, orders, rows, pieces, sems):
    copies = []
    for out, order in zip(outs, orders):
        for k, off in enumerate(order):
            for times, plus, first, size, into in pieces:
                place = pl.multiple_of((index ^ off) * times + plus, 16)
                copies.append(
                    pltpu.make_async_copy(
                        wide.at[pl.ds(place, rows), pl.ds(first, size)],
                        out.at[(k, *into)],
                        sems.at[len(copies)],
                    )
                )
    return copies


def column_sums(value):
    return dot(jnp.ones((8, value.shape[0]), BF), value)[0:1, :]


def expert_grads(rows_in, h, d_out, d_pre, shards, blocks):
    seats, width = rows_in.shape
    hidden = h.shape[1]
    per, shard = hidden // width, width // shards
    total = shards * (1 + per) if blocks else 2

    def kernel(rows_ref, h_ref, out_ref, pre_ref, *refs):
        refs = list(refs)
        outs = [refs.pop(0) for _ in range(1 if blocks else 2)]
        bias_ref, win, woe, sems = refs
        copies = []

        def send(source, target):
            copy = pltpu.make_async_copy(source, target, sems.at[len(copies)])
            copy.start()
            copies.append(copy)

        for k in range(per):
            here = slice(k * width, (k + 1) * width)
            woe[here, :] = dot_tn(h_ref[:, here], out_ref[...]).astype(BF)
            if blocks:
                for d in range(k * shards // per, (k + 1) * shards // per):
                    for q in range(per):
                        send(
                            woe.at[pl.ds((d * per + q) * shard, shard)],
                            outs[0].at[d, 1, :, pl.ds(q * width, width)],
                        )
        for k in range(per):
            here = slice(k * width, (k + 1) * width)
            win[:, here] = dot_tn(rows_ref[...], pre_ref[:, here]).astype(BF)
        if blocks:
            for d in range(shards):
                send(win.at[pl.ds(d * shard, shard)], outs[0].at[d, 0])
        else:
            send(win, outs[0])
            send(woe, outs[1])
        bias_ref[...] = jnp.zeros_like(bias_ref)
        sums = column_sums(pre_ref[...])
        for d in range(shards):
            for q in range(per):
                first = (d * per + q) * shard
                bias_ref[q : q + 1, d * shard : (d + 1) * shard] = sums[:, first : first + shard]
        bias_ref[per : per + 1, :] = column_sums(out_ref[...])
        wait(copies)

    if blocks:
        shapes = [sds((shards, 2, shard, hidden), BF)]
    else:
        shapes = [sds((width, hidden), BF), sds((hidden, width), BF)]
    result = call(
        kernel,
        "expert_grads",
        [rows_in, h, d_out, d_pre],
        [VM] * 4,
        shapes + [sds((8, width), F32)],
        [ANY] * len(shapes) + [VM],
        [
            pltpu.VMEM((width, hidden), BF),
            pltpu.VMEM((hidden, width), BF),
            pltpu.SemaphoreType.DMA((total,)),
        ],
    )
    return result[:-1], result[-1]


def attn_back(me, back_blocks, moe_part, grad, x, x1, qkv, cols, vecs, weights, below, tokens):
    padded, width = grad.shape
    owners = len(back_blocks)
    cap = back_blocks[0].shape[0]
    seats = owners * cap
    count = len(weights.arrays)
    shard = weights.arrays[0].shape[-2]

    def kernel(*refs):
        refs = list(refs)
        me_ref = refs.pop(0)
        back_refs = [refs.pop(0) for _ in range(owners)]
        part_ref, grad_ref, x_ref, x1_ref, qkv_ref, cols_ref, vec_ref = (
            refs.pop(0) for _ in range(7)
        )
        w_refs = [refs.pop(0) for _ in range(count)]
        if below is not None:
            gates_ref, below_cols, below_rows = (refs.pop(0) for _ in range(3))
        dx_out, dy_out, dqkv_out, small_out = (refs.pop(0) for _ in range(4))
        seat_outs = [refs.pop(0) for _ in range(owners)] if below is not None else None
        wqkv, wout, sems, more_sems = refs
        targets = attn_targets(width, shard, wqkv, wout)
        right = fetch(w_refs, weights, me_ref[0], targets, 1, sems)
        left = fetch(w_refs, weights, me_ref[0], targets, 0, more_sems)
        start(right + left)
        vec = lambda k: vec_ref[k : k + 1, :]
        chosen = jnp.logical_or(seat_mask(cols_ref, 0, seats), seat_mask(cols_ref, 1, seats))
        d_moe = dot(one(chosen), join(back_refs)) + part_ref[...]
        normed2, rstd2 = norm_rows(x1_ref[...])
        small_out[...] = jnp.zeros_like(small_out)
        small_out[1:2, :] = jnp.sum(d_moe * normed2, 0, keepdims=True)
        small_out[3:4, :] = jnp.sum(d_moe, 0, keepdims=True)
        d_x1 = grad_ref[...] + norm_back(d_moe * vec(1), normed2, rstd2)
        dy = d_x1.astype(BF)
        dy_out[...] = dy
        small_out[6:7, :] = jnp.sum(dy.astype(F32), 0, keepdims=True)
        wait(right)
        d_mixed = dot_nt(dy, wout[...]).astype(BF)
        masks = head_masks()
        scale = HEAD_DIM ** (-0.5)
        for two in range(HEADS // 2):
            at = two * 2 * HEAD_DIM
            query = qkv_ref[:, at : at + 2 * HEAD_DIM]
            keys = qkv_ref[:, width + at : width + at + 2 * HEAD_DIM]
            values = qkv_ref[:, 2 * width + at : 2 * width + at + 2 * HEAD_DIM]
            d_o = d_mixed[:, at : at + 2 * HEAD_DIM]
            sums = None
            for mask in masks:
                probs = head_probs(query, keys, mask, tokens)
                d_here = jnp.where(mask, d_o, 0).astype(BF)
                d_probs = dot_nt(d_here, values)
                d_values = dot_tn(probs.astype(BF), d_here)
                d_scores = probs * (d_probs - jnp.sum(d_probs * probs, -1, keepdims=True))
                d_scores = d_scores.astype(BF)
                d_query = dot(d_scores, jnp.where(mask, keys, 0).astype(BF))
                d_keys = dot_tn(d_scores, jnp.where(mask, query, 0).astype(BF))
                here = (d_query, d_keys, d_values)
                sums = here if sums is None else tuple(s + h for s, h in zip(sums, here))
            dqkv_out[:, at : at + 2 * HEAD_DIM] = (sums[0] * scale).astype(BF)
            dqkv_out[:, width + at : width + at + 2 * HEAD_DIM] = (sums[1] * scale).astype(BF)
            dqkv_out[:, 2 * width + at : 2 * width + at + 2 * HEAD_DIM] = sums[2].astype(BF)
        wait(left)
        d_normed = None
        for k in range(3):
            here = dqkv_out[:, k * width : (k + 1) * width]
            if k != 1:
                row = 4 if k == 0 else 5
                small_out[row : row + 1, :] = jnp.sum(here.astype(F32), 0, keepdims=True)
            piece = dot_nt(here, wqkv[:, k * width : (k + 1) * width])
            d_normed = piece if d_normed is None else d_normed + piece
        normed1, rstd1 = norm_rows(x_ref[...])
        small_out[0:1, :] = jnp.sum(d_normed * normed1, 0, keepdims=True)
        small_out[2:3, :] = jnp.sum(d_normed, 0, keepdims=True)
        d_x = d_x1 + norm_back(d_normed * vec(0), normed1, rstd1)
        dx_out[...] = d_x[0 : dx_out.shape[0], :]
        if below is not None:
            part(seat_grads(d_x, gates_ref[...], below_cols, below_rows, seats), seat_outs)

    shapes = [
        sds((padded if below is not None else tokens, width), F32),
        sds((padded, width), BF),
        sds((padded, 3 * width), BF),
        sds((16, width), F32),
    ]
    args = [me, *back_blocks, moe_part, grad, x, x1, qkv, cols, vecs, *weights.arrays]
    specs = [SM] + [VM] * (owners + 7) + [ANY] * count
    if below is not None:
        shapes += [sds((cap, width), BF)] * owners
        args += list(below)
        specs += [VM] * 3
    result = call(
        kernel,
        "attn_back",
        args,
        specs,
        shapes,
        [VM] * len(shapes),
        [
            pltpu.VMEM((width, 3 * width), BF),
            pltpu.VMEM((width, width), BF),
            pltpu.SemaphoreType.DMA((copies_in(weights),)),
            pltpu.SemaphoreType.DMA((copies_in(weights),)),
        ],
    )
    return result[:4], result[4:]


def attn_grads(me, z, a_low, o_low, moe_low, dqkv, dy, dz, small, biases, rows, order):
    padded, width = a_low.shape
    half = 2 * width + LANES
    total = 4 * len(order) if order else 2

    def kernel(
        me_ref, z_ref, a_ref, o_ref, moe_ref, dqkv_ref, dy_ref, dz_ref, small_ref, bias_ref, *refs
    ):
        refs = list(refs)
        outs = [refs.pop(0) for _ in range(2)]
        wide, tall, sems = refs
        for k in range(3):
            at = k * width + (LANES if k == 2 else 0)
            wide[:, at : at + width] = dot_tn(
                a_ref[...], dqkv_ref[:, k * width : (k + 1) * width]
            ).astype(BF)
        wide[:, 2 * width : half] = jnp.zeros((width, LANES), BF)
        wide[:, half + width : half + 2 * width] = dot_tn(o_ref[...], dy_ref[...]).astype(BF)
        high, low = split(dz_ref[...])
        d_router = dot_tn(moe_ref[...], high) + dot_tn(moe_ref[...], low)
        tall[...] = jnp.zeros_like(tall)
        tall[16:32, :] = small_ref[...]
        tall[pl.ds(pl.multiple_of(32 + 8 * z_ref[0], 8), 8), :] = bias_ref[...]
        wide[:, half + 2 * width : 2 * half] = (d_router + tall[...].T).astype(BF)
        if order:
            pieces = [(rows, 0, p * half, half, (p, ALL, ALL)) for p in range(2)]
            copies = spread(wide, me_ref[0], outs, (order, [o ^ 1 for o in order]), rows, pieces, sems)
        else:
            copies = [
                pltpu.make_async_copy(wide.at[:, pl.ds(p * half, half)], outs[p], sems.at[p])
                for p in range(2)
            ]
        start(copies)
        wait(copies)

    if order:
        shapes = [sds((len(order), 2, rows, half), BF)] * 2
    else:
        shapes = [sds((width, half), BF)] * 2
    return call(
        kernel,
        "attn_grads",
        [me, z, a_low, o_low, moe_low, dqkv, dy, dz, small, biases],
        [SM, SM] + [VM] * 8,
        shapes,
        [ANY] * 2,
        [
            pltpu.VMEM((width, 2 * half), BF),
            pltpu.VMEM((LANES, width), F32),
            pltpu.SemaphoreType.DMA((total,)),
        ],
    )


def small_out(smalls, z, experts, per):
    layers = len(smalls)
    shard = smalls[0].shape[0]

    def kernel(z_ref, *refs):
        ins = refs[:layers]
        gains, biases, router, bias_in, bias_oe, square = refs[layers:]
        for layer in range(layers):
            square[...] = jnp.zeros_like(square)
            square[0:shard, :] = ins[layer][...]
            square[...] = square[...].T
            router[layer] = square[0:experts, 0:shard]
            gains[layer] = square[16:18, 0:shard]
            for k in range(5):
                biases[k, layer : layer + 1, :] = square[18 + k : 19 + k, 0:shard]
            own = square[pl.ds(pl.multiple_of(32 + 8 * z_ref[0], 8), 8), :]
            for q in range(per):
                bias_in[layer, :, q * shard : (q + 1) * shard] = own[q : q + 1, 0:shard]
            bias_oe[layer] = own[per : per + 1, 0:shard]

    shapes = [
        sds((layers, 2, shard), F32),
        sds((5, layers, shard), F32),
        sds((layers, experts, shard), F32),
        sds((layers, 1, per * shard), F32),
        sds((layers, 1, shard), F32),
    ]
    return call(
        kernel,
        "small_out",
        [z, *smalls],
        [SM] + [VM] * layers,
        shapes,
        [VM] * 5,
        [pltpu.VMEM((LANES, LANES), F32)],
    )


def swap(value, axis, bit):
    size = lax.axis_size(axis)
    return lax.ppermute(value, axis, [(i, i ^ bit) for i in range(size)])


def exchange(blocks):
    order = sorted(range(1, len(blocks)), key=lambda k: -(k & 2))
    got = {k: swap(blocks[k], "expert", k) for k in order}
    return [blocks[0]] + [got[k] for k in range(1, len(blocks))]


def axis_bits(axis, bit):
    bits = []
    while bit < lax.axis_size(axis):
        bits.append(bit)
        bit *= 2
    return bits


def sum_experts(value):
    for bit in axis_bits("expert", 1):
        low = value.astype(BF)
        value = low.astype(F32) + swap(low, "expert", bit).astype(F32)
    return value


def gather_rows(shard):
    return lax.all_gather(shard, "dp", axis=0, tiled=True)


def scatter_rows(whole):
    return lax.psum_scatter(whole, "dp", scatter_dimension=0, tiled=True)


ORDER = [0, 2, 4, 6]


class Gather:
    def __init__(self, shard):
        self.shard = shard
        self.x, self.y = swap(shard, "dp", 2), swap(shard, "dp", 4)

    def turn(self):
        two, rows, width = self.shard.shape
        block = (two, rows, width)
        half = (1, rows, width)
        self.cut = move(
            "cut",
            [self.x, self.y, self.shard],
            [
                (0, (pl.ds(0, 1),), 0, (ALL,), half),
                (1, (pl.ds(1, 1),), 1, (ALL,), half),
                (0, (ALL,), 2, (1,), block),
                (1, (ALL,), 2, (2,), block),
                (2, (ALL,), 2, (0,), block),
            ],
            [sds(half, BF)] * 2 + [sds((3, *block), BF)],
        )

    def send(self, after=()):
        if after:
            self.cut = hold(self.cut, after)
        self.xy = swap(self.cut[0], "dp", 4), swap(self.cut[1], "dp", 2)
        self.other = swap(self.cut[2], "dp", 1)

    def cross(self, after=()):
        if after:
            self.xy = hold(self.xy, after)
        self.across = [swap(value, "dp", 1) for value in self.xy]

    def weights(self):
        pieces = [
            (self.shard, 0, (0, 1)),
            (self.x, 2, (0, 1)),
            (self.y, 4, (0, 1)),
            (self.xy[0], 6, (0,)),
            (self.xy[1], 6, (1,)),
            (self.across[0], 7, (0,)),
            (self.across[1], 7, (1,)),
            (self.other, (1, 3, 5), (0, 1)),
        ]
        return Weights([p[0] for p in pieces], [p[1:] for p in pieces])


def full(rows):
    return (pl.ds(0, rows), ALL)


class AttnSum:
    def __init__(self, grads, after=()):
        self.mine, theirs = grads
        if after:
            theirs = hold([theirs], after)[0]
        self.came = swap(theirs, "dp", 1)
        self.rows, self.width = self.mine.shape[2:]

    def fold0(self):
        shape = (self.rows, self.width)
        flat = full(self.rows)
        places = [(3, 0, 0, flat), (3, 1, 1, flat)]
        places += [(k, p, o, (p,)) for k, o in ((1, 2), (2, 3), (0, 4)) for p in range(2)]
        out = fold(
            "fold0",
            [self.mine, self.came],
            shape,
            [([(0, (k, p)), (1, (k, p))], BF, [(o, into, flat)]) for k, p, o, into in places],
            [sds(shape, BF)] * 2 + [sds((2, *shape), BF)] * 3,
        )
        self.across = out[:2]
        self.x, self.y, self.own = out[2:]

    def send_across(self):
        self.across = swap(self.across[0], "dp", 4), swap(self.across[1], "dp", 2)

    def fold1(self):
        self.x, self.y = fold1(self.x, self.y, self.across)
        self.came = swap(self.x, "dp", 2), swap(self.y, "dp", 4)

    def fold2(self):
        shape = (self.rows, self.width)
        flat = full(self.rows)
        self.parts = fold(
            "fold2",
            [self.own, *self.came],
            shape,
            [([(i, (p,)) for i in range(3)], BF, [(p, flat, flat)]) for p in range(2)],
            [sds(shape, BF)] * 2,
        )
        self.bits = axis_bits("expert", 1)
        self.send()

    def send(self):
        n = len(self.bits)
        up_bit = self.bits[self.done] if hasattr(self, "done") else self.bits[0]
        self.done = getattr(self, "done", 0)
        down_bit = self.bits[n - 1 - self.done]
        self.came = swap(self.parts[0], "expert", up_bit), swap(self.parts[1], "expert", down_bit)

    def fold3(self, layer, layers, given):
        shape = (self.rows, self.width)
        flat = full(self.rows)
        self.done += 1
        terms = [[(0, flat), (2, flat)], [(1, flat), (3, flat)]]
        args = [*self.parts, *self.came]
        if self.done < len(self.bits):
            self.parts = fold(
                "fold3",
                args,
                shape,
                [(terms[p], BF, [(p, flat, flat)]) for p in range(2)],
                [sds(shape, BF)] * 2,
                )
            self.send()
            return None
        wide = (self.width - LANES) // 2
        cut = lambda first, size: (ALL, pl.ds(first, size))
        tasks = [
            (terms[0], F32, [(0, (layer, ALL, pl.ds(0, 2 * wide)), cut(0, 2 * wide))]),
            (
                terms[1],
                F32,
                [
                    (0, (layer, ALL, pl.ds(2 * wide, wide)), cut(0, wide)),
                    (1, (layer,), cut(wide, wide)),
                    (2, flat, cut(2 * wide, LANES)),
                ],
            ),
        ]
        outs = [
            sds((layers, self.rows, 3 * wide), F32),
            sds((layers, self.rows, wide), F32),
            sds((self.rows, LANES), F32),
        ]
        aliases = {4: 0, 5: 1} if given else None
        return fold("attn_out", args + list(given), shape, tasks, outs, aliases)


def fold1(x, y, across):
    shape = x.shape[1:]
    flat = full(shape[0])
    return fold(
        "fold1",
        [x, y, *across],
        shape,
        [
            ([(0, (0,)), (2, flat)], BF, [(0, (0,), flat)]),
            ([(1, (1,)), (3, flat)], BF, [(1, (1,), flat)]),
        ],
        [sds(x.shape, BF)] * 2,
        {0: 0, 1: 1},
    )


def expert_out(total, layer, layers, given, width):
    rows, broad = total.shape[1:]
    per = broad // width
    second = [
        (1, (layer, 0, pl.ds(q * rows, rows)), (ALL, pl.ds(q * width, width))) for q in range(per)
    ]
    outs = [sds((layers, 1, rows, broad), F32), sds((layers, 1, per * rows, width), F32)]
    return fold(
        "expert_out",
        [total, *given],
        (rows, broad),
        [
            ([(0, (0,))], F32, [(0, (layer, 0), full(rows))]),
            ([(0, (1,))], F32, second),
        ],
        outs,
        {1: 0, 2: 1} if given else None,
    )


def per_device(
    image_tokens,
    norm_gains,
    biases,
    w_qkv,
    w_out,
    w_router,
    router_noise,
    w_in,
    b_in,
    w_outexp,
    b_expout,
    routes,
    seat_order,
    cotangent,
):
    layers = w_qkv.shape[0]
    tokens, width = image_tokens.shape
    experts = w_router.shape[2]
    shards = lax.axis_size("dp")
    assert tokens == SEQ and experts == lax.axis_size("expert")
    assert width == HEADS * HEAD_DIM
    padded = up(tokens, 16)
    cap = 2 * tokens // experts
    cap_pad = up(cap, 8)
    shard = w_qkv.shape[1]
    hidden_shard = w_outexp.shape[2]
    hidden = w_in.shape[3]
    per = hidden_shard // shard
    index = lax.axis_index("dp").astype(jnp.int32)
    me = index.reshape(1)
    z = lax.axis_index("expert").astype(jnp.int32).reshape(1)
    bits = axis_bits("dp", 2)
    four = bits == [2, 4] and shard % 16 == 0 and axis_bits("expert", 1) == [1, 2]
    order = ORDER if four else None

    Order.token = None

    def pack_attn(layer):
        return move(
            "pack_attn",
            [w_qkv, w_out],
            [
                (0, (layer, ALL, pl.ds(0, 2 * width)), 0, (0,), (shard, 2 * width)),
                (
                    0,
                    (layer, ALL, pl.ds(2 * width, width)),
                    0,
                    (1, ALL, pl.ds(0, width)),
                    (shard, width),
                ),
                (1, (layer,), 0, (1, ALL, pl.ds(width, width)), (shard, width)),
            ],
            [sds((2, shard, 2 * width), BF)],
        )[0]

    def pack_expert(layer):
        return move(
            "pack_expert",
            [w_in, w_outexp],
            [(0, (layer, 0), 0, (0,), (shard, hidden))]
            + [
                (
                    1,
                    (layer, 0, pl.ds(q * shard, shard)),
                    0,
                    (1, ALL, pl.ds(q * width, width)),
                    (shard, width),
                )
                for q in range(per)
            ],
            [sds((2, shard, hidden), BF)],
        )[0]

    aligned = shard % 16 == 0
    whole = [(None, (0,)), (None, (1,))]

    def fetch_attn(layer):
        if four:
            return Gather(pack_attn(layer))
        right = jnp.concatenate([w_qkv[layer][:, 2 * width :], w_out[layer]], 1)
        attn = [gather_rows(v)[None] for v in (w_qkv[layer][:, : 2 * width], right)]
        return Weights(attn, whole)

    def fetch_expert(layer):
        if aligned:
            both = lax.all_gather(pack_expert(layer), "dp", axis=0)
            return Weights([both], [(OWNERS, (0, 1))])
        both = [gather_rows(w_in[layer, 0])[None], gather_rows(w_outexp[layer, 0])[None]]
        return Weights(both, whole)

    def attn_weights(gathered):
        return gathered.weights() if four else gathered

    last = layers - 1
    attn_w = [fetch_attn(0)]
    expert_w = [fetch_expert(layer) for layer in range(layers)]
    cols, rows = place_pairs(
        routes, seat_order.reshape(layers, tokens, 2), padded, cap, cap_pad, z
    )
    small = pack_small(norm_gains, biases, w_router, b_in, b_expout)
    if four:
        attn_w[0].turn()
        attn_w[0].send()
    small = lax.all_gather(small, "dp", axis=0)
    params = unpack_small(small, layers, shard, per, experts)
    if last > 0:
        attn_w.append(fetch_attn(1))

    saved = []
    x_args = (image_tokens,)
    if four:
        attn_w[0].cross()
    for layer in range(layers):
        vecs, router, bias_in, bias_oe = params[layer]
        attn_w[layer] = attn_weights(attn_w[layer])
        kept, sent = attn_fwd(
            me,
            layer,
            x_args,
            attn_w[layer],
            vecs,
            router,
            router_noise,
            cols[layer],
            rows[layer],
            cap_pad,
        )
        sent = exchange(sent)
        if layer < last:
            if four:
                attn_w[layer + 1].turn()
                attn_w[layer + 1].send(sent[1:])
            if layer + 1 < last:
                attn_w.append(fetch_attn(layer + 2))
        else:
            grad, grad_seats = top_seats(
                cotangent, kept[5], cols[last], rows[last], cap_pad, experts
            )
            grad_seats = exchange(hold(grad_seats, sent[1:]))
        held, made = expert_fwd(me, sent, expert_w[layer], bias_in, bias_oe)
        if four and layer < last:
            attn_w[layer + 1].cross(made[:1])
        returned = exchange(made)
        saved.append((kept, held, returned))
        x_args = (kept[1], kept[5], cols[layer], returned)

    mixed = None
    attn_sums, expert_sums = [None] * layers, [None] * layers
    for layer in reversed(range(layers)):
        (x, x1, a_low, qkv, o_low, gates, moe_low), (seat_rows, h, slope), returned = saved[layer]
        vecs, router = params[layer][:2]

        def gate_part():
            return gate_back(
                grad, x1, gates, cols[layer], router, returned, tokens, layer == last
            )

        if layer < last:
            dz, moe_part = gate_part()
            if four:
                attn_sums[layer + 1] = AttnSum(g_attn, grad_seats[1:])
        d_out, d_pre, d_rows = expert_back(me, grad_seats, slope, expert_w[layer])
        d_back = exchange(d_rows)
        if layer == last:
            dz, moe_part, mixed = gate_part()
        g_expert, g_bias = expert_grads(seat_rows, h, d_out, d_pre, shards, aligned)
        held = list(g_expert)
        above = attn_sums[layer + 1] if four and layer < last else None
        if above:
            above.fold0()
            held += above.across
        held = hold(held, d_back[1:])
        g_expert = held[: len(g_expert)]
        if above:
            above.across = held[len(g_expert) :]
            above.send_across()
        if aligned:
            expert_sums[layer] = lax.psum_scatter(g_expert[0], "dp", scatter_dimension=0)
        else:
            expert_sums[layer] = [scatter_rows(v) for v in g_expert]
        below = None
        if layer > 0:
            below = (saved[layer - 1][0][5], cols[layer - 1], rows[layer - 1])
        (grad, dy, dqkv, small_grads), grad_seats = attn_back(
            me,
            d_back,
            moe_part,
            grad,
            x,
            x1,
            qkv,
            cols[layer],
            vecs,
            attn_w[layer],
            below,
            tokens,
        )
        grad_seats = exchange(grad_seats) if layer > 0 else None
        if above:
            above.fold1()
        g_attn = attn_grads(
            me, z, a_low, o_low, moe_low, dqkv, dy, dz, small_grads, g_bias, shard, order
        )
        if not four:
            attn_sums[layer] = [sum_experts(scatter_rows(v)) for v in g_attn]

    if four:
        done_attn, smalls = (), [None] * layers
        attn_sums[0] = AttnSum(g_attn)
        attn_sums[0].fold0()
        attn_sums[0].send_across()
        for layer in reversed(range(1, layers)):
            attn_sums[layer].fold2()
        attn_sums[0].fold1()
        for layer in reversed(range(1, layers)):
            attn_sums[layer].fold3(layer, layers, done_attn)
        attn_sums[0].fold2()
        for layer in reversed(range(1, layers)):
            out = attn_sums[layer].fold3(layer, layers, done_attn)
            done_attn, smalls[layer] = out[:2], out[2]
    if aligned:
        done_expert = ()
        for layer in reversed(range(layers)):
            done_expert = expert_out(expert_sums[layer], layer, layers, done_expert, width)
            if four and layer == 1:
                attn_sums[0].fold3(0, layers, done_attn)
        grad_in, grad_oe = done_expert
    else:
        grad_in = jnp.stack([item[0] for item in expert_sums])[:, None].astype(F32)
        grad_oe = jnp.stack([item[1] for item in expert_sums])[:, None].astype(F32)
    if four:
        out = attn_sums[0].fold3(0, layers, done_attn)
        (grad_qkv, grad_out), smalls[0] = out[:2], out[2]
    else:
        left = jnp.stack([item[0] for item in attn_sums])
        right = jnp.stack([item[1] for item in attn_sums])
        grad_qkv = jnp.concatenate([left[:, :, : 2 * width], right[:, :, :width]], 2)
        grad_out = right[:, :, width : 2 * width]
        smalls = [right[layer, :, 2 * width :] for layer in range(layers)]
    gains, shifts, grad_router, grad_bin, grad_boe = small_out(smalls, z, experts, per)
    return (
        mixed,
        grad,
        gains,
        jnp.transpose(shifts, (1, 0, 2)),
        grad_qkv,
        grad_out,
        jnp.transpose(grad_router, (0, 2, 1)),
        grad_in,
        grad_bin,
        grad_oe,
        grad_boe,
    )


def solution(mesh):
    return jax.shard_map(
        per_device,
        mesh=mesh,
        in_specs=(
            P(("dp", "expert"), None),
            P(None, None, "dp"),
            P(None, None, "dp"),
            P(None, "dp", None),
            P(None, "dp", None),
            P(None, "dp", None),
            P(None, ("dp", "expert"), None),
            P(None, "expert", "dp", None),
            P(None, "expert", "dp"),
            P(None, "expert", "dp", None),
            P(None, "expert", "dp"),
            P(None, ("dp", "expert"), None),
            P(None, ("dp", "expert"), None),
            P(("dp", "expert"), None),
        ),
        out_specs=(
            P(("dp", "expert"), None),
            P(("dp", "expert"), None),
            P(None, None, "dp"),
            P(None, None, "dp"),
            P(None, "dp", None),
            P(None, "dp", None),
            P(None, "dp", None),
            P(None, "expert", "dp", None),
            P(None, "expert", "dp"),
            P(None, "expert", "dp", None),
            P(None, "expert", "dp"),
        ),
        check_vma=False,
    )
```

```python
import functools

import jax
import jax.numpy as jnp
from jax import lax
from jax.experimental import pallas as pl
from jax.experimental.pallas import tpu as pltpu
from jax.sharding import PartitionSpec as P

HEADS = 12
HEAD_DIM = 64
SEQ = 197
EPS = 1e-06
BF = jnp.bfloat16
F32 = jnp.float32
LANES = 128
NEG = -1e30
VMEM_LIMIT = 60 * 1024 * 1024


def up(value, step):
    return -(-value // step) * step


def dot(left, right):
    return lax.dot_general(left, right, (((1,), (0,)), ((), ())), preferred_element_type=F32)


def dot_nt(left, right):
    return lax.dot_general(left, right, (((1,), (1,)), ((), ())), preferred_element_type=F32)


def dot_tn(left, right):
    return lax.dot_general(left, right, (((0,), (0,)), ((), ())), preferred_element_type=F32)


def norm_rows(x):
    centered = x - jnp.mean(x, -1, keepdims=True)
    rstd = lax.rsqrt(jnp.mean(centered * centered, -1, keepdims=True) + EPS)
    return centered * rstd, rstd


def norm_back(grad_hat, normed, rstd):
    return rstd * (
        grad_hat
        - jnp.mean(grad_hat, -1, keepdims=True)
        - normed * jnp.mean(grad_hat * normed, -1, keepdims=True)
    )


def split(value):
    high = value.astype(BF)
    return high, (value - high.astype(F32)).astype(BF)


def join(refs):
    return jnp.concatenate([ref[...].astype(F32) for ref in refs], 0).astype(BF)


def part(value, refs):
    rows = refs[0].shape[0]
    for number, ref in enumerate(refs):
        ref[...] = value[number * rows : (number + 1) * rows].astype(ref.dtype)


def seat_mask(cols_ref, pair, seats):
    column = cols_ref[:, pair : pair + 1]
    return lax.broadcasted_iota(jnp.int32, (column.shape[0], seats), 1) == column


def token_mask(rows_ref, pair, seats):
    row = rows_ref[pair : pair + 1, :]
    return lax.broadcasted_iota(jnp.int32, (seats, row.shape[1]), 0) == row


def one(mask):
    return jnp.where(mask, 1.0, 0.0).astype(BF)


def pair_gate(gates, cols_ref, pair):
    route = cols_ref[:, 2 + pair : 3 + pair]
    lanes = lax.broadcasted_iota(jnp.int32, gates.shape, 1)
    return jnp.sum(jnp.where(lanes == route, gates, 0.0), -1, keepdims=True)


def combine(x1, gates, cols_ref, returned):
    total = x1
    for pair in range(2):
        piece = dot(one(seat_mask(cols_ref, pair, returned.shape[0])), returned)
        total = total + pair_gate(gates, cols_ref, pair) * piece
    return total


def rows_to_seats(rows_ref, seats, values):
    chosen = jnp.logical_or(token_mask(rows_ref, 0, seats), token_mask(rows_ref, 1, seats))
    return dot(one(chosen), values)


def with_note(block, cap, note):
    base = cap // 8 * 8
    tail = block[base:]
    left = tail[:, 0:LANES]
    row = lax.broadcasted_iota(jnp.int32, left.shape, 0)
    high = note.astype(BF).astype(F32)
    left = jnp.where(row == cap - base, high, left)
    left = jnp.where(row == cap - base + 1, note - high, left)
    return jnp.concatenate([block[:base], jnp.concatenate([left, tail[:, LANES:]], 1)], 0)


def note_of(block, cap):
    return block[cap : cap + 1, 0:LANES] + block[cap + 1 : cap + 2, 0:LANES]


def as_column(note, rows):
    shape = (rows, LANES)
    same = lax.broadcasted_iota(jnp.int32, shape, 0) == lax.broadcasted_iota(jnp.int32, shape, 1)
    return jnp.sum(jnp.where(same, note, 0.0), -1, keepdims=True)


def lane_sums(value):
    rows, width = value.shape
    value = jnp.concatenate([value, jnp.zeros((LANES - rows, width), F32)], 0)
    ones = jnp.ones((8, width), BF)
    high, low = split(value)
    return (dot_nt(ones, high) + dot_nt(ones, low))[0:1, :]


def near_lanes(cols_ref, pair, block, cap_pad):
    column = cols_ref[:, pair : pair + 1] - block * cap_pad
    lanes = lax.broadcasted_iota(jnp.int32, (column.shape[0], LANES), 1)
    return jnp.logical_and(lanes == column, lanes < cap_pad)


def head_masks():
    lanes = lax.broadcasted_iota(jnp.int32, (1, 2 * HEAD_DIM), 1)
    return (lanes < HEAD_DIM, lanes >= HEAD_DIM)


def head_probs(query, keys, mask, tokens):
    query = jnp.where(mask, query, 0).astype(F32) * HEAD_DIM ** (-0.5)
    scores = dot_nt(query.astype(BF), keys)
    lanes = lax.broadcasted_iota(jnp.int32, scores.shape, 1)
    scores = jnp.where(lanes < tokens, scores, NEG)
    raised = jnp.exp(scores - jnp.max(scores, -1, keepdims=True))
    return raised * (1.0 / jnp.sum(raised, -1, keepdims=True))


VM = pl.BlockSpec(memory_space=pltpu.VMEM)
ANY = pl.BlockSpec(memory_space=pl.ANY)
SM = pl.BlockSpec(memory_space=pltpu.SMEM)


def sds(shape, dtype):
    return jax.ShapeDtypeStruct(tuple(shape), dtype)


class Order:
    token = None


LOAD = "load"
STORE = "store"


class Load:
    def __init__(self, source, held, sem):
        self.copy, self.held, self.came = pltpu.make_async_copy(source, held, sem), held, False
        self.shape = held.shape
        self.copy.start()

    def wait(self):
        if not self.came:
            self.copy.wait()
            self.came = True

    def __getitem__(self, index):
        self.wait()
        return self.held[index]


class Store:
    def __init__(self, target, held, sems):
        self.target, self.held, self.sems, self.copies = target, held, sems, []
        self.shape, self.dtype = held.shape, held.dtype

    def __getitem__(self, index):
        return self.held[index]

    def __setitem__(self, index, value):
        self.held[index] = value

    def send(self, *index):
        number = len(self.copies)
        copy = pltpu.make_async_copy(
            self.held.at[index], self.target.at[index], self.sems.at[number]
        )
        copy.start()
        self.copies.append(copy)

    def finish(self):
        if not self.copies:
            self.send(*[slice(None)] * len(self.shape))


PARTS = 8


def call(kernel, name, args, specs, outs, out_specs, scratch, aliases=None):
    after = []
    if Order.token is not None and not any(Order.token is arg for arg in args):
        after = [Order.token]
    given = len(args)
    single = not isinstance(outs, (tuple, list))
    results = [outs] if single else list(outs)
    out_kinds = [out_specs] if single else list(out_specs)
    loads = [i for i, spec in enumerate(specs) if spec is LOAD]
    stores = [i for i, spec in enumerate(out_kinds) if spec is STORE]
    extra = [pltpu.VMEM(args[i].shape, args[i].dtype) for i in loads]
    extra += [pltpu.VMEM(results[i].shape, results[i].dtype) for i in stores]
    extra += [pltpu.SemaphoreType.DMA((max(len(loads), 1),))]
    extra += [pltpu.SemaphoreType.DMA((max(PARTS * len(stores), 1),))]

    def body(*refs):
        ins = list(refs[:given])
        rest = list(refs[given + len(after) :])
        made, own = rest[: len(results)], rest[len(results) : len(rest) - len(extra)]
        held = rest[len(rest) - len(extra) :]
        load_sems, store_sems = held[-2:]
        for n, i in enumerate(loads):
            ins[i] = Load(ins[i], held[n], load_sems.at[n])
        for n, i in enumerate(stores):
            sems = store_sems.at[pl.ds(PARTS * n, PARTS)]
            made[i] = Store(made[i], held[len(loads) + n], sems)
        kernel(*ins, *made, *own)
        for i in loads:
            ins[i].wait()
        for i in stores:
            made[i].finish()
        for i in stores:
            for copy in made[i].copies:
                copy.wait()

    result = pl.pallas_call(
        body,
        name=name,
        in_specs=[ANY if spec is LOAD else spec for spec in specs] + [ANY] * len(after),
        out_specs=ANY if single and out_specs is STORE else (
            out_specs if single else [ANY if spec is STORE else spec for spec in out_kinds]
        ),
        out_shape=outs,
        scratch_shapes=list(scratch) + extra,
        input_output_aliases=aliases or {},
        compiler_params=pltpu.CompilerParams(vmem_limit_bytes=VMEM_LIMIT),
    )(*args, *after)
    Order.token = result[0] if isinstance(result, (tuple, list)) else result
    return result


def hold(values, after):
    def kernel(*refs):
        pass

    return call(
        kernel,
        "hold",
        [*values, *after],
        [ANY] * (len(values) + len(after)),
        [sds(value.shape, value.dtype) for value in values],
        [ANY] * len(values),
        [],
        {i: i for i in range(len(values))},
    )


def move(name, args, copies, outs):
    total = len(copies)

    def kernel(*refs):
        ins, rest = refs[: len(args)], refs[len(args) :]
        results, held = rest[: len(outs)], rest[len(outs) : len(outs) + total]
        in_sems, out_sems = rest[-2:]
        loads = [
            pltpu.make_async_copy(ins[i].at[where], held[n], in_sems.at[n])
            for n, (i, where, _, _, _) in enumerate(copies)
        ]
        stores = [
            pltpu.make_async_copy(held[n], results[o].at[into], out_sems.at[n])
            for n, (_, _, o, into, _) in enumerate(copies)
        ]
        start(loads)
        for load, store in zip(loads, stores):
            load.wait()
            store.start()
        wait(stores)

    return call(
        kernel,
        name,
        args,
        [ANY] * len(args),
        outs,
        [ANY] * len(outs),
        [pltpu.VMEM(shape, BF) for *_, shape in copies]
        + [pltpu.SemaphoreType.DMA((total,)), pltpu.SemaphoreType.DMA((total,))],
    )


def fold(name, args, block, tasks, outs, aliases=None):
    terms = [(t, term) for t, (listed, _, _) in enumerate(tasks) for term in listed]
    writes = [(t, write) for t, (_, _, listed) in enumerate(tasks) for write in listed]
    wide = [t for t, task in enumerate(tasks) if task[1] == F32]
    slim = [t for t, task in enumerate(tasks) if task[1] != F32]

    def kernel(*refs):
        ins, rest = refs[: len(args)], refs[len(args) :]
        results = rest[: len(outs)]
        loaded, wide_ref, slim_ref, in_sems, out_sems = rest[len(outs) :]
        loads = [
            pltpu.make_async_copy(ins[i].at[where], loaded.at[n], in_sems.at[n])
            for n, (_, (i, where)) in enumerate(terms)
        ]
        for copy in loads:
            copy.start()
        stores = []
        for t, (_, kind, _) in enumerate(tasks):
            total = None
            for n, (task, _) in enumerate(terms):
                if task == t:
                    loads[n].wait()
                    piece = loaded[n].astype(F32)
                    total = piece if total is None else total + piece
            holder = wide_ref.at[wide.index(t)] if kind == F32 else slim_ref.at[slim.index(t)]
            holder[...] = total.astype(kind)
            for n, (task, (o, into, within)) in enumerate(writes):
                if task == t:
                    copy = pltpu.make_async_copy(
                        holder.at[within], results[o].at[into], out_sems.at[n]
                    )
                    copy.start()
                    stores.append(copy)
        for copy in stores:
            copy.wait()

    return call(
        kernel,
        name,
        args,
        [ANY] * len(args),
        outs,
        [ANY] * len(outs),
        [
            pltpu.VMEM((len(terms), *block), BF),
            pltpu.VMEM((max(len(wide), 1), *(block if wide else (16, LANES))), F32),
            pltpu.VMEM((max(len(slim), 1), *(block if slim else (16, LANES))), BF),
            pltpu.SemaphoreType.DMA((len(terms),)),
            pltpu.SemaphoreType.DMA((len(writes),)),
        ],
        aliases=aliases,
    )


ALL = slice(None)


class Weights:
    def __init__(self, arrays, places):
        self.arrays, self.places = list(arrays), places


OWNERS = -1


def attn_targets(width, rows, wqkv, wout):
    return {
        0: [(wqkv, 0, 2 * width, 0, rows, 0)],
        1: [(wqkv, 0, width, 2 * width, rows, 0), (wout, width, width, 0, rows, 0)],
    }


def expert_targets(width, hidden, rows, whole, win, woe):
    if whole:
        return {0: [(win, 0, hidden, 0, rows, 0)], 1: [(woe, 0, width, 0, rows, 0)]}
    per = hidden // width
    return {
        0: [(win, 0, hidden, 0, rows, 0)],
        1: [(woe, q * width, width, 0, per * rows, q * rows) for q in range(per)],
    }


class Chunks:
    def __init__(self, refs, weights, width, hidden, rows, whole, win, woe, sems, more=()):
        per = hidden // width
        self.parts = []
        if whole:
            copies = fetch(refs, weights, None, expert_targets(width, hidden, rows, True, win, woe), 0, sems)
            copies += fetch(
                refs, weights, None, expert_targets(width, hidden, rows, True, win, woe), 1, sems
            )
            self.parts = [copies] + [[] for _ in range(per - 1)]
        else:
            ref = refs[0]
            shards = ref.shape[0]
            for c in range(per):
                here = pl.ds(c * width, width)
                copies = [
                    pltpu.make_async_copy(
                        ref.at[d, 0, :, here], win.at[pl.ds(d * rows, rows), here], sems.at[d]
                    )
                    for d in range(shards)
                ]
                first = c * shards // per
                for n in range(shards):
                    d, q = first + n // per, n % per
                    copies.append(
                        pltpu.make_async_copy(
                            ref.at[d, 1, :, pl.ds(q * width, width)],
                            woe.at[pl.ds((d * per + q) * rows, rows)],
                            sems.at[shards + n],
                        )
                    )
                self.parts.append(copies)
        for copies, extra in zip(self.parts, more):
            copies.append(extra)
        start(self.parts[0])

    def take(self, c):
        wait(self.parts[c])
        if c + 1 < len(self.parts):
            start(self.parts[c + 1])


def copies_in(weights):
    return 4 * sum(
        len(parts) if array.ndim == 3 else array.shape[0]
        for array, (off, parts) in zip(weights.arrays, weights.places)
    )


def fetch(refs, weights, me, targets, part_number, sems):
    copies = []
    for ref, (off, parts) in zip(refs, weights.places):
        rows = ref.shape[-2]
        if off == OWNERS:
            sources = [(d, (d, part_number)) for d in range(ref.shape[0])]
        elif isinstance(off, tuple):
            sources = [(me ^ o, (k, part_number)) for k, o in enumerate(off)]
        elif part_number in parts:
            at = None if off is None else me ^ off
            sources = [(at, (parts.index(part_number),))]
        else:
            sources = []
        for at, where in sources:
            for scratch, first, size, into, times, plus in targets[part_number]:
                place = 0 if at is None else at * times + plus
                if off not in (None, OWNERS):
                    place = pl.multiple_of(place, 16)
                copies.append(
                    pltpu.make_async_copy(
                        ref.at[(*where, ALL, pl.ds(first, size))],
                        scratch.at[pl.ds(place, rows), pl.ds(into, size)],
                        sems.at[len(copies)],
                    )
                )
    return copies


def start(copies):
    for copy in copies:
        copy.start()


def wait(copies):
    for copy in copies:
        copy.wait()


def small_rows(per, experts):
    return up(7 + experts + per + 1, 8)


def pack_small(norm_gains, biases, w_router, b_in, b_expout):
    layers, shard, experts = w_router.shape
    per = b_in.shape[2] // shard
    height = small_rows(per, experts)

    def kernel(gain_ref, bias_ref, router_ref, in_ref, oe_ref, out, square):
        out[...] = jnp.zeros_like(out)
        for layer in range(layers):
            at = layer * height
            out[at : at + 2, 0:shard] = gain_ref[layer]
            out[at + 2 : at + 7, 0:shard] = bias_ref[layer]
            square[...] = jnp.zeros_like(square)
            square[0:shard, 0:experts] = router_ref[layer]
            turned = square[...].T
            out[at + 7 : at + 7 + experts, :] = turned[0:experts, :]
            at = at + 7 + experts
            for q in range(per):
                out[at + q : at + q + 1, 0:shard] = in_ref[layer, :, q * shard : (q + 1) * shard]
            out[at + per : at + per + 1, 0:shard] = oe_ref[layer]

    return call(
        kernel,
        "pack_small",
        [norm_gains, biases, w_router, b_in, b_expout],
        [VM] * 5,
        sds((layers * height, LANES), F32),
        VM,
        [pltpu.VMEM((LANES, LANES), F32)],
    )


def unpack_small(gathered, layers, shard, per, experts):
    shards = gathered.shape[0]
    width = shards * shard
    height = small_rows(per, experts)

    def kernel(ref, *refs):
        tall = refs[-1]
        for layer in range(layers):
            vec, router, bias_in, bias_oe = refs[4 * layer : 4 * layer + 4]
            at = layer * height
            vec[...] = jnp.zeros_like(vec)
            tall[...] = jnp.zeros_like(tall)
            for d in range(shards):
                here = slice(d * shard, (d + 1) * shard)
                vec[0:7, here] = ref[d, at : at + 7, 0:shard]
                tall[0:experts, here] = ref[d, at + 7 : at + 7 + experts, 0:shard]
                row = at + 7 + experts
                for q in range(per):
                    first = (d * per + q) * shard
                    bias_in[:, first : first + shard] = ref[d, row + q : row + q + 1, 0:shard]
                bias_oe[:, here] = ref[d, row + per : row + per + 1, 0:shard]
            router[...] = tall[...].T.astype(BF)

    shapes = []
    for _ in range(layers):
        shapes += [
            sds((8, width), F32),
            sds((width, LANES), BF),
            sds((1, width * per), F32),
            sds((1, width), F32),
        ]
    outs = call(
        kernel,
        "unpack_small",
        [gathered],
        [VM],
        shapes,
        [VM] * len(shapes),
        [pltpu.VMEM((LANES, width), F32)],
    )
    return [outs[4 * layer : 4 * layer + 4] for layer in range(layers)]


def place_pairs(routes, seat_order, padded, cap, cap_pad, z):
    layers, tokens, _ = routes.shape
    tall = up(padded, LANES)

    def kernel(z_ref, route_ref, order_ref, *refs):
        outs, wide = refs[:-1], refs[-1]
        lanes = lax.broadcasted_iota(jnp.int32, (tokens, LANES), 1)
        lanes_tall = lax.broadcasted_iota(jnp.int32, (tall, LANES), 1)
        for layer in range(layers):
            given = jnp.full((tokens, LANES), -1.0, F32)
            for k in range(2):
                given = jnp.where(lanes == k, route_ref[layer, :, k : k + 1].astype(F32), given)
                given = jnp.where(lanes == 2 + k, order_ref[layer, :, k : k + 1].astype(F32), given)
            wide[...] = jnp.full((tall, LANES), -1.0, F32)
            wide[0:tokens, :] = given
            table = wide[...]
            turned = table.T
            seats = []
            for k in range(2):
                expert, order = table[:, k : k + 1], table[:, 2 + k : 3 + k]
                rank = jnp.zeros((tall, 1), F32)
                for j in range(2):
                    ahead = jnp.logical_and(
                        turned[j : j + 1, :] == expert, turned[2 + j : 3 + j, :] < order
                    )
                    rank = rank + jnp.sum(jnp.where(ahead, 1.0, 0.0), -1, keepdims=True)
                expert, rank = expert.astype(jnp.int32), rank.astype(jnp.int32)
                near = jnp.bitwise_xor(expert, z_ref[0])
                good = jnp.logical_and(expert >= 0, rank < cap)
                seats.append(jnp.where(good, near * cap_pad + rank, -1).astype(F32))
            table = jnp.where(lanes_tall == 2, table[:, 0:1], table)
            table = jnp.where(lanes_tall == 3, wide[:, 1:2], table)
            table = jnp.where(lanes_tall == 0, seats[0], table)
            table = jnp.where(lanes_tall == 1, seats[1], table)
            cols, rows = outs[2 * layer], outs[2 * layer + 1]
            cols[...] = table[0:padded, :].astype(jnp.int32)
            rows[...] = table.T[0:8, 0:padded].astype(jnp.int32)

    shapes = []
    for _ in range(layers):
        shapes += [sds((padded, LANES), jnp.int32), sds((8, padded), jnp.int32)]
    outs = call(
        kernel,
        "place_pairs",
        [z, routes, seat_order],
        [SM, VM, VM],
        shapes,
        [VM] * len(shapes),
        [pltpu.VMEM((tall, LANES), F32)],
    )
    return outs[0::2], outs[1::2]


def attn_fwd(me, layer, x_args, weights, vecs, router, noise, cols, rows, cap, used):
    first = len(x_args) == 1
    padded, width = cols.shape[0], vecs.shape[1]
    tokens, experts = noise.shape[1:]
    seats = experts * cap
    owners = 0 if first else len(x_args[3])
    count = len(weights.arrays)
    shard = weights.arrays[0].shape[-2]

    def kernel(*refs):
        refs = list(refs)
        me_ref = refs.pop(0)
        if first:
            tok_ref = refs.pop(0)
        else:
            below_x1, below_gates, below_cols = refs.pop(0), refs.pop(0), refs.pop(0)
            below_blocks = [refs.pop(0) for _ in range(owners)]
        w_refs = [refs.pop(0) for _ in range(count)]
        vec_ref, router_ref, noise_ref, cols_ref, rows_ref = (refs.pop(0) for _ in range(5))
        x_out, x1_out, qkv_out, gates_out, ao_out = (refs.pop(0) for _ in range(5))
        seat_outs = [refs.pop(0) for _ in range(experts)]
        wqkv, wout, sems, more_sems = refs
        targets = attn_targets(width, shard, wqkv, wout)
        left = fetch(w_refs, weights, me_ref[0], targets, 0, sems)
        right = fetch(w_refs, weights, me_ref[0], targets, 1, more_sems)
        start(left + right)
        vec = lambda k: vec_ref[k : k + 1, :]
        if first:
            x_out[...] = jnp.zeros_like(x_out)
            x_out[0:tokens, :] = tok_ref[...].astype(F32)
            x = x_out[...]
        else:
            x = combine(below_x1[...], below_gates[...], below_cols, join(below_blocks))
            x_out[...] = x
        normed, rstd = norm_rows(x)
        a_low = (normed * vec(0) + vec(2)).astype(BF)
        ao_out[:, 0:width] = a_low
        gates_out[...] = jnp.zeros_like(gates_out)
        gates_out[0:tokens, 0:experts] = noise_ref[layer]
        noise_here = gates_out[...]
        wait(left)
        for k in range(3):
            if k == 2:
                wait(right)
            piece = dot(a_low, wqkv[:, k * width : (k + 1) * width])
            if k == 0:
                piece = piece + vec(4)
            if k == 2:
                piece = piece + vec(5)
            qkv_out[:, k * width : (k + 1) * width] = piece.astype(BF)
        masks = head_masks()
        for two in range(HEADS // 2):
            at = two * 2 * HEAD_DIM
            query = qkv_out[:, at : at + 2 * HEAD_DIM]
            keys = qkv_out[:, width + at : width + at + 2 * HEAD_DIM]
            values = qkv_out[:, 2 * width + at : 2 * width + at + 2 * HEAD_DIM]
            mixed = None
            for mask in masks:
                probs = head_probs(query, keys, mask, tokens).astype(BF)
                piece = dot(probs, jnp.where(mask, values, 0).astype(BF))
                mixed = piece if mixed is None else mixed + piece
            ao_out[:, width + at : width + at + 2 * HEAD_DIM] = mixed.astype(BF)
        x1 = x + dot(ao_out[:, width : 2 * width], wout[...]) + vec(6)
        x1_out[...] = x1
        normed2, rstd2 = norm_rows(x1)
        moe = normed2 * vec(1) + vec(3)
        high, low = split(moe)
        logits = dot(high, router_ref[...]) + dot(low, router_ref[...]) + noise_here
        lanes = lax.broadcasted_iota(jnp.int32, logits.shape, 1)
        logits = jnp.where(lanes < experts, logits, NEG)
        raised = jnp.exp(logits - jnp.max(logits, -1, keepdims=True))
        gates = raised / jnp.sum(raised, -1, keepdims=True)
        gates_out[...] = gates
        ao_out[:, 2 * width : 3 * width] = high
        sent = rows_to_seats(rows_ref, seats, high)
        chosen = [pair_gate(gates, cols_ref, pair) for pair in range(2)]
        for block, ref in enumerate(seat_outs):
            note = jnp.zeros((1, LANES), F32)
            for pair in range(2):
                here = near_lanes(cols_ref, pair, block, cap)
                note = note + jnp.sum(jnp.where(here, chosen[pair], 0.0), 0, keepdims=True)
            piece = sent[block * cap : (block + 1) * cap]
            ref[...] = with_note(piece, used, note).astype(BF)

    args = [me]
    specs = [SM]
    if first:
        args += [x_args[0]]
        specs += [VM]
    else:
        args += [x_args[0], x_args[1], x_args[2], *x_args[3]]
        specs += [VM] * (3 + owners)
    args += [*weights.arrays, vecs, router, noise, cols, rows]
    specs += [ANY] * count + [VM] * 5
    outs = [
        sds((padded, width), F32),
        sds((padded, width), F32),
        sds((padded, 3 * width), BF),
        sds((padded, LANES), F32),
        sds((padded, 3 * width), BF),
    ] + [sds((cap, width), BF)] * experts
    result = call(
        kernel,
        "attn_fwd",
        args,
        specs,
        outs,
        [VM] * len(outs),
        [
            pltpu.VMEM((width, 3 * width), BF),
            pltpu.VMEM((width, width), BF),
            pltpu.SemaphoreType.DMA((copies_in(weights),)),
            pltpu.SemaphoreType.DMA((copies_in(weights),)),
        ],
    )
    return result[:5], result[5:]


def expert_fwd(me, seat_blocks, weights, bias_in, bias_oe, used):
    owners = len(seat_blocks)
    cap, width = seat_blocks[0].shape
    seats = owners * cap
    hidden = bias_in.shape[1]
    count = len(weights.arrays)
    shard = weights.arrays[0].shape[-2]
    whole = weights.places[0][0] is None
    step = width

    def kernel(*refs):
        refs = list(refs)
        me_ref = refs.pop(0)
        seat_refs = [refs.pop(0) for _ in range(owners)]
        w_refs = [refs.pop(0) for _ in range(count)]
        bin_ref, boe_ref = refs.pop(0), refs.pop(0)
        rh_out, slope_out, gate_out, made_out = (refs.pop(0) for _ in range(4))
        outs = [refs.pop(0) for _ in range(owners)]
        win, woe, sems = refs
        chunks = Chunks(w_refs, weights, width, hidden, shard, whole, win, woe, sems)
        blocks = [ref[...].astype(F32) for ref in seat_refs]
        rows = jnp.concatenate(blocks, 0).astype(BF)
        rh_out[:, 0:width] = rows
        rh_out.send(ALL, pl.ds(0, width))
        columns = [as_column(note_of(block, used), cap) for block in blocks]
        gate_out[...] = jnp.broadcast_to(jnp.concatenate(columns, 0), gate_out.shape)
        total_out = None
        for at in range(0, hidden, step):
            chunks.take(at // step)
            pre = dot(rows, win[:, at : at + step]) + bin_ref[:, at : at + step]
            square = pre * pre
            bend = jnp.tanh(0.7978845608028654 * (pre + 0.044715 * square * pre))
            h = (0.5 * pre * (1.0 + bend)).astype(BF)
            slope = 0.5 * (1.0 + bend) + 0.5 * pre * (1.0 - bend * bend) * (
                0.7978845608028654 * (1.0 + 0.134145 * square)
            )
            rh_out[:, width + at : width + at + step] = h
            slope_out[:, at : at + step] = slope.astype(BF)
            rh_out.send(ALL, pl.ds(width + at, step))
            slope_out.send(ALL, pl.ds(at, step))
            piece = dot(h, woe[at : at + step, :])
            total_out = piece if total_out is None else total_out + piece
        total_out = total_out + boe_ref[...]
        made_out[...] = total_out.astype(BF)
        part(total_out, outs)

    shapes = [
        sds((seats, width + hidden), BF),
        sds((seats, hidden), BF),
        sds((seats, LANES), F32),
        sds((seats, width), BF),
    ] + [sds((cap, width), BF)] * owners
    result = call(
        kernel,
        "expert_fwd",
        [me, *seat_blocks, *weights.arrays, bias_in, bias_oe],
        [SM] + [LOAD] * owners + [ANY] * count + [LOAD] * 2,
        shapes,
        [STORE] * (4 + owners),
        [
            pltpu.VMEM((width, hidden), BF),
            pltpu.VMEM((hidden, width), BF),
            pltpu.SemaphoreType.DMA((2 * copies_in(weights),)),
        ],
    )
    return result[:4], result[4:]


def top_seats(cotangent, rows, cap, experts):
    tokens, width = cotangent.shape
    padded = rows.shape[1]

    def kernel(cot_ref, rows_ref, grad_out, *outs):
        grad_out[...] = jnp.zeros_like(grad_out)
        grad_out[0:tokens, :] = cot_ref[...].astype(F32)
        part(rows_to_seats(rows_ref, cap * experts, grad_out[...].astype(BF)), outs)

    shapes = [sds((padded, width), F32)] + [sds((cap, width), BF)] * experts
    result = call(
        kernel,
        "top_seats",
        [cotangent, rows],
        [VM] * 2,
        shapes,
        [VM] * len(shapes),
        [],
    )
    return result[0], result[1:]


def mix(x1, gates, cols, returned, tokens):
    width = x1.shape[1]

    def kernel(x1_ref, gates_ref, cols_ref, *refs):
        total = combine(x1_ref[...], gates_ref[...], cols_ref, join(refs[:-1]))
        refs[-1][...] = total[0:tokens, :]

    return call(
        kernel,
        "mix",
        [x1, gates, cols, *returned],
        [VM] * (3 + len(returned)),
        sds((tokens, width), F32),
        VM,
        [],
    )


def expert_back(me, grad_blocks, slope, gate, made, weights, used):
    owners = len(grad_blocks)
    cap, width = grad_blocks[0].shape
    seats, hidden = slope.shape
    count = len(weights.arrays)
    shard = weights.arrays[0].shape[-2]
    whole = weights.places[0][0] is None
    step = width

    def kernel(*refs):
        refs = list(refs)
        me_ref = refs.pop(0)
        seat_refs = [refs.pop(0) for _ in range(owners)]
        slope_ref, gate_ref, made_ref = (refs.pop(0) for _ in range(3))
        w_refs = [refs.pop(0) for _ in range(count)]
        gd_out = refs.pop(0)
        outs = [refs.pop(0) for _ in range(owners)]
        win, woe, slopes, sems, slope_sems = refs
        more = [
            pltpu.make_async_copy(
                slope_ref.at[:, pl.ds(at, step)],
                slopes.at[:, pl.ds(at, step)],
                slope_sems.at[at // step],
            )
            for at in range(0, hidden, step)
        ]
        chunks = Chunks(w_refs, weights, width, hidden, shard, whole, win, woe, sems, more)
        given = jnp.concatenate([ref[...].astype(F32) for ref in seat_refs], 0)
        grad = (given * gate_ref[:, 0:1]).astype(BF)
        notes = given * made_ref[...].astype(F32)
        notes = [lane_sums(notes[k * cap : (k + 1) * cap]) for k in range(owners)]
        gd_out[:, 0:width] = grad
        gd_out.send(ALL, pl.ds(0, width))
        total_out = None
        for at in range(0, hidden, step):
            chunks.take(at // step)
            d_hidden = dot_nt(grad, woe[at : at + step, :])
            d_pre = (d_hidden * slopes[:, at : at + step].astype(F32)).astype(BF)
            gd_out[:, width + at : width + at + step] = d_pre
            gd_out.send(ALL, pl.ds(width + at, step))
            piece = dot_nt(d_pre, win[:, at : at + step])
            total_out = piece if total_out is None else total_out + piece
        for k, ref in enumerate(outs):
            ref[...] = with_note(total_out[k * cap : (k + 1) * cap], used, notes[k]).astype(BF)

    shapes = [sds((seats, width + hidden), BF)]
    shapes += [sds((cap, width), BF)] * owners
    result = call(
        kernel,
        "expert_back",
        [me, *grad_blocks, slope, gate, made, *weights.arrays],
        [SM] + [LOAD] * owners + [ANY] + [LOAD] * 2 + [ANY] * count,
        shapes,
        [STORE] * (1 + owners),
        [
            pltpu.VMEM((width, hidden), BF),
            pltpu.VMEM((hidden, width), BF),
            pltpu.VMEM((seats, hidden), BF),
            pltpu.SemaphoreType.DMA((2 * copies_in(weights),)),
            pltpu.SemaphoreType.DMA((hidden // step,)),
        ],
    )
    return result[0], result[1:]


def column_sums(value):
    return dot(jnp.ones((8, value.shape[0]), BF), value)[0:1, :]


def own_columns(width, shards, core):
    shard = width // shards
    half = width // 2
    row = lax.broadcasted_iota(jnp.int32, (width, half), 0)
    column = lax.broadcasted_iota(jnp.int32, (width, half), 1)
    place = column + core * shard
    for k in range(1, shards // 2):
        place = place + jnp.where(column >= k * shard, shard, 0)
    return one(row == place)


def expert_grads(me, own, other, shards):
    seats, both = own[0].shape
    width = HEADS * HEAD_DIM
    hidden = both - width
    per, shard = hidden // width, width // shards
    part_hidden = hidden // shards
    sides = 2 if other else 1
    tall = width // 2 if other else width
    deep = hidden // 2 if other else hidden
    total = shards * per if other else 2

    blocks = shards // 2 if other else per
    size = part_hidden if other else width

    def kernel(me_ref, *refs):
        refs = list(refs)
        rh = [refs.pop(0) for _ in range(sides)]
        gd = [refs.pop(0) for _ in range(sides)]
        outs = [refs.pop(0) for _ in range(1 if other else 2)]
        bias_ref, win, woe, h_held, row_held, gd_held, sems, load_sems = refs
        core = me_ref[0] & 1
        copies = []
        loads = {}

        def fetch_in(key, source, target):
            copy = pltpu.make_async_copy(source, target, load_sems.at[len(loads)])
            copy.start()
            loads[key] = copy

        for i in range(sides):
            fetch_in(("d", i), gd[i].at[:, pl.ds(0, width)], gd_held.at[i, :, pl.ds(0, width)])
        for k in range(blocks):
            first = width + k * size
            if other:
                first = pl.multiple_of(width + (2 * k + core) * size, LANES)
            for i in range(sides):
                here = pl.ds(k * size, size)
                fetch_in(("h", k, i), rh[i].at[:, pl.ds(first, size)], h_held.at[i, :, here])
        for i in range(sides):
            fetch_in(("r", i), rh[i].at[:, pl.ds(0, width)], row_held.at[i])
        for k in range(per):
            here = pl.ds(width + k * width, width)
            for i in range(sides):
                fetch_in(("p", k, i), gd[i].at[:, here], gd_held.at[i, :, here])

        def send(source, target):
            copy = pltpu.make_async_copy(source, target, sems.at[len(copies)])
            copy.start()
            copies.append(copy)

        def summed(pieces):
            total = pieces[0]
            for piece in pieces[1:]:
                total = total + piece
            return total

        for i in range(sides):
            loads["d", i].wait()
        d_outs = [gd_held[i, :, 0:width] for i in range(sides)]
        for k in range(blocks):
            here = slice(k * size, (k + 1) * size)
            for i in range(sides):
                loads["h", k, i].wait()
            total = summed([dot_tn(h_held[i, :, here], d_outs[i]) for i in range(sides)])
            woe[here, :] = total.astype(BF)
            if other:
                for q in range(per):
                    send(
                        woe.at[pl.ds(k * size + q * shard, shard)],
                        outs[0].at[k, 1, :, pl.ds(q * width, width)],
                    )
        for i in range(sides):
            loads["r", i].wait()
        lefts = [row_held[i] for i in range(sides)]
        if other:
            pick = own_columns(width, shards, core)
            lefts = [dot(left, pick).astype(BF) for left in lefts]
        for k in range(per):
            here = slice(width + k * width, width + (k + 1) * width)
            for i in range(sides):
                loads["p", k, i].wait()
            total = summed([dot_tn(lefts[i], gd_held[i, :, here]) for i in range(sides)])
            win[:, k * width : (k + 1) * width] = total.astype(BF)
            if other:
                for n in range(shards // 2):
                    here = pl.ds(k * width, width)
                    send(
                        win.at[pl.ds(n * shard, shard), here], outs[0].at[n, 0, :, here]
                    )
        if not other:
            send(win, outs[0])
            send(woe, outs[1])
        bias_ref[...] = jnp.zeros_like(bias_ref)
        sums = summed([column_sums(gd_held[i]) for i in range(sides)])
        for d in range(shards):
            for q in range(per):
                first = width + (d * per + q) * shard
                bias_ref[q : q + 1, d * shard : (d + 1) * shard] = sums[:, first : first + shard]
        bias_ref[per : per + 1, :] = sums[:, 0:width]
        wait(copies)

    if other:
        shapes = [sds((shards // 2, 2, shard, hidden), BF)]
        args = [own[0], other[0], own[1], other[1]]
    else:
        shapes = [sds((width, hidden), BF), sds((hidden, width), BF)]
        args = list(own)
    result = call(
        kernel,
        "expert_grads",
        [me, *args],
        [SM] + [ANY] * len(args),
        shapes + [sds((8, width), F32)],
        [ANY] * len(shapes) + [VM],
        [
            pltpu.VMEM((tall, hidden), BF),
            pltpu.VMEM((deep, width), BF),
            pltpu.VMEM((sides, seats, blocks * size), BF),
            pltpu.VMEM((sides, seats, width), BF),
            pltpu.VMEM((sides, seats, width + hidden), BF),
            pltpu.SemaphoreType.DMA((total,)),
            pltpu.SemaphoreType.DMA((sides * (2 + blocks + per),)),
        ],
    )
    return result[:-1], result[-1]


def pick_columns(me, value, shards):
    rows, wide = value.shape
    width = wide // 3

    def kernel(me_ref, ref, own, other):
        core = me_ref[0] & 1
        for out, side in ((own, core), (other, 1 - core)):
            pick = own_columns(width, shards, side)
            for k in range(3):
                piece = dot(ref[:, k * width : (k + 1) * width], pick)
                out[:, k * width // 2 : (k + 1) * width // 2] = piece.astype(BF)

    return call(
        kernel,
        "pick_columns",
        [me, value],
        [SM, VM],
        [sds((rows, wide // 2), BF)] * 2,
        [VM] * 2,
        [],
    )


def attn_back(
    me, back_blocks, gates, router, grad, x, x1, qkv, cols, vecs, weights, below, tokens, used
):
    padded, width = grad.shape
    owners = len(back_blocks)
    cap = back_blocks[0].shape[0]
    seats = owners * cap
    count = len(weights.arrays)
    shard = weights.arrays[0].shape[-2]

    def kernel(*refs):
        refs = list(refs)
        me_ref = refs.pop(0)
        back_refs = [refs.pop(0) for _ in range(owners)]
        gates_ref, router_ref, grad_ref, x_ref, x1_ref, qkv_ref, cols_ref, vec_ref = (
            refs.pop(0) for _ in range(8)
        )
        w_refs = [refs.pop(0) for _ in range(count)]
        if below is not None:
            below_rows = refs.pop(0)
        dx_out, back_out = refs.pop(0), refs.pop(0)
        seat_outs = [refs.pop(0) for _ in range(owners)] if below is not None else None
        wqkv, wout, small_out, sems, more_sems = refs
        targets = attn_targets(width, shard, wqkv, wout)
        right = fetch(w_refs, weights, me_ref[0], targets, 1, sems)
        left = fetch(w_refs, weights, me_ref[0], targets, 0, more_sems)
        start(right + left)
        vec = lambda k: vec_ref[k : k + 1, :]
        blocks = [ref[...].astype(F32) for ref in back_refs]
        gates = gates_ref[...]
        lanes = lax.broadcasted_iota(jnp.int32, gates.shape, 1)
        d_gates = jnp.zeros_like(gates)
        for pair in range(2):
            d_pair = jnp.zeros_like(gates)
            for block in range(owners):
                here = near_lanes(cols_ref, pair, block, cap)
                d_pair = d_pair + jnp.where(here, note_of(blocks[block], used), 0.0)
            d_pair = jnp.sum(d_pair, -1, keepdims=True)
            d_gates = d_gates + jnp.where(lanes == cols_ref[:, 2 + pair : 3 + pair], d_pair, 0.0)
        dz = gates * (d_gates - jnp.sum(d_gates * gates, -1, keepdims=True))
        high, low = split(dz)
        moe_part = dot_nt(high, router_ref[...]) + dot_nt(low, router_ref[...])
        back_out[0:padded, 4 * width : 4 * width + LANES] = high
        back_out[0:padded, 4 * width + LANES : 4 * width + 2 * LANES] = low
        chosen = jnp.logical_or(seat_mask(cols_ref, 0, seats), seat_mask(cols_ref, 1, seats))
        d_moe = dot(one(chosen), jnp.concatenate(blocks, 0).astype(BF)) + moe_part
        normed2, rstd2 = norm_rows(x1_ref[...])
        small_out[...] = jnp.zeros_like(small_out)
        small_out[1:2, :] = jnp.sum(d_moe * normed2, 0, keepdims=True)
        small_out[3:4, :] = jnp.sum(d_moe, 0, keepdims=True)
        d_x1 = grad_ref[...] + norm_back(d_moe * vec(1), normed2, rstd2)
        dy = d_x1.astype(BF)
        back_out[0:padded, 3 * width : 4 * width] = dy
        small_out[6:7, :] = column_sums(dy)
        wait(right)
        d_mixed = dot_nt(dy, wout[...]).astype(BF)
        masks = head_masks()
        scale = HEAD_DIM ** (-0.5)
        for two in range(HEADS // 2):
            at = two * 2 * HEAD_DIM
            query = qkv_ref[:, at : at + 2 * HEAD_DIM]
            keys = qkv_ref[:, width + at : width + at + 2 * HEAD_DIM]
            values = qkv_ref[:, 2 * width + at : 2 * width + at + 2 * HEAD_DIM]
            d_o = d_mixed[:, at : at + 2 * HEAD_DIM]
            sums = None
            for mask in masks:
                probs = head_probs(query, keys, mask, tokens)
                d_here = jnp.where(mask, d_o, 0).astype(BF)
                d_probs = dot_nt(d_here, values)
                d_values = dot_tn(probs.astype(BF), d_here)
                d_scores = probs * (d_probs - jnp.sum(d_probs * probs, -1, keepdims=True))
                d_scores = d_scores.astype(BF)
                d_query = dot(d_scores, jnp.where(mask, keys, 0).astype(BF))
                d_keys = dot_tn(d_scores, jnp.where(mask, query, 0).astype(BF))
                here = (d_query, d_keys, d_values)
                sums = here if sums is None else tuple(s + h for s, h in zip(sums, here))
            for k, value in enumerate((sums[0] * scale, sums[1] * scale, sums[2])):
                first = k * width + at
                back_out[0:padded, first : first + 2 * HEAD_DIM] = value.astype(BF)
        wait(left)
        d_normed = None
        for k in range(3):
            here = back_out[0:padded, k * width : (k + 1) * width]
            if k != 1:
                row = 4 if k == 0 else 5
                small_out[row : row + 1, :] = column_sums(here)
            piece = dot_nt(here, wqkv[:, k * width : (k + 1) * width])
            d_normed = piece if d_normed is None else d_normed + piece
        normed1, rstd1 = norm_rows(x_ref[...])
        small_out[0:1, :] = jnp.sum(d_normed * normed1, 0, keepdims=True)
        small_out[2:3, :] = jnp.sum(d_normed, 0, keepdims=True)
        d_x = d_x1 + norm_back(d_normed * vec(0), normed1, rstd1)
        dx_out[...] = d_x[0 : dx_out.shape[0], :]
        if below is not None:
            part(rows_to_seats(below_rows, seats, d_x.astype(BF)), seat_outs)
        high, low = split(small_out[...])
        back_out[padded : padded + 16, 0:width] = high
        back_out[padded : padded + 16, width : 2 * width] = low
        back_out[padded : padded + 16, 2 * width :] = jnp.zeros((16, 2 * width + 2 * LANES), BF)

    shapes = [
        sds((padded if below is not None else tokens, width), F32),
        sds((padded + 16, 4 * width + 2 * LANES), BF),
    ]
    args = [me, *back_blocks, gates, router, grad, x, x1, qkv, cols, vecs, *weights.arrays]
    specs = [SM] + [VM] * (owners + 8) + [ANY] * count
    if below is not None:
        shapes += [sds((cap, width), BF)] * owners
        args += [below]
        specs += [VM]
    result = call(
        kernel,
        "attn_back",
        args,
        specs,
        shapes,
        [VM] * len(shapes),
        [
            pltpu.VMEM((width, 3 * width), BF),
            pltpu.VMEM((width, width), BF),
            pltpu.VMEM((16, width), F32),
            pltpu.SemaphoreType.DMA((copies_in(weights),)),
            pltpu.SemaphoreType.DMA((copies_in(weights),)),
        ],
    )
    return result[:2], result[2:]


def attn_grads(me, z, own, other, biases, shards, ordered):
    padded, wide_ao = own[0].shape
    width = HEADS * HEAD_DIM
    half = 2 * width + LANES
    tall = width // 2 if other else width
    shard = width // shards
    places = [(6, 0, 0), (6, 1, 1), (2, 0, 2), (2, 1, 2), (4, 0, 3), (4, 1, 3), (0, 0, 4), (0, 1, 4)]
    count = 2
    if other:
        count = 1 if ordered else 5

    def kernel(me_ref, z_ref, *refs):
        refs = list(refs)
        ao = [refs.pop(0), refs.pop(0)] if other else [refs.pop(0)]
        back = [refs.pop(0), refs.pop(0)] if other else [refs.pop(0)]
        bias_ref = refs.pop(0)
        outs = [refs.pop(0) for _ in range(count)]
        wide, rows, turned, sems = refs
        copies = []

        def send(p):
            first = p * half
            if not other:
                copies.append(
                    pltpu.make_async_copy(wide.at[:, pl.ds(first, half)], outs[p], sems.at[p])
                )
                copies[-1].start()
                return
            if ordered:
                for k in range(shards // 2):
                    source = wide.at[pl.ds(k * shard, shard), pl.ds(first, half)]
                    copy = pltpu.make_async_copy(source, outs[0].at[k, p], sems.at[2 * k + p])
                    copies.append(copy)
                    copy.start()
                return
            for n, (off, where, o) in enumerate(places):
                if where != p:
                    continue
                at = pl.multiple_of(((me_ref[0] ^ off) >> 1) * shard, 16)
                into = outs[o] if o < 2 else outs[o].at[p]
                copies.append(
                    pltpu.make_async_copy(
                        wide.at[pl.ds(at, shard), pl.ds(first, half)], into, sems.at[n]
                    )
                )
                copies[-1].start()

        def product(which, first):
            total = None
            for left, right in zip(ao, back):
                here = left[:, which * tall : (which + 1) * tall]
                piece = dot_tn(here, right[0:padded, first : first + width])
                total = piece if total is None else total + piece
            return total.astype(BF)

        wide[:, 0:width] = product(0, 0)
        wide[:, width : 2 * width] = product(0, width)
        wide[:, 2 * width : half] = jnp.zeros((tall, LANES), BF)
        send(0)
        wide[:, half : half + width] = product(0, 2 * width)
        wide[:, half + width : half + 2 * width] = product(1, 3 * width)
        rows[...] = jnp.zeros_like(rows)
        small = None
        d_router = None
        for left, right in zip(ao, back):
            for k in range(2):
                piece = right[padded : padded + 16, k * width : (k + 1) * width].astype(F32)
                small = piece if small is None else small + piece
                first = 4 * width + k * LANES
                piece = dot_tn(
                    left[:, 2 * tall : 3 * tall], right[0:padded, first : first + LANES]
                )
                d_router = piece if d_router is None else d_router + piece
        rows[16:32, :] = small
        rows[pl.ds(pl.multiple_of(32 + 8 * z_ref[0], 8), 8), :] = bias_ref[...]
        turned[...] = rows[...].T
        if other:
            core = me_ref[0] & 1
            for k in range(shards // 2):
                at = pl.multiple_of((2 * k + core) * shard, 8)
                here = slice(k * shard, (k + 1) * shard)
                piece = d_router[here, :] + turned[pl.ds(at, shard), :]
                wide[here, half + 2 * width : 2 * half] = piece.astype(BF)
        else:
            wide[:, half + 2 * width : 2 * half] = (d_router + turned[...]).astype(BF)
        send(1)
        wait(copies)

    if other:
        if ordered:
            shapes = [sds((shards // 2, 2, shard, half), BF)]
        else:
            shapes = [sds((shard, half), BF)] * 2 + [sds((2, shard, half), BF)] * 3
        args = [own[0], other[0], own[1], other[1]]
    else:
        shapes = [sds((width, half), BF)] * 2
        args = list(own)
    return call(
        kernel,
        "attn_grads",
        [me, z, *args, biases],
        [SM, SM] + [VM] * (len(args) + 1),
        shapes,
        [ANY] * len(shapes),
        [
            pltpu.VMEM((tall, 2 * half), BF),
            pltpu.VMEM((LANES, width), F32),
            pltpu.VMEM((width, LANES), F32),
            pltpu.SemaphoreType.DMA((max(len(places), shards),)),
        ],
    )


def small_out(smalls, z, experts, per):
    layers = len(smalls)
    shard = smalls[0].shape[0]

    def kernel(z_ref, *refs):
        ins = refs[:layers]
        gains, biases, router, bias_in, bias_oe, square = refs[layers:]
        for layer in range(layers):
            square[...] = jnp.zeros_like(square)
            square[0:shard, :] = ins[layer][...]
            square[...] = square[...].T
            router[layer] = square[0:experts, 0:shard]
            gains[layer] = square[16:18, 0:shard]
            for k in range(5):
                biases[k, layer : layer + 1, :] = square[18 + k : 19 + k, 0:shard]
            own = square[pl.ds(pl.multiple_of(32 + 8 * z_ref[0], 8), 8), :]
            for q in range(per):
                bias_in[layer, :, q * shard : (q + 1) * shard] = own[q : q + 1, 0:shard]
            bias_oe[layer] = own[per : per + 1, 0:shard]

    shapes = [
        sds((layers, 2, shard), F32),
        sds((5, layers, shard), F32),
        sds((layers, experts, shard), F32),
        sds((layers, 1, per * shard), F32),
        sds((layers, 1, shard), F32),
    ]
    return call(
        kernel,
        "small_out",
        [z, *smalls],
        [SM] + [VM] * layers,
        shapes,
        [VM] * 5,
        [pltpu.VMEM((LANES, LANES), F32)],
    )


def swap(value, axis, bit):
    size = lax.axis_size(axis)
    return lax.ppermute(value, axis, [(i, i ^ bit) for i in range(size)])


def exchange(blocks):
    order = sorted(range(1, len(blocks)), key=lambda k: -(k & 2))
    got = {k: swap(blocks[k], "expert", k) for k in order}
    return [blocks[0]] + [got[k] for k in range(1, len(blocks))]


def axis_bits(axis, bit):
    bits = []
    while bit < lax.axis_size(axis):
        bits.append(bit)
        bit *= 2
    return bits


def sum_experts(value):
    for bit in axis_bits("expert", 1):
        low = value.astype(BF)
        value = low.astype(F32) + swap(low, "expert", bit).astype(F32)
    return value


def gather_rows(shard):
    return lax.all_gather(shard, "dp", axis=0, tiled=True)


def scatter_rows(whole):
    return lax.psum_scatter(whole, "dp", scatter_dimension=0, tiled=True)


def scatter_chips(blocks):
    size = lax.axis_size("dp")
    return lax.psum_scatter(
        blocks,
        "dp",
        scatter_dimension=0,
        axis_index_groups=[list(range(core, size, 2)) for core in range(2)],
    )


class Gather:
    def __init__(self, shard):
        self.shard = shard
        self.x, self.y = swap(shard, "dp", 2), swap(shard, "dp", 4)

    def turn(self):
        two, rows, width = self.shard.shape
        block = (two, rows, width)
        half = (1, rows, width)
        self.cut = move(
            "cut",
            [self.x, self.y, self.shard],
            [
                (0, (pl.ds(0, 1),), 0, (ALL,), half),
                (1, (pl.ds(1, 1),), 1, (ALL,), half),
                (0, (ALL,), 2, (1,), block),
                (1, (ALL,), 2, (2,), block),
                (2, (ALL,), 2, (0,), block),
            ],
            [sds(half, BF)] * 2 + [sds((3, *block), BF)],
        )

    def send(self, after=()):
        if after:
            self.cut = hold(self.cut, after)
        self.xy = swap(self.cut[0], "dp", 4), swap(self.cut[1], "dp", 2)
        self.other = swap(self.cut[2], "dp", 1)

    def cross(self, after=()):
        if after:
            self.xy = hold(self.xy, after)
        self.across = [swap(value, "dp", 1) for value in self.xy]

    def weights(self):
        pieces = [
            (self.shard, 0, (0, 1)),
            (self.x, 2, (0, 1)),
            (self.y, 4, (0, 1)),
            (self.xy[0], 6, (0,)),
            (self.xy[1], 6, (1,)),
            (self.across[0], 7, (0,)),
            (self.across[1], 7, (1,)),
            (self.other, (1, 3, 5), (0, 1)),
        ]
        return Weights([p[0] for p in pieces], [p[1:] for p in pieces])


def full(rows):
    return (pl.ds(0, rows), ALL)


class AttnSum:
    def __init__(self, grads):
        self.bits = axis_bits("expert", 1)
        self.done = 0
        if len(grads) == 1:
            self.total = scatter_chips(grads[0])
            return
        self.across, (self.x, self.y, self.own) = list(grads[:2]), grads[2:]
        self.rows, self.width = self.across[0].shape

    def cut(self):
        self.rows, self.width = self.total.shape[1:]
        shape = (self.rows, self.width)
        self.parts = move(
            "parts",
            [self.total],
            [(0, (p,), p, full(self.rows), shape) for p in range(2)],
            [sds(shape, BF)] * 2,
        )
        self.send()

    def send_across(self, after=()):
        if after:
            self.across = hold(self.across, after)
        self.across = swap(self.across[0], "dp", 4), swap(self.across[1], "dp", 2)

    def fold1(self):
        self.x, self.y = fold1(self.x, self.y, self.across)

    def send_on(self, after=()):
        if after:
            self.x, self.y = hold([self.x, self.y], after)
        self.came = swap(self.x, "dp", 2), swap(self.y, "dp", 4)

    def fold2(self):
        shape = (self.rows, self.width)
        flat = full(self.rows)
        self.parts = fold(
            "fold2",
            [self.own, *self.came],
            shape,
            [([(i, (p,)) for i in range(3)], BF, [(p, flat, flat)]) for p in range(2)],
            [sds(shape, BF)] * 2,
        )
        self.send()

    def send(self):
        up_bit, down_bit = self.bits[self.done], self.bits[-1 - self.done]
        self.came = swap(self.parts[0], "expert", up_bit), swap(self.parts[1], "expert", down_bit)

    def fold3(self, layer, layers, given):
        shape = (self.rows, self.width)
        flat = full(self.rows)
        self.done += 1
        terms = [[(0, flat), (2, flat)], [(1, flat), (3, flat)]]
        args = [*self.parts, *self.came]
        if self.done < len(self.bits):
            self.parts = fold(
                "fold3",
                args,
                shape,
                [(terms[p], BF, [(p, flat, flat)]) for p in range(2)],
                [sds(shape, BF)] * 2,
                )
            self.send()
            return None
        wide = (self.width - LANES) // 2
        cut = lambda first, size: (ALL, pl.ds(first, size))
        tasks = [
            (terms[0], F32, [(0, (layer, ALL, pl.ds(0, 2 * wide)), cut(0, 2 * wide))]),
            (
                terms[1],
                F32,
                [
                    (0, (layer, ALL, pl.ds(2 * wide, wide)), cut(0, wide)),
                    (1, (layer,), cut(wide, wide)),
                    (2, flat, cut(2 * wide, LANES)),
                ],
            ),
        ]
        outs = [
            sds((layers, self.rows, 3 * wide), F32),
            sds((layers, self.rows, wide), F32),
            sds((self.rows, LANES), F32),
        ]
        aliases = {4: 0, 5: 1} if given else None
        return fold("attn_out", args + list(given), shape, tasks, outs, aliases)


def fold1(x, y, across):
    shape = x.shape[1:]
    flat = full(shape[0])
    return fold(
        "fold1",
        [x, y, *across],
        shape,
        [
            ([(0, (0,)), (2, flat)], BF, [(0, (0,), flat)]),
            ([(1, (1,)), (3, flat)], BF, [(1, (1,), flat)]),
        ],
        [sds(x.shape, BF)] * 2,
        {0: 0, 1: 1},
    )


def expert_out(total, layer, layers, given, width):
    rows, broad = total.shape[1:]
    per = broad // width
    second = [
        (1, (layer, 0, pl.ds(q * rows, rows)), (ALL, pl.ds(q * width, width))) for q in range(per)
    ]
    outs = [sds((layers, 1, rows, broad), F32), sds((layers, 1, per * rows, width), F32)]
    return fold(
        "expert_out",
        [total, *given],
        (rows, broad),
        [
            ([(0, (0,))], F32, [(0, (layer, 0), full(rows))]),
            ([(0, (1,))], F32, second),
        ],
        outs,
        {1: 0, 2: 1} if given else None,
    )


def per_device(
    image_tokens,
    norm_gains,
    biases,
    w_qkv,
    w_out,
    w_router,
    router_noise,
    w_in,
    b_in,
    w_outexp,
    b_expout,
    routes,
    seat_order,
    cotangent,
):
    layers = w_qkv.shape[0]
    tokens, width = image_tokens.shape
    experts = w_router.shape[2]
    shards = lax.axis_size("dp")
    assert tokens == SEQ and experts == lax.axis_size("expert")
    assert width == HEADS * HEAD_DIM
    padded = up(tokens, 16)
    cap = 2 * tokens // experts
    cap_pad = up(cap + 2, 8)
    assert cap_pad <= LANES
    shard = w_qkv.shape[1]
    hidden_shard = w_outexp.shape[2]
    hidden = w_in.shape[3]
    per = hidden_shard // shard
    index = lax.axis_index("dp").astype(jnp.int32)
    me = index.reshape(1)
    z = lax.axis_index("expert").astype(jnp.int32).reshape(1)
    bits = axis_bits("dp", 2)
    four = bits == [2, 4] and shard % 16 == 0 and axis_bits("expert", 1) == [1, 2]

    Order.token = None

    def pack_attn(layer):
        return move(
            "pack_attn",
            [w_qkv, w_out],
            [
                (0, (layer, ALL, pl.ds(0, 2 * width)), 0, (0,), (shard, 2 * width)),
                (
                    0,
                    (layer, ALL, pl.ds(2 * width, width)),
                    0,
                    (1, ALL, pl.ds(0, width)),
                    (shard, width),
                ),
                (1, (layer,), 0, (1, ALL, pl.ds(width, width)), (shard, width)),
            ],
            [sds((2, shard, 2 * width), BF)],
        )[0]

    def pack_expert(layer):
        return move(
            "pack_expert",
            [w_in, w_outexp],
            [(0, (layer, 0), 0, (0,), (shard, hidden))]
            + [
                (
                    1,
                    (layer, 0, pl.ds(q * shard, shard)),
                    0,
                    (1, ALL, pl.ds(q * width, width)),
                    (shard, width),
                )
                for q in range(per)
            ],
            [sds((2, shard, hidden), BF)],
        )[0]

    whole = [(None, (0,)), (None, (1,))]

    def fetch_attn(layer):
        if four:
            return Gather(pack_attn(layer))
        right = jnp.concatenate([w_qkv[layer][:, 2 * width :], w_out[layer]], 1)
        attn = [gather_rows(v)[None] for v in (w_qkv[layer][:, : 2 * width], right)]
        return Weights(attn, whole)

    def fetch_expert(layer):
        if four:
            both = lax.all_gather(pack_expert(layer), "dp", axis=0)
            return Weights([both], [(OWNERS, (0, 1))])
        both = [gather_rows(w_in[layer, 0])[None], gather_rows(w_outexp[layer, 0])[None]]
        return Weights(both, whole)

    def attn_weights(gathered):
        return gathered.weights() if four else gathered

    last = layers - 1
    attn_w = [fetch_attn(0)]
    expert_w = [fetch_expert(layer) for layer in range(layers)]
    cols, rows = place_pairs(
        routes, seat_order.reshape(layers, tokens, 2), padded, cap, cap_pad, z
    )
    small = pack_small(norm_gains, biases, w_router, b_in, b_expout)
    grad, grad_seats = top_seats(cotangent, rows[last], cap_pad, experts)
    if four:
        attn_w[0].turn()
        attn_w[0].send()
    small = lax.all_gather(small, "dp", axis=0)
    params = unpack_small(small, layers, shard, per, experts)
    if last > 0:
        attn_w.append(fetch_attn(1))

    saved = []
    x_args = (image_tokens,)
    if four:
        attn_w[0].cross()
    for layer in range(layers):
        vecs, router, bias_in, bias_oe = params[layer]
        attn_w[layer] = attn_weights(attn_w[layer])
        kept, sent = attn_fwd(
            me,
            layer,
            x_args,
            attn_w[layer],
            vecs,
            router,
            router_noise,
            cols[layer],
            rows[layer],
            cap_pad,
            cap,
        )
        x, x1, qkv, gates, ao = kept
        sent = exchange(sent)
        other_ao = None
        if four:
            ao, other_ao = pick_columns(me, ao, shards)
            other_ao = swap(other_ao, "dp", 1)
        if layer < last:
            if four:
                attn_w[layer + 1].turn()
                attn_w[layer + 1].send(sent[1:])
            if layer + 1 < last:
                attn_w.append(fetch_attn(layer + 2))
        else:
            grad_seats = exchange(hold(grad_seats, sent[1:]))
        (rh, slope, gate, out), made = expert_fwd(
            me, sent, expert_w[layer], bias_in, bias_oe, cap
        )
        if four and layer < last:
            attn_w[layer + 1].cross(made[:1])
        returned = exchange(made) if layer < last else made
        other_rh = swap(rh, "dp", 1) if four else None
        saved.append((x, x1, qkv, gates, ao, other_ao, rh, other_rh, slope, gate, out))
        x_args = (x1, gates, cols[layer], returned)

    attn_sums, expert_sums = [None] * layers, [None] * layers
    for layer in reversed(range(layers)):
        x, x1, qkv, gates, ao, other_ao, rh, other_rh, slope, gate, out = saved[layer]
        vecs, router = params[layer][:2]
        if four and layer < last:
            g_attn = attn_grads(me, z, *attn_operands, g_bias, shards, True)
            attn_sums[layer + 1] = AttnSum(hold(g_attn, grad_seats[1:]))
        gd, d_rows = expert_back(me, grad_seats, slope, gate, out, expert_w[layer], cap)
        d_back = exchange(d_rows)
        other = (other_rh, swap(gd, "dp", 1)) if four else None
        g_expert, g_bias = expert_grads(me, (rh, gd), other, shards)
        if four:
            (g_expert,) = hold(g_expert, d_back[1:])
            expert_sums[layer] = scatter_chips(g_expert)
        else:
            expert_sums[layer] = [scatter_rows(v) for v in g_expert]
        below = None
        if layer > 0:
            below = rows[layer - 1]
        (grad, back), grad_seats = attn_back(
            me,
            d_back,
            gates,
            router,
            grad,
            x,
            x1,
            qkv,
            cols[layer],
            vecs,
            attn_w[layer],
            below,
            tokens,
            cap,
        )
        grad_seats = exchange(grad_seats) if layer > 0 else None
        if four:
            attn_operands = (ao, back), (other_ao, swap(back, "dp", 1))
        else:
            g_attn = attn_grads(me, z, (ao, back), None, g_bias, shards, False)
            attn_sums[layer] = [sum_experts(scatter_rows(v)) for v in g_attn]

    if four:
        done_attn, smalls, done_expert = (), [None] * layers, ()
        for layer in reversed(range(1, layers)):
            done_expert = expert_out(expert_sums[layer], layer, layers, done_expert, width)
        g_attn = attn_grads(me, z, *attn_operands, g_bias, shards, False)
        attn_sums[0] = AttnSum(g_attn)
        attn_sums[0].send_across()
        attn_sums[0].fold1()
        attn_sums[0].send_on()
        for layer in reversed(range(1, layers)):
            attn_sums[layer].cut()
    returned = exchange(hold(made, g_attn[:1]))
    mixed = mix(x_args[0], x_args[1], x_args[2], returned, tokens)
    if four:
        attn_sums[0].fold2()
        for layer in reversed(range(1, layers)):
            attn_sums[layer].fold3(layer, layers, done_attn)
        attn_sums[0].fold3(0, layers, done_attn)
        for layer in reversed(range(1, layers)):
            out = attn_sums[layer].fold3(layer, layers, done_attn)
            done_attn, smalls[layer] = out[:2], out[2]
        done_expert = expert_out(expert_sums[0], 0, layers, done_expert, width)
        grad_in, grad_oe = done_expert
    else:
        grad_in = jnp.stack([item[0] for item in expert_sums])[:, None].astype(F32)
        grad_oe = jnp.stack([item[1] for item in expert_sums])[:, None].astype(F32)
    if four:
        out = attn_sums[0].fold3(0, layers, done_attn)
        (grad_qkv, grad_out), smalls[0] = out[:2], out[2]
    else:
        left = jnp.stack([item[0] for item in attn_sums])
        right = jnp.stack([item[1] for item in attn_sums])
        grad_qkv = jnp.concatenate([left[:, :, : 2 * width], right[:, :, :width]], 2)
        grad_out = right[:, :, width : 2 * width]
        smalls = [right[layer, :, 2 * width :] for layer in range(layers)]
    gains, shifts, grad_router, grad_bin, grad_boe = small_out(smalls, z, experts, per)
    return (
        mixed,
        grad,
        gains,
        jnp.transpose(shifts, (1, 0, 2)),
        grad_qkv,
        grad_out,
        jnp.transpose(grad_router, (0, 2, 1)),
        grad_in,
        grad_bin,
        grad_oe,
        grad_boe,
    )


def solution(mesh):
    return jax.shard_map(
        per_device,
        mesh=mesh,
        in_specs=(
            P(("dp", "expert"), None),
            P(None, None, "dp"),
            P(None, None, "dp"),
            P(None, "dp", None),
            P(None, "dp", None),
            P(None, "dp", None),
            P(None, ("dp", "expert"), None),
            P(None, "expert", "dp", None),
            P(None, "expert", "dp"),
            P(None, "expert", "dp", None),
            P(None, "expert", "dp"),
            P(None, ("dp", "expert"), None),
            P(None, ("dp", "expert"), None),
            P(("dp", "expert"), None),
        ),
        out_specs=(
            P(("dp", "expert"), None),
            P(("dp", "expert"), None),
            P(None, None, "dp"),
            P(None, None, "dp"),
            P(None, "dp", None),
            P(None, "dp", None),
            P(None, "dp", None),
            P(None, "expert", "dp", None),
            P(None, "expert", "dp"),
            P(None, "expert", "dp", None),
            P(None, "expert", "dp"),
        ),
        check_vma=False,
    )
```

```python
import functools

import jax
import jax.numpy as jnp
from jax import lax
from jax.experimental import pallas as pl
from jax.experimental.pallas import tpu as pltpu
from jax.sharding import PartitionSpec as P

HEADS = 12
HEAD_DIM = 64
SEQ = 197
EPS = 1e-06
BF = jnp.bfloat16
F32 = jnp.float32
LANES = 128
NEG = -1e30
VMEM_LIMIT = 60 * 1024 * 1024


def up(value, step):
    return -(-value // step) * step


def dot(left, right):
    return lax.dot_general(left, right, (((1,), (0,)), ((), ())), preferred_element_type=F32)


def dot_nt(left, right):
    return lax.dot_general(left, right, (((1,), (1,)), ((), ())), preferred_element_type=F32)


def dot_tn(left, right):
    return lax.dot_general(left, right, (((0,), (0,)), ((), ())), preferred_element_type=F32)


def norm_rows(x):
    centered = x - jnp.mean(x, -1, keepdims=True)
    rstd = lax.rsqrt(jnp.mean(centered * centered, -1, keepdims=True) + EPS)
    return centered * rstd, rstd


def norm_back(grad_hat, normed, rstd):
    return rstd * (
        grad_hat
        - jnp.mean(grad_hat, -1, keepdims=True)
        - normed * jnp.mean(grad_hat * normed, -1, keepdims=True)
    )


def split(value):
    high = value.astype(BF)
    return high, (value - high.astype(F32)).astype(BF)


def join(refs):
    return jnp.concatenate([ref[...].astype(F32) for ref in refs], 0).astype(BF)


def part(value, refs):
    rows = refs[0].shape[0]
    for number, ref in enumerate(refs):
        ref[...] = value[number * rows : (number + 1) * rows].astype(ref.dtype)


def seat_mask(cols_ref, pair, seats):
    column = cols_ref[:, pair : pair + 1]
    return lax.broadcasted_iota(jnp.int32, (column.shape[0], seats), 1) == column


def token_mask(rows_ref, pair, seats):
    row = rows_ref[pair : pair + 1, :]
    return lax.broadcasted_iota(jnp.int32, (seats, row.shape[1]), 0) == row


def one(mask):
    return jnp.where(mask, 1.0, 0.0).astype(BF)


def pair_gate(gates, cols_ref, pair):
    route = cols_ref[:, 2 + pair : 3 + pair]
    lanes = lax.broadcasted_iota(jnp.int32, gates.shape, 1)
    return jnp.sum(jnp.where(lanes == route, gates, 0.0), -1, keepdims=True)


def combine(x1, gates, cols_ref, returned):
    total = x1
    for pair in range(2):
        piece = dot(one(seat_mask(cols_ref, pair, returned.shape[0])), returned)
        total = total + pair_gate(gates, cols_ref, pair) * piece
    return total


def rows_to_seats(rows_ref, seats, values):
    chosen = jnp.logical_or(token_mask(rows_ref, 0, seats), token_mask(rows_ref, 1, seats))
    return dot(one(chosen), values)


def with_note(block, cap, note):
    base = cap // 8 * 8
    tail = block[base:]
    left = tail[:, 0:LANES]
    row = lax.broadcasted_iota(jnp.int32, left.shape, 0)
    high = note.astype(BF).astype(F32)
    left = jnp.where(row == cap - base, high, left)
    left = jnp.where(row == cap - base + 1, note - high, left)
    return jnp.concatenate([block[:base], jnp.concatenate([left, tail[:, LANES:]], 1)], 0)


def note_of(block, cap):
    return block[cap : cap + 1, 0:LANES] + block[cap + 1 : cap + 2, 0:LANES]


def as_column(note, rows):
    shape = (rows, LANES)
    same = lax.broadcasted_iota(jnp.int32, shape, 0) == lax.broadcasted_iota(jnp.int32, shape, 1)
    return jnp.sum(jnp.where(same, note, 0.0), -1, keepdims=True)


def lane_sums(value):
    rows, width = value.shape
    value = jnp.concatenate([value, jnp.zeros((LANES - rows, width), F32)], 0)
    ones = jnp.ones((8, width), BF)
    high, low = split(value)
    return (dot_nt(ones, high) + dot_nt(ones, low))[0:1, :]


def near_lanes(cols_ref, pair, block, cap_pad):
    column = cols_ref[:, pair : pair + 1] - block * cap_pad
    lanes = lax.broadcasted_iota(jnp.int32, (column.shape[0], LANES), 1)
    return jnp.logical_and(lanes == column, lanes < cap_pad)


def head_masks():
    lanes = lax.broadcasted_iota(jnp.int32, (1, 2 * HEAD_DIM), 1)
    return (lanes < HEAD_DIM, lanes >= HEAD_DIM)


def head_probs(query, keys, mask, tokens):
    query = jnp.where(mask, query, 0).astype(F32) * HEAD_DIM ** (-0.5)
    scores = dot_nt(query.astype(BF), keys)
    lanes = lax.broadcasted_iota(jnp.int32, scores.shape, 1)
    scores = jnp.where(lanes < tokens, scores, NEG)
    raised = jnp.exp(scores - jnp.max(scores, -1, keepdims=True))
    return raised * (1.0 / jnp.sum(raised, -1, keepdims=True))


VM = pl.BlockSpec(memory_space=pltpu.VMEM)
ANY = pl.BlockSpec(memory_space=pl.ANY)
SM = pl.BlockSpec(memory_space=pltpu.SMEM)


def sds(shape, dtype):
    return jax.ShapeDtypeStruct(tuple(shape), dtype)


class Order:
    token = None


LOAD = "load"
STORE = "store"


class Load:
    def __init__(self, source, held, sem):
        self.copy, self.held, self.came = pltpu.make_async_copy(source, held, sem), held, False
        self.shape = held.shape
        self.copy.start()

    def wait(self):
        if not self.came:
            self.copy.wait()
            self.came = True

    def __getitem__(self, index):
        self.wait()
        return self.held[index]


class Store:
    def __init__(self, target, held, sems):
        self.target, self.held, self.sems, self.copies = target, held, sems, []
        self.shape, self.dtype = held.shape, held.dtype

    def __getitem__(self, index):
        return self.held[index]

    def __setitem__(self, index, value):
        self.held[index] = value

    def send(self, *index):
        number = len(self.copies)
        copy = pltpu.make_async_copy(
            self.held.at[index], self.target.at[index], self.sems.at[number]
        )
        copy.start()
        self.copies.append(copy)

    def finish(self):
        if not self.copies:
            self.send(*[slice(None)] * len(self.shape))


PARTS = 8


def call(kernel, name, args, specs, outs, out_specs, scratch, aliases=None):
    after = []
    if Order.token is not None and not any(Order.token is arg for arg in args):
        after = [Order.token]
    given = len(args)
    single = not isinstance(outs, (tuple, list))
    results = [outs] if single else list(outs)
    out_kinds = [out_specs] if single else list(out_specs)
    loads = [i for i, spec in enumerate(specs) if spec is LOAD]
    stores = [i for i, spec in enumerate(out_kinds) if spec is STORE]
    extra = [pltpu.VMEM(args[i].shape, args[i].dtype) for i in loads]
    extra += [pltpu.VMEM(results[i].shape, results[i].dtype) for i in stores]
    extra += [pltpu.SemaphoreType.DMA((max(len(loads), 1),))]
    extra += [pltpu.SemaphoreType.DMA((max(PARTS * len(stores), 1),))]

    def body(*refs):
        ins = list(refs[:given])
        rest = list(refs[given + len(after) :])
        made, own = rest[: len(results)], rest[len(results) : len(rest) - len(extra)]
        held = rest[len(rest) - len(extra) :]
        load_sems, store_sems = held[-2:]
        for n, i in enumerate(loads):
            ins[i] = Load(ins[i], held[n], load_sems.at[n])
        for n, i in enumerate(stores):
            sems = store_sems.at[pl.ds(PARTS * n, PARTS)]
            made[i] = Store(made[i], held[len(loads) + n], sems)
        kernel(*ins, *made, *own)
        for i in loads:
            ins[i].wait()
        for i in stores:
            made[i].finish()
        for i in stores:
            for copy in made[i].copies:
                copy.wait()

    result = pl.pallas_call(
        body,
        name=name,
        in_specs=[ANY if spec is LOAD else spec for spec in specs] + [ANY] * len(after),
        out_specs=ANY if single and out_specs is STORE else (
            out_specs if single else [ANY if spec is STORE else spec for spec in out_kinds]
        ),
        out_shape=outs,
        scratch_shapes=list(scratch) + extra,
        input_output_aliases=aliases or {},
        compiler_params=pltpu.CompilerParams(vmem_limit_bytes=VMEM_LIMIT),
    )(*args, *after)
    Order.token = result[0] if isinstance(result, (tuple, list)) else result
    return result


def hold(values, after):
    def kernel(*refs):
        pass

    return call(
        kernel,
        "hold",
        [*values, *after],
        [ANY] * (len(values) + len(after)),
        [sds(value.shape, value.dtype) for value in values],
        [ANY] * len(values),
        [],
        {i: i for i in range(len(values))},
    )


def move(name, args, copies, outs):
    total = len(copies)

    def kernel(*refs):
        ins, rest = refs[: len(args)], refs[len(args) :]
        results, held = rest[: len(outs)], rest[len(outs) : len(outs) + total]
        in_sems, out_sems = rest[-2:]
        loads = [
            pltpu.make_async_copy(ins[i].at[where], held[n], in_sems.at[n])
            for n, (i, where, _, _, _) in enumerate(copies)
        ]
        stores = [
            pltpu.make_async_copy(held[n], results[o].at[into], out_sems.at[n])
            for n, (_, _, o, into, _) in enumerate(copies)
        ]
        start(loads)
        for load, store in zip(loads, stores):
            load.wait()
            store.start()
        wait(stores)

    return call(
        kernel,
        name,
        args,
        [ANY] * len(args),
        outs,
        [ANY] * len(outs),
        [pltpu.VMEM(shape, BF) for *_, shape in copies]
        + [pltpu.SemaphoreType.DMA((total,)), pltpu.SemaphoreType.DMA((total,))],
    )


def fold(name, args, block, tasks, outs, aliases=None):
    terms = [(t, term) for t, (listed, _, _) in enumerate(tasks) for term in listed]
    writes = [(t, write) for t, (_, _, listed) in enumerate(tasks) for write in listed]
    wide = [t for t, task in enumerate(tasks) if task[1] == F32]
    slim = [t for t, task in enumerate(tasks) if task[1] != F32]

    def kernel(*refs):
        ins, rest = refs[: len(args)], refs[len(args) :]
        results = rest[: len(outs)]
        loaded, wide_ref, slim_ref, in_sems, out_sems = rest[len(outs) :]
        loads = [
            pltpu.make_async_copy(ins[i].at[where], loaded.at[n], in_sems.at[n])
            for n, (_, (i, where)) in enumerate(terms)
        ]
        for copy in loads:
            copy.start()
        stores = []
        for t, (_, kind, _) in enumerate(tasks):
            total = None
            for n, (task, _) in enumerate(terms):
                if task == t:
                    loads[n].wait()
                    piece = loaded[n].astype(F32)
                    total = piece if total is None else total + piece
            holder = wide_ref.at[wide.index(t)] if kind == F32 else slim_ref.at[slim.index(t)]
            holder[...] = total.astype(kind)
            for n, (task, (o, into, within)) in enumerate(writes):
                if task == t:
                    copy = pltpu.make_async_copy(
                        holder.at[within], results[o].at[into], out_sems.at[n]
                    )
                    copy.start()
                    stores.append(copy)
        for copy in stores:
            copy.wait()

    return call(
        kernel,
        name,
        args,
        [ANY] * len(args),
        outs,
        [ANY] * len(outs),
        [
            pltpu.VMEM((len(terms), *block), BF),
            pltpu.VMEM((max(len(wide), 1), *(block if wide else (16, LANES))), F32),
            pltpu.VMEM((max(len(slim), 1), *(block if slim else (16, LANES))), BF),
            pltpu.SemaphoreType.DMA((len(terms),)),
            pltpu.SemaphoreType.DMA((len(writes),)),
        ],
        aliases=aliases,
    )


ALL = slice(None)


class Weights:
    def __init__(self, arrays, places):
        self.arrays, self.places = list(arrays), places


OWNERS = -1


def attn_targets(width, rows, wqkv, wout):
    return {
        0: [(wqkv, 0, 2 * width, 0, rows, 0)],
        1: [(wqkv, 0, width, 2 * width, rows, 0), (wout, width, width, 0, rows, 0)],
    }


def expert_targets(width, hidden, rows, whole, win, woe):
    if whole:
        return {0: [(win, 0, hidden, 0, rows, 0)], 1: [(woe, 0, width, 0, rows, 0)]}
    per = hidden // width
    return {
        0: [(win, 0, hidden, 0, rows, 0)],
        1: [(woe, q * width, width, 0, per * rows, q * rows) for q in range(per)],
    }


class Chunks:
    def __init__(self, refs, weights, width, hidden, rows, whole, win, woe, sems, more=()):
        per = hidden // width
        self.parts = []
        if whole:
            copies = fetch(refs, weights, None, expert_targets(width, hidden, rows, True, win, woe), 0, sems)
            copies += fetch(
                refs, weights, None, expert_targets(width, hidden, rows, True, win, woe), 1, sems
            )
            self.parts = [copies] + [[] for _ in range(per - 1)]
        else:
            ref = refs[0]
            shards = ref.shape[0]
            for c in range(per):
                here = pl.ds(c * width, width)
                copies = [
                    pltpu.make_async_copy(
                        ref.at[d, 0, :, here], win.at[pl.ds(d * rows, rows), here], sems.at[d]
                    )
                    for d in range(shards)
                ]
                first = c * shards // per
                for n in range(shards):
                    d, q = first + n // per, n % per
                    copies.append(
                        pltpu.make_async_copy(
                            ref.at[d, 1, :, pl.ds(q * width, width)],
                            woe.at[pl.ds((d * per + q) * rows, rows)],
                            sems.at[shards + n],
                        )
                    )
                self.parts.append(copies)
        for copies, extra in zip(self.parts, more):
            copies.append(extra)
        start(self.parts[0])

    def take(self, c):
        wait(self.parts[c])
        if c + 1 < len(self.parts):
            start(self.parts[c + 1])


def copies_in(weights):
    return 4 * sum(
        len(parts) if array.ndim == 3 else array.shape[0]
        for array, (off, parts) in zip(weights.arrays, weights.places)
    )


def fetch(refs, weights, me, targets, part_number, sems):
    copies = []
    for ref, (off, parts) in zip(refs, weights.places):
        rows = ref.shape[-2]
        if off == OWNERS:
            sources = [(d, (d, part_number)) for d in range(ref.shape[0])]
        elif isinstance(off, tuple):
            sources = [(me ^ o, (k, part_number)) for k, o in enumerate(off)]
        elif part_number in parts:
            at = None if off is None else me ^ off
            sources = [(at, (parts.index(part_number),))]
        else:
            sources = []
        for at, where in sources:
            for scratch, first, size, into, times, plus in targets[part_number]:
                place = 0 if at is None else at * times + plus
                if off not in (None, OWNERS):
                    place = pl.multiple_of(place, 16)
                copies.append(
                    pltpu.make_async_copy(
                        ref.at[(*where, ALL, pl.ds(first, size))],
                        scratch.at[pl.ds(place, rows), pl.ds(into, size)],
                        sems.at[len(copies)],
                    )
                )
    return copies


def start(copies):
    for copy in copies:
        copy.start()


def wait(copies):
    for copy in copies:
        copy.wait()


def small_rows(per, experts):
    return up(7 + experts + per + 1, 8)


def pack_small(norm_gains, biases, w_router, b_in, b_expout):
    layers, shard, experts = w_router.shape
    per = b_in.shape[2] // shard
    height = small_rows(per, experts)

    def kernel(gain_ref, bias_ref, router_ref, in_ref, oe_ref, out, square):
        out[...] = jnp.zeros_like(out)
        for layer in range(layers):
            at = layer * height
            out[at : at + 2, 0:shard] = gain_ref[layer]
            out[at + 2 : at + 7, 0:shard] = bias_ref[layer]
            square[...] = jnp.zeros_like(square)
            square[0:shard, 0:experts] = router_ref[layer]
            turned = square[...].T
            out[at + 7 : at + 7 + experts, :] = turned[0:experts, :]
            at = at + 7 + experts
            for q in range(per):
                out[at + q : at + q + 1, 0:shard] = in_ref[layer, :, q * shard : (q + 1) * shard]
            out[at + per : at + per + 1, 0:shard] = oe_ref[layer]

    return call(
        kernel,
        "pack_small",
        [norm_gains, biases, w_router, b_in, b_expout],
        [VM] * 5,
        sds((layers * height, LANES), F32),
        VM,
        [pltpu.VMEM((LANES, LANES), F32)],
    )


def unpack_small(gathered, layers, shard, per, experts, after):
    shards = gathered.shape[0]
    width = shards * shard
    height = small_rows(per, experts)

    def kernel(ref, *refs):
        refs = refs[len(after) :]
        tall = refs[-1]
        for layer in range(layers):
            vec, router, bias_in, bias_oe = refs[4 * layer : 4 * layer + 4]
            at = layer * height
            vec[...] = jnp.zeros_like(vec)
            tall[...] = jnp.zeros_like(tall)
            for d in range(shards):
                here = slice(d * shard, (d + 1) * shard)
                vec[0:7, here] = ref[d, at : at + 7, 0:shard]
                tall[0:experts, here] = ref[d, at + 7 : at + 7 + experts, 0:shard]
                row = at + 7 + experts
                for q in range(per):
                    first = (d * per + q) * shard
                    bias_in[:, first : first + shard] = ref[d, row + q : row + q + 1, 0:shard]
                bias_oe[:, here] = ref[d, row + per : row + per + 1, 0:shard]
            router[...] = tall[...].T.astype(BF)

    shapes = []
    for _ in range(layers):
        shapes += [
            sds((8, width), F32),
            sds((width, LANES), BF),
            sds((1, width * per), F32),
            sds((1, width), F32),
        ]
    outs = call(
        kernel,
        "unpack_small",
        [gathered, *after],
        [VM] + [ANY] * len(after),
        shapes,
        [VM] * len(shapes),
        [pltpu.VMEM((LANES, width), F32)],
    )
    return [outs[4 * layer : 4 * layer + 4] for layer in range(layers)]


def place_pairs(routes, seat_order, padded, cap, cap_pad, z):
    layers, tokens, _ = routes.shape
    tall = up(padded, LANES)

    def kernel(z_ref, route_ref, order_ref, *refs):
        outs, wide = refs[:-1], refs[-1]
        lanes = lax.broadcasted_iota(jnp.int32, (tokens, LANES), 1)
        lanes_tall = lax.broadcasted_iota(jnp.int32, (tall, LANES), 1)
        for layer in range(layers):
            given = jnp.full((tokens, LANES), -1.0, F32)
            for k in range(2):
                given = jnp.where(lanes == k, route_ref[layer, :, k : k + 1].astype(F32), given)
                given = jnp.where(lanes == 2 + k, order_ref[layer, :, k : k + 1].astype(F32), given)
            wide[...] = jnp.full((tall, LANES), -1.0, F32)
            wide[0:tokens, :] = given
            table = wide[...]
            turned = table.T
            seats = []
            for k in range(2):
                expert, order = table[:, k : k + 1], table[:, 2 + k : 3 + k]
                rank = jnp.zeros((tall, 1), F32)
                for j in range(2):
                    ahead = jnp.logical_and(
                        turned[j : j + 1, :] == expert, turned[2 + j : 3 + j, :] < order
                    )
                    rank = rank + jnp.sum(jnp.where(ahead, 1.0, 0.0), -1, keepdims=True)
                expert, rank = expert.astype(jnp.int32), rank.astype(jnp.int32)
                near = jnp.bitwise_xor(expert, z_ref[0])
                good = jnp.logical_and(expert >= 0, rank < cap)
                seats.append(jnp.where(good, near * cap_pad + rank, -1).astype(F32))
            table = jnp.where(lanes_tall == 2, table[:, 0:1], table)
            table = jnp.where(lanes_tall == 3, wide[:, 1:2], table)
            table = jnp.where(lanes_tall == 0, seats[0], table)
            table = jnp.where(lanes_tall == 1, seats[1], table)
            cols, rows = outs[2 * layer], outs[2 * layer + 1]
            cols[...] = table[0:padded, :].astype(jnp.int32)
            rows[...] = table.T[0:8, 0:padded].astype(jnp.int32)

    shapes = []
    for _ in range(layers):
        shapes += [sds((padded, LANES), jnp.int32), sds((8, padded), jnp.int32)]
    outs = call(
        kernel,
        "place_pairs",
        [z, routes, seat_order],
        [SM, VM, VM],
        shapes,
        [VM] * len(shapes),
        [pltpu.VMEM((tall, LANES), F32)],
    )
    return outs[0::2], outs[1::2]


def attn_fwd(me, layer, x_args, weights, vecs, router, noise, cols, rows, cap, used):
    first = len(x_args) == 1
    padded, width = cols.shape[0], vecs.shape[1]
    tokens, experts = noise.shape[1:]
    seats = experts * cap
    owners = 0 if first else len(x_args[3])
    count = len(weights.arrays)
    shard = weights.arrays[0].shape[-2]

    def kernel(*refs):
        refs = list(refs)
        me_ref = refs.pop(0)
        if first:
            tok_ref = refs.pop(0)
        else:
            below_x1, below_gates, below_cols = refs.pop(0), refs.pop(0), refs.pop(0)
            below_blocks = [refs.pop(0) for _ in range(owners)]
        w_refs = [refs.pop(0) for _ in range(count)]
        vec_ref, router_ref, noise_ref, cols_ref, rows_ref = (refs.pop(0) for _ in range(5))
        x_out, x1_out, qkv_out, gates_out, ao_out = (refs.pop(0) for _ in range(5))
        seat_outs = [refs.pop(0) for _ in range(experts)]
        wqkv, wout, sems, more_sems = refs
        targets = attn_targets(width, shard, wqkv, wout)
        left = fetch(w_refs, weights, me_ref[0], targets, 0, sems)
        right = fetch(w_refs, weights, me_ref[0], targets, 1, more_sems)
        start(left + right)
        vec = lambda k: vec_ref[k : k + 1, :]
        if first:
            x_out[...] = jnp.zeros_like(x_out)
            x_out[0:tokens, :] = tok_ref[...].astype(F32)
            x = x_out[...]
        else:
            x = combine(below_x1[...], below_gates[...], below_cols, join(below_blocks))
            x_out[...] = x
        normed, rstd = norm_rows(x)
        a_low = (normed * vec(0) + vec(2)).astype(BF)
        ao_out[:, 0:width] = a_low
        gates_out[...] = jnp.zeros_like(gates_out)
        gates_out[0:tokens, 0:experts] = noise_ref[layer]
        noise_here = gates_out[...]
        wait(left)
        for k in range(3):
            if k == 2:
                wait(right)
            piece = dot(a_low, wqkv[:, k * width : (k + 1) * width])
            if k == 0:
                piece = piece + vec(4)
            if k == 2:
                piece = piece + vec(5)
            qkv_out[:, k * width : (k + 1) * width] = piece.astype(BF)
        masks = head_masks()
        for two in range(HEADS // 2):
            at = two * 2 * HEAD_DIM
            query = qkv_out[:, at : at + 2 * HEAD_DIM]
            keys = qkv_out[:, width + at : width + at + 2 * HEAD_DIM]
            values = qkv_out[:, 2 * width + at : 2 * width + at + 2 * HEAD_DIM]
            mixed = None
            for mask in masks:
                probs = head_probs(query, keys, mask, tokens).astype(BF)
                piece = dot(probs, jnp.where(mask, values, 0).astype(BF))
                mixed = piece if mixed is None else mixed + piece
            ao_out[:, width + at : width + at + 2 * HEAD_DIM] = mixed.astype(BF)
        x1 = x + dot(ao_out[:, width : 2 * width], wout[...]) + vec(6)
        x1_out[...] = x1
        normed2, rstd2 = norm_rows(x1)
        moe = normed2 * vec(1) + vec(3)
        high, low = split(moe)
        logits = dot(high, router_ref[...]) + dot(low, router_ref[...]) + noise_here
        lanes = lax.broadcasted_iota(jnp.int32, logits.shape, 1)
        logits = jnp.where(lanes < experts, logits, NEG)
        raised = jnp.exp(logits - jnp.max(logits, -1, keepdims=True))
        gates = raised / jnp.sum(raised, -1, keepdims=True)
        gates_out[...] = gates
        ao_out[:, 2 * width : 3 * width] = high
        sent = rows_to_seats(rows_ref, seats, high)
        chosen = [pair_gate(gates, cols_ref, pair) for pair in range(2)]
        for block, ref in enumerate(seat_outs):
            note = jnp.zeros((1, LANES), F32)
            for pair in range(2):
                here = near_lanes(cols_ref, pair, block, cap)
                note = note + jnp.sum(jnp.where(here, chosen[pair], 0.0), 0, keepdims=True)
            piece = sent[block * cap : (block + 1) * cap]
            ref[...] = with_note(piece, used, note).astype(BF)

    args = [me]
    specs = [SM]
    if first:
        args += [x_args[0]]
        specs += [VM]
    else:
        args += [x_args[0], x_args[1], x_args[2], *x_args[3]]
        specs += [VM] * (3 + owners)
    args += [*weights.arrays, vecs, router, noise, cols, rows]
    specs += [ANY] * count + [VM] * 5
    outs = [
        sds((padded, width), F32),
        sds((padded, width), F32),
        sds((padded, 3 * width), BF),
        sds((padded, LANES), F32),
        sds((padded, 3 * width), BF),
    ] + [sds((cap, width), BF)] * experts
    result = call(
        kernel,
        "attn_fwd",
        args,
        specs,
        outs,
        [VM] * len(outs),
        [
            pltpu.VMEM((width, 3 * width), BF),
            pltpu.VMEM((width, width), BF),
            pltpu.SemaphoreType.DMA((copies_in(weights),)),
            pltpu.SemaphoreType.DMA((copies_in(weights),)),
        ],
    )
    return result[:5], result[5:]


def expert_fwd(me, z, seat_blocks, weights, bias_in, bias_oe, used, ordered):
    owners = len(seat_blocks)
    cap, width = seat_blocks[0].shape
    seats = owners * cap
    hidden = bias_in.shape[1]
    count = len(weights.arrays)
    shard = weights.arrays[0].shape[-2]
    whole = weights.places[0][0] is None
    step = width

    def kernel(*refs):
        refs = list(refs)
        me_ref, z_ref = refs.pop(0), refs.pop(0)
        seat_refs = [refs.pop(0) for _ in range(owners)]
        w_refs = [refs.pop(0) for _ in range(count)]
        bin_ref, boe_ref = refs.pop(0), refs.pop(0)
        rh_out, slope_out, gate_out, made_out = (refs.pop(0) for _ in range(4))
        outs = [refs.pop(0) for _ in range(1 if ordered else owners)]
        win, woe, sems = refs
        chunks = Chunks(w_refs, weights, width, hidden, shard, whole, win, woe, sems)
        blocks = [ref[...].astype(F32) for ref in seat_refs]
        rows = jnp.concatenate(blocks, 0).astype(BF)
        rh_out[:, 0:width] = rows
        rh_out.send(ALL, pl.ds(0, width))
        columns = [as_column(note_of(block, used), cap) for block in blocks]
        gate_out[...] = jnp.broadcast_to(jnp.concatenate(columns, 0), gate_out.shape)
        total_out = None
        for at in range(0, hidden, step):
            chunks.take(at // step)
            pre = dot(rows, win[:, at : at + step]) + bin_ref[:, at : at + step]
            square = pre * pre
            bend = jnp.tanh(0.7978845608028654 * (pre + 0.044715 * square * pre))
            h = (0.5 * pre * (1.0 + bend)).astype(BF)
            slope = 0.5 * (1.0 + bend) + 0.5 * pre * (1.0 - bend * bend) * (
                0.7978845608028654 * (1.0 + 0.134145 * square)
            )
            rh_out[:, width + at : width + at + step] = h
            slope_out[:, at : at + step] = slope.astype(BF)
            rh_out.send(ALL, pl.ds(width + at, step))
            slope_out.send(ALL, pl.ds(at, step))
            piece = dot(h, woe[at : at + step, :])
            total_out = piece if total_out is None else total_out + piece
        total_out = total_out + boe_ref[...]
        made_out[...] = total_out.astype(BF)
        if ordered:
            outs = [outs[0].held.at[z_ref[0] ^ k] for k in range(owners)]
        part(total_out, outs)

    shapes = [
        sds((seats, width + hidden), BF),
        sds((seats, hidden), BF),
        sds((seats, LANES), F32),
        sds((seats, width), BF),
    ] + ([sds((owners, cap, width), BF)] if ordered else [sds((cap, width), BF)] * owners)
    result = call(
        kernel,
        "expert_fwd",
        [me, z, *seat_blocks, *weights.arrays, bias_in, bias_oe],
        [SM, SM] + [LOAD] * owners + [ANY] * count + [LOAD] * 2,
        shapes,
        [STORE] * len(shapes),
        [
            pltpu.VMEM((width, hidden), BF),
            pltpu.VMEM((hidden, width), BF),
            pltpu.SemaphoreType.DMA((2 * copies_in(weights),)),
        ],
    )
    return result[:4], result[4:]


def top_seats(z, cotangent, rows, cap, experts):
    tokens, width = cotangent.shape
    padded = rows.shape[1]

    def kernel(z_ref, cot_ref, rows_ref, grad_out, out):
        grad_out[...] = jnp.zeros_like(grad_out)
        grad_out[0:tokens, :] = cot_ref[...].astype(F32)
        sent = rows_to_seats(rows_ref, cap * experts, grad_out[...].astype(BF))
        part(sent, [out.at[z_ref[0] ^ k] for k in range(experts)])

    return call(
        kernel,
        "top_seats",
        [z, cotangent, rows],
        [SM, VM, VM],
        [sds((padded, width), F32), sds((experts, cap, width), BF)],
        [VM] * 2,
        [],
    )


def mix(z, x1, gates, cols, returned, tokens):
    width = x1.shape[1]

    def kernel(z_ref, x1_ref, gates_ref, cols_ref, ref, out):
        blocks = join([ref.at[z_ref[0] ^ k] for k in range(ref.shape[0])])
        total = combine(x1_ref[...], gates_ref[...], cols_ref, blocks)
        out[...] = total[0:tokens, :]

    return call(
        kernel,
        "mix",
        [z, x1, gates, cols, returned],
        [SM] + [VM] * 4,
        sds((tokens, width), F32),
        VM,
        [],
    )


def expert_back(me, z, grad_blocks, slope, gate, made, weights, used):
    ordered = grad_blocks[0].ndim == 3
    cap, width = grad_blocks[0].shape[-2:]
    owners = slope.shape[0] // cap
    count_in = len(grad_blocks)
    seats, hidden = slope.shape
    count = len(weights.arrays)
    shard = weights.arrays[0].shape[-2]
    whole = weights.places[0][0] is None
    step = width

    def kernel(*refs):
        refs = list(refs)
        me_ref, z_ref = refs.pop(0), refs.pop(0)
        seat_refs = [refs.pop(0) for _ in range(count_in)]
        slope_ref, gate_ref, made_ref = (refs.pop(0) for _ in range(3))
        w_refs = [refs.pop(0) for _ in range(count)]
        gd_out = refs.pop(0)
        outs = [refs.pop(0) for _ in range(owners)]
        win, woe, slopes, sems, slope_sems = refs
        more = [
            pltpu.make_async_copy(
                slope_ref.at[:, pl.ds(at, step)],
                slopes.at[:, pl.ds(at, step)],
                slope_sems.at[at // step],
            )
            for at in range(0, hidden, step)
        ]
        chunks = Chunks(w_refs, weights, width, hidden, shard, whole, win, woe, sems, more)
        if ordered:
            given = [seat_refs[0][z_ref[0] ^ k].astype(F32) for k in range(owners)]
        else:
            given = [ref[...].astype(F32) for ref in seat_refs]
        given = jnp.concatenate(given, 0)
        grad = (given * gate_ref[:, 0:1]).astype(BF)
        notes = given * made_ref[...].astype(F32)
        notes = [lane_sums(notes[k * cap : (k + 1) * cap]) for k in range(owners)]
        gd_out[:, 0:width] = grad
        gd_out.send(ALL, pl.ds(0, width))
        total_out = None
        for at in range(0, hidden, step):
            chunks.take(at // step)
            d_hidden = dot_nt(grad, woe[at : at + step, :])
            d_pre = (d_hidden * slopes[:, at : at + step].astype(F32)).astype(BF)
            gd_out[:, width + at : width + at + step] = d_pre
            gd_out.send(ALL, pl.ds(width + at, step))
            piece = dot_nt(d_pre, win[:, at : at + step])
            total_out = piece if total_out is None else total_out + piece
        for k, ref in enumerate(outs):
            ref[...] = with_note(total_out[k * cap : (k + 1) * cap], used, notes[k]).astype(BF)

    shapes = [sds((seats, width + hidden), BF)]
    shapes += [sds((cap, width), BF)] * owners
    result = call(
        kernel,
        "expert_back",
        [me, z, *grad_blocks, slope, gate, made, *weights.arrays],
        [SM, SM] + [LOAD] * count_in + [ANY] + [LOAD] * 2 + [ANY] * count,
        shapes,
        [STORE] * (1 + owners),
        [
            pltpu.VMEM((width, hidden), BF),
            pltpu.VMEM((hidden, width), BF),
            pltpu.VMEM((seats, hidden), BF),
            pltpu.SemaphoreType.DMA((2 * copies_in(weights),)),
            pltpu.SemaphoreType.DMA((hidden // step,)),
        ],
    )
    return result[0], result[1:]


def column_sums(value):
    return dot(jnp.ones((8, value.shape[0]), BF), value)[0:1, :]


def own_columns(width, shards, core):
    shard = width // shards
    half = width // 2
    row = lax.broadcasted_iota(jnp.int32, (width, half), 0)
    column = lax.broadcasted_iota(jnp.int32, (width, half), 1)
    place = column + core * shard
    for k in range(1, shards // 2):
        place = place + jnp.where(column >= k * shard, shard, 0)
    return one(row == place)


def expert_grads(me, own, other, shards):
    seats, both = own[0].shape
    width = HEADS * HEAD_DIM
    hidden = both - width
    per, shard = hidden // width, width // shards
    part_hidden = hidden // shards
    sides = 2 if other else 1
    tall = width // 2 if other else width
    deep = hidden // 2 if other else hidden
    total = shards * per if other else 2

    blocks = shards // 2 if other else per
    size = part_hidden if other else width

    def kernel(me_ref, *refs):
        refs = list(refs)
        rh = [refs.pop(0) for _ in range(sides)]
        gd = [refs.pop(0) for _ in range(sides)]
        outs = [refs.pop(0) for _ in range(1 if other else 2)]
        bias_ref, win, woe, h_held, row_held, gd_held, sems, load_sems = refs
        core = me_ref[0] & 1
        copies = []
        loads = {}

        def fetch_in(key, source, target):
            copy = pltpu.make_async_copy(source, target, load_sems.at[len(loads)])
            copy.start()
            loads[key] = copy

        for i in range(sides):
            fetch_in(("d", i), gd[i].at[:, pl.ds(0, width)], gd_held.at[i, :, pl.ds(0, width)])
        for k in range(blocks):
            first = width + k * size
            if other:
                first = pl.multiple_of(width + (2 * k + core) * size, LANES)
            for i in range(sides):
                here = pl.ds(k * size, size)
                fetch_in(("h", k, i), rh[i].at[:, pl.ds(first, size)], h_held.at[i, :, here])
        for i in range(sides):
            fetch_in(("r", i), rh[i].at[:, pl.ds(0, width)], row_held.at[i])
        for k in range(per):
            here = pl.ds(width + k * width, width)
            for i in range(sides):
                fetch_in(("p", k, i), gd[i].at[:, here], gd_held.at[i, :, here])

        def send(source, target):
            copy = pltpu.make_async_copy(source, target, sems.at[len(copies)])
            copy.start()
            copies.append(copy)

        def summed(pieces):
            total = pieces[0]
            for piece in pieces[1:]:
                total = total + piece
            return total

        for i in range(sides):
            loads["d", i].wait()
        d_outs = [gd_held[i, :, 0:width] for i in range(sides)]
        for k in range(blocks):
            here = slice(k * size, (k + 1) * size)
            for i in range(sides):
                loads["h", k, i].wait()
            total = summed([dot_tn(h_held[i, :, here], d_outs[i]) for i in range(sides)])
            woe[here, :] = total.astype(BF)
            if other:
                for q in range(per):
                    send(
                        woe.at[pl.ds(k * size + q * shard, shard)],
                        outs[0].at[k, 1, :, pl.ds(q * width, width)],
                    )
        for i in range(sides):
            loads["r", i].wait()
        lefts = [row_held[i] for i in range(sides)]
        if other:
            pick = own_columns(width, shards, core)
            lefts = [dot(left, pick).astype(BF) for left in lefts]
        for k in range(per):
            here = slice(width + k * width, width + (k + 1) * width)
            for i in range(sides):
                loads["p", k, i].wait()
            total = summed([dot_tn(lefts[i], gd_held[i, :, here]) for i in range(sides)])
            win[:, k * width : (k + 1) * width] = total.astype(BF)
            if other:
                for n in range(shards // 2):
                    here = pl.ds(k * width, width)
                    send(
                        win.at[pl.ds(n * shard, shard), here], outs[0].at[n, 0, :, here]
                    )
        if not other:
            send(win, outs[0])
            send(woe, outs[1])
        bias_ref[...] = jnp.zeros_like(bias_ref)
        sums = summed([column_sums(gd_held[i]) for i in range(sides)])
        for d in range(shards):
            for q in range(per):
                first = width + (d * per + q) * shard
                bias_ref[q : q + 1, d * shard : (d + 1) * shard] = sums[:, first : first + shard]
        bias_ref[per : per + 1, :] = sums[:, 0:width]
        wait(copies)

    if other:
        shapes = [sds((shards // 2, 2, shard, hidden), BF)]
        args = [own[0], other[0], own[1], other[1]]
    else:
        shapes = [sds((width, hidden), BF), sds((hidden, width), BF)]
        args = list(own)
    result = call(
        kernel,
        "expert_grads",
        [me, *args],
        [SM] + [ANY] * len(args),
        shapes + [sds((8, width), F32)],
        [ANY] * len(shapes) + [VM],
        [
            pltpu.VMEM((tall, hidden), BF),
            pltpu.VMEM((deep, width), BF),
            pltpu.VMEM((sides, seats, blocks * size), BF),
            pltpu.VMEM((sides, seats, width), BF),
            pltpu.VMEM((sides, seats, width + hidden), BF),
            pltpu.SemaphoreType.DMA((total,)),
            pltpu.SemaphoreType.DMA((sides * (2 + blocks + per),)),
        ],
    )
    return result[:-1], result[-1]


def pick_columns(me, value, shards):
    rows, wide = value.shape
    width = wide // 3

    def kernel(me_ref, ref, own, other):
        core = me_ref[0] & 1
        for out, side in ((own, core), (other, 1 - core)):
            pick = own_columns(width, shards, side)
            for k in range(3):
                piece = dot(ref[:, k * width : (k + 1) * width], pick)
                out[:, k * width // 2 : (k + 1) * width // 2] = piece.astype(BF)

    return call(
        kernel,
        "pick_columns",
        [me, value],
        [SM, VM],
        [sds((rows, wide // 2), BF)] * 2,
        [VM] * 2,
        [],
    )


def attn_back(
    me, back_blocks, gates, router, grad, x, x1, qkv, cols, vecs, weights, below, tokens, used
):
    padded, width = grad.shape
    owners = len(back_blocks)
    cap = back_blocks[0].shape[0]
    seats = owners * cap
    count = len(weights.arrays)
    shard = weights.arrays[0].shape[-2]

    def kernel(*refs):
        refs = list(refs)
        me_ref = refs.pop(0)
        back_refs = [refs.pop(0) for _ in range(owners)]
        gates_ref, router_ref, grad_ref, x_ref, x1_ref, qkv_ref, cols_ref, vec_ref = (
            refs.pop(0) for _ in range(8)
        )
        w_refs = [refs.pop(0) for _ in range(count)]
        if below is not None:
            below_rows = refs.pop(0)
        dx_out, back_out = refs.pop(0), refs.pop(0)
        seat_outs = [refs.pop(0) for _ in range(owners)] if below is not None else None
        wqkv, wout, small_out, sems, more_sems = refs
        targets = attn_targets(width, shard, wqkv, wout)
        right = fetch(w_refs, weights, me_ref[0], targets, 1, sems)
        left = fetch(w_refs, weights, me_ref[0], targets, 0, more_sems)
        start(right + left)
        vec = lambda k: vec_ref[k : k + 1, :]
        blocks = [ref[...].astype(F32) for ref in back_refs]
        gates = gates_ref[...]
        lanes = lax.broadcasted_iota(jnp.int32, gates.shape, 1)
        d_gates = jnp.zeros_like(gates)
        for pair in range(2):
            d_pair = jnp.zeros_like(gates)
            for block in range(owners):
                here = near_lanes(cols_ref, pair, block, cap)
                d_pair = d_pair + jnp.where(here, note_of(blocks[block], used), 0.0)
            d_pair = jnp.sum(d_pair, -1, keepdims=True)
            d_gates = d_gates + jnp.where(lanes == cols_ref[:, 2 + pair : 3 + pair], d_pair, 0.0)
        dz = gates * (d_gates - jnp.sum(d_gates * gates, -1, keepdims=True))
        high, low = split(dz)
        moe_part = dot_nt(high, router_ref[...]) + dot_nt(low, router_ref[...])
        back_out[0:padded, 4 * width : 4 * width + LANES] = high
        back_out[0:padded, 4 * width + LANES : 4 * width + 2 * LANES] = low
        chosen = jnp.logical_or(seat_mask(cols_ref, 0, seats), seat_mask(cols_ref, 1, seats))
        d_moe = dot(one(chosen), jnp.concatenate(blocks, 0).astype(BF)) + moe_part
        normed2, rstd2 = norm_rows(x1_ref[...])
        small_out[...] = jnp.zeros_like(small_out)
        small_out[1:2, :] = jnp.sum(d_moe * normed2, 0, keepdims=True)
        small_out[3:4, :] = jnp.sum(d_moe, 0, keepdims=True)
        d_x1 = grad_ref[...] + norm_back(d_moe * vec(1), normed2, rstd2)
        dy = d_x1.astype(BF)
        back_out[0:padded, 3 * width : 4 * width] = dy
        small_out[6:7, :] = column_sums(dy)
        wait(right)
        d_mixed = dot_nt(dy, wout[...]).astype(BF)
        masks = head_masks()
        scale = HEAD_DIM ** (-0.5)
        for two in range(HEADS // 2):
            at = two * 2 * HEAD_DIM
            query = qkv_ref[:, at : at + 2 * HEAD_DIM]
            keys = qkv_ref[:, width + at : width + at + 2 * HEAD_DIM]
            values = qkv_ref[:, 2 * width + at : 2 * width + at + 2 * HEAD_DIM]
            d_o = d_mixed[:, at : at + 2 * HEAD_DIM]
            sums = None
            for mask in masks:
                probs = head_probs(query, keys, mask, tokens)
                d_here = jnp.where(mask, d_o, 0).astype(BF)
                d_probs = dot_nt(d_here, values)
                d_values = dot_tn(probs.astype(BF), d_here)
                d_scores = probs * (d_probs - jnp.sum(d_probs * probs, -1, keepdims=True))
                d_scores = d_scores.astype(BF)
                d_query = dot(d_scores, jnp.where(mask, keys, 0).astype(BF))
                d_keys = dot_tn(d_scores, jnp.where(mask, query, 0).astype(BF))
                here = (d_query, d_keys, d_values)
                sums = here if sums is None else tuple(s + h for s, h in zip(sums, here))
            for k, value in enumerate((sums[0] * scale, sums[1] * scale, sums[2])):
                first = k * width + at
                back_out[0:padded, first : first + 2 * HEAD_DIM] = value.astype(BF)
        wait(left)
        d_normed = None
        for k in range(3):
            here = back_out[0:padded, k * width : (k + 1) * width]
            if k != 1:
                row = 4 if k == 0 else 5
                small_out[row : row + 1, :] = column_sums(here)
            piece = dot_nt(here, wqkv[:, k * width : (k + 1) * width])
            d_normed = piece if d_normed is None else d_normed + piece
        normed1, rstd1 = norm_rows(x_ref[...])
        small_out[0:1, :] = jnp.sum(d_normed * normed1, 0, keepdims=True)
        small_out[2:3, :] = jnp.sum(d_normed, 0, keepdims=True)
        d_x = d_x1 + norm_back(d_normed * vec(0), normed1, rstd1)
        dx_out[...] = d_x[0 : dx_out.shape[0], :]
        if below is not None:
            part(rows_to_seats(below_rows, seats, d_x.astype(BF)), seat_outs)
        high, low = split(small_out[...])
        back_out[padded : padded + 16, 0:width] = high
        back_out[padded : padded + 16, width : 2 * width] = low
        back_out[padded : padded + 16, 2 * width :] = jnp.zeros((16, 2 * width + 2 * LANES), BF)

    shapes = [
        sds((padded if below is not None else tokens, width), F32),
        sds((padded + 16, 4 * width + 2 * LANES), BF),
    ]
    args = [me, *back_blocks, gates, router, grad, x, x1, qkv, cols, vecs, *weights.arrays]
    specs = [SM] + [VM] * (owners + 8) + [ANY] * count
    if below is not None:
        shapes += [sds((cap, width), BF)] * owners
        args += [below]
        specs += [VM]
    result = call(
        kernel,
        "attn_back",
        args,
        specs,
        shapes,
        [VM] * len(shapes),
        [
            pltpu.VMEM((width, 3 * width), BF),
            pltpu.VMEM((width, width), BF),
            pltpu.VMEM((16, width), F32),
            pltpu.SemaphoreType.DMA((copies_in(weights),)),
            pltpu.SemaphoreType.DMA((copies_in(weights),)),
        ],
    )
    return result[:2], result[2:]


def attn_grads(me, z, own, other, biases, shards, ordered):
    padded, wide_ao = own[0].shape
    width = HEADS * HEAD_DIM
    half = 2 * width + LANES
    tall = width // 2 if other else width
    shard = width // shards
    places = [(6, 0, 0), (6, 1, 1), (2, 0, 2), (2, 1, 2), (4, 0, 3), (4, 1, 3), (0, 0, 4), (0, 1, 4)]
    count = 2
    if other:
        count = 1 if ordered else 5

    def kernel(me_ref, z_ref, *refs):
        refs = list(refs)
        ao = [refs.pop(0), refs.pop(0)] if other else [refs.pop(0)]
        back = [refs.pop(0), refs.pop(0)] if other else [refs.pop(0)]
        bias_ref = refs.pop(0)
        outs = [refs.pop(0) for _ in range(count)]
        wide, rows, turned, sems = refs
        copies = []

        def send(p):
            first = p * half
            if not other:
                copies.append(
                    pltpu.make_async_copy(wide.at[:, pl.ds(first, half)], outs[p], sems.at[p])
                )
                copies[-1].start()
                return
            if ordered:
                for k in range(shards // 2):
                    source = wide.at[pl.ds(k * shard, shard), pl.ds(first, half)]
                    copy = pltpu.make_async_copy(source, outs[0].at[k, p], sems.at[2 * k + p])
                    copies.append(copy)
                    copy.start()
                return
            for n, (off, where, o) in enumerate(places):
                if where != p:
                    continue
                at = pl.multiple_of(((me_ref[0] ^ off) >> 1) * shard, 16)
                into = outs[o] if o < 2 else outs[o].at[p]
                copies.append(
                    pltpu.make_async_copy(
                        wide.at[pl.ds(at, shard), pl.ds(first, half)], into, sems.at[n]
                    )
                )
                copies[-1].start()

        def product(which, first):
            total = None
            for left, right in zip(ao, back):
                here = left[:, which * tall : (which + 1) * tall]
                piece = dot_tn(here, right[0:padded, first : first + width])
                total = piece if total is None else total + piece
            return total.astype(BF)

        wide[:, 0:width] = product(0, 0)
        wide[:, width : 2 * width] = product(0, width)
        wide[:, 2 * width : half] = jnp.zeros((tall, LANES), BF)
        send(0)
        wide[:, half : half + width] = product(0, 2 * width)
        wide[:, half + width : half + 2 * width] = product(1, 3 * width)
        rows[...] = jnp.zeros_like(rows)
        small = None
        d_router = None
        for left, right in zip(ao, back):
            for k in range(2):
                piece = right[padded : padded + 16, k * width : (k + 1) * width].astype(F32)
                small = piece if small is None else small + piece
                first = 4 * width + k * LANES
                piece = dot_tn(
                    left[:, 2 * tall : 3 * tall], right[0:padded, first : first + LANES]
                )
                d_router = piece if d_router is None else d_router + piece
        rows[16:32, :] = small
        rows[pl.ds(pl.multiple_of(32 + 8 * z_ref[0], 8), 8), :] = bias_ref[...]
        turned[...] = rows[...].T
        if other:
            core = me_ref[0] & 1
            for k in range(shards // 2):
                at = pl.multiple_of((2 * k + core) * shard, 8)
                here = slice(k * shard, (k + 1) * shard)
                piece = d_router[here, :] + turned[pl.ds(at, shard), :]
                wide[here, half + 2 * width : 2 * half] = piece.astype(BF)
        else:
            wide[:, half + 2 * width : 2 * half] = (d_router + turned[...]).astype(BF)
        send(1)
        wait(copies)

    if other:
        if ordered:
            shapes = [sds((shards // 2, 2, shard, half), BF)]
        else:
            shapes = [sds((shard, half), BF)] * 2 + [sds((2, shard, half), BF)] * 3
        args = [own[0], other[0], own[1], other[1]]
    else:
        shapes = [sds((width, half), BF)] * 2
        args = list(own)
    return call(
        kernel,
        "attn_grads",
        [me, z, *args, biases],
        [SM, SM] + [VM] * (len(args) + 1),
        shapes,
        [ANY] * len(shapes),
        [
            pltpu.VMEM((tall, 2 * half), BF),
            pltpu.VMEM((LANES, width), F32),
            pltpu.VMEM((width, LANES), F32),
            pltpu.SemaphoreType.DMA((max(len(places), shards),)),
        ],
    )


def small_out(smalls, z, experts, per):
    layers = len(smalls)
    shard = smalls[0].shape[0]

    def kernel(z_ref, *refs):
        ins = refs[:layers]
        gains, biases, router, bias_in, bias_oe, square = refs[layers:]
        for layer in range(layers):
            square[...] = jnp.zeros_like(square)
            square[0:shard, :] = ins[layer][...]
            square[...] = square[...].T
            router[layer] = square[0:experts, 0:shard]
            gains[layer] = square[16:18, 0:shard]
            for k in range(5):
                biases[k, layer : layer + 1, :] = square[18 + k : 19 + k, 0:shard]
            own = square[pl.ds(pl.multiple_of(32 + 8 * z_ref[0], 8), 8), :]
            for q in range(per):
                bias_in[layer, :, q * shard : (q + 1) * shard] = own[q : q + 1, 0:shard]
            bias_oe[layer] = own[per : per + 1, 0:shard]

    shapes = [
        sds((layers, 2, shard), F32),
        sds((5, layers, shard), F32),
        sds((layers, experts, shard), F32),
        sds((layers, 1, per * shard), F32),
        sds((layers, 1, shard), F32),
    ]
    return call(
        kernel,
        "small_out",
        [z, *smalls],
        [SM] + [VM] * layers,
        shapes,
        [VM] * 5,
        [pltpu.VMEM((LANES, LANES), F32)],
    )


def swap(value, axis, bit):
    size = lax.axis_size(axis)
    return lax.ppermute(value, axis, [(i, i ^ bit) for i in range(size)])


def exchange(blocks):
    order = sorted(range(1, len(blocks)), key=lambda k: -(k & 2))
    got = {k: swap(blocks[k], "expert", k) for k in order}
    return [blocks[0]] + [got[k] for k in range(1, len(blocks))]


def axis_bits(axis, bit):
    bits = []
    while bit < lax.axis_size(axis):
        bits.append(bit)
        bit *= 2
    return bits


def sum_experts(value):
    for bit in axis_bits("expert", 1):
        low = value.astype(BF)
        value = low.astype(F32) + swap(low, "expert", bit).astype(F32)
    return value


def gather_rows(shard):
    return lax.all_gather(shard, "dp", axis=0, tiled=True)


def scatter_rows(whole):
    return lax.psum_scatter(whole, "dp", scatter_dimension=0, tiled=True)


def scatter_chips(blocks):
    size = lax.axis_size("dp")
    return lax.psum_scatter(
        blocks,
        "dp",
        scatter_dimension=0,
        axis_index_groups=[list(range(core, size, 2)) for core in range(2)],
    )


class Gather:
    def __init__(self, shard):
        self.shard = shard
        self.x, self.y = swap(shard, "dp", 2), swap(shard, "dp", 4)

    def turn(self):
        _, rows, width = self.shard.shape
        half = (1, rows, width)
        self.cut = move(
            "cut",
            [self.x, self.y],
            [(0, (pl.ds(0, 1),), 0, (ALL,), half), (1, (pl.ds(1, 1),), 1, (ALL,), half)],
            [sds(half, BF)] * 2,
        )

    def send(self, after=()):
        if after:
            self.cut = hold(self.cut, after)
        self.xy = swap(self.cut[0], "dp", 4), swap(self.cut[1], "dp", 2)
        self.other = [swap(value, "dp", 1) for value in (self.shard, self.x, self.y)]

    def cross(self, after=()):
        if after:
            self.xy = hold(self.xy, after)
        self.across = [swap(value, "dp", 1) for value in self.xy]

    def weights(self):
        pieces = [
            (self.shard, 0, (0, 1)),
            (self.x, 2, (0, 1)),
            (self.y, 4, (0, 1)),
            (self.xy[0], 6, (0,)),
            (self.xy[1], 6, (1,)),
            (self.across[0], 7, (0,)),
            (self.across[1], 7, (1,)),
            (self.other[0], 1, (0, 1)),
            (self.other[1], 3, (0, 1)),
            (self.other[2], 5, (0, 1)),
        ]
        return Weights([p[0] for p in pieces], [p[1:] for p in pieces])


def full(rows):
    return (pl.ds(0, rows), ALL)


class AttnSum:
    def __init__(self, grads):
        self.bits = axis_bits("expert", 1)
        self.done = 0
        if len(grads) == 1:
            self.total = scatter_chips(grads[0])
            return
        self.across, (self.x, self.y, self.own) = list(grads[:2]), grads[2:]
        self.rows, self.width = self.across[0].shape

    def cut(self, z):
        self.rows, self.width = self.total.shape[1:]
        shape = (self.rows, self.width)

        def kernel(z_ref, total, keep, give, held, in_sems, out_sems):
            here = z_ref[0] & 1
            loads = [
                pltpu.make_async_copy(total.at[k], held.at[k], in_sems.at[k]) for k in range(2)
            ]
            start(loads)
            wait(loads)
            stores = [
                pltpu.make_async_copy(held.at[here], keep, out_sems.at[0]),
                pltpu.make_async_copy(held.at[1 - here], give, out_sems.at[1]),
            ]
            start(stores)
            wait(stores)

        self.keep, give = call(
            kernel,
            "parts",
            [z, self.total],
            [SM, ANY],
            [sds(shape, BF)] * 2,
            [ANY] * 2,
            [
                pltpu.VMEM((2, *shape), BF),
                pltpu.SemaphoreType.DMA((2,)),
                pltpu.SemaphoreType.DMA((2,)),
            ],
        )
        self.come = swap(give, "expert", 1)

    def halves(self):
        shape = (self.rows, self.width)
        flat = full(self.rows)
        (self.keep,) = fold(
            "fold3",
            [self.keep, self.come],
            shape,
            [([(0, flat), (1, flat)], BF, [(0, flat, flat)])],
            [sds(shape, BF)],
        )
        if self.done == 0:
            self.come = swap(self.keep, "expert", 2)
        else:
            self.come = swap(self.keep, "expert", 1)
        self.done += 1

    def put(self, z, layer, layers, given):
        shape = (self.rows, self.width)
        wide = (self.width - LANES) // 2
        count = len(given)

        def kernel(z_ref, keep, come, *refs):
            refs = refs[count:]
            qkv, out, small, low, high, in_sems, out_sems = refs
            here = z_ref[0] & 1
            loads = [
                pltpu.make_async_copy(keep, low.at[here], in_sems.at[0]),
                pltpu.make_async_copy(come, low.at[1 - here], in_sems.at[1]),
            ]
            start(loads)
            wait(loads)
            high[...] = low[...].astype(F32)
            stores = [
                (high.at[0, :, pl.ds(0, 2 * wide)], qkv.at[layer, :, pl.ds(0, 2 * wide)]),
                (high.at[1, :, pl.ds(0, wide)], qkv.at[layer, :, pl.ds(2 * wide, wide)]),
                (high.at[1, :, pl.ds(wide, wide)], out.at[layer]),
                (high.at[1, :, pl.ds(2 * wide, LANES)], small),
            ]
            stores = [
                pltpu.make_async_copy(a, b, out_sems.at[n]) for n, (a, b) in enumerate(stores)
            ]
            start(stores)
            wait(stores)

        return call(
            kernel,
            "attn_out",
            [z, self.keep, self.come, *given],
            [SM] + [ANY] * (2 + count),
            [
                sds((layers, self.rows, 3 * wide), F32),
                sds((layers, self.rows, wide), F32),
                sds((self.rows, LANES), F32),
            ],
            [ANY] * 3,
            [
                pltpu.VMEM((2, *shape), BF),
                pltpu.VMEM((2, *shape), F32),
                pltpu.SemaphoreType.DMA((2,)),
                pltpu.SemaphoreType.DMA((4,)),
            ],
            {3: 0, 4: 1} if given else None,
        )

    def send_across(self, after=()):
        if after:
            self.across = hold(self.across, after)
        self.across = swap(self.across[0], "dp", 4), swap(self.across[1], "dp", 2)

    def fold1(self):
        self.x, self.y = fold1(self.x, self.y, self.across)

    def send_on(self, after=()):
        if after:
            self.x, self.y = hold([self.x, self.y], after)
        self.came = swap(self.x, "dp", 2), swap(self.y, "dp", 4)

    def fold2(self):
        shape = (self.rows, self.width)
        flat = full(self.rows)
        self.parts = fold(
            "fold2",
            [self.own, *self.came],
            shape,
            [([(i, (p,)) for i in range(3)], BF, [(p, flat, flat)]) for p in range(2)],
            [sds(shape, BF)] * 2,
        )
        self.send()

    def send(self):
        up_bit, down_bit = self.bits[self.done], self.bits[-1 - self.done]
        self.came = swap(self.parts[0], "expert", up_bit), swap(self.parts[1], "expert", down_bit)

    def fold3(self, layer, layers, given):
        shape = (self.rows, self.width)
        flat = full(self.rows)
        self.done += 1
        terms = [[(0, flat), (2, flat)], [(1, flat), (3, flat)]]
        args = [*self.parts, *self.came]
        if self.done < len(self.bits):
            self.parts = fold(
                "fold3",
                args,
                shape,
                [(terms[p], BF, [(p, flat, flat)]) for p in range(2)],
                [sds(shape, BF)] * 2,
                )
            self.send()
            return None
        wide = (self.width - LANES) // 2
        cut = lambda first, size: (ALL, pl.ds(first, size))
        tasks = [
            (terms[0], F32, [(0, (layer, ALL, pl.ds(0, 2 * wide)), cut(0, 2 * wide))]),
            (
                terms[1],
                F32,
                [
                    (0, (layer, ALL, pl.ds(2 * wide, wide)), cut(0, wide)),
                    (1, (layer,), cut(wide, wide)),
                    (2, flat, cut(2 * wide, LANES)),
                ],
            ),
        ]
        outs = [
            sds((layers, self.rows, 3 * wide), F32),
            sds((layers, self.rows, wide), F32),
            sds((self.rows, LANES), F32),
        ]
        aliases = {4: 0, 5: 1} if given else None
        return fold("attn_out", args + list(given), shape, tasks, outs, aliases)


def fold1(x, y, across):
    shape = x.shape[1:]
    flat = full(shape[0])
    return fold(
        "fold1",
        [x, y, *across],
        shape,
        [
            ([(0, (0,)), (2, flat)], BF, [(0, (0,), flat)]),
            ([(1, (1,)), (3, flat)], BF, [(1, (1,), flat)]),
        ],
        [sds(x.shape, BF)] * 2,
        {0: 0, 1: 1},
    )


def expert_out(total, layer, layers, given, width):
    rows, broad = total.shape[1:]
    per = broad // width
    second = [
        (1, (layer, 0, pl.ds(q * rows, rows)), (ALL, pl.ds(q * width, width))) for q in range(per)
    ]
    outs = [sds((layers, 1, rows, broad), F32), sds((layers, 1, per * rows, width), F32)]
    return fold(
        "expert_out",
        [total, *given],
        (rows, broad),
        [
            ([(0, (0,))], F32, [(0, (layer, 0), full(rows))]),
            ([(0, (1,))], F32, second),
        ],
        outs,
        {1: 0, 2: 1} if given else None,
    )


def per_device(
    image_tokens,
    norm_gains,
    biases,
    w_qkv,
    w_out,
    w_router,
    router_noise,
    w_in,
    b_in,
    w_outexp,
    b_expout,
    routes,
    seat_order,
    cotangent,
):
    layers = w_qkv.shape[0]
    tokens, width = image_tokens.shape
    experts = w_router.shape[2]
    shards = lax.axis_size("dp")
    assert tokens == SEQ and experts == lax.axis_size("expert")
    assert width == HEADS * HEAD_DIM
    padded = up(tokens, 16)
    cap = 2 * tokens // experts
    cap_pad = up(cap + 2, 8)
    assert cap_pad <= LANES
    shard = w_qkv.shape[1]
    hidden_shard = w_outexp.shape[2]
    hidden = w_in.shape[3]
    per = hidden_shard // shard
    index = lax.axis_index("dp").astype(jnp.int32)
    me = index.reshape(1)
    z = lax.axis_index("expert").astype(jnp.int32).reshape(1)
    bits = axis_bits("dp", 2)
    four = bits == [2, 4] and shard % 16 == 0 and axis_bits("expert", 1) == [1, 2]

    Order.token = None

    def pack_attn(layer):
        return move(
            "pack_attn",
            [w_qkv, w_out],
            [
                (0, (layer, ALL, pl.ds(0, 2 * width)), 0, (0,), (shard, 2 * width)),
                (
                    0,
                    (layer, ALL, pl.ds(2 * width, width)),
                    0,
                    (1, ALL, pl.ds(0, width)),
                    (shard, width),
                ),
                (1, (layer,), 0, (1, ALL, pl.ds(width, width)), (shard, width)),
            ],
            [sds((2, shard, 2 * width), BF)],
        )[0]

    def pack_expert(layer):
        return move(
            "pack_expert",
            [w_in, w_outexp],
            [(0, (layer, 0), 0, (0,), (shard, hidden))]
            + [
                (
                    1,
                    (layer, 0, pl.ds(q * shard, shard)),
                    0,
                    (1, ALL, pl.ds(q * width, width)),
                    (shard, width),
                )
                for q in range(per)
            ],
            [sds((2, shard, hidden), BF)],
        )[0]

    whole = [(None, (0,)), (None, (1,))]

    def fetch_attn(layer):
        if four:
            return Gather(pack_attn(layer))
        right = jnp.concatenate([w_qkv[layer][:, 2 * width :], w_out[layer]], 1)
        attn = [gather_rows(v)[None] for v in (w_qkv[layer][:, : 2 * width], right)]
        return Weights(attn, whole)

    def fetch_expert(layer):
        if four:
            both = lax.all_gather(pack_expert(layer), "dp", axis=0)
            return Weights([both], [(OWNERS, (0, 1))])
        both = [gather_rows(w_in[layer, 0])[None], gather_rows(w_outexp[layer, 0])[None]]
        return Weights(both, whole)

    def attn_weights(gathered):
        return gathered.weights() if four else gathered

    last = layers - 1
    attn_w = [fetch_attn(0)]
    expert_w = [fetch_expert(layer) for layer in range(layers)]
    cols, rows = place_pairs(
        routes, seat_order.reshape(layers, tokens, 2), padded, cap, cap_pad, z
    )
    small = pack_small(norm_gains, biases, w_router, b_in, b_expout)
    grad, grad_seats = top_seats(z, cotangent, rows[last], cap_pad, experts)
    grad_seats = [lax.all_to_all(grad_seats, "expert", 0, 0, tiled=True)]
    if four:
        attn_w[0].turn()
        attn_w[0].send()
    small = lax.all_gather(small, "dp", axis=0)
    params = unpack_small(small, layers, shard, per, experts, grad_seats)
    if last > 0:
        attn_w.append(fetch_attn(1))

    saved = []
    x_args = (image_tokens,)
    if four:
        attn_w[0].cross()
    for layer in range(layers):
        vecs, router, bias_in, bias_oe = params[layer]
        attn_w[layer] = attn_weights(attn_w[layer])
        kept, sent = attn_fwd(
            me,
            layer,
            x_args,
            attn_w[layer],
            vecs,
            router,
            router_noise,
            cols[layer],
            rows[layer],
            cap_pad,
            cap,
        )
        x, x1, qkv, gates, ao = kept
        sent = exchange(sent)
        other_ao = None
        if four:
            ao, other_ao = pick_columns(me, ao, shards)
            other_ao = swap(other_ao, "dp", 1)
        if layer < last:
            if four:
                attn_w[layer + 1].turn()
                attn_w[layer + 1].send(sent[1:])
            if layer + 1 < last:
                attn_w.append(fetch_attn(layer + 2))
        (rh, slope, gate, out), made = expert_fwd(
            me, z, sent, expert_w[layer], bias_in, bias_oe, cap, layer == last
        )
        if four and layer < last:
            attn_w[layer + 1].cross(made[:1])
        returned = exchange(made) if layer < last else made
        other_rh = swap(rh, "dp", 1) if four else None
        saved.append((x, x1, qkv, gates, ao, other_ao, rh, other_rh, slope, gate, out))
        x_args = (x1, gates, cols[layer], returned)

    attn_sums, expert_sums = [None] * layers, [None] * layers
    for layer in reversed(range(layers)):
        x, x1, qkv, gates, ao, other_ao, rh, other_rh, slope, gate, out = saved[layer]
        vecs, router = params[layer][:2]
        if four and layer < last:
            g_attn = attn_grads(me, z, *attn_operands, g_bias, shards, True)
            attn_sums[layer + 1] = AttnSum(hold(g_attn, grad_seats[1:]))
        gd, d_rows = expert_back(me, z, grad_seats, slope, gate, out, expert_w[layer], cap)
        d_back = exchange(d_rows)
        other = (other_rh, swap(gd, "dp", 1)) if four else None
        g_expert, g_bias = expert_grads(me, (rh, gd), other, shards)
        if four:
            (g_expert,) = hold(g_expert, d_back[1:])
            expert_sums[layer] = scatter_chips(g_expert)
        else:
            expert_sums[layer] = [scatter_rows(v) for v in g_expert]
        below = None
        if layer > 0:
            below = rows[layer - 1]
        (grad, back), grad_seats = attn_back(
            me,
            d_back,
            gates,
            router,
            grad,
            x,
            x1,
            qkv,
            cols[layer],
            vecs,
            attn_w[layer],
            below,
            tokens,
            cap,
        )
        grad_seats = exchange(grad_seats) if layer > 0 else None
        if four:
            attn_operands = (ao, back), (other_ao, swap(back, "dp", 1))
        else:
            g_attn = attn_grads(me, z, (ao, back), None, g_bias, shards, False)
            attn_sums[layer] = [sum_experts(scatter_rows(v)) for v in g_attn]

    if four:
        done_attn, smalls, done_expert = (), [None] * layers, ()
        for layer in reversed(range(1, layers)):
            done_expert = expert_out(expert_sums[layer], layer, layers, done_expert, width)
        made = hold(made, [back])
        g_attn = attn_grads(me, z, *attn_operands, g_bias, shards, False)
        attn_sums[0] = AttnSum(g_attn)
        attn_sums[0].send_across()
        attn_sums[0].fold1()
        attn_sums[0].send_on()
        for layer in reversed(range(1, layers)):
            attn_sums[layer].cut(z)
        for layer in reversed(range(1, layers)):
            attn_sums[layer].halves()
    returned = lax.all_to_all(made[0], "expert", 0, 0, tiled=True)
    mixed = mix(z, x_args[0], x_args[1], x_args[2], returned, tokens)
    if four:
        attn_sums[0].fold2()
        for layer in reversed(range(1, layers)):
            attn_sums[layer].halves()
        attn_sums[0].fold3(0, layers, done_attn)
        for layer in reversed(range(1, layers)):
            out = attn_sums[layer].put(z, layer, layers, done_attn)
            done_attn, smalls[layer] = out[:2], out[2]
        done_expert = expert_out(expert_sums[0], 0, layers, done_expert, width)
        grad_in, grad_oe = done_expert
    else:
        grad_in = jnp.stack([item[0] for item in expert_sums])[:, None].astype(F32)
        grad_oe = jnp.stack([item[1] for item in expert_sums])[:, None].astype(F32)
    if four:
        out = attn_sums[0].fold3(0, layers, done_attn)
        (grad_qkv, grad_out), smalls[0] = out[:2], out[2]
    else:
        left = jnp.stack([item[0] for item in attn_sums])
        right = jnp.stack([item[1] for item in attn_sums])
        grad_qkv = jnp.concatenate([left[:, :, : 2 * width], right[:, :, :width]], 2)
        grad_out = right[:, :, width : 2 * width]
        smalls = [right[layer, :, 2 * width :] for layer in range(layers)]
    gains, shifts, grad_router, grad_bin, grad_boe = small_out(smalls, z, experts, per)
    return (
        mixed,
        grad,
        gains,
        jnp.transpose(shifts, (1, 0, 2)),
        grad_qkv,
        grad_out,
        jnp.transpose(grad_router, (0, 2, 1)),
        grad_in,
        grad_bin,
        grad_oe,
        grad_boe,
    )


def solution(mesh):
    return jax.shard_map(
        per_device,
        mesh=mesh,
        in_specs=(
            P(("dp", "expert"), None),
            P(None, None, "dp"),
            P(None, None, "dp"),
            P(None, "dp", None),
            P(None, "dp", None),
            P(None, "dp", None),
            P(None, ("dp", "expert"), None),
            P(None, "expert", "dp", None),
            P(None, "expert", "dp"),
            P(None, "expert", "dp", None),
            P(None, "expert", "dp"),
            P(None, ("dp", "expert"), None),
            P(None, ("dp", "expert"), None),
            P(("dp", "expert"), None),
        ),
        out_specs=(
            P(("dp", "expert"), None),
            P(("dp", "expert"), None),
            P(None, None, "dp"),
            P(None, None, "dp"),
            P(None, "dp", None),
            P(None, "dp", None),
            P(None, "dp", None),
            P(None, "expert", "dp", None),
            P(None, "expert", "dp"),
            P(None, "expert", "dp", None),
            P(None, "expert", "dp"),
        ),
        check_vma=False,
    )
```

```python
import functools

import jax
import jax.numpy as jnp
from jax import lax
from jax.experimental import pallas as pl
from jax.experimental.pallas import tpu as pltpu
from jax.sharding import PartitionSpec as P

HEADS = 12
HEAD_DIM = 64
SEQ = 197
EPS = 1e-06
BF = jnp.bfloat16
F32 = jnp.float32
LANES = 128
NEG = -1e30
VMEM_LIMIT = 60 * 1024 * 1024
LIMITS = {name: 16 * 1024 * 1024 for name in ("fold1", "fold2", "fold3", "mix")}
LIMITS["attn_grads"] = 24 * 1024 * 1024


def up(value, step):
    return -(-value // step) * step


def dot(left, right):
    return lax.dot_general(left, right, (((1,), (0,)), ((), ())), preferred_element_type=F32)


def dot_nt(left, right):
    return lax.dot_general(left, right, (((1,), (1,)), ((), ())), preferred_element_type=F32)


def dot_tn(left, right):
    return lax.dot_general(left, right, (((0,), (0,)), ((), ())), preferred_element_type=F32)


def norm_rows(x):
    centered = x - jnp.mean(x, -1, keepdims=True)
    rstd = lax.rsqrt(jnp.mean(centered * centered, -1, keepdims=True) + EPS)
    return centered * rstd, rstd


def norm_back(grad_hat, normed, rstd):
    return rstd * (
        grad_hat
        - jnp.mean(grad_hat, -1, keepdims=True)
        - normed * jnp.mean(grad_hat * normed, -1, keepdims=True)
    )


def split(value):
    high = value.astype(BF)
    return high, (value - high.astype(F32)).astype(BF)


def join(refs):
    return jnp.concatenate([ref[...].astype(F32) for ref in refs], 0).astype(BF)


def part(value, refs):
    rows = refs[0].shape[0]
    for number, ref in enumerate(refs):
        ref[...] = value[number * rows : (number + 1) * rows].astype(ref.dtype)


def seat_mask(cols_ref, pair, seats):
    column = cols_ref[:, pair : pair + 1]
    return lax.broadcasted_iota(jnp.int32, (column.shape[0], seats), 1) == column


def token_mask(rows_ref, pair, seats):
    row = rows_ref[pair : pair + 1, :]
    return lax.broadcasted_iota(jnp.int32, (seats, row.shape[1]), 0) == row


def one(mask):
    return jnp.where(mask, 1.0, 0.0).astype(BF)


def pair_gate(gates, cols_ref, pair):
    route = cols_ref[:, 2 + pair : 3 + pair]
    lanes = lax.broadcasted_iota(jnp.int32, gates.shape, 1)
    return jnp.sum(jnp.where(lanes == route, gates, 0.0), -1, keepdims=True)


def combine(x1, gates, cols_ref, returned):
    total = x1
    for pair in range(2):
        piece = dot(one(seat_mask(cols_ref, pair, returned.shape[0])), returned)
        total = total + pair_gate(gates, cols_ref, pair) * piece
    return total


def rows_to_seats(rows_ref, seats, values):
    chosen = jnp.logical_or(token_mask(rows_ref, 0, seats), token_mask(rows_ref, 1, seats))
    return dot(one(chosen), values)


def with_note(block, cap, note):
    base = cap // 8 * 8
    tail = block[base:]
    left = tail[:, 0:LANES]
    row = lax.broadcasted_iota(jnp.int32, left.shape, 0)
    high = note.astype(BF).astype(F32)
    left = jnp.where(row == cap - base, high, left)
    left = jnp.where(row == cap - base + 1, note - high, left)
    return jnp.concatenate([block[:base], jnp.concatenate([left, tail[:, LANES:]], 1)], 0)


def note_of(block, cap):
    return block[cap : cap + 1, 0:LANES] + block[cap + 1 : cap + 2, 0:LANES]


def as_column(note, rows):
    shape = (rows, LANES)
    same = lax.broadcasted_iota(jnp.int32, shape, 0) == lax.broadcasted_iota(jnp.int32, shape, 1)
    return jnp.sum(jnp.where(same, note, 0.0), -1, keepdims=True)


def lane_sums(value):
    rows, width = value.shape
    value = jnp.concatenate([value, jnp.zeros((LANES - rows, width), F32)], 0)
    ones = jnp.ones((8, width), BF)
    high, low = split(value)
    return (dot_nt(ones, high) + dot_nt(ones, low))[0:1, :]


def near_lanes(cols_ref, pair, block, cap_pad):
    column = cols_ref[:, pair : pair + 1] - block * cap_pad
    lanes = lax.broadcasted_iota(jnp.int32, (column.shape[0], LANES), 1)
    return jnp.logical_and(lanes == column, lanes < cap_pad)


def head_masks():
    lanes = lax.broadcasted_iota(jnp.int32, (1, 2 * HEAD_DIM), 1)
    return (lanes < HEAD_DIM, lanes >= HEAD_DIM)


def head_probs(query, keys, mask, tokens):
    query = jnp.where(mask, query, 0).astype(F32) * HEAD_DIM ** (-0.5)
    scores = dot_nt(query.astype(BF), keys)
    lanes = lax.broadcasted_iota(jnp.int32, scores.shape, 1)
    scores = jnp.where(lanes < tokens, scores, NEG)
    raised = jnp.exp(scores - jnp.max(scores, -1, keepdims=True))
    return raised * (1.0 / jnp.sum(raised, -1, keepdims=True))


VM = pl.BlockSpec(memory_space=pltpu.VMEM)
ANY = pl.BlockSpec(memory_space=pl.ANY)
SM = pl.BlockSpec(memory_space=pltpu.SMEM)


def sds(shape, dtype):
    return jax.ShapeDtypeStruct(tuple(shape), dtype)


class Order:
    token = None


LOAD = "load"
STORE = "store"


class Load:
    def __init__(self, source, held, sem):
        self.copy, self.held, self.came = pltpu.make_async_copy(source, held, sem), held, False
        self.shape = held.shape
        self.copy.start()

    def wait(self):
        if not self.came:
            self.copy.wait()
            self.came = True

    def __getitem__(self, index):
        self.wait()
        return self.held[index]


class Store:
    def __init__(self, target, held, sems):
        self.target, self.held, self.sems, self.copies = target, held, sems, []
        self.shape, self.dtype = held.shape, held.dtype

    def __getitem__(self, index):
        return self.held[index]

    def __setitem__(self, index, value):
        self.held[index] = value

    def send(self, *index):
        number = len(self.copies)
        copy = pltpu.make_async_copy(
            self.held.at[index], self.target.at[index], self.sems.at[number]
        )
        copy.start()
        self.copies.append(copy)

    def finish(self):
        if not self.copies:
            self.send(*[slice(None)] * len(self.shape))


PARTS = 8


def call(kernel, name, args, specs, outs, out_specs, scratch, aliases=None):
    after = []
    if Order.token is not None and not any(Order.token is arg for arg in args):
        after = [Order.token]
    given = len(args)
    single = not isinstance(outs, (tuple, list))
    results = [outs] if single else list(outs)
    out_kinds = [out_specs] if single else list(out_specs)
    loads = [i for i, spec in enumerate(specs) if spec is LOAD]
    stores = [i for i, spec in enumerate(out_kinds) if spec is STORE]
    extra = [pltpu.VMEM(args[i].shape, args[i].dtype) for i in loads]
    extra += [pltpu.VMEM(results[i].shape, results[i].dtype) for i in stores]
    extra += [pltpu.SemaphoreType.DMA((max(len(loads), 1),))]
    extra += [pltpu.SemaphoreType.DMA((max(PARTS * len(stores), 1),))]

    def body(*refs):
        ins = list(refs[:given])
        rest = list(refs[given + len(after) :])
        made, own = rest[: len(results)], rest[len(results) : len(rest) - len(extra)]
        held = rest[len(rest) - len(extra) :]
        load_sems, store_sems = held[-2:]
        for n, i in enumerate(loads):
            ins[i] = Load(ins[i], held[n], load_sems.at[n])
        for n, i in enumerate(stores):
            sems = store_sems.at[pl.ds(PARTS * n, PARTS)]
            made[i] = Store(made[i], held[len(loads) + n], sems)
        kernel(*ins, *made, *own)
        for i in loads:
            ins[i].wait()
        for i in stores:
            made[i].finish()
        for i in stores:
            for copy in made[i].copies:
                copy.wait()

    result = pl.pallas_call(
        body,
        name=name,
        in_specs=[ANY if spec is LOAD else spec for spec in specs] + [ANY] * len(after),
        out_specs=ANY if single and out_specs is STORE else (
            out_specs if single else [ANY if spec is STORE else spec for spec in out_kinds]
        ),
        out_shape=outs,
        scratch_shapes=list(scratch) + extra,
        input_output_aliases=aliases or {},
        compiler_params=pltpu.CompilerParams(
            vmem_limit_bytes=LIMITS.get(name, VMEM_LIMIT)
        ),
    )(*args, *after)
    Order.token = result[0] if isinstance(result, (tuple, list)) else result
    return result


def hold(values, after):
    def kernel(*refs):
        pass

    return call(
        kernel,
        "hold",
        [*values, *after],
        [ANY] * (len(values) + len(after)),
        [sds(value.shape, value.dtype) for value in values],
        [ANY] * len(values),
        [],
        {i: i for i in range(len(values))},
    )


def move(name, args, copies, outs, aliases=None):
    total = len(copies)

    def kernel(*refs):
        ins, rest = refs[: len(args)], refs[len(args) :]
        results, held = rest[: len(outs)], rest[len(outs) : len(outs) + total]
        in_sems, out_sems = rest[-2:]
        loads = [
            pltpu.make_async_copy(ins[i].at[where], held[n], in_sems.at[n])
            for n, (i, where, _, _, _) in enumerate(copies)
        ]
        stores = [
            pltpu.make_async_copy(held[n], results[o].at[into], out_sems.at[n])
            for n, (_, _, o, into, _) in enumerate(copies)
        ]
        start(loads)
        for load, store in zip(loads, stores):
            load.wait()
            store.start()
        wait(stores)

    return call(
        kernel,
        name,
        args,
        [ANY] * len(args),
        outs,
        [ANY] * len(outs),
        [pltpu.VMEM(shape, BF) for *_, shape in copies]
        + [pltpu.SemaphoreType.DMA((total,)), pltpu.SemaphoreType.DMA((total,))],
        aliases,
    )


def fold(name, args, block, tasks, outs, aliases=None):
    terms = [(t, term) for t, (listed, _, _) in enumerate(tasks) for term in listed]
    writes = [(t, write) for t, (_, _, listed) in enumerate(tasks) for write in listed]
    wide = [t for t, task in enumerate(tasks) if task[1] == F32]
    slim = [t for t, task in enumerate(tasks) if task[1] != F32]

    def kernel(*refs):
        ins, rest = refs[: len(args)], refs[len(args) :]
        results = rest[: len(outs)]
        loaded, wide_ref, slim_ref, in_sems, out_sems = rest[len(outs) :]
        loads = [
            pltpu.make_async_copy(ins[i].at[where], loaded.at[n], in_sems.at[n])
            for n, (_, (i, where)) in enumerate(terms)
        ]
        for copy in loads:
            copy.start()
        stores = []
        for t, (_, kind, _) in enumerate(tasks):
            total = None
            for n, (task, _) in enumerate(terms):
                if task == t:
                    loads[n].wait()
                    piece = loaded[n].astype(F32)
                    total = piece if total is None else total + piece
            holder = wide_ref.at[wide.index(t)] if kind == F32 else slim_ref.at[slim.index(t)]
            holder[...] = total.astype(kind)
            for n, (task, (o, into, within)) in enumerate(writes):
                if task == t:
                    copy = pltpu.make_async_copy(
                        holder.at[within], results[o].at[into], out_sems.at[n]
                    )
                    copy.start()
                    stores.append(copy)
        for copy in stores:
            copy.wait()

    return call(
        kernel,
        name,
        args,
        [ANY] * len(args),
        outs,
        [ANY] * len(outs),
        [
            pltpu.VMEM((len(terms), *block), BF),
            pltpu.VMEM((max(len(wide), 1), *(block if wide else (16, LANES))), F32),
            pltpu.VMEM((max(len(slim), 1), *(block if slim else (16, LANES))), BF),
            pltpu.SemaphoreType.DMA((len(terms),)),
            pltpu.SemaphoreType.DMA((len(writes),)),
        ],
        aliases=aliases,
    )


ALL = slice(None)


class Weights:
    def __init__(self, arrays, places):
        self.arrays, self.places = list(arrays), places


OWNERS = -1


def attn_targets(width, rows, wqkv, wout):
    return {
        0: [(wqkv, 0, 2 * width, 0, rows, 0)],
        1: [(wqkv, 0, width, 2 * width, rows, 0), (wout, width, width, 0, rows, 0)],
    }


def expert_targets(width, hidden, rows, whole, win, woe):
    if whole:
        return {0: [(win, 0, hidden, 0, rows, 0)], 1: [(woe, 0, width, 0, rows, 0)]}
    per = hidden // width
    return {
        0: [(win, 0, hidden, 0, rows, 0)],
        1: [(woe, q * width, width, 0, per * rows, q * rows) for q in range(per)],
    }


class Chunks:
    def __init__(self, refs, weights, width, hidden, rows, whole, win, woe, sems, more=()):
        per = hidden // width
        self.parts = []
        if whole:
            copies = fetch(refs, weights, None, expert_targets(width, hidden, rows, True, win, woe), 0, sems)
            copies += fetch(
                refs, weights, None, expert_targets(width, hidden, rows, True, win, woe), 1, sems
            )
            self.parts = [copies] + [[] for _ in range(per - 1)]
        else:
            ref = refs[0]
            shards = ref.shape[0]
            for c in range(per):
                here = pl.ds(c * width, width)
                copies = [
                    pltpu.make_async_copy(
                        ref.at[d, 0, :, here], win.at[pl.ds(d * rows, rows), here], sems.at[d]
                    )
                    for d in range(shards)
                ]
                first = c * shards // per
                for n in range(shards):
                    d, q = first + n // per, n % per
                    copies.append(
                        pltpu.make_async_copy(
                            ref.at[d, 1, :, pl.ds(q * width, width)],
                            woe.at[pl.ds((d * per + q) * rows, rows)],
                            sems.at[shards + n],
                        )
                    )
                self.parts.append(copies)
        for copies, extra in zip(self.parts, more):
            copies.append(extra)
        start(self.parts[0])

    def take(self, c):
        wait(self.parts[c])
        if c + 1 < len(self.parts):
            start(self.parts[c + 1])


def copies_in(weights):
    return 4 * sum(
        len(parts) if array.ndim == 3 else array.shape[0]
        for array, (off, parts) in zip(weights.arrays, weights.places)
    )


def fetch(refs, weights, me, targets, part_number, sems):
    copies = []
    for ref, (off, parts) in zip(refs, weights.places):
        rows = ref.shape[-2]
        if off == OWNERS:
            sources = [(d, (d, part_number)) for d in range(ref.shape[0])]
        elif isinstance(off, tuple):
            sources = [(me ^ o, (k, part_number)) for k, o in enumerate(off)]
        elif part_number in parts:
            at = None if off is None else me ^ off
            sources = [(at, (parts.index(part_number),))]
        else:
            sources = []
        for at, where in sources:
            for scratch, first, size, into, times, plus in targets[part_number]:
                place = 0 if at is None else at * times + plus
                if off not in (None, OWNERS):
                    place = pl.multiple_of(place, 16)
                copies.append(
                    pltpu.make_async_copy(
                        ref.at[(*where, ALL, pl.ds(first, size))],
                        scratch.at[pl.ds(place, rows), pl.ds(into, size)],
                        sems.at[len(copies)],
                    )
                )
    return copies


def start(copies):
    for copy in copies:
        copy.start()


def wait(copies):
    for copy in copies:
        copy.wait()


def small_rows(per, experts):
    return up(7 + experts + per + 1, 8)


def pack_small(norm_gains, biases, w_router, b_in, b_expout):
    layers, shard, experts = w_router.shape
    per = b_in.shape[2] // shard
    height = small_rows(per, experts)

    def kernel(gain_ref, bias_ref, router_ref, in_ref, oe_ref, out, square):
        out[...] = jnp.zeros_like(out)
        for layer in range(layers):
            at = layer * height
            out[at : at + 2, 0:shard] = gain_ref[layer]
            out[at + 2 : at + 7, 0:shard] = bias_ref[layer]
            square[...] = jnp.zeros_like(square)
            square[0:shard, 0:experts] = router_ref[layer]
            turned = square[...].T
            out[at + 7 : at + 7 + experts, :] = turned[0:experts, :]
            at = at + 7 + experts
            for q in range(per):
                out[at + q : at + q + 1, 0:shard] = in_ref[layer, :, q * shard : (q + 1) * shard]
            out[at + per : at + per + 1, 0:shard] = oe_ref[layer]

    return call(
        kernel,
        "pack_small",
        [norm_gains, biases, w_router, b_in, b_expout],
        [VM] * 5,
        sds((layers * height, LANES), F32),
        VM,
        [pltpu.VMEM((LANES, LANES), F32)],
    )


def unpack_small(gathered, layers, shard, per, experts, after):
    shards = gathered.shape[0]
    width = shards * shard
    height = small_rows(per, experts)

    def kernel(ref, *refs):
        refs = refs[len(after) :]
        tall = refs[-1]
        for layer in range(layers):
            vec, router, bias_in, bias_oe = refs[4 * layer : 4 * layer + 4]
            at = layer * height
            vec[...] = jnp.zeros_like(vec)
            tall[...] = jnp.zeros_like(tall)
            for d in range(shards):
                here = slice(d * shard, (d + 1) * shard)
                vec[0:7, here] = ref[d, at : at + 7, 0:shard]
                tall[0:experts, here] = ref[d, at + 7 : at + 7 + experts, 0:shard]
                row = at + 7 + experts
                for q in range(per):
                    first = (d * per + q) * shard
                    bias_in[:, first : first + shard] = ref[d, row + q : row + q + 1, 0:shard]
                bias_oe[:, here] = ref[d, row + per : row + per + 1, 0:shard]
            router[...] = tall[...].T.astype(BF)

    shapes = []
    for _ in range(layers):
        shapes += [
            sds((8, width), F32),
            sds((width, LANES), BF),
            sds((1, width * per), F32),
            sds((1, width), F32),
        ]
    outs = call(
        kernel,
        "unpack_small",
        [gathered, *after],
        [VM] + [ANY] * len(after),
        shapes,
        [VM] * len(shapes),
        [pltpu.VMEM((LANES, width), F32)],
    )
    return [outs[4 * layer : 4 * layer + 4] for layer in range(layers)]


def place_pairs(routes, seat_order, padded, cap, cap_pad, z):
    layers, tokens, _ = routes.shape
    tall = up(padded, LANES)

    def kernel(z_ref, route_ref, order_ref, *refs):
        outs, wide = refs[:-1], refs[-1]
        lanes = lax.broadcasted_iota(jnp.int32, (tokens, LANES), 1)
        lanes_tall = lax.broadcasted_iota(jnp.int32, (tall, LANES), 1)
        for layer in range(layers):
            given = jnp.full((tokens, LANES), -1.0, F32)
            for k in range(2):
                given = jnp.where(lanes == k, route_ref[layer, :, k : k + 1].astype(F32), given)
                given = jnp.where(lanes == 2 + k, order_ref[layer, :, k : k + 1].astype(F32), given)
            wide[...] = jnp.full((tall, LANES), -1.0, F32)
            wide[0:tokens, :] = given
            table = wide[...]
            turned = table.T
            seats = []
            for k in range(2):
                expert, order = table[:, k : k + 1], table[:, 2 + k : 3 + k]
                rank = jnp.zeros((tall, 1), F32)
                for j in range(2):
                    ahead = jnp.logical_and(
                        turned[j : j + 1, :] == expert, turned[2 + j : 3 + j, :] < order
                    )
                    rank = rank + jnp.sum(jnp.where(ahead, 1.0, 0.0), -1, keepdims=True)
                expert, rank = expert.astype(jnp.int32), rank.astype(jnp.int32)
                near = jnp.bitwise_xor(expert, z_ref[0])
                good = jnp.logical_and(expert >= 0, rank < cap)
                seats.append(jnp.where(good, near * cap_pad + rank, -1).astype(F32))
            table = jnp.where(lanes_tall == 2, table[:, 0:1], table)
            table = jnp.where(lanes_tall == 3, wide[:, 1:2], table)
            table = jnp.where(lanes_tall == 0, seats[0], table)
            table = jnp.where(lanes_tall == 1, seats[1], table)
            cols, rows = outs[2 * layer], outs[2 * layer + 1]
            cols[...] = table[0:padded, :].astype(jnp.int32)
            rows[...] = table.T[0:8, 0:padded].astype(jnp.int32)

    shapes = []
    for _ in range(layers):
        shapes += [sds((padded, LANES), jnp.int32), sds((8, padded), jnp.int32)]
    outs = call(
        kernel,
        "place_pairs",
        [z, routes, seat_order],
        [SM, VM, VM],
        shapes,
        [VM] * len(shapes),
        [pltpu.VMEM((tall, LANES), F32)],
    )
    return outs[0::2], outs[1::2]


def attn_fwd(me, layer, x_args, weights, vecs, router, noise, cols, rows, cap, used):
    first = len(x_args) == 1
    padded, width = cols.shape[0], vecs.shape[1]
    tokens, experts = noise.shape[1:]
    seats = experts * cap
    owners = 0 if first else len(x_args[3])
    count = len(weights.arrays)
    shard = weights.arrays[0].shape[-2]

    def kernel(*refs):
        refs = list(refs)
        me_ref = refs.pop(0)
        if first:
            tok_ref = refs.pop(0)
        else:
            below_x1, below_gates, below_cols = refs.pop(0), refs.pop(0), refs.pop(0)
            below_blocks = [refs.pop(0) for _ in range(owners)]
        w_refs = [refs.pop(0) for _ in range(count)]
        vec_ref, router_ref, noise_ref, cols_ref, rows_ref = (refs.pop(0) for _ in range(5))
        x_out, x1_out, qkv_out, gates_out, ao_out = (refs.pop(0) for _ in range(5))
        seat_outs = [refs.pop(0) for _ in range(experts)]
        wqkv, wout, sems, more_sems = refs
        targets = attn_targets(width, shard, wqkv, wout)
        left = fetch(w_refs, weights, me_ref[0], targets, 0, sems)
        right = fetch(w_refs, weights, me_ref[0], targets, 1, more_sems)
        start(left + right)
        vec = lambda k: vec_ref[k : k + 1, :]
        if first:
            x_out[...] = jnp.zeros_like(x_out)
            x_out[0:tokens, :] = tok_ref[...].astype(F32)
            x = x_out[...]
        else:
            x = combine(below_x1[...], below_gates[...], below_cols, join(below_blocks))
            x_out[...] = x
        normed, rstd = norm_rows(x)
        a_low = (normed * vec(0) + vec(2)).astype(BF)
        ao_out[:, 0:width] = a_low
        gates_out[...] = jnp.zeros_like(gates_out)
        gates_out[0:tokens, 0:experts] = noise_ref[layer]
        noise_here = gates_out[...]
        wait(left)
        for k in range(3):
            if k == 2:
                wait(right)
            piece = dot(a_low, wqkv[:, k * width : (k + 1) * width])
            if k == 0:
                piece = piece + vec(4)
            if k == 2:
                piece = piece + vec(5)
            qkv_out[:, k * width : (k + 1) * width] = piece.astype(BF)
        masks = head_masks()
        for two in range(HEADS // 2):
            at = two * 2 * HEAD_DIM
            query = qkv_out[:, at : at + 2 * HEAD_DIM]
            keys = qkv_out[:, width + at : width + at + 2 * HEAD_DIM]
            values = qkv_out[:, 2 * width + at : 2 * width + at + 2 * HEAD_DIM]
            mixed = None
            for mask in masks:
                probs = head_probs(query, keys, mask, tokens).astype(BF)
                piece = dot(probs, jnp.where(mask, values, 0).astype(BF))
                mixed = piece if mixed is None else mixed + piece
            ao_out[:, width + at : width + at + 2 * HEAD_DIM] = mixed.astype(BF)
        x1 = x + dot(ao_out[:, width : 2 * width], wout[...]) + vec(6)
        x1_out[...] = x1
        normed2, rstd2 = norm_rows(x1)
        moe = normed2 * vec(1) + vec(3)
        high, low = split(moe)
        logits = dot(high, router_ref[...]) + dot(low, router_ref[...]) + noise_here
        lanes = lax.broadcasted_iota(jnp.int32, logits.shape, 1)
        logits = jnp.where(lanes < experts, logits, NEG)
        raised = jnp.exp(logits - jnp.max(logits, -1, keepdims=True))
        gates = raised / jnp.sum(raised, -1, keepdims=True)
        gates_out[...] = gates
        ao_out[:, 2 * width : 3 * width] = high
        sent = rows_to_seats(rows_ref, seats, high)
        chosen = [pair_gate(gates, cols_ref, pair) for pair in range(2)]
        for block, ref in enumerate(seat_outs):
            note = jnp.zeros((1, LANES), F32)
            for pair in range(2):
                here = near_lanes(cols_ref, pair, block, cap)
                note = note + jnp.sum(jnp.where(here, chosen[pair], 0.0), 0, keepdims=True)
            piece = sent[block * cap : (block + 1) * cap]
            ref[...] = with_note(piece, used, note).astype(BF)

    args = [me]
    specs = [SM]
    if first:
        args += [x_args[0]]
        specs += [VM]
    else:
        args += [x_args[0], x_args[1], x_args[2], *x_args[3]]
        specs += [VM] * (3 + owners)
    args += [*weights.arrays, vecs, router, noise, cols, rows]
    specs += [ANY] * count + [VM] * 5
    outs = [
        sds((padded, width), F32),
        sds((padded, width), F32),
        sds((padded, 3 * width), BF),
        sds((padded, LANES), F32),
        sds((padded, 3 * width), BF),
    ] + [sds((cap, width), BF)] * experts
    result = call(
        kernel,
        "attn_fwd",
        args,
        specs,
        outs,
        [VM] * len(outs),
        [
            pltpu.VMEM((width, 3 * width), BF),
            pltpu.VMEM((width, width), BF),
            pltpu.SemaphoreType.DMA((copies_in(weights),)),
            pltpu.SemaphoreType.DMA((copies_in(weights),)),
        ],
    )
    return result[:5], result[5:]


def expert_fwd(me, seat_blocks, weights, bias_in, bias_oe, used):
    owners = len(seat_blocks)
    cap, width = seat_blocks[0].shape
    seats = owners * cap
    hidden = bias_in.shape[1]
    count = len(weights.arrays)
    shard = weights.arrays[0].shape[-2]
    whole = weights.places[0][0] is None
    step = width

    def kernel(*refs):
        refs = list(refs)
        me_ref = refs.pop(0)
        seat_refs = [refs.pop(0) for _ in range(owners)]
        w_refs = [refs.pop(0) for _ in range(count)]
        bin_ref, boe_ref = refs.pop(0), refs.pop(0)
        rh_out, slope_out, gate_out, made_out = (refs.pop(0) for _ in range(4))
        outs = [refs.pop(0) for _ in range(owners)]
        win, woe, sems = refs
        chunks = Chunks(w_refs, weights, width, hidden, shard, whole, win, woe, sems)
        blocks = [ref[...].astype(F32) for ref in seat_refs]
        rows = jnp.concatenate(blocks, 0).astype(BF)
        rh_out[:, 0:width] = rows
        rh_out.send(ALL, pl.ds(0, width))
        columns = [as_column(note_of(block, used), cap) for block in blocks]
        gate_out[...] = jnp.broadcast_to(jnp.concatenate(columns, 0), gate_out.shape)
        total_out = None
        for at in range(0, hidden, step):
            chunks.take(at // step)
            pre = dot(rows, win[:, at : at + step]) + bin_ref[:, at : at + step]
            square = pre * pre
            bend = jnp.tanh(0.7978845608028654 * (pre + 0.044715 * square * pre))
            h = (0.5 * pre * (1.0 + bend)).astype(BF)
            slope = 0.5 * (1.0 + bend) + 0.5 * pre * (1.0 - bend * bend) * (
                0.7978845608028654 * (1.0 + 0.134145 * square)
            )
            rh_out[:, width + at : width + at + step] = h
            slope_out[:, at : at + step] = slope.astype(BF)
            rh_out.send(ALL, pl.ds(width + at, step))
            slope_out.send(ALL, pl.ds(at, step))
            piece = dot(h, woe[at : at + step, :])
            total_out = piece if total_out is None else total_out + piece
        total_out = total_out + boe_ref[...]
        made_out[...] = total_out.astype(BF)
        part(total_out, outs)

    shapes = [
        sds((seats, width + hidden), BF),
        sds((seats, hidden), BF),
        sds((seats, LANES), F32),
        sds((seats, width), BF),
    ] + [sds((cap, width), BF)] * owners
    result = call(
        kernel,
        "expert_fwd",
        [me, *seat_blocks, *weights.arrays, bias_in, bias_oe],
        [SM] + [LOAD] * owners + [ANY] * count + [LOAD] * 2,
        shapes,
        [STORE] * len(shapes),
        [
            pltpu.VMEM((width, hidden), BF),
            pltpu.VMEM((hidden, width), BF),
            pltpu.SemaphoreType.DMA((2 * copies_in(weights),)),
        ],
    )
    return result[:4], result[4:]


def expert_both(me, z, seat_blocks, grads, weights, bias_in, bias_oe, used, shards):
    size = bias_in.shape[1] // shards
    owners = len(seat_blocks)
    cap, width = seat_blocks[0].shape
    seats = owners * cap
    hidden = bias_in.shape[1]
    count = len(weights.arrays)
    shard = weights.arrays[0].shape[-2]
    whole = weights.places[0][0] is None
    step = width

    def kernel(*refs):
        refs = list(refs)
        me_ref, z_ref = refs.pop(0), refs.pop(0)
        seat_refs = [refs.pop(0) for _ in range(owners)]
        grad_ref = refs.pop(0)
        w_refs = [refs.pop(0) for _ in range(count)]
        bin_ref, boe_ref = refs.pop(0), refs.pop(0)
        rp_out, hd_out, give_out, made_out = (refs.pop(0) for _ in range(4))
        outs = [refs.pop(0) for _ in range(owners)]
        win, woe, slopes, sems = refs
        chunks = Chunks(w_refs, weights, width, hidden, shard, whole, win, woe, sems)
        blocks = [ref[...].astype(F32) for ref in seat_refs]
        rows = jnp.concatenate(blocks, 0).astype(BF)
        rp_out[:, 0:width] = rows
        other = 1 - (me_ref[0] & 1)
        gate = jnp.concatenate([as_column(note_of(block, used), cap) for block in blocks], 0)
        total_out = None
        for at in range(0, hidden, step):
            chunks.take(at // step)
            pre = dot(rows, win[:, at : at + step]) + bin_ref[:, at : at + step]
            square = pre * pre
            bend = jnp.tanh(0.7978845608028654 * (pre + 0.044715 * square * pre))
            h = (0.5 * pre * (1.0 + bend)).astype(BF)
            slope = 0.5 * (1.0 + bend) + 0.5 * pre * (1.0 - bend * bend) * (
                0.7978845608028654 * (1.0 + 0.134145 * square)
            )
            hd_out[:, at : at + step] = h
            slopes[:, at : at + step] = slope.astype(BF)
            piece = dot(h, woe[at : at + step, :])
            total_out = piece if total_out is None else total_out + piece
        made = (total_out + boe_ref[...]).astype(BF).astype(F32)
        for k in range(owners):
            made_out.held[z_ref[0] ^ k] = made[k * cap : (k + 1) * cap].astype(BF)
        given = [grad_ref[z_ref[0] ^ k].astype(F32) for k in range(owners)]
        given = jnp.concatenate(given, 0)
        grad = (given * gate).astype(BF)
        hd_out[:, hidden : hidden + width] = grad
        for k in range(shards // 2):
            first = pl.multiple_of((2 * k + other) * size, LANES)
            give_out[:, k * size : (k + 1) * size] = hd_out.held[:, pl.ds(first, size)]
        give_out[:, hidden // 2 : hidden // 2 + width] = grad
        hd_out.send(ALL, ALL)
        give_out.send(ALL, ALL)
        made_out.send(ALL)
        notes = given * made
        notes = [lane_sums(notes[k * cap : (k + 1) * cap]) for k in range(owners)]
        total_out = None
        for at in range(0, hidden, step):
            d_hidden = dot_nt(grad, woe[at : at + step, :])
            d_pre = (d_hidden * slopes[:, at : at + step].astype(F32)).astype(BF)
            rp_out[:, width + at : width + at + step] = d_pre
            piece = dot_nt(d_pre, win[:, at : at + step])
            total_out = piece if total_out is None else total_out + piece
            if at == hidden // 2 - step:
                rp_out.send(ALL, pl.ds(0, width + hidden // 2))
        rp_out.send(ALL, pl.ds(width + hidden // 2, hidden // 2))
        for k, ref in enumerate(outs):
            ref[...] = with_note(total_out[k * cap : (k + 1) * cap], used, notes[k]).astype(BF)

    shapes = [
        sds((seats, width + hidden), BF),
        sds((seats, hidden + width), BF),
        sds((seats, hidden // 2 + width), BF),
        sds((owners, cap, width), BF),
    ] + [sds((cap, width), BF)] * owners
    result = call(
        kernel,
        "expert_both",
        [me, z, *seat_blocks, grads, *weights.arrays, bias_in, bias_oe],
        [SM, SM] + [LOAD] * (owners + 1) + [ANY] * count + [LOAD] * 2,
        shapes,
        [STORE] * len(shapes),
        [
            pltpu.VMEM((width, hidden), BF),
            pltpu.VMEM((hidden, width), BF),
            pltpu.VMEM((seats, hidden), BF),
            pltpu.SemaphoreType.DMA((2 * copies_in(weights),)),
        ],
    )
    return result[:4], result[4:]


def top_seats(z, cotangent, rows, cap, experts):
    tokens, width = cotangent.shape
    padded = rows.shape[1]

    def kernel(z_ref, cot_ref, rows_ref, grad_out, out):
        grad_out[...] = jnp.zeros_like(grad_out)
        grad_out[0:tokens, :] = cot_ref[...].astype(F32)
        sent = rows_to_seats(rows_ref, cap * experts, grad_out[...].astype(BF))
        for k in range(experts):
            out[z_ref[0] ^ k] = sent[k * cap : (k + 1) * cap].astype(BF)

    return call(
        kernel,
        "top_seats",
        [z, cotangent, rows],
        [SM, VM, VM],
        [sds((padded, width), F32), sds((experts, cap, width), BF)],
        [VM] * 2,
        [],
    )


def mix(z, x1, gates, cols, returned, tokens):
    width = x1.shape[1]

    def kernel(z_ref, x1_ref, gates_ref, cols_ref, ref, out):
        blocks = join([ref.at[z_ref[0] ^ k] for k in range(ref.shape[0])])
        total = combine(x1_ref[...], gates_ref[...], cols_ref, blocks)
        out[...] = total[0:tokens, :]

    return call(
        kernel,
        "mix",
        [z, x1, gates, cols, returned],
        [SM] + [VM] * 4,
        sds((tokens, width), F32),
        VM,
        [],
    )


def expert_back(me, grad_blocks, slope, gate, made, weights, used):
    owners = len(grad_blocks)
    cap, width = grad_blocks[0].shape
    seats, hidden = slope.shape
    count = len(weights.arrays)
    shard = weights.arrays[0].shape[-2]
    whole = weights.places[0][0] is None
    step = width

    def kernel(*refs):
        refs = list(refs)
        me_ref = refs.pop(0)
        seat_refs = [refs.pop(0) for _ in range(owners)]
        slope_ref, gate_ref, made_ref = (refs.pop(0) for _ in range(3))
        w_refs = [refs.pop(0) for _ in range(count)]
        gd_out = refs.pop(0)
        outs = [refs.pop(0) for _ in range(owners)]
        win, woe, slopes, sems, slope_sems = refs
        more = [
            pltpu.make_async_copy(
                slope_ref.at[:, pl.ds(at, step)],
                slopes.at[:, pl.ds(at, step)],
                slope_sems.at[at // step],
            )
            for at in range(0, hidden, step)
        ]
        chunks = Chunks(w_refs, weights, width, hidden, shard, whole, win, woe, sems, more)
        given = jnp.concatenate([ref[...].astype(F32) for ref in seat_refs], 0)
        grad = (given * gate_ref[:, 0:1]).astype(BF)
        notes = given * made_ref[...].astype(F32)
        notes = [lane_sums(notes[k * cap : (k + 1) * cap]) for k in range(owners)]
        gd_out[:, 0:width] = grad
        gd_out.send(ALL, pl.ds(0, width))
        total_out = None
        for at in range(0, hidden, step):
            chunks.take(at // step)
            d_hidden = dot_nt(grad, woe[at : at + step, :])
            d_pre = (d_hidden * slopes[:, at : at + step].astype(F32)).astype(BF)
            gd_out[:, width + at : width + at + step] = d_pre
            gd_out.send(ALL, pl.ds(width + at, step))
            piece = dot_nt(d_pre, win[:, at : at + step])
            total_out = piece if total_out is None else total_out + piece
        for k, ref in enumerate(outs):
            ref[...] = with_note(total_out[k * cap : (k + 1) * cap], used, notes[k]).astype(BF)

    shapes = [sds((seats, width + hidden), BF)]
    shapes += [sds((cap, width), BF)] * owners
    result = call(
        kernel,
        "expert_back",
        [me, *grad_blocks, slope, gate, made, *weights.arrays],
        [SM] + [LOAD] * owners + [ANY] + [LOAD] * 2 + [ANY] * count,
        shapes,
        [STORE] * (1 + owners),
        [
            pltpu.VMEM((width, hidden), BF),
            pltpu.VMEM((hidden, width), BF),
            pltpu.VMEM((seats, hidden), BF),
            pltpu.SemaphoreType.DMA((2 * copies_in(weights),)),
            pltpu.SemaphoreType.DMA((hidden // step,)),
        ],
    )
    return result[0], result[1:]


def column_sums(value):
    return dot(jnp.ones((8, value.shape[0]), BF), value)[0:1, :]


def own_columns(width, shards, core):
    shard = width // shards
    half = width // 2
    row = lax.broadcasted_iota(jnp.int32, (width, half), 0)
    column = lax.broadcasted_iota(jnp.int32, (width, half), 1)
    place = column + core * shard
    for k in range(1, shards // 2):
        place = place + jnp.where(column >= k * shard, shard, 0)
    return one(row == place)


def expert_grads(me, rows_in, h, d_out, d_pre, sizes, paired, shards, given=()):
    width = HEADS * HEAD_DIM
    seats, hidden = sizes
    sides = 2 if paired else 1
    per, shard = hidden // width, width // shards
    part_hidden = hidden // shards
    tall = width // 2 if paired else width
    deep = hidden // 2 if paired else hidden
    total = shards * per if paired else 2
    blocks = shards // 2 if paired else per
    size = part_hidden if paired else width
    arrays = []
    for operand in (*rows_in, *h, *d_out, *d_pre):
        if not any(operand[0] is known for known in arrays):
            arrays.append(operand[0])
    place = lambda operand: [operand[0] is known for known in arrays].index(True)

    def kernel(me_ref, *refs):
        refs = list(refs)
        ins = [refs.pop(0) for _ in arrays]
        bias_given = [refs.pop(0) for _ in given][-1:]
        outs = [refs.pop(0) for _ in range(1 if paired else 2)]
        bias_ref, win, woe, h_held, row_held, out_held, pre_held, sems, load_sems = refs
        core = me_ref[0] & 1
        copies = []
        loads = {}

        def send(source, target):
            copy = pltpu.make_async_copy(source, target, sems.at[len(copies)])
            copy.start()
            copies.append(copy)

        def fetch_in(key, source, target):
            copy = pltpu.make_async_copy(source, target, load_sems.at[len(loads)])
            copy.start()
            loads[key] = copy

        def summed(pieces):
            total = pieces[0]
            for piece in pieces[1:]:
                total = total + piece
            return total

        for i, operand in enumerate(d_out):
            source = ins[place(operand)].at[:, pl.ds(operand[1], width)]
            fetch_in(("d", i), source, out_held.at[i])
        for k in range(blocks):
            for i, operand in enumerate(h):
                first = operand[1] + k * size
                if paired and operand[2]:
                    first = pl.multiple_of(operand[1] + (2 * k + core) * size, LANES)
                source = ins[place(operand)].at[:, pl.ds(first, size)]
                fetch_in(("h", k, i), source, h_held.at[i, :, pl.ds(k * size, size)])
        for i, operand in enumerate(rows_in):
            source = ins[place(operand)].at[:, pl.ds(operand[1], width)]
            fetch_in(("r", i), source, row_held.at[i])
        for k in range(per):
            for i, operand in enumerate(d_pre):
                source = ins[place(operand)].at[:, pl.ds(operand[1] + k * width, width)]
                fetch_in(("p", k, i), source, pre_held.at[i, :, pl.ds(k * width, width)])
        if bias_given:
            bias_ref[...] = bias_given[0][...]
        else:
            bias_ref[...] = jnp.zeros_like(bias_ref)
        if h:
            for i in range(sides):
                loads["d", i].wait()
            for k in range(blocks):
                here = slice(k * size, (k + 1) * size)
                for i in range(sides):
                    loads["h", k, i].wait()
                total = summed([dot_tn(h_held[i, :, here], out_held[i]) for i in range(sides)])
                woe[here, :] = total.astype(BF)
                if paired:
                    for q in range(per):
                        send(
                            woe.at[pl.ds(k * size + q * shard, shard)],
                            outs[0].at[k, 1, :, pl.ds(q * width, width)],
                        )
            bias_ref[per : per + 1, :] = summed([column_sums(out_held[i]) for i in range(sides)])
        if rows_in:
            for i in range(sides):
                loads["r", i].wait()
            lefts = [row_held[i] for i in range(sides)]
            if paired:
                pick = own_columns(width, shards, core)
                lefts = [dot(value, pick).astype(BF) for value in lefts]
            for k in range(per):
                here = slice(k * width, (k + 1) * width)
                for i in range(sides):
                    loads["p", k, i].wait()
                total = summed([dot_tn(lefts[i], pre_held[i, :, here]) for i in range(sides)])
                win[:, here] = total.astype(BF)
                if paired:
                    for n in range(shards // 2):
                        into = pl.ds(k * width, width)
                        send(win.at[pl.ds(n * shard, shard), into], outs[0].at[n, 0, :, into])
            sums = summed([column_sums(pre_held[i]) for i in range(sides)])
            for d in range(shards):
                for q in range(per):
                    first = (d * per + q) * shard
                    bias_ref[q : q + 1, d * shard : (d + 1) * shard] = sums[:, first : first + shard]
        if not paired:
            send(win, outs[0])
            send(woe, outs[1])
        wait(copies)

    if paired:
        shapes = [sds((shards // 2, 2, shard, hidden), BF)]
    else:
        shapes = [sds((width, hidden), BF), sds((hidden, width), BF)]
    result = call(
        kernel,
        "expert_grads",
        [me, *arrays, *given],
        [SM] + [ANY] * (len(arrays) + max(len(given) - 1, 0)) + [VM] * min(len(given), 1),
        shapes + [sds((8, width), F32)],
        [ANY] * len(shapes) + [VM],
        [
            pltpu.VMEM((tall, hidden), BF),
            pltpu.VMEM((deep, width), BF),
            pltpu.VMEM((sides, seats, blocks * size), BF),
            pltpu.VMEM((sides, seats, width), BF),
            pltpu.VMEM((sides, seats, width), BF),
            pltpu.VMEM((sides, seats, hidden), BF),
            pltpu.SemaphoreType.DMA((total,)),
            pltpu.SemaphoreType.DMA((sides * (2 + blocks + per),)),
        ],
        {1 + len(arrays): 0} if given else None,
    )
    return result[:-1], result[-1]


def pick_columns(me, value, shards):
    rows, wide = value.shape
    width = wide // 3

    def kernel(me_ref, ref, own, other):
        core = me_ref[0] & 1
        for out, side in ((own, core), (other, 1 - core)):
            pick = own_columns(width, shards, side)
            for k in range(3):
                piece = dot(ref[:, k * width : (k + 1) * width], pick)
                out[:, k * width // 2 : (k + 1) * width // 2] = piece.astype(BF)

    return call(
        kernel,
        "pick_columns",
        [me, value],
        [SM, VM],
        [sds((rows, wide // 2), BF)] * 2,
        [VM] * 2,
        [],
    )


def attn_back(
    me, back_blocks, gates, router, grad, x, x1, qkv, cols, vecs, weights, below, tokens, used
):
    padded, width = grad.shape
    owners = len(back_blocks)
    cap = back_blocks[0].shape[0]
    seats = owners * cap
    count = len(weights.arrays)
    shard = weights.arrays[0].shape[-2]

    def kernel(*refs):
        refs = list(refs)
        me_ref = refs.pop(0)
        back_refs = [refs.pop(0) for _ in range(owners)]
        gates_ref, router_ref, grad_ref, x_ref, x1_ref, qkv_ref, cols_ref, vec_ref = (
            refs.pop(0) for _ in range(8)
        )
        w_refs = [refs.pop(0) for _ in range(count)]
        if below is not None:
            below_rows = refs.pop(0)
        dx_out, back_out = refs.pop(0), refs.pop(0)
        seat_outs = [refs.pop(0) for _ in range(owners)] if below is not None else None
        wqkv, wout, small_out, sems, more_sems = refs
        targets = attn_targets(width, shard, wqkv, wout)
        right = fetch(w_refs, weights, me_ref[0], targets, 1, sems)
        left = fetch(w_refs, weights, me_ref[0], targets, 0, more_sems)
        start(right + left)
        vec = lambda k: vec_ref[k : k + 1, :]
        blocks = [ref[...].astype(F32) for ref in back_refs]
        gates = gates_ref[...]
        lanes = lax.broadcasted_iota(jnp.int32, gates.shape, 1)
        d_gates = jnp.zeros_like(gates)
        for pair in range(2):
            d_pair = jnp.zeros_like(gates)
            for block in range(owners):
                here = near_lanes(cols_ref, pair, block, cap)
                d_pair = d_pair + jnp.where(here, note_of(blocks[block], used), 0.0)
            d_pair = jnp.sum(d_pair, -1, keepdims=True)
            d_gates = d_gates + jnp.where(lanes == cols_ref[:, 2 + pair : 3 + pair], d_pair, 0.0)
        dz = gates * (d_gates - jnp.sum(d_gates * gates, -1, keepdims=True))
        high, low = split(dz)
        moe_part = dot_nt(high, router_ref[...]) + dot_nt(low, router_ref[...])
        back_out[0:padded, 4 * width : 4 * width + LANES] = high
        back_out[0:padded, 4 * width + LANES : 4 * width + 2 * LANES] = low
        chosen = jnp.logical_or(seat_mask(cols_ref, 0, seats), seat_mask(cols_ref, 1, seats))
        d_moe = dot(one(chosen), jnp.concatenate(blocks, 0).astype(BF)) + moe_part
        normed2, rstd2 = norm_rows(x1_ref[...])
        small_out[...] = jnp.zeros_like(small_out)
        small_out[1:2, :] = jnp.sum(d_moe * normed2, 0, keepdims=True)
        small_out[3:4, :] = jnp.sum(d_moe, 0, keepdims=True)
        d_x1 = grad_ref[...] + norm_back(d_moe * vec(1), normed2, rstd2)
        dy = d_x1.astype(BF)
        back_out[0:padded, 3 * width : 4 * width] = dy
        small_out[6:7, :] = column_sums(dy)
        wait(right)
        d_mixed = dot_nt(dy, wout[...]).astype(BF)
        masks = head_masks()
        scale = HEAD_DIM ** (-0.5)
        for two in range(HEADS // 2):
            at = two * 2 * HEAD_DIM
            query = qkv_ref[:, at : at + 2 * HEAD_DIM]
            keys = qkv_ref[:, width + at : width + at + 2 * HEAD_DIM]
            values = qkv_ref[:, 2 * width + at : 2 * width + at + 2 * HEAD_DIM]
            d_o = d_mixed[:, at : at + 2 * HEAD_DIM]
            sums = None
            for mask in masks:
                probs = head_probs(query, keys, mask, tokens)
                d_here = jnp.where(mask, d_o, 0).astype(BF)
                d_probs = dot_nt(d_here, values)
                d_values = dot_tn(probs.astype(BF), d_here)
                d_scores = probs * (d_probs - jnp.sum(d_probs * probs, -1, keepdims=True))
                d_scores = d_scores.astype(BF)
                d_query = dot(d_scores, jnp.where(mask, keys, 0).astype(BF))
                d_keys = dot_tn(d_scores, jnp.where(mask, query, 0).astype(BF))
                here = (d_query, d_keys, d_values)
                sums = here if sums is None else tuple(s + h for s, h in zip(sums, here))
            for k, value in enumerate((sums[0] * scale, sums[1] * scale, sums[2])):
                first = k * width + at
                back_out[0:padded, first : first + 2 * HEAD_DIM] = value.astype(BF)
        wait(left)
        d_normed = None
        for k in range(3):
            here = back_out[0:padded, k * width : (k + 1) * width]
            if k != 1:
                row = 4 if k == 0 else 5
                small_out[row : row + 1, :] = column_sums(here)
            piece = dot_nt(here, wqkv[:, k * width : (k + 1) * width])
            d_normed = piece if d_normed is None else d_normed + piece
        normed1, rstd1 = norm_rows(x_ref[...])
        small_out[0:1, :] = jnp.sum(d_normed * normed1, 0, keepdims=True)
        small_out[2:3, :] = jnp.sum(d_normed, 0, keepdims=True)
        d_x = d_x1 + norm_back(d_normed * vec(0), normed1, rstd1)
        dx_out[...] = d_x[0 : dx_out.shape[0], :]
        if below is not None:
            part(rows_to_seats(below_rows, seats, d_x.astype(BF)), seat_outs)
        high, low = split(small_out[...])
        back_out[padded : padded + 16, 0:width] = high
        back_out[padded : padded + 16, width : 2 * width] = low
        back_out[padded : padded + 16, 2 * width :] = jnp.zeros((16, 2 * width + 2 * LANES), BF)

    shapes = [
        sds((padded if below is not None else tokens, width), F32),
        sds((padded + 16, 4 * width + 2 * LANES), BF),
    ]
    args = [me, *back_blocks, gates, router, grad, x, x1, qkv, cols, vecs, *weights.arrays]
    specs = [SM] + [VM] * (owners + 8) + [ANY] * count
    if below is not None:
        shapes += [sds((cap, width), BF)] * owners
        args += [below]
        specs += [VM]
    result = call(
        kernel,
        "attn_back",
        args,
        specs,
        shapes,
        [VM] * len(shapes),
        [
            pltpu.VMEM((width, 3 * width), BF),
            pltpu.VMEM((width, width), BF),
            pltpu.VMEM((16, width), F32),
            pltpu.SemaphoreType.DMA((copies_in(weights),)),
            pltpu.SemaphoreType.DMA((copies_in(weights),)),
        ],
    )
    return result[:2], result[2:]


def attn_grads(me, z, own, other, biases, shards, ordered):
    padded, wide_ao = own[0].shape
    width = HEADS * HEAD_DIM
    half = 2 * width + LANES
    tall = width // 2 if other else width
    shard = width // shards
    places = [(6, 0, 0), (6, 1, 1), (2, 0, 2), (2, 1, 2), (4, 0, 3), (4, 1, 3), (0, 0, 4), (0, 1, 4)]
    count = 2
    if other:
        count = 1 if ordered else 5

    def kernel(me_ref, z_ref, *refs):
        refs = list(refs)
        ao = [refs.pop(0), refs.pop(0)] if other else [refs.pop(0)]
        back = [refs.pop(0), refs.pop(0)] if other else [refs.pop(0)]
        bias_ref = refs.pop(0)
        outs = [refs.pop(0) for _ in range(count)]
        wide, rows, turned, sems = refs
        copies = []

        def send(p):
            first = p * half
            if not other:
                copies.append(
                    pltpu.make_async_copy(wide.at[:, pl.ds(first, half)], outs[p], sems.at[p])
                )
                copies[-1].start()
                return
            if ordered:
                for k in range(shards // 2):
                    source = wide.at[pl.ds(k * shard, shard), pl.ds(first, half)]
                    copy = pltpu.make_async_copy(source, outs[0].at[k, p], sems.at[2 * k + p])
                    copies.append(copy)
                    copy.start()
                return
            for n, (off, where, o) in enumerate(places):
                if where != p:
                    continue
                at = pl.multiple_of(((me_ref[0] ^ off) >> 1) * shard, 16)
                into = outs[o] if o < 2 else outs[o].at[p]
                copies.append(
                    pltpu.make_async_copy(
                        wide.at[pl.ds(at, shard), pl.ds(first, half)], into, sems.at[n]
                    )
                )
                copies[-1].start()

        def product(which, first):
            total = None
            for left, right in zip(ao, back):
                here = left[:, which * tall : (which + 1) * tall]
                piece = dot_tn(here, right[0:padded, first : first + width])
                total = piece if total is None else total + piece
            return total.astype(BF)

        wide[:, 0:width] = product(0, 0)
        wide[:, width : 2 * width] = product(0, width)
        wide[:, 2 * width : half] = jnp.zeros((tall, LANES), BF)
        send(0)
        wide[:, half : half + width] = product(0, 2 * width)
        wide[:, half + width : half + 2 * width] = product(1, 3 * width)
        rows[...] = jnp.zeros_like(rows)
        small = None
        d_router = None
        for left, right in zip(ao, back):
            for k in range(2):
                piece = right[padded : padded + 16, k * width : (k + 1) * width].astype(F32)
                small = piece if small is None else small + piece
                first = 4 * width + k * LANES
                piece = dot_tn(
                    left[:, 2 * tall : 3 * tall], right[0:padded, first : first + LANES]
                )
                d_router = piece if d_router is None else d_router + piece
        rows[16:32, :] = small
        rows[pl.ds(pl.multiple_of(32 + 8 * z_ref[0], 8), 8), :] = bias_ref[...]
        turned[...] = rows[...].T
        if other:
            core = me_ref[0] & 1
            for k in range(shards // 2):
                at = pl.multiple_of((2 * k + core) * shard, 8)
                here = slice(k * shard, (k + 1) * shard)
                piece = d_router[here, :] + turned[pl.ds(at, shard), :]
                wide[here, half + 2 * width : 2 * half] = piece.astype(BF)
        else:
            wide[:, half + 2 * width : 2 * half] = (d_router + turned[...]).astype(BF)
        send(1)
        wait(copies)

    if other:
        if ordered:
            shapes = [sds((shards // 2, 2, shard, half), BF)]
        else:
            shapes = [sds((shard, half), BF)] * 2 + [sds((2, shard, half), BF)] * 3
        args = [own[0], other[0], own[1], other[1]]
    else:
        shapes = [sds((width, half), BF)] * 2
        args = list(own)
    return call(
        kernel,
        "attn_grads",
        [me, z, *args, biases],
        [SM, SM] + [VM] * (len(args) + 1),
        shapes,
        [ANY] * len(shapes),
        [
            pltpu.VMEM((tall, 2 * half), BF),
            pltpu.VMEM((LANES, width), F32),
            pltpu.VMEM((width, LANES), F32),
            pltpu.SemaphoreType.DMA((max(len(places), shards),)),
        ],
    )


def small_out(smalls, z, experts, per):
    layers = len(smalls)
    shard = smalls[0].shape[0]

    def kernel(z_ref, *refs):
        ins = refs[:layers]
        gains, biases, router, bias_in, bias_oe, square = refs[layers:]
        for layer in range(layers):
            square[...] = jnp.zeros_like(square)
            square[0:shard, :] = ins[layer][...]
            square[...] = square[...].T
            router[layer] = square[0:experts, 0:shard]
            gains[layer] = square[16:18, 0:shard]
            for k in range(5):
                biases[k, layer : layer + 1, :] = square[18 + k : 19 + k, 0:shard]
            own = square[pl.ds(pl.multiple_of(32 + 8 * z_ref[0], 8), 8), :]
            for q in range(per):
                bias_in[layer, :, q * shard : (q + 1) * shard] = own[q : q + 1, 0:shard]
            bias_oe[layer] = own[per : per + 1, 0:shard]

    shapes = [
        sds((layers, 2, shard), F32),
        sds((5, layers, shard), F32),
        sds((layers, experts, shard), F32),
        sds((layers, 1, per * shard), F32),
        sds((layers, 1, shard), F32),
    ]
    return call(
        kernel,
        "small_out",
        [z, *smalls],
        [SM] + [VM] * layers,
        shapes,
        [VM] * 5,
        [pltpu.VMEM((LANES, LANES), F32)],
    )


def swap(value, axis, bit):
    size = lax.axis_size(axis)
    return lax.ppermute(value, axis, [(i, i ^ bit) for i in range(size)])


def exchange(blocks):
    order = sorted(range(1, len(blocks)), key=lambda k: -(k & 2))
    got = {k: swap(blocks[k], "expert", k) for k in order}
    return [blocks[0]] + [got[k] for k in range(1, len(blocks))]


def axis_bits(axis, bit):
    bits = []
    while bit < lax.axis_size(axis):
        bits.append(bit)
        bit *= 2
    return bits


def sum_experts(value):
    for bit in axis_bits("expert", 1):
        low = value.astype(BF)
        value = low.astype(F32) + swap(low, "expert", bit).astype(F32)
    return value


def gather_rows(shard):
    return lax.all_gather(shard, "dp", axis=0, tiled=True)


def scatter_rows(whole):
    return lax.psum_scatter(whole, "dp", scatter_dimension=0, tiled=True)


def scatter_chips(blocks):
    size = lax.axis_size("dp")
    return lax.psum_scatter(
        blocks,
        "dp",
        scatter_dimension=0,
        axis_index_groups=[list(range(core, size, 2)) for core in range(2)],
    )


class Gather:
    def __init__(self, shard):
        self.shard = shard
        self.x, self.y = swap(shard, "dp", 2), swap(shard, "dp", 4)

    def turn(self):
        _, rows, width = self.shard.shape
        half = (1, rows, width)
        *self.cut, self.x, self.y = move(
            "cut",
            [self.x, self.y],
            [(0, (pl.ds(0, 1),), 0, (ALL,), half), (1, (pl.ds(1, 1),), 1, (ALL,), half)],
            [sds(half, BF)] * 2 + [sds(self.x.shape, BF)] * 2,
            {0: 2, 1: 3},
        )

    def send(self, after=()):
        if after:
            self.cut = hold(self.cut, after)
        self.xy = swap(self.cut[0], "dp", 4), swap(self.cut[1], "dp", 2)
        self.other = [swap(value, "dp", 1) for value in (self.shard, self.x, self.y)]

    def cross(self, after=()):
        if after:
            self.xy = hold(self.xy, after)
        self.across = [swap(value, "dp", 1) for value in self.xy]

    def weights(self):
        pieces = [
            (self.shard, 0, (0, 1)),
            (self.x, 2, (0, 1)),
            (self.y, 4, (0, 1)),
            (self.xy[0], 6, (0,)),
            (self.xy[1], 6, (1,)),
            (self.across[0], 7, (0,)),
            (self.across[1], 7, (1,)),
            (self.other[0], 1, (0, 1)),
            (self.other[1], 3, (0, 1)),
            (self.other[2], 5, (0, 1)),
        ]
        return Weights([p[0] for p in pieces], [p[1:] for p in pieces])


def full(rows):
    return (pl.ds(0, rows), ALL)


class AttnSum:
    def __init__(self, grads):
        self.bits = axis_bits("expert", 1)
        self.done = 0
        if len(grads) == 1:
            self.total = scatter_chips(grads[0])
            return
        self.across, (self.x, self.y, self.own) = list(grads[:2]), grads[2:]
        self.rows, self.width = self.across[0].shape

    def cut(self, z):
        self.rows, self.width = self.total.shape[1:]
        shape = (self.rows, self.width)

        def kernel(z_ref, total, keep, give, held, in_sems, out_sems):
            here = z_ref[0] & 1
            loads = [
                pltpu.make_async_copy(total.at[k], held.at[k], in_sems.at[k]) for k in range(2)
            ]
            start(loads)
            wait(loads)
            stores = [
                pltpu.make_async_copy(held.at[here], keep, out_sems.at[0]),
                pltpu.make_async_copy(held.at[1 - here], give, out_sems.at[1]),
            ]
            start(stores)
            wait(stores)

        self.keep, give = call(
            kernel,
            "parts",
            [z, self.total],
            [SM, ANY],
            [sds(shape, BF)] * 2,
            [ANY] * 2,
            [
                pltpu.VMEM((2, *shape), BF),
                pltpu.SemaphoreType.DMA((2,)),
                pltpu.SemaphoreType.DMA((2,)),
            ],
        )
        self.come = swap(give, "expert", 1)

    def halves(self):
        shape = (self.rows, self.width)
        flat = full(self.rows)
        (self.keep,) = fold(
            "fold3",
            [self.keep, self.come],
            shape,
            [([(0, flat), (1, flat)], BF, [(0, flat, flat)])],
            [sds(shape, BF)],
        )
        if self.done == 0:
            self.come = swap(self.keep, "expert", 2)
        else:
            self.come = swap(self.keep, "expert", 1)
        self.done += 1

    def put(self, z, layer, layers, given):
        shape = (self.rows, self.width)
        wide = (self.width - LANES) // 2
        count = len(given)

        def kernel(z_ref, keep, come, *refs):
            refs = refs[count:]
            qkv, out, small, low, high, in_sems, out_sems = refs
            here = z_ref[0] & 1
            loads = [
                pltpu.make_async_copy(keep, low.at[here], in_sems.at[0]),
                pltpu.make_async_copy(come, low.at[1 - here], in_sems.at[1]),
            ]
            start(loads)
            wait(loads)
            high[...] = low[...].astype(F32)
            stores = [
                (high.at[0, :, pl.ds(0, 2 * wide)], qkv.at[layer, :, pl.ds(0, 2 * wide)]),
                (high.at[1, :, pl.ds(0, wide)], qkv.at[layer, :, pl.ds(2 * wide, wide)]),
                (high.at[1, :, pl.ds(wide, wide)], out.at[layer]),
                (high.at[1, :, pl.ds(2 * wide, LANES)], small),
            ]
            stores = [
                pltpu.make_async_copy(a, b, out_sems.at[n]) for n, (a, b) in enumerate(stores)
            ]
            start(stores)
            wait(stores)

        return call(
            kernel,
            "attn_out",
            [z, self.keep, self.come, *given],
            [SM] + [ANY] * (2 + count),
            [
                sds((layers, self.rows, 3 * wide), F32),
                sds((layers, self.rows, wide), F32),
                sds((self.rows, LANES), F32),
            ],
            [ANY] * 3,
            [
                pltpu.VMEM((2, *shape), BF),
                pltpu.VMEM((2, *shape), F32),
                pltpu.SemaphoreType.DMA((2,)),
                pltpu.SemaphoreType.DMA((4,)),
            ],
            {3: 0, 4: 1} if given else None,
        )

    def send_across(self, after=()):
        if after:
            self.across = hold(self.across, after)
        self.across = swap(self.across[0], "dp", 4), swap(self.across[1], "dp", 2)

    def fold1(self):
        self.x, self.y = fold1(self.x, self.y, self.across)

    def send_on(self, after=()):
        if after:
            self.x, self.y = hold([self.x, self.y], after)
        self.came = swap(self.x, "dp", 2), swap(self.y, "dp", 4)

    def fold2(self):
        shape = (self.rows, self.width)
        flat = full(self.rows)
        self.parts = fold(
            "fold2",
            [self.own, *self.came],
            shape,
            [([(i, (p,)) for i in range(3)], BF, [(p, flat, flat)]) for p in range(2)],
            [sds(shape, BF)] * 2,
        )
        self.send()

    def send(self):
        up_bit, down_bit = self.bits[self.done], self.bits[-1 - self.done]
        self.came = swap(self.parts[0], "expert", up_bit), swap(self.parts[1], "expert", down_bit)

    def fold3(self, layer, layers, given):
        shape = (self.rows, self.width)
        flat = full(self.rows)
        self.done += 1
        terms = [[(0, flat), (2, flat)], [(1, flat), (3, flat)]]
        args = [*self.parts, *self.came]
        if self.done < len(self.bits):
            self.parts = fold(
                "fold3",
                args,
                shape,
                [(terms[p], BF, [(p, flat, flat)]) for p in range(2)],
                [sds(shape, BF)] * 2,
                )
            self.send()
            return None
        wide = (self.width - LANES) // 2
        cut = lambda first, size: (ALL, pl.ds(first, size))
        tasks = [
            (terms[0], F32, [(0, (layer, ALL, pl.ds(0, 2 * wide)), cut(0, 2 * wide))]),
            (
                terms[1],
                F32,
                [
                    (0, (layer, ALL, pl.ds(2 * wide, wide)), cut(0, wide)),
                    (1, (layer,), cut(wide, wide)),
                    (2, flat, cut(2 * wide, LANES)),
                ],
            ),
        ]
        outs = [
            sds((layers, self.rows, 3 * wide), F32),
            sds((layers, self.rows, wide), F32),
            sds((self.rows, LANES), F32),
        ]
        aliases = {4: 0, 5: 1} if given else None
        return fold("attn_out", args + list(given), shape, tasks, outs, aliases)


def fold1(x, y, across):
    shape = x.shape[1:]
    flat = full(shape[0])
    return fold(
        "fold1",
        [x, y, *across],
        shape,
        [
            ([(0, (0,)), (2, flat)], BF, [(0, (0,), flat)]),
            ([(1, (1,)), (3, flat)], BF, [(1, (1,), flat)]),
        ],
        [sds(x.shape, BF)] * 2,
        {0: 0, 1: 1},
    )


def expert_out(total, layer, layers, given, width):
    rows, broad = total.shape[1:]
    per = broad // width
    second = [
        (1, (layer, 0, pl.ds(q * rows, rows)), (ALL, pl.ds(q * width, width))) for q in range(per)
    ]
    outs = [sds((layers, 1, rows, broad), F32), sds((layers, 1, per * rows, width), F32)]
    return fold(
        "expert_out",
        [total, *given],
        (rows, broad),
        [
            ([(0, (0,))], F32, [(0, (layer, 0), full(rows))]),
            ([(0, (1,))], F32, second),
        ],
        outs,
        {1: 0, 2: 1} if given else None,
    )


def per_device(
    image_tokens,
    norm_gains,
    biases,
    w_qkv,
    w_out,
    w_router,
    router_noise,
    w_in,
    b_in,
    w_outexp,
    b_expout,
    routes,
    seat_order,
    cotangent,
):
    layers = w_qkv.shape[0]
    tokens, width = image_tokens.shape
    experts = w_router.shape[2]
    shards = lax.axis_size("dp")
    assert tokens == SEQ and experts == lax.axis_size("expert")
    assert width == HEADS * HEAD_DIM
    padded = up(tokens, 16)
    cap = 2 * tokens // experts
    cap_pad = up(cap + 2, 8)
    assert cap_pad <= LANES
    shard = w_qkv.shape[1]
    hidden_shard = w_outexp.shape[2]
    hidden = w_in.shape[3]
    per = hidden_shard // shard
    index = lax.axis_index("dp").astype(jnp.int32)
    me = index.reshape(1)
    z = lax.axis_index("expert").astype(jnp.int32).reshape(1)
    bits = axis_bits("dp", 2)
    four = bits == [2, 4] and shard % 16 == 0 and axis_bits("expert", 1) == [1, 2]

    Order.token = None

    def pack_attn(layer):
        return move(
            "pack_attn",
            [w_qkv, w_out],
            [
                (0, (layer, ALL, pl.ds(0, 2 * width)), 0, (0,), (shard, 2 * width)),
                (
                    0,
                    (layer, ALL, pl.ds(2 * width, width)),
                    0,
                    (1, ALL, pl.ds(0, width)),
                    (shard, width),
                ),
                (1, (layer,), 0, (1, ALL, pl.ds(width, width)), (shard, width)),
            ],
            [sds((2, shard, 2 * width), BF)],
        )[0]

    def pack_expert(layer):
        return move(
            "pack_expert",
            [w_in, w_outexp],
            [(0, (layer, 0), 0, (0,), (shard, hidden))]
            + [
                (
                    1,
                    (layer, 0, pl.ds(q * shard, shard)),
                    0,
                    (1, ALL, pl.ds(q * width, width)),
                    (shard, width),
                )
                for q in range(per)
            ],
            [sds((2, shard, hidden), BF)],
        )[0]

    whole = [(None, (0,)), (None, (1,))]

    def fetch_attn(layer):
        if four:
            return Gather(pack_attn(layer))
        right = jnp.concatenate([w_qkv[layer][:, 2 * width :], w_out[layer]], 1)
        attn = [gather_rows(v)[None] for v in (w_qkv[layer][:, : 2 * width], right)]
        return Weights(attn, whole)

    def fetch_expert(layer):
        if four:
            both = lax.all_gather(pack_expert(layer), "dp", axis=0)
            return Weights([both], [(OWNERS, (0, 1))])
        both = [gather_rows(w_in[layer, 0])[None], gather_rows(w_outexp[layer, 0])[None]]
        return Weights(both, whole)

    def attn_weights(gathered):
        return gathered.weights() if four else gathered

    last = layers - 1
    attn_w = [fetch_attn(0)]
    expert_w = [fetch_expert(layer) for layer in range(layers)]
    cols, rows = place_pairs(
        routes, seat_order.reshape(layers, tokens, 2), padded, cap, cap_pad, z
    )
    small = pack_small(norm_gains, biases, w_router, b_in, b_expout)
    grad, grad_seats = top_seats(z, cotangent, rows[last], cap_pad, experts)
    grad_seats = [lax.all_to_all(grad_seats, "expert", 0, 0, tiled=True)]
    if four:
        attn_w[0].turn()
        attn_w[0].send()
    small = lax.all_gather(small, "dp", axis=0)
    params = unpack_small(small, layers, shard, per, experts, grad_seats)
    if last > 0:
        attn_w.append(fetch_attn(1))

    saved = []
    x_args = (image_tokens,)
    if four:
        attn_w[0].cross()
    for layer in range(layers):
        vecs, router, bias_in, bias_oe = params[layer]
        attn_w[layer] = attn_weights(attn_w[layer])
        kept, sent = attn_fwd(
            me,
            layer,
            x_args,
            attn_w[layer],
            vecs,
            router,
            router_noise,
            cols[layer],
            rows[layer],
            cap_pad,
            cap,
        )
        x, x1, qkv, gates, ao = kept
        sent = exchange(sent)
        other_ao = None
        if four:
            ao, other_ao = pick_columns(me, ao, shards)
            other_ao = swap(other_ao, "dp", 1)
        if layer < last:
            if four:
                attn_w[layer + 1].turn()
                attn_w[layer + 1].send(sent[1:])
            if layer + 1 < last:
                attn_w.append(fetch_attn(layer + 2))
        common = (x, x1, qkv, gates, ao, other_ao)
        if layer < last:
            (rh, slope, gate, out), made = expert_fwd(
                me, sent, expert_w[layer], bias_in, bias_oe, cap
            )
            if four:
                attn_w[layer + 1].cross(made[:1])
            returned = exchange(made)
            other_rh = swap(rh, "dp", 1) if four else None
            saved.append((*common, rh, other_rh, slope, gate, out))
            x_args = (x1, gates, cols[layer], returned)
        else:
            (rp, hd, give, made), d_rows = expert_both(
                me, z, sent, grad_seats[0], expert_w[layer], bias_in, bias_oe, cap, shards
            )
            saved.append(common)

    attn_sums, expert_sums = [None] * layers, [None] * layers
    for layer in reversed(range(layers)):
        x, x1, qkv, gates, ao, other_ao = saved[layer][:6]
        vecs, router = params[layer][:2]
        sizes = (experts * cap_pad, w_in.shape[3])
        if layer == last:
            rows_at, pre_at = [(rp, 0)], [(rp, width)]
            h_at, out_at = [(hd, 0, True)], [(hd, sizes[1])]
            if four:
                other = swap(give, "dp", 1)
                h_at, out_at = h_at + [(other, 0, False)], out_at + [(other, sizes[1] // 2)]
                other = swap(rp, "dp", 1)
                rows_at, pre_at = rows_at + [(other, 0)], pre_at + [(other, width)]
            d_back = exchange(d_rows)
            g_expert, g_bias = expert_grads(
                me, rows_at, h_at, out_at, pre_at, sizes, four, shards
            )
        else:
            rh, other_rh, slope, gate, out = saved[layer][6:]
            if four:
                g_attn = attn_grads(me, z, *attn_operands, g_bias, shards, True)
                attn_sums[layer + 1] = AttnSum(hold(g_attn, grad_seats[1:]))
            gd, d_rows = expert_back(me, grad_seats, slope, gate, out, expert_w[layer], cap)
            d_back = exchange(d_rows)
            lefts, backs = [rh], [gd]
            if four:
                lefts, backs = [rh, other_rh], [gd, swap(gd, "dp", 1)]
            g_expert, g_bias = expert_grads(
                me,
                [(v, 0) for v in lefts],
                [(v, width, True) for v in lefts],
                [(v, 0) for v in backs],
                [(v, width) for v in backs],
                sizes,
                four,
                shards,
            )
        if four:
            (g_expert,) = hold(g_expert, d_back[1:])
            expert_sums[layer] = scatter_chips(g_expert)
        else:
            expert_sums[layer] = [scatter_rows(v) for v in g_expert]
        below = None
        if layer > 0:
            below = rows[layer - 1]
        (grad, back), grad_seats = attn_back(
            me,
            d_back,
            gates,
            router,
            grad,
            x,
            x1,
            qkv,
            cols[layer],
            vecs,
            attn_w[layer],
            below,
            tokens,
            cap,
        )
        grad_seats = exchange(grad_seats) if layer > 0 else None
        if four:
            attn_operands = (ao, back), (other_ao, swap(back, "dp", 1))
        else:
            g_attn = attn_grads(me, z, (ao, back), None, g_bias, shards, False)
            attn_sums[layer] = [sum_experts(scatter_rows(v)) for v in g_attn]

    if four:
        done_attn, smalls, done_expert = (), [None] * layers, ()
        for layer in reversed(range(1, layers)):
            done_expert = expert_out(expert_sums[layer], layer, layers, done_expert, width)
        (made,) = hold([made], [back])
        g_attn = attn_grads(me, z, *attn_operands, g_bias, shards, False)
        attn_sums[0] = AttnSum(g_attn)
        attn_sums[0].send_across()
        attn_sums[0].fold1()
        attn_sums[0].send_on()
        for layer in reversed(range(1, layers)):
            attn_sums[layer].cut(z)
        for layer in reversed(range(1, layers)):
            attn_sums[layer].halves()
    returned = lax.all_to_all(made, "expert", 0, 0, tiled=True)
    mixed = mix(z, saved[last][1], saved[last][3], cols[last], returned, tokens)
    if four:
        attn_sums[0].fold2()
        for layer in reversed(range(1, layers)):
            attn_sums[layer].halves()
        attn_sums[0].fold3(0, layers, done_attn)
        for layer in reversed(range(1, layers)):
            out = attn_sums[layer].put(z, layer, layers, done_attn)
            done_attn, smalls[layer] = out[:2], out[2]
        done_expert = expert_out(expert_sums[0], 0, layers, done_expert, width)
        grad_in, grad_oe = done_expert
    else:
        grad_in = jnp.stack([item[0] for item in expert_sums])[:, None].astype(F32)
        grad_oe = jnp.stack([item[1] for item in expert_sums])[:, None].astype(F32)
    if four:
        out = attn_sums[0].fold3(0, layers, done_attn)
        (grad_qkv, grad_out), smalls[0] = out[:2], out[2]
    else:
        left = jnp.stack([item[0] for item in attn_sums])
        right = jnp.stack([item[1] for item in attn_sums])
        grad_qkv = jnp.concatenate([left[:, :, : 2 * width], right[:, :, :width]], 2)
        grad_out = right[:, :, width : 2 * width]
        smalls = [right[layer, :, 2 * width :] for layer in range(layers)]
    gains, shifts, grad_router, grad_bin, grad_boe = small_out(smalls, z, experts, per)
    return (
        mixed,
        grad,
        gains,
        jnp.transpose(shifts, (1, 0, 2)),
        grad_qkv,
        grad_out,
        jnp.transpose(grad_router, (0, 2, 1)),
        grad_in,
        grad_bin,
        grad_oe,
        grad_boe,
    )


def solution(mesh):
    return jax.shard_map(
        per_device,
        mesh=mesh,
        in_specs=(
            P(("dp", "expert"), None),
            P(None, None, "dp"),
            P(None, None, "dp"),
            P(None, "dp", None),
            P(None, "dp", None),
            P(None, "dp", None),
            P(None, ("dp", "expert"), None),
            P(None, "expert", "dp", None),
            P(None, "expert", "dp"),
            P(None, "expert", "dp", None),
            P(None, "expert", "dp"),
            P(None, ("dp", "expert"), None),
            P(None, ("dp", "expert"), None),
            P(("dp", "expert"), None),
        ),
        out_specs=(
            P(("dp", "expert"), None),
            P(("dp", "expert"), None),
            P(None, None, "dp"),
            P(None, None, "dp"),
            P(None, "dp", None),
            P(None, "dp", None),
            P(None, "dp", None),
            P(None, "expert", "dp", None),
            P(None, "expert", "dp"),
            P(None, "expert", "dp", None),
            P(None, "expert", "dp"),
        ),
        check_vma=False,
    )
```

```python
import functools

import jax
import jax.numpy as jnp
from jax import lax
from jax.experimental import pallas as pl
from jax.experimental.pallas import tpu as pltpu
from jax.sharding import PartitionSpec as P

HEADS = 12
HEAD_DIM = 64
SEQ = 197
EPS = 1e-06
BF = jnp.bfloat16
F32 = jnp.float32
LANES = 128
NEG = -1e30
VMEM_LIMIT = 60 * 1024 * 1024
LIMITS = {name: 16 * 1024 * 1024 for name in ("fold1", "fold2", "fold3", "mix", "attn_last")}
LIMITS["attn_grads"] = 24 * 1024 * 1024
LIMITS["pick_columns"] = 62 * 1024 * 1024


def up(value, step):
    return -(-value // step) * step


def dot(left, right):
    return lax.dot_general(left, right, (((1,), (0,)), ((), ())), preferred_element_type=F32)


def dot_nt(left, right):
    return lax.dot_general(left, right, (((1,), (1,)), ((), ())), preferred_element_type=F32)


def dot_tn(left, right):
    return lax.dot_general(left, right, (((0,), (0,)), ((), ())), preferred_element_type=F32)


def norm_rows(x):
    centered = x - jnp.mean(x, -1, keepdims=True)
    rstd = lax.rsqrt(jnp.mean(centered * centered, -1, keepdims=True) + EPS)
    return centered * rstd, rstd


def norm_back(grad_hat, normed, rstd):
    return rstd * (
        grad_hat
        - jnp.mean(grad_hat, -1, keepdims=True)
        - normed * jnp.mean(grad_hat * normed, -1, keepdims=True)
    )


def split(value):
    high = value.astype(BF)
    return high, (value - high.astype(F32)).astype(BF)


def join(refs):
    return jnp.concatenate([ref[...].astype(F32) for ref in refs], 0).astype(BF)


def part(value, refs):
    rows = refs[0].shape[0]
    for number, ref in enumerate(refs):
        ref[...] = value[number * rows : (number + 1) * rows].astype(ref.dtype)


def seat_mask(cols_ref, pair, seats):
    column = cols_ref[:, pair : pair + 1]
    return lax.broadcasted_iota(jnp.int32, (column.shape[0], seats), 1) == column


def token_mask(rows_ref, pair, seats):
    row = rows_ref[pair : pair + 1, :]
    return lax.broadcasted_iota(jnp.int32, (seats, row.shape[1]), 0) == row


def one(mask):
    return jnp.where(mask, 1.0, 0.0).astype(BF)


def pair_gate(gates, cols_ref, pair):
    route = cols_ref[:, 2 + pair : 3 + pair]
    lanes = lax.broadcasted_iota(jnp.int32, gates.shape, 1)
    return jnp.sum(jnp.where(lanes == route, gates, 0.0), -1, keepdims=True)


def combine(x1, gates, cols_ref, returned):
    total = x1
    for pair in range(2):
        piece = dot(one(seat_mask(cols_ref, pair, returned.shape[0])), returned)
        total = total + pair_gate(gates, cols_ref, pair) * piece
    return total


def rows_to_seats(rows_ref, seats, values):
    chosen = jnp.logical_or(token_mask(rows_ref, 0, seats), token_mask(rows_ref, 1, seats))
    return dot(one(chosen), values)


def with_note(block, cap, note):
    base = cap // 8 * 8
    tail = block[base:]
    left = tail[:, 0:LANES]
    row = lax.broadcasted_iota(jnp.int32, left.shape, 0)
    high = note.astype(BF).astype(F32)
    left = jnp.where(row == cap - base, high, left)
    left = jnp.where(row == cap - base + 1, note - high, left)
    return jnp.concatenate([block[:base], jnp.concatenate([left, tail[:, LANES:]], 1)], 0)


def note_of(block, cap):
    return block[cap : cap + 1, 0:LANES] + block[cap + 1 : cap + 2, 0:LANES]


def as_column(note, rows):
    shape = (rows, LANES)
    same = lax.broadcasted_iota(jnp.int32, shape, 0) == lax.broadcasted_iota(jnp.int32, shape, 1)
    return jnp.sum(jnp.where(same, note, 0.0), -1, keepdims=True)


def lane_sums(value):
    rows, width = value.shape
    value = jnp.concatenate([value, jnp.zeros((LANES - rows, width), F32)], 0)
    ones = jnp.ones((8, width), BF)
    high, low = split(value)
    return (dot_nt(ones, high) + dot_nt(ones, low))[0:1, :]


def near_lanes(cols_ref, pair, block, cap_pad):
    column = cols_ref[:, pair : pair + 1] - block * cap_pad
    lanes = lax.broadcasted_iota(jnp.int32, (column.shape[0], LANES), 1)
    return jnp.logical_and(lanes == column, lanes < cap_pad)


def head_masks():
    lanes = lax.broadcasted_iota(jnp.int32, (1, 2 * HEAD_DIM), 1)
    return (lanes < HEAD_DIM, lanes >= HEAD_DIM)


def stacked(value, masks):
    return jnp.concatenate([jnp.where(mask, value, 0).astype(value.dtype) for mask in masks], 0)


def unstacked(value, masks):
    rows = value.shape[0] // 2
    return jnp.where(masks[0], value[:rows], value[rows:])


def pair_probs(query, keys, masks, tokens):
    query = stacked(query, masks).astype(F32) * HEAD_DIM ** (-0.5)
    scores = dot_nt(query.astype(BF), keys)
    lanes = lax.broadcasted_iota(jnp.int32, scores.shape, 1)
    scores = jnp.where(lanes < tokens, scores, NEG)
    raised = jnp.exp(scores - jnp.max(scores, -1, keepdims=True))
    return raised * (1.0 / jnp.sum(raised, -1, keepdims=True))


VM = pl.BlockSpec(memory_space=pltpu.VMEM)
ANY = pl.BlockSpec(memory_space=pl.ANY)
HBM = pl.BlockSpec(memory_space=pltpu.HBM)
SM = pl.BlockSpec(memory_space=pltpu.SMEM)


def sds(shape, dtype):
    return jax.ShapeDtypeStruct(tuple(shape), dtype)


class Order:
    token = None


LOAD = "load"
STORE = "store"


class Load:
    def __init__(self, source, held, sem):
        self.copy, self.held, self.came = pltpu.make_async_copy(source, held, sem), held, False
        self.shape = held.shape
        self.copy.start()

    def wait(self):
        if not self.came:
            self.copy.wait()
            self.came = True

    def __getitem__(self, index):
        self.wait()
        return self.held[index]


class Store:
    def __init__(self, target, held, sems):
        self.target, self.held, self.sems, self.copies = target, held, sems, []
        self.shape, self.dtype = held.shape, held.dtype

    def __getitem__(self, index):
        return self.held[index]

    def __setitem__(self, index, value):
        self.held[index] = value

    def send(self, *index):
        number = len(self.copies)
        copy = pltpu.make_async_copy(
            self.held.at[index], self.target.at[index], self.sems.at[number]
        )
        copy.start()
        self.copies.append(copy)

    def finish(self):
        if not self.copies:
            self.send(*[slice(None)] * len(self.shape))


PARTS = 8


def call(kernel, name, args, specs, outs, out_specs, scratch, aliases=None):
    after = []
    if Order.token is not None and not any(Order.token is arg for arg in args):
        after = [Order.token]
    given = len(args)
    single = not isinstance(outs, (tuple, list))
    results = [outs] if single else list(outs)
    out_kinds = [out_specs] if single else list(out_specs)
    loads = [i for i, spec in enumerate(specs) if spec is LOAD]
    stores = [i for i, spec in enumerate(out_kinds) if spec is STORE]
    extra = [pltpu.VMEM(args[i].shape, args[i].dtype) for i in loads]
    extra += [pltpu.VMEM(results[i].shape, results[i].dtype) for i in stores]
    extra += [pltpu.SemaphoreType.DMA((max(len(loads), 1),))]
    extra += [pltpu.SemaphoreType.DMA((max(PARTS * len(stores), 1),))]

    def body(*refs):
        ins = list(refs[:given])
        rest = list(refs[given + len(after) :])
        made, own = rest[: len(results)], rest[len(results) : len(rest) - len(extra)]
        held = rest[len(rest) - len(extra) :]
        load_sems, store_sems = held[-2:]
        for n, i in enumerate(loads):
            ins[i] = Load(ins[i], held[n], load_sems.at[n])
        for n, i in enumerate(stores):
            sems = store_sems.at[pl.ds(PARTS * n, PARTS)]
            made[i] = Store(made[i], held[len(loads) + n], sems)
        kernel(*ins, *made, *own)
        for i in loads:
            ins[i].wait()
        for i in stores:
            made[i].finish()
        for i in stores:
            for copy in made[i].copies:
                copy.wait()

    result = pl.pallas_call(
        body,
        name=name,
        in_specs=[HBM if spec is LOAD else spec for spec in specs] + [ANY] * len(after),
        out_specs=ANY if single and out_specs is STORE else (
            out_specs if single else [ANY if spec is STORE else spec for spec in out_kinds]
        ),
        out_shape=outs,
        scratch_shapes=list(scratch) + extra,
        input_output_aliases=aliases or {},
        compiler_params=pltpu.CompilerParams(
            vmem_limit_bytes=LIMITS.get(name, VMEM_LIMIT)
        ),
    )(*args, *after)
    Order.token = result if single else min(result, key=lambda value: value.size)
    return result


def hold(values, after):
    def kernel(*refs):
        pass

    return call(
        kernel,
        "hold",
        [*values, *after],
        [ANY] * (len(values) + len(after)),
        [sds(value.shape, value.dtype) for value in values],
        [ANY] * len(values),
        [],
        {i: i for i in range(len(values))},
    )


def move(name, args, copies, outs, aliases=None):
    total = len(copies)

    def kernel(*refs):
        ins, rest = refs[: len(args)], refs[len(args) :]
        results, held = rest[: len(outs)], rest[len(outs) : len(outs) + total]
        in_sems, out_sems = rest[-2:]
        loads = [
            pltpu.make_async_copy(ins[i].at[where], held[n], in_sems.at[n])
            for n, (i, where, _, _, _) in enumerate(copies)
        ]
        stores = [
            pltpu.make_async_copy(held[n], results[o].at[into], out_sems.at[n])
            for n, (_, _, o, into, _) in enumerate(copies)
        ]
        start(loads)
        for load, store in zip(loads, stores):
            load.wait()
            store.start()
        wait(stores)

    return call(
        kernel,
        name,
        args,
        [ANY] * len(args),
        outs,
        [ANY] * len(outs),
        [pltpu.VMEM(shape, BF) for *_, shape in copies]
        + [pltpu.SemaphoreType.DMA((total,)), pltpu.SemaphoreType.DMA((total,))],
        aliases,
    )


def fold(name, args, block, tasks, outs, aliases=None):
    terms = [(t, term) for t, (listed, _, _) in enumerate(tasks) for term in listed]
    writes = [(t, write) for t, (_, _, listed) in enumerate(tasks) for write in listed]
    wide = [t for t, task in enumerate(tasks) if task[1] == F32]
    slim = [t for t, task in enumerate(tasks) if task[1] != F32]

    last = name.endswith("_out")
    mark = [sds((8, LANES), F32)] if last else []

    def kernel(*refs):
        ins, rest = refs[: len(args)], refs[len(args) :]
        results = rest[: len(outs)]
        loaded, wide_ref, slim_ref, in_sems, out_sems = rest[len(outs) + len(mark) :]
        for ref in rest[len(outs) : len(outs) + len(mark)]:
            ref[...] = jnp.zeros_like(ref)
        loads = [
            pltpu.make_async_copy(ins[i].at[where], loaded.at[n], in_sems.at[n])
            for n, (_, (i, where)) in enumerate(terms)
        ]
        for copy in loads:
            copy.start()
        stores = []
        for t, (_, kind, _) in enumerate(tasks):
            total = None
            for n, (task, _) in enumerate(terms):
                if task == t:
                    loads[n].wait()
                    piece = loaded[n].astype(F32)
                    total = piece if total is None else total + piece
            holder = wide_ref.at[wide.index(t)] if kind == F32 else slim_ref.at[slim.index(t)]
            holder[...] = total.astype(kind)
            for n, (task, (o, into, within)) in enumerate(writes):
                if task == t:
                    copy = pltpu.make_async_copy(
                        holder.at[within], results[o].at[into], out_sems.at[n]
                    )
                    copy.start()
                    stores.append(copy)
        for copy in stores:
            copy.wait()

    result = call(
        kernel,
        name,
        args,
        [ANY] * len(args),
        list(outs) + mark,
        [HBM if last else ANY] * len(outs) + [VM] * len(mark),
        [
            pltpu.VMEM((len(terms), *block), BF),
            pltpu.VMEM((max(len(wide), 1), *(block if wide else (16, LANES))), F32),
            pltpu.VMEM((max(len(slim), 1), *(block if slim else (16, LANES))), BF),
            pltpu.SemaphoreType.DMA((len(terms),)),
            pltpu.SemaphoreType.DMA((len(writes),)),
        ],
        aliases=aliases,
    )
    return result[: len(outs)]


ALL = slice(None)


class Weights:
    def __init__(self, arrays, places):
        self.arrays, self.places = list(arrays), places


OWNERS = -1


def attn_targets(width, rows, wqkv, wout):
    return {
        0: [(wqkv, 0, 2 * width, 0, rows, 0)],
        1: [(wqkv, 0, width, 2 * width, rows, 0), (wout, width, width, 0, rows, 0)],
    }


def expert_targets(width, hidden, rows, whole, win, woe):
    if whole:
        return {0: [(win, 0, hidden, 0, rows, 0)], 1: [(woe, 0, width, 0, rows, 0)]}
    per = hidden // width
    return {
        0: [(win, 0, hidden, 0, rows, 0)],
        1: [(woe, q * width, width, 0, per * rows, q * rows) for q in range(per)],
    }


class Chunks:
    def __init__(self, refs, weights, width, hidden, rows, whole, win, woe, sems, more=()):
        per = hidden // width
        self.parts = []
        if whole:
            copies = fetch(refs, weights, None, expert_targets(width, hidden, rows, True, win, woe), 0, sems)
            copies += fetch(
                refs, weights, None, expert_targets(width, hidden, rows, True, win, woe), 1, sems
            )
            self.parts = [copies] + [[] for _ in range(per - 1)]
        else:
            ref = refs[0]
            shards = ref.shape[0]
            for c in range(per):
                here = pl.ds(c * width, width)
                copies = [
                    pltpu.make_async_copy(
                        ref.at[d, 0, :, here], win.at[pl.ds(d * rows, rows), here], sems.at[d]
                    )
                    for d in range(shards)
                ]
                first = c * shards // per
                for n in range(shards):
                    d, q = first + n // per, n % per
                    copies.append(
                        pltpu.make_async_copy(
                            ref.at[d, 1, :, pl.ds(q * width, width)],
                            woe.at[pl.ds((d * per + q) * rows, rows)],
                            sems.at[shards + n],
                        )
                    )
                self.parts.append(copies)
        for copies, extra in zip(self.parts, more):
            copies.append(extra)
        start(self.parts[0])

    def take(self, c):
        wait(self.parts[c])
        if c + 1 < len(self.parts):
            start(self.parts[c + 1])


def copies_in(weights):
    return 4 * sum(
        len(parts) if array.ndim == 3 else array.shape[0]
        for array, (off, parts) in zip(weights.arrays, weights.places)
    )


def fetch(refs, weights, me, targets, part_number, sems):
    copies = []
    for ref, (off, parts) in zip(refs, weights.places):
        rows = ref.shape[-2]
        if off == OWNERS:
            sources = [(d, (d, part_number)) for d in range(ref.shape[0])]
        elif isinstance(off, tuple):
            sources = [(me ^ o, (k, part_number)) for k, o in enumerate(off)]
        elif part_number in parts:
            at = None if off is None else me ^ off
            sources = [(at, (parts.index(part_number),))]
        else:
            sources = []
        for at, where in sources:
            for scratch, first, size, into, times, plus in targets[part_number]:
                place = 0 if at is None else at * times + plus
                if off not in (None, OWNERS):
                    place = pl.multiple_of(place, 16)
                copies.append(
                    pltpu.make_async_copy(
                        ref.at[(*where, ALL, pl.ds(first, size))],
                        scratch.at[pl.ds(place, rows), pl.ds(into, size)],
                        sems.at[len(copies)],
                    )
                )
    return copies


def start(copies):
    for copy in copies:
        copy.start()


def wait(copies):
    for copy in copies:
        copy.wait()


def small_rows(per, experts):
    return up(7 + experts + per + 1, 8)


def pack_small(norm_gains, biases, w_router, b_in, b_expout):
    layers, shard, experts = w_router.shape
    per = b_in.shape[2] // shard
    height = small_rows(per, experts)

    def kernel(gain_ref, bias_ref, router_ref, in_ref, oe_ref, out, square):
        out[...] = jnp.zeros_like(out)
        for layer in range(layers):
            at = layer * height
            out[at : at + 2, 0:shard] = gain_ref[layer]
            out[at + 2 : at + 7, 0:shard] = bias_ref[layer]
            square[...] = jnp.zeros_like(square)
            square[0:shard, 0:experts] = router_ref[layer]
            turned = square[...].T
            out[at + 7 : at + 7 + experts, :] = turned[0:experts, :]
            at = at + 7 + experts
            for q in range(per):
                out[at + q : at + q + 1, 0:shard] = in_ref[layer, :, q * shard : (q + 1) * shard]
            out[at + per : at + per + 1, 0:shard] = oe_ref[layer]

    return call(
        kernel,
        "pack_small",
        [norm_gains, biases, w_router, b_in, b_expout],
        [VM] * 5,
        sds((layers * height, LANES), F32),
        VM,
        [pltpu.VMEM((LANES, LANES), F32)],
    )


def unpack_small(gathered, layers, shard, per, experts, after):
    shards = gathered.shape[0]
    width = shards * shard
    height = small_rows(per, experts)

    def kernel(ref, *refs):
        refs = refs[len(after) :]
        tall = refs[-1]
        for layer in range(layers):
            vec, router, bias_in, bias_oe = refs[4 * layer : 4 * layer + 4]
            at = layer * height
            vec[...] = jnp.zeros_like(vec)
            tall[...] = jnp.zeros_like(tall)
            for d in range(shards):
                here = slice(d * shard, (d + 1) * shard)
                vec[0:7, here] = ref[d, at : at + 7, 0:shard]
                tall[0:experts, here] = ref[d, at + 7 : at + 7 + experts, 0:shard]
                row = at + 7 + experts
                for q in range(per):
                    first = (d * per + q) * shard
                    bias_in[:, first : first + shard] = ref[d, row + q : row + q + 1, 0:shard]
                bias_oe[:, here] = ref[d, row + per : row + per + 1, 0:shard]
            router[...] = tall[...].T.astype(BF)

    shapes = []
    for _ in range(layers):
        shapes += [
            sds((8, width), F32),
            sds((width, LANES), BF),
            sds((1, width * per), F32),
            sds((1, width), F32),
        ]
    outs = call(
        kernel,
        "unpack_small",
        [gathered, *after],
        [VM] + [ANY] * len(after),
        shapes,
        [VM] * len(shapes),
        [pltpu.VMEM((LANES, width), F32)],
    )
    return [outs[4 * layer : 4 * layer + 4] for layer in range(layers)]


def place_pairs(routes, seat_order, padded, cap, cap_pad, z):
    layers, tokens, _ = routes.shape
    tall = up(padded, LANES)

    def kernel(z_ref, route_ref, order_ref, *refs):
        outs, wide = refs[:-1], refs[-1]
        lanes = lax.broadcasted_iota(jnp.int32, (tokens, LANES), 1)
        lanes_tall = lax.broadcasted_iota(jnp.int32, (tall, LANES), 1)
        for layer in range(layers):
            given = jnp.full((tokens, LANES), -1.0, F32)
            for k in range(2):
                given = jnp.where(lanes == k, route_ref[layer, :, k : k + 1].astype(F32), given)
                given = jnp.where(lanes == 2 + k, order_ref[layer, :, k : k + 1].astype(F32), given)
            wide[...] = jnp.full((tall, LANES), -1.0, F32)
            wide[0:tokens, :] = given
            table = wide[...]
            turned = table.T
            seats = []
            for k in range(2):
                expert, order = table[:, k : k + 1], table[:, 2 + k : 3 + k]
                rank = jnp.zeros((tall, 1), F32)
                for j in range(2):
                    ahead = jnp.logical_and(
                        turned[j : j + 1, :] == expert, turned[2 + j : 3 + j, :] < order
                    )
                    rank = rank + jnp.sum(jnp.where(ahead, 1.0, 0.0), -1, keepdims=True)
                expert, rank = expert.astype(jnp.int32), rank.astype(jnp.int32)
                near = jnp.bitwise_xor(expert, z_ref[0])
                good = jnp.logical_and(expert >= 0, rank < cap)
                seats.append(jnp.where(good, near * cap_pad + rank, -1).astype(F32))
            table = jnp.where(lanes_tall == 2, table[:, 0:1], table)
            table = jnp.where(lanes_tall == 3, wide[:, 1:2], table)
            table = jnp.where(lanes_tall == 0, seats[0], table)
            table = jnp.where(lanes_tall == 1, seats[1], table)
            cols, rows = outs[2 * layer], outs[2 * layer + 1]
            cols[...] = table[0:padded, :].astype(jnp.int32)
            rows[...] = table.T[0:8, 0:padded].astype(jnp.int32)

    shapes = []
    for _ in range(layers):
        shapes += [sds((padded, LANES), jnp.int32), sds((8, padded), jnp.int32)]
    outs = call(
        kernel,
        "place_pairs",
        [z, routes, seat_order],
        [SM, VM, VM],
        shapes,
        [VM] * len(shapes),
        [pltpu.VMEM((tall, LANES), F32)],
    )
    return outs[0::2], outs[1::2]


def attn_fwd(me, layer, x_args, weights, vecs, router, noise, cols, rows, cap, used):
    first = len(x_args) == 1
    padded, width = cols.shape[0], vecs.shape[1]
    tokens, experts = noise.shape[1:]
    seats = experts * cap
    owners = 0 if first else len(x_args[3])
    count = len(weights.arrays)
    shard = weights.arrays[0].shape[-2]

    def kernel(*refs):
        refs = list(refs)
        me_ref = refs.pop(0)
        if first:
            tok_ref = refs.pop(0)
        else:
            below_x1, below_gates, below_cols = refs.pop(0), refs.pop(0), refs.pop(0)
            below_blocks = [refs.pop(0) for _ in range(owners)]
        w_refs = [refs.pop(0) for _ in range(count)]
        vec_ref, router_ref, noise_ref, cols_ref, rows_ref = (refs.pop(0) for _ in range(5))
        x_out, x1_out, qkv_out, gates_out, ao_out = (refs.pop(0) for _ in range(5))
        seat_outs = [refs.pop(0) for _ in range(experts)]
        wqkv, wout, sems, more_sems = refs
        targets = attn_targets(width, shard, wqkv, wout)
        left = fetch(w_refs, weights, me_ref[0], targets, 0, sems)
        right = fetch(w_refs, weights, me_ref[0], targets, 1, more_sems)
        start(left + right)
        vec = lambda k: vec_ref[k : k + 1, :]
        if first:
            x_out[...] = jnp.zeros_like(x_out)
            x_out[0:tokens, :] = tok_ref[...].astype(F32)
            x = x_out[...]
        else:
            x = combine(below_x1[...], below_gates[...], below_cols, join(below_blocks))
            x_out[...] = x
        normed, rstd = norm_rows(x)
        a_low = (normed * vec(0) + vec(2)).astype(BF)
        ao_out[:, 0:width] = a_low
        gates_out[...] = jnp.zeros_like(gates_out)
        gates_out[0:tokens, 0:experts] = noise_ref[layer]
        noise_here = gates_out[...]
        wait(left)
        for k in range(3):
            if k == 2:
                wait(right)
            piece = dot(a_low, wqkv[:, k * width : (k + 1) * width])
            if k == 0:
                piece = piece + vec(4)
            if k == 2:
                piece = piece + vec(5)
            qkv_out[:, k * width : (k + 1) * width] = piece.astype(BF)
        masks = head_masks()
        for two in range(HEADS // 2):
            at = two * 2 * HEAD_DIM
            query = qkv_out[:, at : at + 2 * HEAD_DIM]
            keys = qkv_out[:, width + at : width + at + 2 * HEAD_DIM]
            values = qkv_out[:, 2 * width + at : 2 * width + at + 2 * HEAD_DIM]
            probs = pair_probs(query, keys, masks, tokens).astype(BF)
            mixed = unstacked(dot(probs, values), masks)
            ao_out[:, width + at : width + at + 2 * HEAD_DIM] = mixed.astype(BF)
        x1 = x + dot(ao_out[:, width : 2 * width], wout[...]) + vec(6)
        x1_out[...] = x1
        normed2, rstd2 = norm_rows(x1)
        moe = normed2 * vec(1) + vec(3)
        high, low = split(moe)
        logits = dot(high, router_ref[...]) + dot(low, router_ref[...]) + noise_here
        lanes = lax.broadcasted_iota(jnp.int32, logits.shape, 1)
        logits = jnp.where(lanes < experts, logits, NEG)
        raised = jnp.exp(logits - jnp.max(logits, -1, keepdims=True))
        gates = raised / jnp.sum(raised, -1, keepdims=True)
        gates_out[...] = gates
        ao_out[:, 2 * width : 3 * width] = high
        sent = rows_to_seats(rows_ref, seats, high)
        chosen = [pair_gate(gates, cols_ref, pair) for pair in range(2)]
        for block, ref in enumerate(seat_outs):
            note = jnp.zeros((1, LANES), F32)
            for pair in range(2):
                here = near_lanes(cols_ref, pair, block, cap)
                note = note + jnp.sum(jnp.where(here, chosen[pair], 0.0), 0, keepdims=True)
            piece = sent[block * cap : (block + 1) * cap]
            ref[...] = with_note(piece, used, note).astype(BF)

    args = [me]
    specs = [SM]
    if first:
        args += [x_args[0]]
        specs += [VM]
    else:
        args += [x_args[0], x_args[1], x_args[2], *x_args[3]]
        specs += [VM] * (3 + owners)
    args += [*weights.arrays, vecs, router, noise, cols, rows]
    specs += [ANY] * count + [VM] * 5
    outs = [
        sds((padded, width), F32),
        sds((padded, width), F32),
        sds((padded, 3 * width), BF),
        sds((padded, LANES), F32),
        sds((padded, 3 * width), BF),
    ] + [sds((cap, width), BF)] * experts
    result = call(
        kernel,
        "attn_fwd",
        args,
        specs,
        outs,
        [VM] * len(outs),
        [
            pltpu.VMEM((width, 3 * width), BF),
            pltpu.VMEM((width, width), BF),
            pltpu.SemaphoreType.DMA((copies_in(weights),)),
            pltpu.SemaphoreType.DMA((copies_in(weights),)),
        ],
    )
    return result[:5], result[5:]


def expert_fwd(me, seat_blocks, weights, bias_in, bias_oe, used):
    owners = len(seat_blocks)
    cap, width = seat_blocks[0].shape
    seats = owners * cap
    hidden = bias_in.shape[1]
    count = len(weights.arrays)
    shard = weights.arrays[0].shape[-2]
    whole = weights.places[0][0] is None
    step = width

    def kernel(*refs):
        refs = list(refs)
        me_ref = refs.pop(0)
        seat_refs = [refs.pop(0) for _ in range(owners)]
        w_refs = [refs.pop(0) for _ in range(count)]
        bin_ref, boe_ref = refs.pop(0), refs.pop(0)
        rh_out, slope_out, gate_out, made_out = (refs.pop(0) for _ in range(4))
        outs = [refs.pop(0) for _ in range(owners)]
        win, woe, sems = refs
        chunks = Chunks(w_refs, weights, width, hidden, shard, whole, win, woe, sems)
        blocks = [ref[...].astype(F32) for ref in seat_refs]
        rows = jnp.concatenate(blocks, 0).astype(BF)
        rh_out[:, 0:width] = rows
        rh_out.send(ALL, pl.ds(0, width))
        columns = [as_column(note_of(block, used), cap) for block in blocks]
        gate_out[...] = jnp.broadcast_to(jnp.concatenate(columns, 0), gate_out.shape)
        total_out = None
        for at in range(0, hidden, step):
            chunks.take(at // step)
            pre = dot(rows, win[:, at : at + step]) + bin_ref[:, at : at + step]
            square = pre * pre
            bend = jnp.tanh(0.7978845608028654 * (pre + 0.044715 * square * pre))
            h = (0.5 * pre * (1.0 + bend)).astype(BF)
            slope = 0.5 * (1.0 + bend) + 0.5 * pre * (1.0 - bend * bend) * (
                0.7978845608028654 * (1.0 + 0.134145 * square)
            )
            rh_out[:, width + at : width + at + step] = h
            slope_out[:, at : at + step] = slope.astype(BF)
            rh_out.send(ALL, pl.ds(width + at, step))
            slope_out.send(ALL, pl.ds(at, step))
            piece = dot(h, woe[at : at + step, :])
            total_out = piece if total_out is None else total_out + piece
        total_out = total_out + boe_ref[...]
        made_out[...] = total_out.astype(BF)
        part(total_out, outs)

    shapes = [
        sds((seats, width + hidden), BF),
        sds((seats, hidden), BF),
        sds((seats, LANES), F32),
        sds((seats, width), BF),
    ] + [sds((cap, width), BF)] * owners
    result = call(
        kernel,
        "expert_fwd",
        [me, *seat_blocks, *weights.arrays, bias_in, bias_oe],
        [SM] + [LOAD] * owners + [ANY] * count + [LOAD] * 2,
        shapes,
        [STORE] * len(shapes),
        [
            pltpu.VMEM((width, hidden), BF),
            pltpu.VMEM((hidden, width), BF),
            pltpu.SemaphoreType.DMA((2 * copies_in(weights),)),
        ],
    )
    return result[:4], result[4:]


def expert_both(me, z, seat_blocks, grads, weights, bias_in, bias_oe, used, shards):
    size = bias_in.shape[1] // shards
    owners = len(seat_blocks)
    cap, width = seat_blocks[0].shape
    seats = owners * cap
    hidden = bias_in.shape[1]
    count = len(weights.arrays)
    shard = weights.arrays[0].shape[-2]
    whole = weights.places[0][0] is None
    step = width

    def kernel(*refs):
        refs = list(refs)
        me_ref, z_ref = refs.pop(0), refs.pop(0)
        seat_refs = [refs.pop(0) for _ in range(owners)]
        grad_ref = refs.pop(0)
        w_refs = [refs.pop(0) for _ in range(count)]
        bin_ref, boe_ref = refs.pop(0), refs.pop(0)
        rp_out, hd_out, give_out, made_out = (refs.pop(0) for _ in range(4))
        outs = [refs.pop(0) for _ in range(owners)]
        win, woe, slopes, sems = refs
        chunks = Chunks(w_refs, weights, width, hidden, shard, whole, win, woe, sems)
        blocks = [ref[...].astype(F32) for ref in seat_refs]
        rows = jnp.concatenate(blocks, 0).astype(BF)
        rp_out[:, 0:width] = rows
        other = 1 - (me_ref[0] & 1)
        gate = jnp.concatenate([as_column(note_of(block, used), cap) for block in blocks], 0)
        total_out = None
        for at in range(0, hidden, step):
            chunks.take(at // step)
            pre = dot(rows, win[:, at : at + step]) + bin_ref[:, at : at + step]
            square = pre * pre
            bend = jnp.tanh(0.7978845608028654 * (pre + 0.044715 * square * pre))
            h = (0.5 * pre * (1.0 + bend)).astype(BF)
            slope = 0.5 * (1.0 + bend) + 0.5 * pre * (1.0 - bend * bend) * (
                0.7978845608028654 * (1.0 + 0.134145 * square)
            )
            hd_out[:, at : at + step] = h
            slopes[:, at : at + step] = slope.astype(BF)
            piece = dot(h, woe[at : at + step, :])
            total_out = piece if total_out is None else total_out + piece
        made = (total_out + boe_ref[...]).astype(BF).astype(F32)
        for k in range(owners):
            made_out.held[z_ref[0] ^ k] = made[k * cap : (k + 1) * cap].astype(BF)
        given = [grad_ref[z_ref[0] ^ k].astype(F32) for k in range(owners)]
        given = jnp.concatenate(given, 0)
        grad = (given * gate).astype(BF)
        hd_out[:, hidden : hidden + width] = grad
        for k in range(shards // 2):
            first = pl.multiple_of((2 * k + other) * size, LANES)
            give_out[:, k * size : (k + 1) * size] = hd_out.held[:, pl.ds(first, size)]
        give_out[:, hidden // 2 : hidden // 2 + width] = grad
        hd_out.send(ALL, ALL)
        give_out.send(ALL, ALL)
        made_out.send(ALL)
        notes = given * made
        notes = [lane_sums(notes[k * cap : (k + 1) * cap]) for k in range(owners)]
        total_out = None
        for at in range(0, hidden, step):
            d_hidden = dot_nt(grad, woe[at : at + step, :])
            d_pre = (d_hidden * slopes[:, at : at + step].astype(F32)).astype(BF)
            rp_out[:, width + at : width + at + step] = d_pre
            piece = dot_nt(d_pre, win[:, at : at + step])
            total_out = piece if total_out is None else total_out + piece
            if at == hidden // 2 - step:
                rp_out.send(ALL, pl.ds(0, width + hidden // 2))
        rp_out.send(ALL, pl.ds(width + hidden // 2, hidden // 2))
        for k, ref in enumerate(outs):
            ref[...] = with_note(total_out[k * cap : (k + 1) * cap], used, notes[k]).astype(BF)

    shapes = [
        sds((seats, width + hidden), BF),
        sds((seats, hidden + width), BF),
        sds((seats, hidden // 2 + width), BF),
        sds((owners, cap, width), BF),
    ] + [sds((cap, width), BF)] * owners
    result = call(
        kernel,
        "expert_both",
        [me, z, *seat_blocks, grads, *weights.arrays, bias_in, bias_oe],
        [SM, SM] + [LOAD] * (owners + 1) + [ANY] * count + [LOAD] * 2,
        shapes,
        [STORE] * len(shapes),
        [
            pltpu.VMEM((width, hidden), BF),
            pltpu.VMEM((hidden, width), BF),
            pltpu.VMEM((seats, hidden), BF),
            pltpu.SemaphoreType.DMA((2 * copies_in(weights),)),
        ],
    )
    return result[:4], result[4:]


def top_seats(z, cotangent, rows, cap, experts):
    tokens, width = cotangent.shape
    padded = rows.shape[1]

    def kernel(z_ref, cot_ref, rows_ref, grad_out, out):
        grad_out[...] = jnp.zeros_like(grad_out)
        grad_out[0:tokens, :] = cot_ref[...].astype(F32)
        sent = rows_to_seats(rows_ref, cap * experts, grad_out[...].astype(BF))
        for k in range(experts):
            out[z_ref[0] ^ k] = sent[k * cap : (k + 1) * cap].astype(BF)

    return call(
        kernel,
        "top_seats",
        [z, cotangent, rows],
        [SM, VM, VM],
        [sds((padded, width), F32), sds((experts, cap, width), BF)],
        [VM] * 2,
        [],
    )


def mix(z, x1, gates, cols, returned, tokens):
    width = x1.shape[1]

    def kernel(z_ref, x1_ref, gates_ref, cols_ref, ref, out):
        blocks = join([ref.at[z_ref[0] ^ k] for k in range(ref.shape[0])])
        total = combine(x1_ref[...], gates_ref[...], cols_ref, blocks)
        out[...] = total[0:tokens, :]

    return call(
        kernel,
        "mix",
        [z, x1, gates, cols, returned],
        [SM] + [VM] * 4,
        sds((tokens, width), F32),
        VM,
        [],
    )


def expert_back(me, grad_blocks, slope, gate, made, weights, used):
    owners = len(grad_blocks)
    cap, width = grad_blocks[0].shape
    seats, hidden = slope.shape
    count = len(weights.arrays)
    shard = weights.arrays[0].shape[-2]
    whole = weights.places[0][0] is None
    step = width

    def kernel(*refs):
        refs = list(refs)
        me_ref = refs.pop(0)
        seat_refs = [refs.pop(0) for _ in range(owners)]
        slope_ref, gate_ref, made_ref = (refs.pop(0) for _ in range(3))
        w_refs = [refs.pop(0) for _ in range(count)]
        gd_out = refs.pop(0)
        outs = [refs.pop(0) for _ in range(owners)]
        win, woe, slopes, sems, slope_sems = refs
        more = [
            pltpu.make_async_copy(
                slope_ref.at[:, pl.ds(at, step)],
                slopes.at[:, pl.ds(at, step)],
                slope_sems.at[at // step],
            )
            for at in range(0, hidden, step)
        ]
        chunks = Chunks(w_refs, weights, width, hidden, shard, whole, win, woe, sems, more)
        given = jnp.concatenate([ref[...].astype(F32) for ref in seat_refs], 0)
        grad = (given * gate_ref[:, 0:1]).astype(BF)
        notes = given * made_ref[...].astype(F32)
        notes = [lane_sums(notes[k * cap : (k + 1) * cap]) for k in range(owners)]
        gd_out[:, 0:width] = grad
        gd_out.send(ALL, pl.ds(0, width))
        total_out = None
        for at in range(0, hidden, step):
            chunks.take(at // step)
            d_hidden = dot_nt(grad, woe[at : at + step, :])
            d_pre = (d_hidden * slopes[:, at : at + step].astype(F32)).astype(BF)
            gd_out[:, width + at : width + at + step] = d_pre
            gd_out.send(ALL, pl.ds(width + at, step))
            piece = dot_nt(d_pre, win[:, at : at + step])
            total_out = piece if total_out is None else total_out + piece
        for k, ref in enumerate(outs):
            ref[...] = with_note(total_out[k * cap : (k + 1) * cap], used, notes[k]).astype(BF)

    shapes = [sds((seats, width + hidden), BF)]
    shapes += [sds((cap, width), BF)] * owners
    result = call(
        kernel,
        "expert_back",
        [me, *grad_blocks, slope, gate, made, *weights.arrays],
        [SM] + [LOAD] * owners + [ANY] + [LOAD] * 2 + [ANY] * count,
        shapes,
        [STORE] * (1 + owners),
        [
            pltpu.VMEM((width, hidden), BF),
            pltpu.VMEM((hidden, width), BF),
            pltpu.VMEM((seats, hidden), BF),
            pltpu.SemaphoreType.DMA((2 * copies_in(weights),)),
            pltpu.SemaphoreType.DMA((hidden // step,)),
        ],
    )
    return result[0], result[1:]


def column_sums(value):
    return dot(jnp.ones((8, value.shape[0]), BF), value)[0:1, :]


def own_columns(width, shards, core):
    shard = width // shards
    half = width // 2
    row = lax.broadcasted_iota(jnp.int32, (width, half), 0)
    column = lax.broadcasted_iota(jnp.int32, (width, half), 1)
    place = column + core * shard
    for k in range(1, shards // 2):
        place = place + jnp.where(column >= k * shard, shard, 0)
    return one(row == place)


def expert_grads(me, rows_in, h, d_out, d_pre, sizes, paired, shards, given=()):
    width = HEADS * HEAD_DIM
    seats, hidden = sizes
    sides = 2 if paired else 1
    per, shard = hidden // width, width // shards
    part_hidden = hidden // shards
    tall = width // 2 if paired else width
    deep = hidden // 2 if paired else hidden
    total = shards * per if paired else 2
    blocks = shards // 2 if paired else per
    size = part_hidden if paired else width
    arrays = []
    for operand in (*rows_in, *h, *d_out, *d_pre):
        if not any(operand[0] is known for known in arrays):
            arrays.append(operand[0])
    place = lambda operand: [operand[0] is known for known in arrays].index(True)

    def kernel(me_ref, *refs):
        refs = list(refs)
        ins = [refs.pop(0) for _ in arrays]
        bias_given = [refs.pop(0) for _ in given][-1:]
        outs = [refs.pop(0) for _ in range(1 if paired else 2)]
        bias_ref, win, woe, h_held, row_held, out_held, pre_held, sems, load_sems = refs
        core = me_ref[0] & 1
        copies = []
        loads = {}

        def send(source, target):
            copy = pltpu.make_async_copy(source, target, sems.at[len(copies)])
            copy.start()
            copies.append(copy)

        def fetch_in(key, source, target):
            copy = pltpu.make_async_copy(source, target, load_sems.at[len(loads)])
            copy.start()
            loads[key] = copy

        def summed(pieces):
            total = pieces[0]
            for piece in pieces[1:]:
                total = total + piece
            return total

        for i, operand in enumerate(d_out):
            source = ins[place(operand)].at[:, pl.ds(operand[1], width)]
            fetch_in(("d", i), source, out_held.at[i])
        for k in range(blocks):
            for i, operand in enumerate(h):
                first = operand[1] + k * size
                if paired and operand[2]:
                    first = pl.multiple_of(operand[1] + (2 * k + core) * size, LANES)
                source = ins[place(operand)].at[:, pl.ds(first, size)]
                fetch_in(("h", k, i), source, h_held.at[i, :, pl.ds(k * size, size)])
        for i, operand in enumerate(rows_in):
            source = ins[place(operand)].at[:, pl.ds(operand[1], width)]
            fetch_in(("r", i), source, row_held.at[i])
        for k in range(per):
            for i, operand in enumerate(d_pre):
                source = ins[place(operand)].at[:, pl.ds(operand[1] + k * width, width)]
                fetch_in(("p", k, i), source, pre_held.at[i, :, pl.ds(k * width, width)])
        if bias_given:
            bias_ref[...] = bias_given[0][...]
        else:
            bias_ref[...] = jnp.zeros_like(bias_ref)
        if h:
            for i in range(sides):
                loads["d", i].wait()
            for k in range(blocks):
                here = slice(k * size, (k + 1) * size)
                for i in range(sides):
                    loads["h", k, i].wait()
                total = summed([dot_tn(h_held[i, :, here], out_held[i]) for i in range(sides)])
                woe[here, :] = total.astype(BF)
                if paired:
                    for q in range(per):
                        send(
                            woe.at[pl.ds(k * size + q * shard, shard)],
                            outs[0].at[k, 1, :, pl.ds(q * width, width)],
                        )
            bias_ref[per : per + 1, :] = summed([column_sums(out_held[i]) for i in range(sides)])
        if rows_in:
            for i in range(sides):
                loads["r", i].wait()
            lefts = [row_held[i] for i in range(sides)]
            if paired:
                pick = own_columns(width, shards, core)
                lefts = [dot(value, pick).astype(BF) for value in lefts]
            for k in range(per):
                here = slice(k * width, (k + 1) * width)
                for i in range(sides):
                    loads["p", k, i].wait()
                total = summed([dot_tn(lefts[i], pre_held[i, :, here]) for i in range(sides)])
                win[:, here] = total.astype(BF)
                if paired:
                    for n in range(shards // 2):
                        into = pl.ds(k * width, width)
                        send(win.at[pl.ds(n * shard, shard), into], outs[0].at[n, 0, :, into])
            sums = summed([column_sums(pre_held[i]) for i in range(sides)])
            for d in range(shards):
                for q in range(per):
                    first = (d * per + q) * shard
                    bias_ref[q : q + 1, d * shard : (d + 1) * shard] = sums[:, first : first + shard]
        if not paired:
            send(win, outs[0])
            send(woe, outs[1])
        wait(copies)

    if paired:
        shapes = [sds((shards // 2, 2, shard, hidden), BF)]
    else:
        shapes = [sds((width, hidden), BF), sds((hidden, width), BF)]
    result = call(
        kernel,
        "expert_grads",
        [me, *arrays, *given],
        [SM] + [ANY] * (len(arrays) + max(len(given) - 1, 0)) + [VM] * min(len(given), 1),
        shapes + [sds((8, width), F32)],
        [ANY] * len(shapes) + [VM],
        [
            pltpu.VMEM((tall, hidden), BF),
            pltpu.VMEM((deep, width), BF),
            pltpu.VMEM((sides, seats, blocks * size), BF),
            pltpu.VMEM((sides, seats, width), BF),
            pltpu.VMEM((sides, seats, width), BF),
            pltpu.VMEM((sides, seats, hidden), BF),
            pltpu.SemaphoreType.DMA((total,)),
            pltpu.SemaphoreType.DMA((sides * (2 + blocks + per),)),
        ],
        {1 + len(arrays): 0} if given else None,
    )
    return result[:-1], result[-1]


def pick_columns(me, value, shards):
    rows, wide = value.shape
    width = wide // 3

    def kernel(me_ref, ref, own, other):
        core = me_ref[0] & 1
        for out, side in ((own, core), (other, 1 - core)):
            pick = own_columns(width, shards, side)
            for k in range(3):
                piece = dot(ref[:, k * width : (k + 1) * width], pick)
                out[:, k * width // 2 : (k + 1) * width // 2] = piece.astype(BF)

    return call(
        kernel,
        "pick_columns",
        [me, value],
        [SM, VM],
        [sds((rows, wide // 2), BF)] * 2,
        [VM] * 2,
        [],
    )


def attn_back(
    me, back_blocks, gates, router, grad, x, x1, qkv, cols, vecs, weights, below, tokens, used
):
    padded, width = grad.shape
    owners = len(back_blocks)
    cap = back_blocks[0].shape[0]
    seats = owners * cap
    count = len(weights.arrays)
    shard = weights.arrays[0].shape[-2]

    def kernel(*refs):
        refs = list(refs)
        me_ref = refs.pop(0)
        back_refs = [refs.pop(0) for _ in range(owners)]
        gates_ref, router_ref, grad_ref, x_ref, x1_ref, qkv_ref, cols_ref, vec_ref = (
            refs.pop(0) for _ in range(8)
        )
        w_refs = [refs.pop(0) for _ in range(count)]
        if below is not None:
            below_rows = refs.pop(0)
        dx_out, back_out = refs.pop(0), refs.pop(0)
        seat_outs = [refs.pop(0) for _ in range(owners)] if below is not None else None
        wqkv, wout, small_out, sems, more_sems = refs
        targets = attn_targets(width, shard, wqkv, wout)
        right = fetch(w_refs, weights, me_ref[0], targets, 1, sems)
        left = fetch(w_refs, weights, me_ref[0], targets, 0, more_sems)
        start(right + left)
        vec = lambda k: vec_ref[k : k + 1, :]
        blocks = [ref[...].astype(F32) for ref in back_refs]
        gates = gates_ref[...]
        lanes = lax.broadcasted_iota(jnp.int32, gates.shape, 1)
        d_gates = jnp.zeros_like(gates)
        for pair in range(2):
            d_pair = jnp.zeros_like(gates)
            for block in range(owners):
                here = near_lanes(cols_ref, pair, block, cap)
                d_pair = d_pair + jnp.where(here, note_of(blocks[block], used), 0.0)
            d_pair = jnp.sum(d_pair, -1, keepdims=True)
            d_gates = d_gates + jnp.where(lanes == cols_ref[:, 2 + pair : 3 + pair], d_pair, 0.0)
        dz = gates * (d_gates - jnp.sum(d_gates * gates, -1, keepdims=True))
        high, low = split(dz)
        moe_part = dot_nt(high, router_ref[...]) + dot_nt(low, router_ref[...])
        back_out[0:padded, 4 * width : 4 * width + LANES] = high
        back_out[0:padded, 4 * width + LANES : 4 * width + 2 * LANES] = low
        chosen = jnp.logical_or(seat_mask(cols_ref, 0, seats), seat_mask(cols_ref, 1, seats))
        d_moe = dot(one(chosen), jnp.concatenate(blocks, 0).astype(BF)) + moe_part
        normed2, rstd2 = norm_rows(x1_ref[...])
        small_out[...] = jnp.zeros_like(small_out)
        small_out[1:2, :] = jnp.sum(d_moe * normed2, 0, keepdims=True)
        small_out[3:4, :] = jnp.sum(d_moe, 0, keepdims=True)
        d_x1 = grad_ref[...] + norm_back(d_moe * vec(1), normed2, rstd2)
        dy = d_x1.astype(BF)
        back_out[0:padded, 3 * width : 4 * width] = dy
        small_out[6:7, :] = column_sums(dy)
        wait(right)
        d_mixed = dot_nt(dy, wout[...]).astype(BF)
        masks = head_masks()
        scale = HEAD_DIM ** (-0.5)
        for two in range(HEADS // 2):
            at = two * 2 * HEAD_DIM
            query = qkv_ref[:, at : at + 2 * HEAD_DIM]
            keys = qkv_ref[:, width + at : width + at + 2 * HEAD_DIM]
            values = qkv_ref[:, 2 * width + at : 2 * width + at + 2 * HEAD_DIM]
            d_o = d_mixed[:, at : at + 2 * HEAD_DIM]
            probs = pair_probs(query, keys, masks, tokens)
            d_here = stacked(d_o, masks)
            d_probs = dot_nt(d_here, values)
            d_values = dot_tn(probs.astype(BF), d_here)
            d_scores = probs * (d_probs - jnp.sum(d_probs * probs, -1, keepdims=True))
            d_scores = d_scores.astype(BF)
            d_query = unstacked(dot(d_scores, keys), masks)
            d_keys = dot_tn(d_scores, stacked(query, masks))
            sums = (d_query, d_keys, d_values)
            for k, value in enumerate((sums[0] * scale, sums[1] * scale, sums[2])):
                first = k * width + at
                back_out[0:padded, first : first + 2 * HEAD_DIM] = value.astype(BF)
        wait(left)
        d_normed = None
        for k in range(3):
            here = back_out[0:padded, k * width : (k + 1) * width]
            if k != 1:
                row = 4 if k == 0 else 5
                small_out[row : row + 1, :] = column_sums(here)
            piece = dot_nt(here, wqkv[:, k * width : (k + 1) * width])
            d_normed = piece if d_normed is None else d_normed + piece
        normed1, rstd1 = norm_rows(x_ref[...])
        small_out[0:1, :] = jnp.sum(d_normed * normed1, 0, keepdims=True)
        small_out[2:3, :] = jnp.sum(d_normed, 0, keepdims=True)
        d_x = d_x1 + norm_back(d_normed * vec(0), normed1, rstd1)
        dx_out[...] = d_x[0 : dx_out.shape[0], :]
        if below is not None:
            part(rows_to_seats(below_rows, seats, d_x.astype(BF)), seat_outs)
        high, low = split(small_out[...])
        back_out[padded : padded + 16, 0:width] = high
        back_out[padded : padded + 16, width : 2 * width] = low
        back_out[padded : padded + 16, 2 * width :] = jnp.zeros((16, 2 * width + 2 * LANES), BF)

    shapes = [
        sds((padded if below is not None else tokens, width), F32),
        sds((padded + 16, 4 * width + 2 * LANES), BF),
    ]
    args = [me, *back_blocks, gates, router, grad, x, x1, qkv, cols, vecs, *weights.arrays]
    specs = [SM] + [VM] * (owners + 8) + [ANY] * count
    if below is not None:
        shapes += [sds((cap, width), BF)] * owners
        args += [below]
        specs += [VM]
    result = call(
        kernel,
        "attn_back",
        args,
        specs,
        shapes,
        [VM] * len(shapes),
        [
            pltpu.VMEM((width, 3 * width), BF),
            pltpu.VMEM((width, width), BF),
            pltpu.VMEM((16, width), F32),
            pltpu.SemaphoreType.DMA((copies_in(weights),)),
            pltpu.SemaphoreType.DMA((copies_in(weights),)),
        ],
    )
    return result[:2], result[2:]


def attn_grads(me, z, own, other, biases, shards, ordered):
    padded, wide_ao = own[0].shape
    width = HEADS * HEAD_DIM
    half = 2 * width + LANES
    tall = width // 2 if other else width
    shard = width // shards
    places = [(6, 0, 0), (6, 1, 1), (2, 0, 2), (2, 1, 2), (4, 0, 3), (4, 1, 3), (0, 0, 4), (0, 1, 4)]
    count = 2
    if other:
        count = 1 if ordered else 5

    def kernel(me_ref, z_ref, *refs):
        refs = list(refs)
        ao = [refs.pop(0), refs.pop(0)] if other else [refs.pop(0)]
        back = [refs.pop(0), refs.pop(0)] if other else [refs.pop(0)]
        bias_ref = refs.pop(0)
        outs = [refs.pop(0) for _ in range(count)]
        wide, rows, turned, sems = refs
        copies = []

        def send(p):
            first = p * half
            if not other:
                copies.append(
                    pltpu.make_async_copy(wide.at[:, pl.ds(first, half)], outs[p], sems.at[p])
                )
                copies[-1].start()
                return
            if ordered:
                for k in range(shards // 2):
                    source = wide.at[pl.ds(k * shard, shard), pl.ds(first, half)]
                    copy = pltpu.make_async_copy(source, outs[0].at[k, p], sems.at[2 * k + p])
                    copies.append(copy)
                    copy.start()
                return
            for n, (off, where, o) in enumerate(places):
                if where != p:
                    continue
                at = pl.multiple_of(((me_ref[0] ^ off) >> 1) * shard, 16)
                into = outs[o] if o < 2 else outs[o].at[p]
                copies.append(
                    pltpu.make_async_copy(
                        wide.at[pl.ds(at, shard), pl.ds(first, half)], into, sems.at[n]
                    )
                )
                copies[-1].start()

        def product(which, first):
            total = None
            for left, right in zip(ao, back):
                here = left[:, which * tall : (which + 1) * tall]
                piece = dot_tn(here, right[0:padded, first : first + width])
                total = piece if total is None else total + piece
            return total.astype(BF)

        wide[:, 0:width] = product(0, 0)
        wide[:, width : 2 * width] = product(0, width)
        wide[:, 2 * width : half] = jnp.zeros((tall, LANES), BF)
        send(0)
        wide[:, half : half + width] = product(0, 2 * width)
        wide[:, half + width : half + 2 * width] = product(1, 3 * width)
        rows[...] = jnp.zeros_like(rows)
        small = None
        d_router = None
        for left, right in zip(ao, back):
            for k in range(2):
                piece = right[padded : padded + 16, k * width : (k + 1) * width].astype(F32)
                small = piece if small is None else small + piece
                first = 4 * width + k * LANES
                piece = dot_tn(
                    left[:, 2 * tall : 3 * tall], right[0:padded, first : first + LANES]
                )
                d_router = piece if d_router is None else d_router + piece
        rows[16:32, :] = small
        rows[pl.ds(pl.multiple_of(32 + 8 * z_ref[0], 8), 8), :] = bias_ref[...]
        turned[...] = rows[...].T
        if other:
            core = me_ref[0] & 1
            for k in range(shards // 2):
                at = pl.multiple_of((2 * k + core) * shard, 8)
                here = slice(k * shard, (k + 1) * shard)
                piece = d_router[here, :] + turned[pl.ds(at, shard), :]
                wide[here, half + 2 * width : 2 * half] = piece.astype(BF)
        else:
            wide[:, half + 2 * width : 2 * half] = (d_router + turned[...]).astype(BF)
        send(1)
        wait(copies)

    if other:
        if ordered:
            shapes = [sds((shards // 2, 2, shard, half), BF)]
        else:
            shapes = [sds((shard, half), BF)] * 2 + [sds((2, shard, half), BF)] * 3
        args = [own[0], other[0], own[1], other[1]]
    else:
        shapes = [sds((width, half), BF)] * 2
        args = list(own)
    return call(
        kernel,
        "attn_grads",
        [me, z, *args, biases],
        [SM, SM] + [VM] * (len(args) + 1),
        shapes,
        [ANY] * len(shapes),
        [
            pltpu.VMEM((tall, 2 * half), BF),
            pltpu.VMEM((LANES, width), F32),
            pltpu.VMEM((width, LANES), F32),
            pltpu.SemaphoreType.DMA((max(len(places), shards),)),
        ],
    )


def small_out(smalls, z, experts, per):
    layers = len(smalls)
    shard = smalls[0].shape[0]

    def kernel(z_ref, *refs):
        ins = refs[:layers]
        gains, biases, router, bias_in, bias_oe, square = refs[layers:]
        for layer in range(layers):
            square[...] = jnp.zeros_like(square)
            square[0:shard, :] = ins[layer][...]
            square[...] = square[...].T
            router[layer] = square[0:experts, 0:shard]
            gains[layer] = square[16:18, 0:shard]
            for k in range(5):
                biases[k, layer : layer + 1, :] = square[18 + k : 19 + k, 0:shard]
            own = square[pl.ds(pl.multiple_of(32 + 8 * z_ref[0], 8), 8), :]
            for q in range(per):
                bias_in[layer, :, q * shard : (q + 1) * shard] = own[q : q + 1, 0:shard]
            bias_oe[layer] = own[per : per + 1, 0:shard]

    shapes = [
        sds((layers, 2, shard), F32),
        sds((5, layers, shard), F32),
        sds((layers, experts, shard), F32),
        sds((layers, 1, per * shard), F32),
        sds((layers, 1, shard), F32),
    ]
    return call(
        kernel,
        "small_out",
        [z, *smalls],
        [SM] + [VM] * layers,
        shapes,
        [VM] * 5,
        [pltpu.VMEM((LANES, LANES), F32)],
    )


def swap(value, axis, bit):
    size = lax.axis_size(axis)
    return lax.ppermute(value, axis, [(i, i ^ bit) for i in range(size)])


def exchange(blocks):
    order = sorted(range(1, len(blocks)), key=lambda k: -(k & 2))
    got = {k: swap(blocks[k], "expert", k) for k in order}
    return [blocks[0]] + [got[k] for k in range(1, len(blocks))]


def axis_bits(axis, bit):
    bits = []
    while bit < lax.axis_size(axis):
        bits.append(bit)
        bit *= 2
    return bits


def sum_experts(value):
    for bit in axis_bits("expert", 1):
        low = value.astype(BF)
        value = low.astype(F32) + swap(low, "expert", bit).astype(F32)
    return value


def gather_rows(shard):
    return lax.all_gather(shard, "dp", axis=0, tiled=True)


def scatter_rows(whole):
    return lax.psum_scatter(whole, "dp", scatter_dimension=0, tiled=True)


def scatter_chips(blocks):
    size = lax.axis_size("dp")
    return lax.psum_scatter(
        blocks,
        "dp",
        scatter_dimension=0,
        axis_index_groups=[list(range(core, size, 2)) for core in range(2)],
    )


class Gather:
    def __init__(self, shard):
        self.shard = shard
        self.x, self.y = swap(shard, "dp", 2), swap(shard, "dp", 4)

    def turn(self):
        _, rows, width = self.shard.shape
        half = (1, rows, width)
        *self.cut, self.x, self.y = move(
            "cut",
            [self.x, self.y],
            [(0, (pl.ds(0, 1),), 0, (ALL,), half), (1, (pl.ds(1, 1),), 1, (ALL,), half)],
            [sds(half, BF)] * 2 + [sds(self.x.shape, BF)] * 2,
            {0: 2, 1: 3},
        )

    def send(self, after=()):
        if after:
            self.cut = hold(self.cut, after)
        self.xy = swap(self.cut[0], "dp", 4), swap(self.cut[1], "dp", 2)
        self.other = [swap(value, "dp", 1) for value in (self.shard, self.x, self.y)]

    def cross(self, after=()):
        if after:
            self.xy = hold(self.xy, after)
        self.across = [swap(value, "dp", 1) for value in self.xy]

    def weights(self):
        pieces = [
            (self.shard, 0, (0, 1)),
            (self.x, 2, (0, 1)),
            (self.y, 4, (0, 1)),
            (self.xy[0], 6, (0,)),
            (self.xy[1], 6, (1,)),
            (self.across[0], 7, (0,)),
            (self.across[1], 7, (1,)),
            (self.other[0], 1, (0, 1)),
            (self.other[1], 3, (0, 1)),
            (self.other[2], 5, (0, 1)),
        ]
        return Weights([p[0] for p in pieces], [p[1:] for p in pieces])


def full(rows):
    return (pl.ds(0, rows), ALL)


class AttnSum:
    def __init__(self, grads):
        self.bits = axis_bits("expert", 1)
        self.done = 0
        if len(grads) == 1:
            self.total = scatter_chips(grads[0])
            return
        self.across, (self.x, self.y, self.own) = list(grads[:2]), grads[2:]
        self.rows, self.width = self.across[0].shape

    def cut(self, z):
        self.rows, self.width = self.total.shape[1:]
        shape = (self.rows, self.width)

        def kernel(z_ref, total, keep, give, held, in_sems, out_sems):
            here = z_ref[0] & 1
            loads = [
                pltpu.make_async_copy(total.at[k], held.at[k], in_sems.at[k]) for k in range(2)
            ]
            start(loads)
            wait(loads)
            stores = [
                pltpu.make_async_copy(held.at[here], keep, out_sems.at[0]),
                pltpu.make_async_copy(held.at[1 - here], give, out_sems.at[1]),
            ]
            start(stores)
            wait(stores)

        self.keep, give = call(
            kernel,
            "parts",
            [z, self.total],
            [SM, ANY],
            [sds(shape, BF)] * 2,
            [ANY] * 2,
            [
                pltpu.VMEM((2, *shape), BF),
                pltpu.SemaphoreType.DMA((2,)),
                pltpu.SemaphoreType.DMA((2,)),
            ],
        )
        self.come = swap(give, "expert", 1)

    def halves(self):
        shape = (self.rows, self.width)
        flat = full(self.rows)
        (self.keep,) = fold(
            "fold3",
            [self.keep, self.come],
            shape,
            [([(0, flat), (1, flat)], BF, [(0, flat, flat)])],
            [sds(shape, BF)],
        )
        if self.done == 0:
            self.come = swap(self.keep, "expert", 2)
        else:
            self.come = swap(self.keep, "expert", 1)
        self.done += 1

    def finish(self, z, layer, layers, given, smalls, experts, per):
        rows, half = self.rows, self.width
        wide = (half - LANES) // 2
        others = sorted(smalls)
        count = len(given)

        def kernel(z_ref, *refs):
            refs = list(refs)
            terms = [refs.pop(0) for _ in range(4)]
            ins = {n: refs.pop(0) for n in others}
            del refs[:count]
            qkv, out, gains, biases, router, bias_in, bias_oe, high, square, sems = refs
            for p in range(2):
                high[p] = terms[p][...].astype(F32) + terms[2 + p][...].astype(F32)
            copies = [
                (high.at[0, :, pl.ds(0, 2 * wide)], qkv.at[layer, :, pl.ds(0, 2 * wide)]),
                (high.at[1, :, pl.ds(0, wide)], qkv.at[layer, :, pl.ds(2 * wide, wide)]),
                (high.at[1, :, pl.ds(wide, wide)], out.at[layer]),
            ]
            copies = [pltpu.make_async_copy(a, b, sems.at[n]) for n, (a, b) in enumerate(copies)]
            start(copies)
            for n in range(layers):
                square[...] = jnp.zeros_like(square)
                if n == layer:
                    square[0:rows, :] = high[1, :, 2 * wide : 2 * wide + LANES]
                else:
                    square[0:rows, :] = ins[n][...]
                square[...] = square[...].T
                router[n] = square[0:experts, 0:rows]
                gains[n] = square[16:18, 0:rows]
                for k in range(5):
                    biases[k, n : n + 1, :] = square[18 + k : 19 + k, 0:rows]
                own = square[pl.ds(pl.multiple_of(32 + 8 * z_ref[0], 8), 8), :]
                for q in range(per):
                    bias_in[n, :, q * rows : (q + 1) * rows] = own[q : q + 1, 0:rows]
                bias_oe[n] = own[per : per + 1, 0:rows]
            wait(copies)

        return call(
            kernel,
            "attn_last",
            [z, *self.parts, *self.came, *[smalls[n] for n in others], *given],
            [SM] + [VM] * (4 + len(others)) + [HBM] * count,
            [
                sds((layers, rows, 3 * wide), F32),
                sds((layers, rows, wide), F32),
                sds((layers, 2, rows), F32),
                sds((5, layers, rows), F32),
                sds((layers, experts, rows), F32),
                sds((layers, 1, per * rows), F32),
                sds((layers, 1, rows), F32),
            ],
            [HBM] * 2 + [VM] * 5,
            [
                pltpu.VMEM((2, rows, half), F32),
                pltpu.VMEM((LANES, LANES), F32),
                pltpu.SemaphoreType.DMA((3,)),
            ],
            {5 + len(others): 0, 6 + len(others): 1} if given else None,
        )

    def put(self, z, layer, layers, given):
        shape = (self.rows, self.width)
        wide = (self.width - LANES) // 2
        count = len(given)

        def kernel(z_ref, keep, come, *refs):
            refs = refs[count:]
            qkv, out, small, low, high, in_sems, out_sems = refs
            here = z_ref[0] & 1
            loads = [
                pltpu.make_async_copy(keep, low.at[here], in_sems.at[0]),
                pltpu.make_async_copy(come, low.at[1 - here], in_sems.at[1]),
            ]
            start(loads)
            wait(loads)
            high[...] = low[...].astype(F32)
            stores = [
                (high.at[0, :, pl.ds(0, 2 * wide)], qkv.at[layer, :, pl.ds(0, 2 * wide)]),
                (high.at[1, :, pl.ds(0, wide)], qkv.at[layer, :, pl.ds(2 * wide, wide)]),
                (high.at[1, :, pl.ds(wide, wide)], out.at[layer]),
                (high.at[1, :, pl.ds(2 * wide, LANES)], small),
            ]
            stores = [
                pltpu.make_async_copy(a, b, out_sems.at[n]) for n, (a, b) in enumerate(stores)
            ]
            start(stores)
            wait(stores)

        return call(
            kernel,
            "attn_out",
            [z, self.keep, self.come, *given],
            [SM] + [ANY] * (2 + count),
            [
                sds((layers, self.rows, 3 * wide), F32),
                sds((layers, self.rows, wide), F32),
                sds((self.rows, LANES), F32),
            ],
            [HBM] * 3,
            [
                pltpu.VMEM((2, *shape), BF),
                pltpu.VMEM((2, *shape), F32),
                pltpu.SemaphoreType.DMA((2,)),
                pltpu.SemaphoreType.DMA((4,)),
            ],
            {3: 0, 4: 1} if given else None,
        )

    def send_across(self, after=()):
        if after:
            self.across = hold(self.across, after)
        self.across = swap(self.across[0], "dp", 4), swap(self.across[1], "dp", 2)

    def fold1(self):
        self.x, self.y = fold1(self.x, self.y, self.across)

    def send_on(self, after=()):
        if after:
            self.x, self.y = hold([self.x, self.y], after)
        self.came = swap(self.x, "dp", 2), swap(self.y, "dp", 4)

    def fold2(self):
        shape = (self.rows, self.width)
        flat = full(self.rows)
        self.parts = fold(
            "fold2",
            [self.own, *self.came],
            shape,
            [([(i, (p,)) for i in range(3)], BF, [(p, flat, flat)]) for p in range(2)],
            [sds(shape, BF)] * 2,
        )
        self.send()

    def send(self):
        up_bit, down_bit = self.bits[self.done], self.bits[-1 - self.done]
        self.came = swap(self.parts[0], "expert", up_bit), swap(self.parts[1], "expert", down_bit)

    def fold3(self, layer, layers, given):
        shape = (self.rows, self.width)
        flat = full(self.rows)
        self.done += 1
        terms = [[(0, flat), (2, flat)], [(1, flat), (3, flat)]]
        args = [*self.parts, *self.came]
        if self.done < len(self.bits):
            self.parts = fold(
                "fold3",
                args,
                shape,
                [(terms[p], BF, [(p, flat, flat)]) for p in range(2)],
                [sds(shape, BF)] * 2,
                )
            self.send()
            return None
        wide = (self.width - LANES) // 2
        cut = lambda first, size: (ALL, pl.ds(first, size))
        tasks = [
            (terms[0], F32, [(0, (layer, ALL, pl.ds(0, 2 * wide)), cut(0, 2 * wide))]),
            (
                terms[1],
                F32,
                [
                    (0, (layer, ALL, pl.ds(2 * wide, wide)), cut(0, wide)),
                    (1, (layer,), cut(wide, wide)),
                    (2, flat, cut(2 * wide, LANES)),
                ],
            ),
        ]
        outs = [
            sds((layers, self.rows, 3 * wide), F32),
            sds((layers, self.rows, wide), F32),
            sds((self.rows, LANES), F32),
        ]
        aliases = {4: 0, 5: 1} if given else None
        return fold("attn_out", args + list(given), shape, tasks, outs, aliases)


def fold1(x, y, across):
    shape = x.shape[1:]
    flat = full(shape[0])
    return fold(
        "fold1",
        [x, y, *across],
        shape,
        [
            ([(0, (0,)), (2, flat)], BF, [(0, (0,), flat)]),
            ([(1, (1,)), (3, flat)], BF, [(1, (1,), flat)]),
        ],
        [sds(x.shape, BF)] * 2,
        {0: 0, 1: 1},
    )


def expert_out(total, layer, layers, given, width):
    rows, broad = total.shape[1:]
    per = broad // width
    second = [
        (1, (layer, 0, pl.ds(q * rows, rows)), (ALL, pl.ds(q * width, width))) for q in range(per)
    ]
    outs = [sds((layers, 1, rows, broad), F32), sds((layers, 1, per * rows, width), F32)]
    return fold(
        "expert_out",
        [total, *given],
        (rows, broad),
        [
            ([(0, (0,))], F32, [(0, (layer, 0), full(rows))]),
            ([(0, (1,))], F32, second),
        ],
        outs,
        {1: 0, 2: 1} if given else None,
    )


def per_device(
    image_tokens,
    norm_gains,
    biases,
    w_qkv,
    w_out,
    w_router,
    router_noise,
    w_in,
    b_in,
    w_outexp,
    b_expout,
    routes,
    seat_order,
    cotangent,
):
    layers = w_qkv.shape[0]
    tokens, width = image_tokens.shape
    experts = w_router.shape[2]
    shards = lax.axis_size("dp")
    assert tokens == SEQ and experts == lax.axis_size("expert")
    assert width == HEADS * HEAD_DIM
    padded = up(tokens, 16)
    cap = 2 * tokens // experts
    cap_pad = up(cap + 2, 8)
    assert cap_pad <= LANES
    shard = w_qkv.shape[1]
    hidden_shard = w_outexp.shape[2]
    hidden = w_in.shape[3]
    per = hidden_shard // shard
    index = lax.axis_index("dp").astype(jnp.int32)
    me = index.reshape(1)
    z = lax.axis_index("expert").astype(jnp.int32).reshape(1)
    bits = axis_bits("dp", 2)
    four = bits == [2, 4] and shard % 16 == 0 and axis_bits("expert", 1) == [1, 2]

    Order.token = None

    def pack_attn(layer):
        return move(
            "pack_attn",
            [w_qkv, w_out],
            [
                (0, (layer, ALL, pl.ds(0, 2 * width)), 0, (0,), (shard, 2 * width)),
                (
                    0,
                    (layer, ALL, pl.ds(2 * width, width)),
                    0,
                    (1, ALL, pl.ds(0, width)),
                    (shard, width),
                ),
                (1, (layer,), 0, (1, ALL, pl.ds(width, width)), (shard, width)),
            ],
            [sds((2, shard, 2 * width), BF)],
        )[0]

    def pack_expert(layer):
        return move(
            "pack_expert",
            [w_in, w_outexp],
            [(0, (layer, 0), 0, (0,), (shard, hidden))]
            + [
                (
                    1,
                    (layer, 0, pl.ds(q * shard, shard)),
                    0,
                    (1, ALL, pl.ds(q * width, width)),
                    (shard, width),
                )
                for q in range(per)
            ],
            [sds((2, shard, hidden), BF)],
        )[0]

    whole = [(None, (0,)), (None, (1,))]

    def fetch_attn(layer):
        if four:
            return Gather(pack_attn(layer))
        right = jnp.concatenate([w_qkv[layer][:, 2 * width :], w_out[layer]], 1)
        attn = [gather_rows(v)[None] for v in (w_qkv[layer][:, : 2 * width], right)]
        return Weights(attn, whole)

    def fetch_expert(layer):
        if four:
            both = lax.all_gather(pack_expert(layer), "dp", axis=0)
            return Weights([both], [(OWNERS, (0, 1))])
        both = [gather_rows(w_in[layer, 0])[None], gather_rows(w_outexp[layer, 0])[None]]
        return Weights(both, whole)

    def attn_weights(gathered):
        return gathered.weights() if four else gathered

    last = layers - 1
    attn_w = [fetch_attn(0)]
    expert_w = [fetch_expert(layer) for layer in range(layers)]
    cols, rows = place_pairs(
        routes, seat_order.reshape(layers, tokens, 2), padded, cap, cap_pad, z
    )
    small = pack_small(norm_gains, biases, w_router, b_in, b_expout)
    grad, grad_seats = top_seats(z, cotangent, rows[last], cap_pad, experts)
    grad_seats = [lax.all_to_all(grad_seats, "expert", 0, 0, tiled=True)]
    if four:
        attn_w[0].turn()
        attn_w[0].send()
    small = lax.all_gather(small, "dp", axis=0)
    params = unpack_small(small, layers, shard, per, experts, grad_seats)
    if last > 0:
        attn_w.append(fetch_attn(1))

    saved = []
    x_args = (image_tokens,)
    if four:
        attn_w[0].cross()
    for layer in range(layers):
        vecs, router, bias_in, bias_oe = params[layer]
        attn_w[layer] = attn_weights(attn_w[layer])
        kept, sent = attn_fwd(
            me,
            layer,
            x_args,
            attn_w[layer],
            vecs,
            router,
            router_noise,
            cols[layer],
            rows[layer],
            cap_pad,
            cap,
        )
        x, x1, qkv, gates, ao = kept
        sent = exchange(sent)
        other_ao = None
        if four and layer < last:
            ao, other_ao = pick_columns(me, ao, shards)
            other_ao = swap(other_ao, "dp", 1)
        if layer < last:
            if four:
                attn_w[layer + 1].turn()
                attn_w[layer + 1].send(sent[1:])
            if layer + 1 < last:
                attn_w.append(fetch_attn(layer + 2))
        common = (x, x1, qkv, gates, ao, other_ao)
        if layer < last:
            (rh, slope, gate, out), made = expert_fwd(
                me, sent, expert_w[layer], bias_in, bias_oe, cap
            )
            if four:
                attn_w[layer + 1].cross(made[:1])
            returned = exchange(made)
            other_rh = swap(rh, "dp", 1) if four else None
            saved.append((*common, rh, other_rh, slope, gate, out))
            x_args = (x1, gates, cols[layer], returned)
        else:
            (rp, hd, give, made), d_rows = expert_both(
                me, z, sent, grad_seats[0], expert_w[layer], bias_in, bias_oe, cap, shards
            )
            if four:
                ao, other_ao = pick_columns(me, ao, shards)
                other_ao = swap(other_ao, "dp", 1)
            saved.append((x, x1, qkv, gates, ao, other_ao))

    attn_sums, expert_sums = [None] * layers, [None] * layers
    for layer in reversed(range(layers)):
        x, x1, qkv, gates, ao, other_ao = saved[layer][:6]
        vecs, router = params[layer][:2]
        sizes = (experts * cap_pad, w_in.shape[3])
        if layer == last:
            rows_at, pre_at = [(rp, 0)], [(rp, width)]
            h_at, out_at = [(hd, 0, True)], [(hd, sizes[1])]
            if four:
                other = swap(give, "dp", 1)
                h_at, out_at = h_at + [(other, 0, False)], out_at + [(other, sizes[1] // 2)]
                other = swap(rp, "dp", 1)
                rows_at, pre_at = rows_at + [(other, 0)], pre_at + [(other, width)]
            d_back = exchange(d_rows)
            g_expert, g_bias = expert_grads(
                me, rows_at, h_at, out_at, pre_at, sizes, four, shards
            )
        else:
            rh, other_rh, slope, gate, out = saved[layer][6:]
            if four:
                g_attn = attn_grads(me, z, *attn_operands, g_bias, shards, True)
                attn_sums[layer + 1] = AttnSum(hold(g_attn, grad_seats[1:]))
            gd, d_rows = expert_back(me, grad_seats, slope, gate, out, expert_w[layer], cap)
            d_back = exchange(d_rows)
            lefts, backs = [rh], [gd]
            if four:
                lefts, backs = [rh, other_rh], [gd, swap(gd, "dp", 1)]
            g_expert, g_bias = expert_grads(
                me,
                [(v, 0) for v in lefts],
                [(v, width, True) for v in lefts],
                [(v, 0) for v in backs],
                [(v, width) for v in backs],
                sizes,
                four,
                shards,
            )
        if four:
            (g_expert,) = hold(g_expert, d_back[1:])
            expert_sums[layer] = scatter_chips(g_expert)
        else:
            expert_sums[layer] = [scatter_rows(v) for v in g_expert]
        below = None
        if layer > 0:
            below = rows[layer - 1]
        (grad, back), grad_seats = attn_back(
            me,
            d_back,
            gates,
            router,
            grad,
            x,
            x1,
            qkv,
            cols[layer],
            vecs,
            attn_w[layer],
            below,
            tokens,
            cap,
        )
        grad_seats = exchange(grad_seats) if layer > 0 else None
        if four:
            attn_operands = (ao, back), (other_ao, swap(back, "dp", 1))
        else:
            g_attn = attn_grads(me, z, (ao, back), None, g_bias, shards, False)
            attn_sums[layer] = [sum_experts(scatter_rows(v)) for v in g_attn]

    if four:
        done_attn, smalls, done_expert = (), [None] * layers, ()
        for layer in reversed(range(1, layers)):
            done_expert = expert_out(expert_sums[layer], layer, layers, done_expert, width)
        (made,) = hold([made], [back])
        g_attn = attn_grads(me, z, *attn_operands, g_bias, shards, False)
        attn_sums[0] = AttnSum(g_attn)
        attn_sums[0].send_across()
        attn_sums[0].fold1()
        attn_sums[0].send_on()
        for layer in reversed(range(1, layers)):
            attn_sums[layer].cut(z)
        for layer in reversed(range(1, layers)):
            attn_sums[layer].halves()
    returned = lax.all_to_all(made, "expert", 0, 0, tiled=True)
    mixed = mix(z, saved[last][1], saved[last][3], cols[last], returned, tokens)
    if four:
        attn_sums[0].fold2()
        for layer in reversed(range(1, layers)):
            attn_sums[layer].halves()
        attn_sums[0].fold3(0, layers, done_attn)
        for layer in reversed(range(1, layers)):
            out = attn_sums[layer].put(z, layer, layers, done_attn)
            done_attn, smalls[layer] = out[:2], out[2]
        done_expert = expert_out(expert_sums[0], 0, layers, done_expert, width)
        grad_in, grad_oe = done_expert
    else:
        grad_in = jnp.stack([item[0] for item in expert_sums])[:, None].astype(F32)
        grad_oe = jnp.stack([item[1] for item in expert_sums])[:, None].astype(F32)
    if four:
        smalls = {n: smalls[n] for n in range(1, layers)}
        out = attn_sums[0].finish(z, 0, layers, done_attn, smalls, experts, per)
        grad_qkv, grad_out, gains, shifts, grad_router, grad_bin, grad_boe = out
    else:
        left = jnp.stack([item[0] for item in attn_sums])
        right = jnp.stack([item[1] for item in attn_sums])
        grad_qkv = jnp.concatenate([left[:, :, : 2 * width], right[:, :, :width]], 2)
        grad_out = right[:, :, width : 2 * width]
        smalls = [right[layer, :, 2 * width :] for layer in range(layers)]
        small = small_out(smalls, z, experts, per)
        gains, shifts, grad_router, grad_bin, grad_boe = small
    return (
        mixed,
        grad,
        gains,
        jnp.transpose(shifts, (1, 0, 2)),
        grad_qkv,
        grad_out,
        jnp.transpose(grad_router, (0, 2, 1)),
        grad_in,
        grad_bin,
        grad_oe,
        grad_boe,
    )


def solution(mesh):
    return jax.shard_map(
        per_device,
        mesh=mesh,
        in_specs=(
            P(("dp", "expert"), None),
            P(None, None, "dp"),
            P(None, None, "dp"),
            P(None, "dp", None),
            P(None, "dp", None),
            P(None, "dp", None),
            P(None, ("dp", "expert"), None),
            P(None, "expert", "dp", None),
            P(None, "expert", "dp"),
            P(None, "expert", "dp", None),
            P(None, "expert", "dp"),
            P(None, ("dp", "expert"), None),
            P(None, ("dp", "expert"), None),
            P(("dp", "expert"), None),
        ),
        out_specs=(
            P(("dp", "expert"), None),
            P(("dp", "expert"), None),
            P(None, None, "dp"),
            P(None, None, "dp"),
            P(None, "dp", None),
            P(None, "dp", None),
            P(None, "dp", None),
            P(None, "expert", "dp", None),
            P(None, "expert", "dp"),
            P(None, "expert", "dp", None),
            P(None, "expert", "dp"),
        ),
        check_vma=False,
    )
```

```python
import functools

import jax
import jax.numpy as jnp
from jax import lax
from jax.experimental import pallas as pl
from jax.experimental.pallas import tpu as pltpu
from jax.sharding import PartitionSpec as P

HEADS = 12
HEAD_DIM = 64
SEQ = 197
EPS = 1e-06
BF = jnp.bfloat16
F32 = jnp.float32
LANES = 128
NEG = -1e30
VMEM_LIMIT = 60 * 1024 * 1024
LIMITS = {name: 16 * 1024 * 1024 for name in ("fold1", "fold2", "fold3", "mix", "attn_last")}
LIMITS["attn_grads"] = 24 * 1024 * 1024
LIMITS["pick_columns"] = 63 * 1024 * 1024


def up(value, step):
    return -(-value // step) * step


def dot(left, right):
    return lax.dot_general(left, right, (((1,), (0,)), ((), ())), preferred_element_type=F32)


def dot_nt(left, right):
    return lax.dot_general(left, right, (((1,), (1,)), ((), ())), preferred_element_type=F32)


def dot_tn(left, right):
    return lax.dot_general(left, right, (((0,), (0,)), ((), ())), preferred_element_type=F32)


def norm_rows(x):
    centered = x - jnp.mean(x, -1, keepdims=True)
    rstd = lax.rsqrt(jnp.mean(centered * centered, -1, keepdims=True) + EPS)
    return centered * rstd, rstd


def norm_back(grad_hat, normed, rstd):
    return rstd * (
        grad_hat
        - jnp.mean(grad_hat, -1, keepdims=True)
        - normed * jnp.mean(grad_hat * normed, -1, keepdims=True)
    )


def split(value):
    high = value.astype(BF)
    return high, (value - high.astype(F32)).astype(BF)


def join(refs):
    return jnp.concatenate([ref[...].astype(F32) for ref in refs], 0).astype(BF)


def part(value, refs):
    rows = refs[0].shape[0]
    for number, ref in enumerate(refs):
        ref[...] = value[number * rows : (number + 1) * rows].astype(ref.dtype)


def seat_mask(cols_ref, pair, seats):
    column = cols_ref[:, pair : pair + 1]
    return lax.broadcasted_iota(jnp.int32, (column.shape[0], seats), 1) == column


def token_mask(rows_ref, pair, seats):
    row = rows_ref[pair : pair + 1, :]
    return lax.broadcasted_iota(jnp.int32, (seats, row.shape[1]), 0) == row


def one(mask):
    return jnp.where(mask, 1.0, 0.0).astype(BF)


def pair_gate(gates, cols_ref, pair):
    route = cols_ref[:, 2 + pair : 3 + pair]
    lanes = lax.broadcasted_iota(jnp.int32, gates.shape, 1)
    return jnp.sum(jnp.where(lanes == route, gates, 0.0), -1, keepdims=True)


def combine(x1, gates, cols_ref, returned):
    total = x1
    for pair in range(2):
        piece = dot(one(seat_mask(cols_ref, pair, returned.shape[0])), returned)
        total = total + pair_gate(gates, cols_ref, pair) * piece
    return total


def rows_to_seats(rows_ref, seats, values):
    chosen = jnp.logical_or(token_mask(rows_ref, 0, seats), token_mask(rows_ref, 1, seats))
    return dot(one(chosen), values)


def with_note(block, cap, note):
    base = cap // 8 * 8
    tail = block[base:]
    left = tail[:, 0:LANES]
    row = lax.broadcasted_iota(jnp.int32, left.shape, 0)
    high = note.astype(BF).astype(F32)
    left = jnp.where(row == cap - base, high, left)
    left = jnp.where(row == cap - base + 1, note - high, left)
    return jnp.concatenate([block[:base], jnp.concatenate([left, tail[:, LANES:]], 1)], 0)


def note_of(block, cap):
    return block[cap : cap + 1, 0:LANES] + block[cap + 1 : cap + 2, 0:LANES]


def as_column(note, rows):
    shape = (rows, LANES)
    same = lax.broadcasted_iota(jnp.int32, shape, 0) == lax.broadcasted_iota(jnp.int32, shape, 1)
    return jnp.sum(jnp.where(same, note, 0.0), -1, keepdims=True)


def lane_sums(value):
    rows, width = value.shape
    value = jnp.concatenate([value, jnp.zeros((LANES - rows, width), F32)], 0)
    ones = jnp.ones((8, width), BF)
    high, low = split(value)
    return (dot_nt(ones, high) + dot_nt(ones, low))[0:1, :]


def near_lanes(cols_ref, pair, block, cap_pad):
    column = cols_ref[:, pair : pair + 1] - block * cap_pad
    lanes = lax.broadcasted_iota(jnp.int32, (column.shape[0], LANES), 1)
    return jnp.logical_and(lanes == column, lanes < cap_pad)


def head_masks():
    lanes = lax.broadcasted_iota(jnp.int32, (1, 2 * HEAD_DIM), 1)
    return (lanes < HEAD_DIM, lanes >= HEAD_DIM)


def stacked(value, masks):
    return jnp.concatenate([jnp.where(mask, value, 0).astype(value.dtype) for mask in masks], 0)


def unstacked(value, masks):
    rows = value.shape[0] // 2
    return jnp.where(masks[0], value[:rows], value[rows:])


def pair_probs(query, keys, masks, tokens):
    query = stacked(query, masks).astype(F32) * HEAD_DIM ** (-0.5)
    scores = dot_nt(query.astype(BF), keys)
    lanes = lax.broadcasted_iota(jnp.int32, scores.shape, 1)
    scores = jnp.where(lanes < tokens, scores, NEG)
    raised = jnp.exp(scores - jnp.max(scores, -1, keepdims=True))
    return raised * (1.0 / jnp.sum(raised, -1, keepdims=True))


VM = pl.BlockSpec(memory_space=pltpu.VMEM)
ANY = pl.BlockSpec(memory_space=pl.ANY)
HBM = pl.BlockSpec(memory_space=pltpu.HBM)
SM = pl.BlockSpec(memory_space=pltpu.SMEM)


def sds(shape, dtype):
    return jax.ShapeDtypeStruct(tuple(shape), dtype)


class Order:
    token = None


LOAD = "load"
STORE = "store"


class Load:
    def __init__(self, source, held, sem):
        self.copy, self.held, self.came = pltpu.make_async_copy(source, held, sem), held, False
        self.shape = held.shape
        self.copy.start()

    def wait(self):
        if not self.came:
            self.copy.wait()
            self.came = True

    def __getitem__(self, index):
        self.wait()
        return self.held[index]


class Store:
    def __init__(self, target, held, sems):
        self.target, self.held, self.sems, self.copies = target, held, sems, []
        self.shape, self.dtype = held.shape, held.dtype

    def __getitem__(self, index):
        return self.held[index]

    def __setitem__(self, index, value):
        self.held[index] = value

    def send(self, *index):
        number = len(self.copies)
        copy = pltpu.make_async_copy(
            self.held.at[index], self.target.at[index], self.sems.at[number]
        )
        copy.start()
        self.copies.append(copy)

    def finish(self):
        if not self.copies:
            self.send(*[slice(None)] * len(self.shape))


PARTS = 8


def call(kernel, name, args, specs, outs, out_specs, scratch, aliases=None):
    after = []
    if Order.token is not None and not any(Order.token is arg for arg in args):
        after = [Order.token]
    given = len(args)
    single = not isinstance(outs, (tuple, list))
    results = [outs] if single else list(outs)
    out_kinds = [out_specs] if single else list(out_specs)
    loads = [i for i, spec in enumerate(specs) if spec is LOAD]
    stores = [i for i, spec in enumerate(out_kinds) if spec is STORE]
    extra = [pltpu.VMEM(args[i].shape, args[i].dtype) for i in loads]
    extra += [pltpu.VMEM(results[i].shape, results[i].dtype) for i in stores]
    extra += [pltpu.SemaphoreType.DMA((max(len(loads), 1),))]
    extra += [pltpu.SemaphoreType.DMA((max(PARTS * len(stores), 1),))]

    def body(*refs):
        ins = list(refs[:given])
        rest = list(refs[given + len(after) :])
        made, own = rest[: len(results)], rest[len(results) : len(rest) - len(extra)]
        held = rest[len(rest) - len(extra) :]
        load_sems, store_sems = held[-2:]
        for n, i in enumerate(loads):
            ins[i] = Load(ins[i], held[n], load_sems.at[n])
        for n, i in enumerate(stores):
            sems = store_sems.at[pl.ds(PARTS * n, PARTS)]
            made[i] = Store(made[i], held[len(loads) + n], sems)
        kernel(*ins, *made, *own)
        for i in loads:
            ins[i].wait()
        for i in stores:
            made[i].finish()
        for i in stores:
            for copy in made[i].copies:
                copy.wait()

    result = pl.pallas_call(
        body,
        name=name,
        in_specs=[HBM if spec is LOAD else spec for spec in specs] + [ANY] * len(after),
        out_specs=ANY if single and out_specs is STORE else (
            out_specs if single else [ANY if spec is STORE else spec for spec in out_kinds]
        ),
        out_shape=outs,
        scratch_shapes=list(scratch) + extra,
        input_output_aliases=aliases or {},
        compiler_params=pltpu.CompilerParams(
            vmem_limit_bytes=LIMITS.get(name, VMEM_LIMIT)
        ),
    )(*args, *after)
    Order.token = result if single else min(result, key=lambda value: value.size)
    return result


def hold(values, after):
    def kernel(*refs):
        pass

    return call(
        kernel,
        "hold",
        [*values, *after],
        [ANY] * (len(values) + len(after)),
        [sds(value.shape, value.dtype) for value in values],
        [ANY] * len(values),
        [],
        {i: i for i in range(len(values))},
    )


def move(name, args, copies, outs, aliases=None):
    total = len(copies)

    def kernel(*refs):
        ins, rest = refs[: len(args)], refs[len(args) :]
        results, held = rest[: len(outs)], rest[len(outs) : len(outs) + total]
        in_sems, out_sems = rest[-2:]
        loads = [
            pltpu.make_async_copy(ins[i].at[where], held[n], in_sems.at[n])
            for n, (i, where, _, _, _) in enumerate(copies)
        ]
        stores = [
            pltpu.make_async_copy(held[n], results[o].at[into], out_sems.at[n])
            for n, (_, _, o, into, _) in enumerate(copies)
        ]
        start(loads)
        for load, store in zip(loads, stores):
            load.wait()
            store.start()
        wait(stores)

    return call(
        kernel,
        name,
        args,
        [ANY] * len(args),
        outs,
        [ANY] * len(outs),
        [pltpu.VMEM(shape, BF) for *_, shape in copies]
        + [pltpu.SemaphoreType.DMA((total,)), pltpu.SemaphoreType.DMA((total,))],
        aliases,
    )


def fold(name, args, block, tasks, outs, aliases=None):
    terms = [(t, term) for t, (listed, _, _) in enumerate(tasks) for term in listed]
    writes = [(t, write) for t, (_, _, listed) in enumerate(tasks) for write in listed]
    wide = [t for t, task in enumerate(tasks) if task[1] == F32]
    slim = [t for t, task in enumerate(tasks) if task[1] != F32]

    last = name.endswith("_out")
    mark = [sds((8, LANES), F32)] if last else []

    def kernel(*refs):
        ins, rest = refs[: len(args)], refs[len(args) :]
        results = rest[: len(outs)]
        loaded, wide_ref, slim_ref, in_sems, out_sems = rest[len(outs) + len(mark) :]
        for ref in rest[len(outs) : len(outs) + len(mark)]:
            ref[...] = jnp.zeros_like(ref)
        loads = [
            pltpu.make_async_copy(ins[i].at[where], loaded.at[n], in_sems.at[n])
            for n, (_, (i, where)) in enumerate(terms)
        ]
        for copy in loads:
            copy.start()
        stores = []
        for t, (_, kind, _) in enumerate(tasks):
            total = None
            for n, (task, _) in enumerate(terms):
                if task == t:
                    loads[n].wait()
                    piece = loaded[n].astype(F32)
                    total = piece if total is None else total + piece
            holder = wide_ref.at[wide.index(t)] if kind == F32 else slim_ref.at[slim.index(t)]
            holder[...] = total.astype(kind)
            for n, (task, (o, into, within)) in enumerate(writes):
                if task == t:
                    copy = pltpu.make_async_copy(
                        holder.at[within], results[o].at[into], out_sems.at[n]
                    )
                    copy.start()
                    stores.append(copy)
        for copy in stores:
            copy.wait()

    result = call(
        kernel,
        name,
        args,
        [ANY] * len(args),
        list(outs) + mark,
        [HBM if last else ANY] * len(outs) + [VM] * len(mark),
        [
            pltpu.VMEM((len(terms), *block), BF),
            pltpu.VMEM((max(len(wide), 1), *(block if wide else (16, LANES))), F32),
            pltpu.VMEM((max(len(slim), 1), *(block if slim else (16, LANES))), BF),
            pltpu.SemaphoreType.DMA((len(terms),)),
            pltpu.SemaphoreType.DMA((len(writes),)),
        ],
        aliases=aliases,
    )
    return result[: len(outs)]


ALL = slice(None)


class Weights:
    def __init__(self, arrays, places):
        self.arrays, self.places = list(arrays), places


OWNERS = -1


def attn_targets(width, rows, wqkv, wout):
    return {
        0: [(wqkv, 0, 2 * width, 0, rows, 0)],
        1: [(wqkv, 0, width, 2 * width, rows, 0), (wout, width, width, 0, rows, 0)],
    }


def expert_targets(width, hidden, rows, whole, win, woe):
    if whole:
        return {0: [(win, 0, hidden, 0, rows, 0)], 1: [(woe, 0, width, 0, rows, 0)]}
    per = hidden // width
    return {
        0: [(win, 0, hidden, 0, rows, 0)],
        1: [(woe, q * width, width, 0, per * rows, q * rows) for q in range(per)],
    }


class Chunks:
    def __init__(self, refs, weights, width, hidden, rows, whole, win, woe, sems, more=()):
        per = hidden // width
        self.parts = []
        if whole:
            copies = fetch(refs, weights, None, expert_targets(width, hidden, rows, True, win, woe), 0, sems)
            copies += fetch(
                refs, weights, None, expert_targets(width, hidden, rows, True, win, woe), 1, sems
            )
            self.parts = [copies] + [[] for _ in range(per - 1)]
        else:
            ref = refs[0]
            shards = ref.shape[0]
            for c in range(per):
                here = pl.ds(c * width, width)
                copies = [
                    pltpu.make_async_copy(
                        ref.at[d, 0, :, here], win.at[pl.ds(d * rows, rows), here], sems.at[d]
                    )
                    for d in range(shards)
                ]
                first = c * shards // per
                for n in range(shards):
                    d, q = first + n // per, n % per
                    copies.append(
                        pltpu.make_async_copy(
                            ref.at[d, 1, :, pl.ds(q * width, width)],
                            woe.at[pl.ds((d * per + q) * rows, rows)],
                            sems.at[shards + n],
                        )
                    )
                self.parts.append(copies)
        for copies, extra in zip(self.parts, more):
            copies.append(extra)
        start(self.parts[0])

    def take(self, c):
        wait(self.parts[c])
        if c + 1 < len(self.parts):
            start(self.parts[c + 1])


def copies_in(weights):
    return 4 * sum(
        len(parts) if array.ndim == 3 else array.shape[0]
        for array, (off, parts) in zip(weights.arrays, weights.places)
    )


def fetch(refs, weights, me, targets, part_number, sems):
    copies = []
    for ref, (off, parts) in zip(refs, weights.places):
        rows = ref.shape[-2]
        if off == OWNERS:
            sources = [(d, (d, part_number)) for d in range(ref.shape[0])]
        elif isinstance(off, tuple):
            sources = [(me ^ o, (k, part_number)) for k, o in enumerate(off)]
        elif part_number in parts:
            at = None if off is None else me ^ off
            sources = [(at, (parts.index(part_number),))]
        else:
            sources = []
        for at, where in sources:
            for scratch, first, size, into, times, plus in targets[part_number]:
                place = 0 if at is None else at * times + plus
                if off not in (None, OWNERS):
                    place = pl.multiple_of(place, 16)
                copies.append(
                    pltpu.make_async_copy(
                        ref.at[(*where, ALL, pl.ds(first, size))],
                        scratch.at[pl.ds(place, rows), pl.ds(into, size)],
                        sems.at[len(copies)],
                    )
                )
    return copies


def start(copies):
    for copy in copies:
        copy.start()


def wait(copies):
    for copy in copies:
        copy.wait()


def small_rows(per, experts):
    return up(7 + experts + per + 1, 8)


def pack_small(norm_gains, biases, w_router, b_in, b_expout):
    layers, shard, experts = w_router.shape
    per = b_in.shape[2] // shard
    height = small_rows(per, experts)

    def kernel(gain_ref, bias_ref, router_ref, in_ref, oe_ref, out, square):
        out[...] = jnp.zeros_like(out)
        for layer in range(layers):
            at = layer * height
            out[at : at + 2, 0:shard] = gain_ref[layer]
            out[at + 2 : at + 7, 0:shard] = bias_ref[layer]
            square[...] = jnp.zeros_like(square)
            square[0:shard, 0:experts] = router_ref[layer]
            turned = square[...].T
            out[at + 7 : at + 7 + experts, :] = turned[0:experts, :]
            at = at + 7 + experts
            for q in range(per):
                out[at + q : at + q + 1, 0:shard] = in_ref[layer, :, q * shard : (q + 1) * shard]
            out[at + per : at + per + 1, 0:shard] = oe_ref[layer]

    return call(
        kernel,
        "pack_small",
        [norm_gains, biases, w_router, b_in, b_expout],
        [VM] * 5,
        sds((layers * height, LANES), F32),
        VM,
        [pltpu.VMEM((LANES, LANES), F32)],
    )


def unpack_small(gathered, layers, shard, per, experts, after):
    shards = gathered.shape[0]
    width = shards * shard
    height = small_rows(per, experts)

    def kernel(ref, *refs):
        refs = refs[len(after) :]
        tall = refs[-1]
        for layer in range(layers):
            vec, router, bias_in, bias_oe = refs[4 * layer : 4 * layer + 4]
            at = layer * height
            vec[...] = jnp.zeros_like(vec)
            tall[...] = jnp.zeros_like(tall)
            for d in range(shards):
                here = slice(d * shard, (d + 1) * shard)
                vec[0:7, here] = ref[d, at : at + 7, 0:shard]
                tall[0:experts, here] = ref[d, at + 7 : at + 7 + experts, 0:shard]
                row = at + 7 + experts
                for q in range(per):
                    first = (d * per + q) * shard
                    bias_in[:, first : first + shard] = ref[d, row + q : row + q + 1, 0:shard]
                bias_oe[:, here] = ref[d, row + per : row + per + 1, 0:shard]
            router[...] = tall[...].T.astype(BF)

    shapes = []
    for _ in range(layers):
        shapes += [
            sds((8, width), F32),
            sds((width, LANES), BF),
            sds((1, width * per), F32),
            sds((1, width), F32),
        ]
    outs = call(
        kernel,
        "unpack_small",
        [gathered, *after],
        [VM] + [ANY] * len(after),
        shapes,
        [VM] * len(shapes),
        [pltpu.VMEM((LANES, width), F32)],
    )
    return [outs[4 * layer : 4 * layer + 4] for layer in range(layers)]


def place_pairs(routes, seat_order, padded, cap, cap_pad, z):
    layers, tokens, _ = routes.shape
    tall = up(padded, LANES)

    def kernel(z_ref, route_ref, order_ref, *refs):
        outs, wide = refs[:-1], refs[-1]
        lanes = lax.broadcasted_iota(jnp.int32, (tokens, LANES), 1)
        lanes_tall = lax.broadcasted_iota(jnp.int32, (tall, LANES), 1)
        for layer in range(layers):
            given = jnp.full((tokens, LANES), -1.0, F32)
            for k in range(2):
                given = jnp.where(lanes == k, route_ref[layer, :, k : k + 1].astype(F32), given)
                given = jnp.where(lanes == 2 + k, order_ref[layer, :, k : k + 1].astype(F32), given)
            wide[...] = jnp.full((tall, LANES), -1.0, F32)
            wide[0:tokens, :] = given
            table = wide[...]
            turned = table.T
            seats = []
            for k in range(2):
                expert, order = table[:, k : k + 1], table[:, 2 + k : 3 + k]
                rank = jnp.zeros((tall, 1), F32)
                for j in range(2):
                    ahead = jnp.logical_and(
                        turned[j : j + 1, :] == expert, turned[2 + j : 3 + j, :] < order
                    )
                    rank = rank + jnp.sum(jnp.where(ahead, 1.0, 0.0), -1, keepdims=True)
                expert, rank = expert.astype(jnp.int32), rank.astype(jnp.int32)
                near = jnp.bitwise_xor(expert, z_ref[0])
                good = jnp.logical_and(expert >= 0, rank < cap)
                seats.append(jnp.where(good, near * cap_pad + rank, -1).astype(F32))
            table = jnp.where(lanes_tall == 2, table[:, 0:1], table)
            table = jnp.where(lanes_tall == 3, wide[:, 1:2], table)
            table = jnp.where(lanes_tall == 0, seats[0], table)
            table = jnp.where(lanes_tall == 1, seats[1], table)
            cols, rows = outs[2 * layer], outs[2 * layer + 1]
            cols[...] = table[0:padded, :].astype(jnp.int32)
            rows[...] = table.T[0:8, 0:padded].astype(jnp.int32)

    shapes = []
    for _ in range(layers):
        shapes += [sds((padded, LANES), jnp.int32), sds((8, padded), jnp.int32)]
    outs = call(
        kernel,
        "place_pairs",
        [z, routes, seat_order],
        [SM, VM, VM],
        shapes,
        [VM] * len(shapes),
        [pltpu.VMEM((tall, LANES), F32)],
    )
    return outs[0::2], outs[1::2]


def attn_fwd(me, layer, x_args, weights, vecs, router, noise, cols, rows, cap, used):
    first = len(x_args) == 1
    padded, width = cols.shape[0], vecs.shape[1]
    tokens, experts = noise.shape[1:]
    seats = experts * cap
    owners = 0 if first else len(x_args[3])
    count = len(weights.arrays)
    shard = weights.arrays[0].shape[-2]

    def kernel(*refs):
        refs = list(refs)
        me_ref = refs.pop(0)
        if first:
            tok_ref = refs.pop(0)
        else:
            below_x1, below_gates, below_cols = refs.pop(0), refs.pop(0), refs.pop(0)
            below_blocks = [refs.pop(0) for _ in range(owners)]
        w_refs = [refs.pop(0) for _ in range(count)]
        vec_ref, router_ref, noise_ref, cols_ref, rows_ref = (refs.pop(0) for _ in range(5))
        x_out, x1_out, qkv_out, gates_out, ao_out = (refs.pop(0) for _ in range(5))
        seat_outs = [refs.pop(0) for _ in range(experts)]
        wqkv, wout, sems, more_sems = refs
        targets = attn_targets(width, shard, wqkv, wout)
        left = fetch(w_refs, weights, me_ref[0], targets, 0, sems)
        right = fetch(w_refs, weights, me_ref[0], targets, 1, more_sems)
        start(left + right)
        vec = lambda k: vec_ref[k : k + 1, :]
        if first:
            x_out[...] = jnp.zeros_like(x_out)
            x_out[0:tokens, :] = tok_ref[...].astype(F32)
            x = x_out[...]
        else:
            x = combine(below_x1[...], below_gates[...], below_cols, join(below_blocks))
            x_out[...] = x
        normed, rstd = norm_rows(x)
        a_low = (normed * vec(0) + vec(2)).astype(BF)
        ao_out[:, 0:width] = a_low
        gates_out[...] = jnp.zeros_like(gates_out)
        gates_out[0:tokens, 0:experts] = noise_ref[layer]
        noise_here = gates_out[...]
        wait(left)
        for k in range(3):
            if k == 2:
                wait(right)
            piece = dot(a_low, wqkv[:, k * width : (k + 1) * width])
            if k == 0:
                piece = piece + vec(4)
            if k == 2:
                piece = piece + vec(5)
            qkv_out[:, k * width : (k + 1) * width] = piece.astype(BF)
        masks = head_masks()
        for two in range(HEADS // 2):
            at = two * 2 * HEAD_DIM
            query = qkv_out[:, at : at + 2 * HEAD_DIM]
            keys = qkv_out[:, width + at : width + at + 2 * HEAD_DIM]
            values = qkv_out[:, 2 * width + at : 2 * width + at + 2 * HEAD_DIM]
            probs = pair_probs(query, keys, masks, tokens).astype(BF)
            mixed = unstacked(dot(probs, values), masks)
            ao_out[:, width + at : width + at + 2 * HEAD_DIM] = mixed.astype(BF)
        x1 = x + dot(ao_out[:, width : 2 * width], wout[...]) + vec(6)
        x1_out[...] = x1
        normed2, rstd2 = norm_rows(x1)
        moe = normed2 * vec(1) + vec(3)
        high, low = split(moe)
        logits = dot(high, router_ref[...]) + dot(low, router_ref[...]) + noise_here
        lanes = lax.broadcasted_iota(jnp.int32, logits.shape, 1)
        logits = jnp.where(lanes < experts, logits, NEG)
        raised = jnp.exp(logits - jnp.max(logits, -1, keepdims=True))
        gates = raised / jnp.sum(raised, -1, keepdims=True)
        gates_out[...] = gates
        ao_out[:, 2 * width : 3 * width] = high
        sent = rows_to_seats(rows_ref, seats, high)
        chosen = [pair_gate(gates, cols_ref, pair) for pair in range(2)]
        for block, ref in enumerate(seat_outs):
            note = jnp.zeros((1, LANES), F32)
            for pair in range(2):
                here = near_lanes(cols_ref, pair, block, cap)
                note = note + jnp.sum(jnp.where(here, chosen[pair], 0.0), 0, keepdims=True)
            piece = sent[block * cap : (block + 1) * cap]
            ref[...] = with_note(piece, used, note).astype(BF)

    args = [me]
    specs = [SM]
    if first:
        args += [x_args[0]]
        specs += [VM]
    else:
        args += [x_args[0], x_args[1], x_args[2], *x_args[3]]
        specs += [VM] * (3 + owners)
    args += [*weights.arrays, vecs, router, noise, cols, rows]
    specs += [ANY] * count + [VM] * 5
    outs = [
        sds((padded, width), F32),
        sds((padded, width), F32),
        sds((padded, 3 * width), BF),
        sds((padded, LANES), F32),
        sds((padded, 3 * width), BF),
    ] + [sds((cap, width), BF)] * experts
    result = call(
        kernel,
        "attn_fwd",
        args,
        specs,
        outs,
        [VM] * len(outs),
        [
            pltpu.VMEM((width, 3 * width), BF),
            pltpu.VMEM((width, width), BF),
            pltpu.SemaphoreType.DMA((copies_in(weights),)),
            pltpu.SemaphoreType.DMA((copies_in(weights),)),
        ],
    )
    return result[:5], result[5:]


def expert_fwd(me, seat_blocks, weights, bias_in, bias_oe, used):
    owners = len(seat_blocks)
    cap, width = seat_blocks[0].shape
    seats = owners * cap
    hidden = bias_in.shape[1]
    count = len(weights.arrays)
    shard = weights.arrays[0].shape[-2]
    whole = weights.places[0][0] is None
    step = width

    def kernel(*refs):
        refs = list(refs)
        me_ref = refs.pop(0)
        seat_refs = [refs.pop(0) for _ in range(owners)]
        w_refs = [refs.pop(0) for _ in range(count)]
        bin_ref, boe_ref = refs.pop(0), refs.pop(0)
        rh_out, slope_out, gate_out, made_out = (refs.pop(0) for _ in range(4))
        outs = [refs.pop(0) for _ in range(owners)]
        win, woe, sems = refs
        chunks = Chunks(w_refs, weights, width, hidden, shard, whole, win, woe, sems)
        blocks = [ref[...].astype(F32) for ref in seat_refs]
        rows = jnp.concatenate(blocks, 0).astype(BF)
        rh_out[:, 0:width] = rows
        rh_out.send(ALL, pl.ds(0, width))
        columns = [as_column(note_of(block, used), cap) for block in blocks]
        gate_out[...] = jnp.broadcast_to(jnp.concatenate(columns, 0), gate_out.shape)
        total_out = None
        for at in range(0, hidden, step):
            chunks.take(at // step)
            pre = dot(rows, win[:, at : at + step]) + bin_ref[:, at : at + step]
            square = pre * pre
            bend = jnp.tanh(0.7978845608028654 * (pre + 0.044715 * square * pre))
            h = (0.5 * pre * (1.0 + bend)).astype(BF)
            slope = 0.5 * (1.0 + bend) + 0.5 * pre * (1.0 - bend * bend) * (
                0.7978845608028654 * (1.0 + 0.134145 * square)
            )
            rh_out[:, width + at : width + at + step] = h
            slope_out[:, at : at + step] = slope.astype(BF)
            rh_out.send(ALL, pl.ds(width + at, step))
            slope_out.send(ALL, pl.ds(at, step))
            piece = dot(h, woe[at : at + step, :])
            total_out = piece if total_out is None else total_out + piece
        total_out = total_out + boe_ref[...]
        made_out[...] = total_out.astype(BF)
        part(total_out, outs)

    shapes = [
        sds((seats, width + hidden), BF),
        sds((seats, hidden), BF),
        sds((seats, LANES), F32),
        sds((seats, width), BF),
    ] + [sds((cap, width), BF)] * owners
    result = call(
        kernel,
        "expert_fwd",
        [me, *seat_blocks, *weights.arrays, bias_in, bias_oe],
        [SM] + [LOAD] * owners + [ANY] * count + [LOAD] * 2,
        shapes,
        [STORE] * len(shapes),
        [
            pltpu.VMEM((width, hidden), BF),
            pltpu.VMEM((hidden, width), BF),
            pltpu.SemaphoreType.DMA((2 * copies_in(weights),)),
        ],
    )
    return result[:4], result[4:]


def expert_both(me, z, seat_blocks, grads, weights, bias_in, bias_oe, used, shards):
    size = bias_in.shape[1] // shards
    owners = len(seat_blocks)
    cap, width = seat_blocks[0].shape
    seats = owners * cap
    hidden = bias_in.shape[1]
    count = len(weights.arrays)
    shard = weights.arrays[0].shape[-2]
    whole = weights.places[0][0] is None
    step = width

    def kernel(*refs):
        refs = list(refs)
        me_ref, z_ref = refs.pop(0), refs.pop(0)
        seat_refs = [refs.pop(0) for _ in range(owners)]
        grad_ref = refs.pop(0)
        w_refs = [refs.pop(0) for _ in range(count)]
        bin_ref, boe_ref = refs.pop(0), refs.pop(0)
        rp_out, hd_out, give_out, made_out = (refs.pop(0) for _ in range(4))
        outs = [refs.pop(0) for _ in range(owners)]
        win, woe, slopes, sems = refs
        chunks = Chunks(w_refs, weights, width, hidden, shard, whole, win, woe, sems)
        blocks = [ref[...].astype(F32) for ref in seat_refs]
        rows = jnp.concatenate(blocks, 0).astype(BF)
        rp_out[:, 0:width] = rows
        other = 1 - (me_ref[0] & 1)
        gate = jnp.concatenate([as_column(note_of(block, used), cap) for block in blocks], 0)
        total_out = None
        for at in range(0, hidden, step):
            chunks.take(at // step)
            pre = dot(rows, win[:, at : at + step]) + bin_ref[:, at : at + step]
            square = pre * pre
            bend = jnp.tanh(0.7978845608028654 * (pre + 0.044715 * square * pre))
            h = (0.5 * pre * (1.0 + bend)).astype(BF)
            slope = 0.5 * (1.0 + bend) + 0.5 * pre * (1.0 - bend * bend) * (
                0.7978845608028654 * (1.0 + 0.134145 * square)
            )
            hd_out[:, at : at + step] = h
            slopes[:, at : at + step] = slope.astype(BF)
            piece = dot(h, woe[at : at + step, :])
            total_out = piece if total_out is None else total_out + piece
        made = (total_out + boe_ref[...]).astype(BF).astype(F32)
        for k in range(owners):
            made_out.held[z_ref[0] ^ k] = made[k * cap : (k + 1) * cap].astype(BF)
        given = [grad_ref[z_ref[0] ^ k].astype(F32) for k in range(owners)]
        given = jnp.concatenate(given, 0)
        grad = (given * gate).astype(BF)
        hd_out[:, hidden : hidden + width] = grad
        for k in range(shards // 2):
            first = pl.multiple_of((2 * k + other) * size, LANES)
            give_out[:, k * size : (k + 1) * size] = hd_out.held[:, pl.ds(first, size)]
        give_out[:, hidden // 2 : hidden // 2 + width] = grad
        hd_out.send(ALL, ALL)
        give_out.send(ALL, ALL)
        made_out.send(ALL)
        notes = given * made
        notes = [lane_sums(notes[k * cap : (k + 1) * cap]) for k in range(owners)]
        total_out = None
        for at in range(0, hidden, step):
            d_hidden = dot_nt(grad, woe[at : at + step, :])
            d_pre = (d_hidden * slopes[:, at : at + step].astype(F32)).astype(BF)
            rp_out[:, width + at : width + at + step] = d_pre
            piece = dot_nt(d_pre, win[:, at : at + step])
            total_out = piece if total_out is None else total_out + piece
            if at == hidden // 2 - step:
                rp_out.send(ALL, pl.ds(0, width + hidden // 2))
        rp_out.send(ALL, pl.ds(width + hidden // 2, hidden // 2))
        for k, ref in enumerate(outs):
            ref[...] = with_note(total_out[k * cap : (k + 1) * cap], used, notes[k]).astype(BF)

    shapes = [
        sds((seats, width + hidden), BF),
        sds((seats, hidden + width), BF),
        sds((seats, hidden // 2 + width), BF),
        sds((owners, cap, width), BF),
    ] + [sds((cap, width), BF)] * owners
    result = call(
        kernel,
        "expert_both",
        [me, z, *seat_blocks, grads, *weights.arrays, bias_in, bias_oe],
        [SM, SM] + [LOAD] * (owners + 1) + [ANY] * count + [LOAD] * 2,
        shapes,
        [STORE] * len(shapes),
        [
            pltpu.VMEM((width, hidden), BF),
            pltpu.VMEM((hidden, width), BF),
            pltpu.VMEM((seats, hidden), BF),
            pltpu.SemaphoreType.DMA((2 * copies_in(weights),)),
        ],
    )
    return result[:4], result[4:]


def top_seats(z, cotangent, rows, cap, experts):
    tokens, width = cotangent.shape
    padded = rows.shape[1]

    def kernel(z_ref, cot_ref, rows_ref, grad_out, out):
        grad_out[...] = jnp.zeros_like(grad_out)
        grad_out[0:tokens, :] = cot_ref[...].astype(F32)
        sent = rows_to_seats(rows_ref, cap * experts, grad_out[...].astype(BF))
        for k in range(experts):
            out[z_ref[0] ^ k] = sent[k * cap : (k + 1) * cap].astype(BF)

    return call(
        kernel,
        "top_seats",
        [z, cotangent, rows],
        [SM, VM, VM],
        [sds((padded, width), F32), sds((experts, cap, width), BF)],
        [VM] * 2,
        [],
    )


def mix(z, x1, gates, cols, returned, tokens):
    width = x1.shape[1]

    def kernel(z_ref, x1_ref, gates_ref, cols_ref, ref, out):
        blocks = join([ref.at[z_ref[0] ^ k] for k in range(ref.shape[0])])
        total = combine(x1_ref[...], gates_ref[...], cols_ref, blocks)
        out[...] = total[0:tokens, :]

    return call(
        kernel,
        "mix",
        [z, x1, gates, cols, returned],
        [SM] + [VM] * 4,
        sds((tokens, width), F32),
        VM,
        [],
    )


def expert_back(me, grad_blocks, slope, gate, made, weights, used):
    owners = len(grad_blocks)
    cap, width = grad_blocks[0].shape
    seats, hidden = slope.shape
    count = len(weights.arrays)
    shard = weights.arrays[0].shape[-2]
    whole = weights.places[0][0] is None
    step = width

    def kernel(*refs):
        refs = list(refs)
        me_ref = refs.pop(0)
        seat_refs = [refs.pop(0) for _ in range(owners)]
        slope_ref, gate_ref, made_ref = (refs.pop(0) for _ in range(3))
        w_refs = [refs.pop(0) for _ in range(count)]
        gd_out = refs.pop(0)
        outs = [refs.pop(0) for _ in range(owners)]
        win, woe, slopes, sems, slope_sems = refs
        more = [
            pltpu.make_async_copy(
                slope_ref.at[:, pl.ds(at, step)],
                slopes.at[:, pl.ds(at, step)],
                slope_sems.at[at // step],
            )
            for at in range(0, hidden, step)
        ]
        chunks = Chunks(w_refs, weights, width, hidden, shard, whole, win, woe, sems, more)
        given = jnp.concatenate([ref[...].astype(F32) for ref in seat_refs], 0)
        grad = (given * gate_ref[:, 0:1]).astype(BF)
        notes = given * made_ref[...].astype(F32)
        notes = [lane_sums(notes[k * cap : (k + 1) * cap]) for k in range(owners)]
        gd_out[:, 0:width] = grad
        gd_out.send(ALL, pl.ds(0, width))
        total_out = None
        for at in range(0, hidden, step):
            chunks.take(at // step)
            d_hidden = dot_nt(grad, woe[at : at + step, :])
            d_pre = (d_hidden * slopes[:, at : at + step].astype(F32)).astype(BF)
            gd_out[:, width + at : width + at + step] = d_pre
            gd_out.send(ALL, pl.ds(width + at, step))
            piece = dot_nt(d_pre, win[:, at : at + step])
            total_out = piece if total_out is None else total_out + piece
        for k, ref in enumerate(outs):
            ref[...] = with_note(total_out[k * cap : (k + 1) * cap], used, notes[k]).astype(BF)

    shapes = [sds((seats, width + hidden), BF)]
    shapes += [sds((cap, width), BF)] * owners
    result = call(
        kernel,
        "expert_back",
        [me, *grad_blocks, slope, gate, made, *weights.arrays],
        [SM] + [LOAD] * owners + [ANY] + [LOAD] * 2 + [ANY] * count,
        shapes,
        [STORE] * (1 + owners),
        [
            pltpu.VMEM((width, hidden), BF),
            pltpu.VMEM((hidden, width), BF),
            pltpu.VMEM((seats, hidden), BF),
            pltpu.SemaphoreType.DMA((2 * copies_in(weights),)),
            pltpu.SemaphoreType.DMA((hidden // step,)),
        ],
    )
    return result[0], result[1:]


def column_sums(value):
    return dot(jnp.ones((8, value.shape[0]), BF), value)[0:1, :]


def own_columns(width, shards, core):
    shard = width // shards
    half = width // 2
    row = lax.broadcasted_iota(jnp.int32, (width, half), 0)
    column = lax.broadcasted_iota(jnp.int32, (width, half), 1)
    place = column + core * shard
    for k in range(1, shards // 2):
        place = place + jnp.where(column >= k * shard, shard, 0)
    return one(row == place)


def expert_grads(me, rows_in, h, d_out, d_pre, sizes, paired, shards, given=()):
    width = HEADS * HEAD_DIM
    seats, hidden = sizes
    sides = 2 if paired else 1
    per, shard = hidden // width, width // shards
    part_hidden = hidden // shards
    tall = width // 2 if paired else width
    deep = hidden // 2 if paired else hidden
    total = shards * per if paired else 2
    blocks = shards // 2 if paired else per
    size = part_hidden if paired else width
    arrays = []
    for operand in (*rows_in, *h, *d_out, *d_pre):
        if not any(operand[0] is known for known in arrays):
            arrays.append(operand[0])
    place = lambda operand: [operand[0] is known for known in arrays].index(True)

    def kernel(me_ref, *refs):
        refs = list(refs)
        ins = [refs.pop(0) for _ in arrays]
        bias_given = [refs.pop(0) for _ in given][-1:]
        outs = [refs.pop(0) for _ in range(1 if paired else 2)]
        bias_ref, win, woe, h_held, row_held, out_held, pre_held, sems, load_sems = refs
        core = me_ref[0] & 1
        copies = []
        loads = {}

        def send(source, target):
            copy = pltpu.make_async_copy(source, target, sems.at[len(copies)])
            copy.start()
            copies.append(copy)

        def fetch_in(key, source, target):
            copy = pltpu.make_async_copy(source, target, load_sems.at[len(loads)])
            copy.start()
            loads[key] = copy

        def summed(pieces):
            total = pieces[0]
            for piece in pieces[1:]:
                total = total + piece
            return total

        for i, operand in enumerate(d_out):
            source = ins[place(operand)].at[:, pl.ds(operand[1], width)]
            fetch_in(("d", i), source, out_held.at[i])
        for k in range(blocks):
            for i, operand in enumerate(h):
                first = operand[1] + k * size
                if paired and operand[2]:
                    first = pl.multiple_of(operand[1] + (2 * k + core) * size, LANES)
                source = ins[place(operand)].at[:, pl.ds(first, size)]
                fetch_in(("h", k, i), source, h_held.at[i, :, pl.ds(k * size, size)])
        for i, operand in enumerate(rows_in):
            source = ins[place(operand)].at[:, pl.ds(operand[1], width)]
            fetch_in(("r", i), source, row_held.at[i])
        for k in range(per):
            for i, operand in enumerate(d_pre):
                source = ins[place(operand)].at[:, pl.ds(operand[1] + k * width, width)]
                fetch_in(("p", k, i), source, pre_held.at[i, :, pl.ds(k * width, width)])
        if bias_given:
            bias_ref[...] = bias_given[0][...]
        else:
            bias_ref[...] = jnp.zeros_like(bias_ref)
        if h:
            for i in range(sides):
                loads["d", i].wait()
            for k in range(blocks):
                here = slice(k * size, (k + 1) * size)
                for i in range(sides):
                    loads["h", k, i].wait()
                total = summed([dot_tn(h_held[i, :, here], out_held[i]) for i in range(sides)])
                woe[here, :] = total.astype(BF)
                if paired:
                    for q in range(per):
                        send(
                            woe.at[pl.ds(k * size + q * shard, shard)],
                            outs[0].at[k, 1, :, pl.ds(q * width, width)],
                        )
            bias_ref[per : per + 1, :] = summed([column_sums(out_held[i]) for i in range(sides)])
        if rows_in:
            for i in range(sides):
                loads["r", i].wait()
            lefts = [row_held[i] for i in range(sides)]
            if paired:
                pick = own_columns(width, shards, core)
                lefts = [dot(value, pick).astype(BF) for value in lefts]
            for k in range(per):
                here = slice(k * width, (k + 1) * width)
                for i in range(sides):
                    loads["p", k, i].wait()
                total = summed([dot_tn(lefts[i], pre_held[i, :, here]) for i in range(sides)])
                win[:, here] = total.astype(BF)
                if paired:
                    for n in range(shards // 2):
                        into = pl.ds(k * width, width)
                        send(win.at[pl.ds(n * shard, shard), into], outs[0].at[n, 0, :, into])
            sums = summed([column_sums(pre_held[i]) for i in range(sides)])
            for d in range(shards):
                for q in range(per):
                    first = (d * per + q) * shard
                    bias_ref[q : q + 1, d * shard : (d + 1) * shard] = sums[:, first : first + shard]
        if not paired:
            send(win, outs[0])
            send(woe, outs[1])
        wait(copies)

    if paired:
        shapes = [sds((shards // 2, 2, shard, hidden), BF)]
    else:
        shapes = [sds((width, hidden), BF), sds((hidden, width), BF)]
    result = call(
        kernel,
        "expert_grads",
        [me, *arrays, *given],
        [SM] + [ANY] * (len(arrays) + max(len(given) - 1, 0)) + [VM] * min(len(given), 1),
        shapes + [sds((8, width), F32)],
        [ANY] * len(shapes) + [VM],
        [
            pltpu.VMEM((tall, hidden), BF),
            pltpu.VMEM((deep, width), BF),
            pltpu.VMEM((sides, seats, blocks * size), BF),
            pltpu.VMEM((sides, seats, width), BF),
            pltpu.VMEM((sides, seats, width), BF),
            pltpu.VMEM((sides, seats, hidden), BF),
            pltpu.SemaphoreType.DMA((total,)),
            pltpu.SemaphoreType.DMA((sides * (2 + blocks + per),)),
        ],
        {1 + len(arrays): 0} if given else None,
    )
    return result[:-1], result[-1]


def pick_columns(me, value, shards):
    rows, wide = value.shape
    width = wide // 3

    def kernel(me_ref, ref, own, other):
        core = me_ref[0] & 1
        for out, side in ((own, core), (other, 1 - core)):
            pick = own_columns(width, shards, side)
            for k in range(3):
                piece = dot(ref[:, k * width : (k + 1) * width], pick)
                out[:, k * width // 2 : (k + 1) * width // 2] = piece.astype(BF)

    return call(
        kernel,
        "pick_columns",
        [me, value],
        [SM, VM],
        [sds((rows, wide // 2), BF)] * 2,
        [VM] * 2,
        [],
    )


def attn_back(
    me, back_blocks, gates, router, grad, x, x1, qkv, cols, vecs, weights, below, tokens, used
):
    padded, width = grad.shape
    owners = len(back_blocks)
    cap = back_blocks[0].shape[0]
    seats = owners * cap
    count = len(weights.arrays)
    shard = weights.arrays[0].shape[-2]

    def kernel(*refs):
        refs = list(refs)
        me_ref = refs.pop(0)
        back_refs = [refs.pop(0) for _ in range(owners)]
        gates_ref, router_ref, grad_ref, x_ref, x1_ref, qkv_ref, cols_ref, vec_ref = (
            refs.pop(0) for _ in range(8)
        )
        w_refs = [refs.pop(0) for _ in range(count)]
        if below is not None:
            below_rows = refs.pop(0)
        dx_out, back_out = refs.pop(0), refs.pop(0)
        seat_outs = [refs.pop(0) for _ in range(owners)] if below is not None else None
        wqkv, wout, small_out, sems, more_sems = refs
        targets = attn_targets(width, shard, wqkv, wout)
        right = fetch(w_refs, weights, me_ref[0], targets, 1, sems)
        left = fetch(w_refs, weights, me_ref[0], targets, 0, more_sems)
        start(right + left)
        vec = lambda k: vec_ref[k : k + 1, :]
        blocks = [ref[...].astype(F32) for ref in back_refs]
        gates = gates_ref[...]
        lanes = lax.broadcasted_iota(jnp.int32, gates.shape, 1)
        d_gates = jnp.zeros_like(gates)
        for pair in range(2):
            d_pair = jnp.zeros_like(gates)
            for block in range(owners):
                here = near_lanes(cols_ref, pair, block, cap)
                d_pair = d_pair + jnp.where(here, note_of(blocks[block], used), 0.0)
            d_pair = jnp.sum(d_pair, -1, keepdims=True)
            d_gates = d_gates + jnp.where(lanes == cols_ref[:, 2 + pair : 3 + pair], d_pair, 0.0)
        dz = gates * (d_gates - jnp.sum(d_gates * gates, -1, keepdims=True))
        high, low = split(dz)
        moe_part = dot_nt(high, router_ref[...]) + dot_nt(low, router_ref[...])
        back_out[0:padded, 4 * width : 4 * width + LANES] = high
        back_out[0:padded, 4 * width + LANES : 4 * width + 2 * LANES] = low
        chosen = jnp.logical_or(seat_mask(cols_ref, 0, seats), seat_mask(cols_ref, 1, seats))
        d_moe = dot(one(chosen), jnp.concatenate(blocks, 0).astype(BF)) + moe_part
        normed2, rstd2 = norm_rows(x1_ref[...])
        small_out[...] = jnp.zeros_like(small_out)
        small_out[1:2, :] = jnp.sum(d_moe * normed2, 0, keepdims=True)
        small_out[3:4, :] = jnp.sum(d_moe, 0, keepdims=True)
        d_x1 = grad_ref[...] + norm_back(d_moe * vec(1), normed2, rstd2)
        dy = d_x1.astype(BF)
        back_out[0:padded, 3 * width : 4 * width] = dy
        small_out[6:7, :] = column_sums(dy)
        wait(right)
        d_mixed = dot_nt(dy, wout[...]).astype(BF)
        masks = head_masks()
        scale = HEAD_DIM ** (-0.5)
        for two in range(HEADS // 2):
            at = two * 2 * HEAD_DIM
            query = qkv_ref[:, at : at + 2 * HEAD_DIM]
            keys = qkv_ref[:, width + at : width + at + 2 * HEAD_DIM]
            values = qkv_ref[:, 2 * width + at : 2 * width + at + 2 * HEAD_DIM]
            d_o = d_mixed[:, at : at + 2 * HEAD_DIM]
            probs = pair_probs(query, keys, masks, tokens)
            d_here = stacked(d_o, masks)
            d_probs = dot_nt(d_here, values)
            d_values = dot_tn(probs.astype(BF), d_here)
            d_scores = probs * (d_probs - jnp.sum(d_probs * probs, -1, keepdims=True))
            d_scores = d_scores.astype(BF)
            d_query = unstacked(dot(d_scores, keys), masks)
            d_keys = dot_tn(d_scores, stacked(query, masks))
            sums = (d_query, d_keys, d_values)
            for k, value in enumerate((sums[0] * scale, sums[1] * scale, sums[2])):
                first = k * width + at
                back_out[0:padded, first : first + 2 * HEAD_DIM] = value.astype(BF)
        wait(left)
        d_normed = None
        for k in range(3):
            here = back_out[0:padded, k * width : (k + 1) * width]
            if k != 1:
                row = 4 if k == 0 else 5
                small_out[row : row + 1, :] = column_sums(here)
            piece = dot_nt(here, wqkv[:, k * width : (k + 1) * width])
            d_normed = piece if d_normed is None else d_normed + piece
        normed1, rstd1 = norm_rows(x_ref[...])
        small_out[0:1, :] = jnp.sum(d_normed * normed1, 0, keepdims=True)
        small_out[2:3, :] = jnp.sum(d_normed, 0, keepdims=True)
        d_x = d_x1 + norm_back(d_normed * vec(0), normed1, rstd1)
        dx_out[...] = d_x[0 : dx_out.shape[0], :]
        if below is not None:
            part(rows_to_seats(below_rows, seats, d_x.astype(BF)), seat_outs)
        high, low = split(small_out[...])
        back_out[padded : padded + 16, 0:width] = high
        back_out[padded : padded + 16, width : 2 * width] = low
        back_out[padded : padded + 16, 2 * width :] = jnp.zeros((16, 2 * width + 2 * LANES), BF)

    shapes = [
        sds((padded if below is not None else tokens, width), F32),
        sds((padded + 16, 4 * width + 2 * LANES), BF),
    ]
    args = [me, *back_blocks, gates, router, grad, x, x1, qkv, cols, vecs, *weights.arrays]
    specs = [SM] + [VM] * (owners + 8) + [ANY] * count
    if below is not None:
        shapes += [sds((cap, width), BF)] * owners
        args += [below]
        specs += [VM]
    result = call(
        kernel,
        "attn_back",
        args,
        specs,
        shapes,
        [VM] * len(shapes),
        [
            pltpu.VMEM((width, 3 * width), BF),
            pltpu.VMEM((width, width), BF),
            pltpu.VMEM((16, width), F32),
            pltpu.SemaphoreType.DMA((copies_in(weights),)),
            pltpu.SemaphoreType.DMA((copies_in(weights),)),
        ],
    )
    return result[:2], result[2:]


def attn_grads(me, z, own, other, biases, shards, ordered):
    padded, wide_ao = own[0].shape
    width = HEADS * HEAD_DIM
    half = 2 * width + LANES
    tall = width // 2 if other else width
    shard = width // shards
    places = [(6, 0, 0), (6, 1, 1), (2, 0, 2), (2, 1, 2), (4, 0, 3), (4, 1, 3), (0, 0, 4), (0, 1, 4)]
    count = 2
    if other:
        count = 1 if ordered else 5

    def kernel(me_ref, z_ref, *refs):
        refs = list(refs)
        ao = [refs.pop(0), refs.pop(0)] if other else [refs.pop(0)]
        back = [refs.pop(0), refs.pop(0)] if other else [refs.pop(0)]
        bias_ref = refs.pop(0)
        outs = [refs.pop(0) for _ in range(count)]
        wide, rows, turned, sems = refs
        copies = []

        def send(p):
            first = p * half
            if not other:
                copies.append(
                    pltpu.make_async_copy(wide.at[:, pl.ds(first, half)], outs[p], sems.at[p])
                )
                copies[-1].start()
                return
            if ordered:
                for k in range(shards // 2):
                    source = wide.at[pl.ds(k * shard, shard), pl.ds(first, half)]
                    copy = pltpu.make_async_copy(source, outs[0].at[k, p], sems.at[2 * k + p])
                    copies.append(copy)
                    copy.start()
                return
            for n, (off, where, o) in enumerate(places):
                if where != p:
                    continue
                at = pl.multiple_of(((me_ref[0] ^ off) >> 1) * shard, 16)
                into = outs[o] if o < 2 else outs[o].at[p]
                copies.append(
                    pltpu.make_async_copy(
                        wide.at[pl.ds(at, shard), pl.ds(first, half)], into, sems.at[n]
                    )
                )
                copies[-1].start()

        def product(which, first):
            total = None
            for left, right in zip(ao, back):
                here = left[:, which * tall : (which + 1) * tall]
                piece = dot_tn(here, right[0:padded, first : first + width])
                total = piece if total is None else total + piece
            return total.astype(BF)

        wide[:, 0:width] = product(0, 0)
        wide[:, width : 2 * width] = product(0, width)
        wide[:, 2 * width : half] = jnp.zeros((tall, LANES), BF)
        send(0)
        wide[:, half : half + width] = product(0, 2 * width)
        wide[:, half + width : half + 2 * width] = product(1, 3 * width)
        rows[...] = jnp.zeros_like(rows)
        small = None
        d_router = None
        for left, right in zip(ao, back):
            for k in range(2):
                piece = right[padded : padded + 16, k * width : (k + 1) * width].astype(F32)
                small = piece if small is None else small + piece
                first = 4 * width + k * LANES
                piece = dot_tn(
                    left[:, 2 * tall : 3 * tall], right[0:padded, first : first + LANES]
                )
                d_router = piece if d_router is None else d_router + piece
        rows[16:32, :] = small
        rows[pl.ds(pl.multiple_of(32 + 8 * z_ref[0], 8), 8), :] = bias_ref[...]
        turned[...] = rows[...].T
        if other:
            core = me_ref[0] & 1
            for k in range(shards // 2):
                at = pl.multiple_of((2 * k + core) * shard, 8)
                here = slice(k * shard, (k + 1) * shard)
                piece = d_router[here, :] + turned[pl.ds(at, shard), :]
                wide[here, half + 2 * width : 2 * half] = piece.astype(BF)
        else:
            wide[:, half + 2 * width : 2 * half] = (d_router + turned[...]).astype(BF)
        send(1)
        wait(copies)

    if other:
        if ordered:
            shapes = [sds((shards // 2, 2, shard, half), BF)]
        else:
            shapes = [sds((shard, half), BF)] * 2 + [sds((2, shard, half), BF)] * 3
        args = [own[0], other[0], own[1], other[1]]
    else:
        shapes = [sds((width, half), BF)] * 2
        args = list(own)
    return call(
        kernel,
        "attn_grads",
        [me, z, *args, biases],
        [SM, SM] + [VM] * (len(args) + 1),
        shapes,
        [ANY] * len(shapes),
        [
            pltpu.VMEM((tall, 2 * half), BF),
            pltpu.VMEM((LANES, width), F32),
            pltpu.VMEM((width, LANES), F32),
            pltpu.SemaphoreType.DMA((max(len(places), shards),)),
        ],
    )


def small_out(smalls, z, experts, per):
    layers = len(smalls)
    shard = smalls[0].shape[0]

    def kernel(z_ref, *refs):
        ins = refs[:layers]
        gains, biases, router, bias_in, bias_oe, square = refs[layers:]
        for layer in range(layers):
            square[...] = jnp.zeros_like(square)
            square[0:shard, :] = ins[layer][...]
            square[...] = square[...].T
            router[layer] = square[0:experts, 0:shard]
            gains[layer] = square[16:18, 0:shard]
            for k in range(5):
                biases[k, layer : layer + 1, :] = square[18 + k : 19 + k, 0:shard]
            own = square[pl.ds(pl.multiple_of(32 + 8 * z_ref[0], 8), 8), :]
            for q in range(per):
                bias_in[layer, :, q * shard : (q + 1) * shard] = own[q : q + 1, 0:shard]
            bias_oe[layer] = own[per : per + 1, 0:shard]

    shapes = [
        sds((layers, 2, shard), F32),
        sds((5, layers, shard), F32),
        sds((layers, experts, shard), F32),
        sds((layers, 1, per * shard), F32),
        sds((layers, 1, shard), F32),
    ]
    return call(
        kernel,
        "small_out",
        [z, *smalls],
        [SM] + [VM] * layers,
        shapes,
        [VM] * 5,
        [pltpu.VMEM((LANES, LANES), F32)],
    )


def swap(value, axis, bit):
    size = lax.axis_size(axis)
    return lax.ppermute(value, axis, [(i, i ^ bit) for i in range(size)])


def exchange(blocks):
    order = sorted(range(1, len(blocks)), key=lambda k: -(k & 2))
    got = {k: swap(blocks[k], "expert", k) for k in order}
    return [blocks[0]] + [got[k] for k in range(1, len(blocks))]


def axis_bits(axis, bit):
    bits = []
    while bit < lax.axis_size(axis):
        bits.append(bit)
        bit *= 2
    return bits


def sum_experts(value):
    for bit in axis_bits("expert", 1):
        low = value.astype(BF)
        value = low.astype(F32) + swap(low, "expert", bit).astype(F32)
    return value


def gather_rows(shard):
    return lax.all_gather(shard, "dp", axis=0, tiled=True)


def scatter_rows(whole):
    return lax.psum_scatter(whole, "dp", scatter_dimension=0, tiled=True)


def scatter_chips(blocks):
    size = lax.axis_size("dp")
    return lax.psum_scatter(
        blocks,
        "dp",
        scatter_dimension=0,
        axis_index_groups=[list(range(core, size, 2)) for core in range(2)],
    )


class Gather:
    def __init__(self, shard):
        self.shard = shard
        self.x, self.y = swap(shard, "dp", 2), swap(shard, "dp", 4)

    def turn(self):
        _, rows, width = self.shard.shape
        half = (1, rows, width)
        *self.cut, self.x, self.y = move(
            "cut",
            [self.x, self.y],
            [(0, (pl.ds(0, 1),), 0, (ALL,), half), (1, (pl.ds(1, 1),), 1, (ALL,), half)],
            [sds(half, BF)] * 2 + [sds(self.x.shape, BF)] * 2,
            {0: 2, 1: 3},
        )

    def send(self, after=()):
        if after:
            self.cut = hold(self.cut, after)
        self.xy = swap(self.cut[0], "dp", 4), swap(self.cut[1], "dp", 2)
        self.other = [swap(value, "dp", 1) for value in (self.shard, self.x, self.y)]

    def cross(self, after=()):
        if after:
            self.xy = hold(self.xy, after)
        self.across = [swap(value, "dp", 1) for value in self.xy]

    def weights(self):
        pieces = [
            (self.shard, 0, (0, 1)),
            (self.x, 2, (0, 1)),
            (self.y, 4, (0, 1)),
            (self.xy[0], 6, (0,)),
            (self.xy[1], 6, (1,)),
            (self.across[0], 7, (0,)),
            (self.across[1], 7, (1,)),
            (self.other[0], 1, (0, 1)),
            (self.other[1], 3, (0, 1)),
            (self.other[2], 5, (0, 1)),
        ]
        return Weights([p[0] for p in pieces], [p[1:] for p in pieces])


def full(rows):
    return (pl.ds(0, rows), ALL)


class AttnSum:
    def __init__(self, grads):
        self.bits = axis_bits("expert", 1)
        self.done = 0
        if len(grads) == 1:
            self.total = scatter_chips(grads[0])
            return
        self.across, (self.x, self.y, self.own) = list(grads[:2]), grads[2:]
        self.rows, self.width = self.across[0].shape

    def cut(self, z):
        self.rows, self.width = self.total.shape[1:]
        shape = (self.rows, self.width)

        def kernel(z_ref, total, keep, give, held, in_sems, out_sems):
            here = z_ref[0] & 1
            loads = [
                pltpu.make_async_copy(total.at[k], held.at[k], in_sems.at[k]) for k in range(2)
            ]
            start(loads)
            wait(loads)
            stores = [
                pltpu.make_async_copy(held.at[here], keep, out_sems.at[0]),
                pltpu.make_async_copy(held.at[1 - here], give, out_sems.at[1]),
            ]
            start(stores)
            wait(stores)

        self.keep, give = call(
            kernel,
            "parts",
            [z, self.total],
            [SM, ANY],
            [sds(shape, BF)] * 2,
            [ANY] * 2,
            [
                pltpu.VMEM((2, *shape), BF),
                pltpu.SemaphoreType.DMA((2,)),
                pltpu.SemaphoreType.DMA((2,)),
            ],
        )
        self.come = swap(give, "expert", 1)

    def halves(self):
        shape = (self.rows, self.width)
        flat = full(self.rows)
        (self.keep,) = fold(
            "fold3",
            [self.keep, self.come],
            shape,
            [([(0, flat), (1, flat)], BF, [(0, flat, flat)])],
            [sds(shape, BF)],
        )
        if self.done == 0:
            self.come = swap(self.keep, "expert", 2)
        else:
            self.come = swap(self.keep, "expert", 1)
        self.done += 1

    def finish(self, z, layer, layers, given, smalls, experts, per):
        rows, half = self.rows, self.width
        wide = (half - LANES) // 2
        others = sorted(smalls)
        count = len(given)

        def kernel(z_ref, *refs):
            refs = list(refs)
            terms = [refs.pop(0) for _ in range(4)]
            ins = {n: refs.pop(0) for n in others}
            del refs[:count]
            qkv, out, gains, biases, router, bias_in, bias_oe, high, square, sems = refs
            for p in range(2):
                high[p] = terms[p][...].astype(F32) + terms[2 + p][...].astype(F32)
            copies = [
                (high.at[0, :, pl.ds(0, 2 * wide)], qkv.at[layer, :, pl.ds(0, 2 * wide)]),
                (high.at[1, :, pl.ds(0, wide)], qkv.at[layer, :, pl.ds(2 * wide, wide)]),
                (high.at[1, :, pl.ds(wide, wide)], out.at[layer]),
            ]
            copies = [pltpu.make_async_copy(a, b, sems.at[n]) for n, (a, b) in enumerate(copies)]
            start(copies)
            for n in range(layers):
                square[...] = jnp.zeros_like(square)
                if n == layer:
                    square[0:rows, :] = high[1, :, 2 * wide : 2 * wide + LANES]
                else:
                    square[0:rows, :] = ins[n][...]
                square[...] = square[...].T
                router[n] = square[0:experts, 0:rows]
                gains[n] = square[16:18, 0:rows]
                for k in range(5):
                    biases[k, n : n + 1, :] = square[18 + k : 19 + k, 0:rows]
                own = square[pl.ds(pl.multiple_of(32 + 8 * z_ref[0], 8), 8), :]
                for q in range(per):
                    bias_in[n, :, q * rows : (q + 1) * rows] = own[q : q + 1, 0:rows]
                bias_oe[n] = own[per : per + 1, 0:rows]
            wait(copies)

        return call(
            kernel,
            "attn_last",
            [z, *self.parts, *self.came, *[smalls[n] for n in others], *given],
            [SM] + [VM] * (4 + len(others)) + [HBM] * count,
            [
                sds((layers, rows, 3 * wide), F32),
                sds((layers, rows, wide), F32),
                sds((layers, 2, rows), F32),
                sds((5, layers, rows), F32),
                sds((layers, experts, rows), F32),
                sds((layers, 1, per * rows), F32),
                sds((layers, 1, rows), F32),
            ],
            [HBM] * 2 + [VM] * 5,
            [
                pltpu.VMEM((2, rows, half), F32),
                pltpu.VMEM((LANES, LANES), F32),
                pltpu.SemaphoreType.DMA((3,)),
            ],
            {5 + len(others): 0, 6 + len(others): 1} if given else None,
        )

    def put(self, z, layer, layers, given):
        shape = (self.rows, self.width)
        wide = (self.width - LANES) // 2
        count = len(given)

        def kernel(z_ref, keep, come, *refs):
            refs = refs[count:]
            qkv, out, small, low, high, in_sems, out_sems = refs
            here = z_ref[0] & 1
            loads = [
                pltpu.make_async_copy(keep, low.at[here], in_sems.at[0]),
                pltpu.make_async_copy(come, low.at[1 - here], in_sems.at[1]),
            ]
            start(loads)
            wait(loads)
            high[...] = low[...].astype(F32)
            stores = [
                (high.at[0, :, pl.ds(0, 2 * wide)], qkv.at[layer, :, pl.ds(0, 2 * wide)]),
                (high.at[1, :, pl.ds(0, wide)], qkv.at[layer, :, pl.ds(2 * wide, wide)]),
                (high.at[1, :, pl.ds(wide, wide)], out.at[layer]),
                (high.at[1, :, pl.ds(2 * wide, LANES)], small),
            ]
            stores = [
                pltpu.make_async_copy(a, b, out_sems.at[n]) for n, (a, b) in enumerate(stores)
            ]
            start(stores)
            wait(stores)

        return call(
            kernel,
            "attn_out",
            [z, self.keep, self.come, *given],
            [SM] + [ANY] * (2 + count),
            [
                sds((layers, self.rows, 3 * wide), F32),
                sds((layers, self.rows, wide), F32),
                sds((self.rows, LANES), F32),
            ],
            [HBM] * 3,
            [
                pltpu.VMEM((2, *shape), BF),
                pltpu.VMEM((2, *shape), F32),
                pltpu.SemaphoreType.DMA((2,)),
                pltpu.SemaphoreType.DMA((4,)),
            ],
            {3: 0, 4: 1} if given else None,
        )

    def send_across(self, after=()):
        if after:
            self.across = hold(self.across, after)
        self.across = swap(self.across[0], "dp", 4), swap(self.across[1], "dp", 2)

    def fold1(self):
        self.x, self.y = fold1(self.x, self.y, self.across)

    def send_on(self, after=()):
        if after:
            self.x, self.y = hold([self.x, self.y], after)
        self.came = swap(self.x, "dp", 2), swap(self.y, "dp", 4)

    def fold2(self):
        shape = (self.rows, self.width)
        flat = full(self.rows)
        self.parts = fold(
            "fold2",
            [self.own, *self.came],
            shape,
            [([(i, (p,)) for i in range(3)], BF, [(p, flat, flat)]) for p in range(2)],
            [sds(shape, BF)] * 2,
        )
        self.send()

    def send(self):
        up_bit, down_bit = self.bits[self.done], self.bits[-1 - self.done]
        self.came = swap(self.parts[0], "expert", up_bit), swap(self.parts[1], "expert", down_bit)

    def fold3(self, layer, layers, given):
        shape = (self.rows, self.width)
        flat = full(self.rows)
        self.done += 1
        terms = [[(0, flat), (2, flat)], [(1, flat), (3, flat)]]
        args = [*self.parts, *self.came]
        if self.done < len(self.bits):
            self.parts = fold(
                "fold3",
                args,
                shape,
                [(terms[p], BF, [(p, flat, flat)]) for p in range(2)],
                [sds(shape, BF)] * 2,
                )
            self.send()
            return None
        wide = (self.width - LANES) // 2
        cut = lambda first, size: (ALL, pl.ds(first, size))
        tasks = [
            (terms[0], F32, [(0, (layer, ALL, pl.ds(0, 2 * wide)), cut(0, 2 * wide))]),
            (
                terms[1],
                F32,
                [
                    (0, (layer, ALL, pl.ds(2 * wide, wide)), cut(0, wide)),
                    (1, (layer,), cut(wide, wide)),
                    (2, flat, cut(2 * wide, LANES)),
                ],
            ),
        ]
        outs = [
            sds((layers, self.rows, 3 * wide), F32),
            sds((layers, self.rows, wide), F32),
            sds((self.rows, LANES), F32),
        ]
        aliases = {4: 0, 5: 1} if given else None
        return fold("attn_out", args + list(given), shape, tasks, outs, aliases)


def fold1(x, y, across):
    shape = x.shape[1:]
    flat = full(shape[0])
    return fold(
        "fold1",
        [x, y, *across],
        shape,
        [
            ([(0, (0,)), (2, flat)], BF, [(0, (0,), flat)]),
            ([(1, (1,)), (3, flat)], BF, [(1, (1,), flat)]),
        ],
        [sds(x.shape, BF)] * 2,
        {0: 0, 1: 1},
    )


def expert_out(total, layer, layers, given, width):
    rows, broad = total.shape[1:]
    per = broad // width
    second = [
        (1, (layer, 0, pl.ds(q * rows, rows)), (ALL, pl.ds(q * width, width))) for q in range(per)
    ]
    outs = [sds((layers, 1, rows, broad), F32), sds((layers, 1, per * rows, width), F32)]
    return fold(
        "expert_out",
        [total, *given],
        (rows, broad),
        [
            ([(0, (0,))], F32, [(0, (layer, 0), full(rows))]),
            ([(0, (1,))], F32, second),
        ],
        outs,
        {1: 0, 2: 1} if given else None,
    )


def per_device(
    image_tokens,
    norm_gains,
    biases,
    w_qkv,
    w_out,
    w_router,
    router_noise,
    w_in,
    b_in,
    w_outexp,
    b_expout,
    routes,
    seat_order,
    cotangent,
):
    layers = w_qkv.shape[0]
    tokens, width = image_tokens.shape
    experts = w_router.shape[2]
    shards = lax.axis_size("dp")
    assert tokens == SEQ and experts == lax.axis_size("expert")
    assert width == HEADS * HEAD_DIM
    padded = up(tokens, 16)
    cap = 2 * tokens // experts
    cap_pad = up(cap + 2, 8)
    assert cap_pad <= LANES
    shard = w_qkv.shape[1]
    hidden_shard = w_outexp.shape[2]
    hidden = w_in.shape[3]
    per = hidden_shard // shard
    index = lax.axis_index("dp").astype(jnp.int32)
    me = index.reshape(1)
    z = lax.axis_index("expert").astype(jnp.int32).reshape(1)
    bits = axis_bits("dp", 2)
    four = bits == [2, 4] and shard % 16 == 0 and axis_bits("expert", 1) == [1, 2]

    Order.token = None

    def pack_attn(layer):
        return move(
            "pack_attn",
            [w_qkv, w_out],
            [
                (0, (layer, ALL, pl.ds(0, 2 * width)), 0, (0,), (shard, 2 * width)),
                (
                    0,
                    (layer, ALL, pl.ds(2 * width, width)),
                    0,
                    (1, ALL, pl.ds(0, width)),
                    (shard, width),
                ),
                (1, (layer,), 0, (1, ALL, pl.ds(width, width)), (shard, width)),
            ],
            [sds((2, shard, 2 * width), BF)],
        )[0]

    def pack_expert(layer):
        return move(
            "pack_expert",
            [w_in, w_outexp],
            [(0, (layer, 0), 0, (0,), (shard, hidden))]
            + [
                (
                    1,
                    (layer, 0, pl.ds(q * shard, shard)),
                    0,
                    (1, ALL, pl.ds(q * width, width)),
                    (shard, width),
                )
                for q in range(per)
            ],
            [sds((2, shard, hidden), BF)],
        )[0]

    whole = [(None, (0,)), (None, (1,))]

    def fetch_attn(layer):
        if four:
            return Gather(pack_attn(layer))
        right = jnp.concatenate([w_qkv[layer][:, 2 * width :], w_out[layer]], 1)
        attn = [gather_rows(v)[None] for v in (w_qkv[layer][:, : 2 * width], right)]
        return Weights(attn, whole)

    def fetch_expert(layer):
        if four:
            both = lax.all_gather(pack_expert(layer), "dp", axis=0)
            return Weights([both], [(OWNERS, (0, 1))])
        both = [gather_rows(w_in[layer, 0])[None], gather_rows(w_outexp[layer, 0])[None]]
        return Weights(both, whole)

    def attn_weights(gathered):
        return gathered.weights() if four else gathered

    last = layers - 1
    attn_w = [fetch_attn(0)]
    expert_w = [fetch_expert(layer) for layer in range(layers)]
    cols, rows = place_pairs(
        routes, seat_order.reshape(layers, tokens, 2), padded, cap, cap_pad, z
    )
    small = pack_small(norm_gains, biases, w_router, b_in, b_expout)
    grad, grad_seats = top_seats(z, cotangent, rows[last], cap_pad, experts)
    grad_seats = [lax.all_to_all(grad_seats, "expert", 0, 0, tiled=True)]
    if four:
        attn_w[0].turn()
        attn_w[0].send()
    small = lax.all_gather(small, "dp", axis=0)
    params = unpack_small(small, layers, shard, per, experts, grad_seats)
    if last > 0:
        attn_w.append(fetch_attn(1))

    saved = []
    x_args = (image_tokens,)
    if four:
        attn_w[0].cross()
    for layer in range(layers):
        vecs, router, bias_in, bias_oe = params[layer]
        attn_w[layer] = attn_weights(attn_w[layer])
        kept, sent = attn_fwd(
            me,
            layer,
            x_args,
            attn_w[layer],
            vecs,
            router,
            router_noise,
            cols[layer],
            rows[layer],
            cap_pad,
            cap,
        )
        x, x1, qkv, gates, ao = kept
        sent = exchange(sent)
        other_ao = None
        if four and layer < last:
            ao, other_ao = pick_columns(me, ao, shards)
            other_ao = swap(other_ao, "dp", 1)
        if layer < last:
            if four:
                attn_w[layer + 1].turn()
                attn_w[layer + 1].send(sent[1:])
            if layer + 1 < last:
                attn_w.append(fetch_attn(layer + 2))
        common = (x, x1, qkv, gates, ao, other_ao)
        if layer < last:
            (rh, slope, gate, out), made = expert_fwd(
                me, sent, expert_w[layer], bias_in, bias_oe, cap
            )
            if four:
                attn_w[layer + 1].cross(made[:1])
            returned = exchange(made)
            other_rh = swap(rh, "dp", 1) if four else None
            saved.append((*common, rh, other_rh, slope, gate, out))
            x_args = (x1, gates, cols[layer], returned)
        else:
            (rp, hd, give, made), d_rows = expert_both(
                me, z, sent, grad_seats[0], expert_w[layer], bias_in, bias_oe, cap, shards
            )
            if four:
                ao, other_ao = pick_columns(me, ao, shards)
                other_ao = swap(other_ao, "dp", 1)
            saved.append((x, x1, qkv, gates, ao, other_ao))

    attn_sums, expert_sums = [None] * layers, [None] * layers
    for layer in reversed(range(layers)):
        x, x1, qkv, gates, ao, other_ao = saved[layer][:6]
        vecs, router = params[layer][:2]
        sizes = (experts * cap_pad, w_in.shape[3])
        if layer == last:
            rows_at, pre_at = [(rp, 0)], [(rp, width)]
            h_at, out_at = [(hd, 0, True)], [(hd, sizes[1])]
            if four:
                other = swap(give, "dp", 1)
                h_at, out_at = h_at + [(other, 0, False)], out_at + [(other, sizes[1] // 2)]
                other = swap(rp, "dp", 1)
                rows_at, pre_at = rows_at + [(other, 0)], pre_at + [(other, width)]
            d_back = exchange(d_rows)
            g_expert, g_bias = expert_grads(
                me, rows_at, h_at, out_at, pre_at, sizes, four, shards
            )
        else:
            rh, other_rh, slope, gate, out = saved[layer][6:]
            if four:
                g_attn = attn_grads(me, z, *attn_operands, g_bias, shards, True)
                attn_sums[layer + 1] = AttnSum(hold(g_attn, grad_seats[1:]))
            gd, d_rows = expert_back(me, grad_seats, slope, gate, out, expert_w[layer], cap)
            d_back = exchange(d_rows)
            lefts, backs = [rh], [gd]
            if four:
                lefts, backs = [rh, other_rh], [gd, swap(gd, "dp", 1)]
            g_expert, g_bias = expert_grads(
                me,
                [(v, 0) for v in lefts],
                [(v, width, True) for v in lefts],
                [(v, 0) for v in backs],
                [(v, width) for v in backs],
                sizes,
                four,
                shards,
            )
        if four:
            (g_expert,) = hold(g_expert, d_back[1:])
            expert_sums[layer] = scatter_chips(g_expert)
        else:
            expert_sums[layer] = [scatter_rows(v) for v in g_expert]
        below = None
        if layer > 0:
            below = rows[layer - 1]
        (grad, back), grad_seats = attn_back(
            me,
            d_back,
            gates,
            router,
            grad,
            x,
            x1,
            qkv,
            cols[layer],
            vecs,
            attn_w[layer],
            below,
            tokens,
            cap,
        )
        grad_seats = exchange(grad_seats) if layer > 0 else None
        if four:
            attn_operands = (ao, back), (other_ao, swap(back, "dp", 1))
        else:
            g_attn = attn_grads(me, z, (ao, back), None, g_bias, shards, False)
            attn_sums[layer] = [sum_experts(scatter_rows(v)) for v in g_attn]

    if four:
        done_attn, smalls, done_expert = (), [None] * layers, ()
        for layer in reversed(range(1, layers)):
            done_expert = expert_out(expert_sums[layer], layer, layers, done_expert, width)
        (made,) = hold([made], [back])
        g_attn = attn_grads(me, z, *attn_operands, g_bias, shards, False)
        attn_sums[0] = AttnSum(g_attn)
        attn_sums[0].send_across()
        attn_sums[0].fold1()
        attn_sums[0].send_on()
        for layer in reversed(range(1, layers)):
            attn_sums[layer].cut(z)
        for layer in reversed(range(1, layers)):
            attn_sums[layer].halves()
    returned = lax.all_to_all(made, "expert", 0, 0, tiled=True)
    mixed = mix(z, saved[last][1], saved[last][3], cols[last], returned, tokens)
    if four:
        attn_sums[0].fold2()
        for layer in reversed(range(1, layers)):
            attn_sums[layer].halves()
        attn_sums[0].fold3(0, layers, done_attn)
        for layer in reversed(range(1, layers)):
            out = attn_sums[layer].put(z, layer, layers, done_attn)
            done_attn, smalls[layer] = out[:2], out[2]
        done_expert = expert_out(expert_sums[0], 0, layers, done_expert, width)
        grad_in, grad_oe = done_expert
    else:
        grad_in = jnp.stack([item[0] for item in expert_sums])[:, None].astype(F32)
        grad_oe = jnp.stack([item[1] for item in expert_sums])[:, None].astype(F32)
    if four:
        smalls = {n: smalls[n] for n in range(1, layers)}
        out = attn_sums[0].finish(z, 0, layers, done_attn, smalls, experts, per)
        grad_qkv, grad_out, gains, shifts, grad_router, grad_bin, grad_boe = out
    else:
        left = jnp.stack([item[0] for item in attn_sums])
        right = jnp.stack([item[1] for item in attn_sums])
        grad_qkv = jnp.concatenate([left[:, :, : 2 * width], right[:, :, :width]], 2)
        grad_out = right[:, :, width : 2 * width]
        smalls = [right[layer, :, 2 * width :] for layer in range(layers)]
        small = small_out(smalls, z, experts, per)
        gains, shifts, grad_router, grad_bin, grad_boe = small
    return (
        mixed,
        grad,
        gains,
        jnp.transpose(shifts, (1, 0, 2)),
        grad_qkv,
        grad_out,
        jnp.transpose(grad_router, (0, 2, 1)),
        grad_in,
        grad_bin,
        grad_oe,
        grad_boe,
    )


def solution(mesh):
    return jax.shard_map(
        per_device,
        mesh=mesh,
        in_specs=(
            P(("dp", "expert"), None),
            P(None, None, "dp"),
            P(None, None, "dp"),
            P(None, "dp", None),
            P(None, "dp", None),
            P(None, "dp", None),
            P(None, ("dp", "expert"), None),
            P(None, "expert", "dp", None),
            P(None, "expert", "dp"),
            P(None, "expert", "dp", None),
            P(None, "expert", "dp"),
            P(None, ("dp", "expert"), None),
            P(None, ("dp", "expert"), None),
            P(("dp", "expert"), None),
        ),
        out_specs=(
            P(("dp", "expert"), None),
            P(("dp", "expert"), None),
            P(None, None, "dp"),
            P(None, None, "dp"),
            P(None, "dp", None),
            P(None, "dp", None),
            P(None, "dp", None),
            P(None, "expert", "dp", None),
            P(None, "expert", "dp"),
            P(None, "expert", "dp", None),
            P(None, "expert", "dp"),
        ),
        check_vma=False,
    )
```
